32 devices in a mesh: chol: 8 (over z, y), walk: 4 (over x, core).
Axes of the slice: x: 2, y: 2, z: 4, core: 2. Of those that a mesh axis runs over, the one named last changes fastest.
Arguments:
- green_rows: bfloat16 [2048, 8, 256], P('chol', 'walk'), may hold values from -0.119628906 to 0.119628906
- cholesky_rot: bfloat16 [64, 256, 2048], P('chol'), may hold values from -0.125 to 0.125
- one_body: bfloat16 [2048, 256], P('chol'), may hold values from -0.25 to 0.25
- fields: float32 [64, 16], P('chol', 'walk'), may hold values from -5 to 5
- weights: float32 [8], P('walk'), may hold values from 0.3 to 3
- sources: int32 [16], P('walk'), may hold values from 0 to 7, as said below
- counts: int32 [4], replicated, may hold values from 0 to 4, as said below
- owners: int32 [4], replicated, may hold values from 0 to 3, each once
Outputs:
- energies: float32 [16], P('walk')
- new_weights: float32 [16], P('walk')
- density_panels: float32 [4, 131072], P('walk', 'chol')
The draws below stay inside these ranges and needn't reach their ends.
Inputs may be any that keep to these rules, and one draw needn't show every extreme that they name: Slot j of group g is live exactly when j < counts[g]; the counts sum to 8, and some group has all 4 slots live. `sources`: entries of slots that are not live are read by no output.
All inputs are finite; a program needn't handle non-finite values.
Results may differ from the reference program's by a relative error of at most 0.0003.
Values may be sent and summed in bfloat16 or wider, within the bound.
No kernel may reach another device: no remote copies, remote signals or barrier semaphores. Data moves between devices by JAX's collectives and lax.ppermute only.
A program may use at most 192 MiB of HBM per device.

```python
import math
import jax
import jax.numpy as jnp
from jax import lax

M = 2048
N = 256
CHOL_DEV = 8
W_CAP = 4
W_TOT = 8
W_SLOTS = 16
NCHOL = 64
N_WALK = 4


def draw_sources(key, part):
    return jax.random.randint(jax.random.fold_in(key, 11), (W_SLOTS,), 0, W_TOT).astype(jnp.int32)


def draw_counts(key, part):
    first_key = jax.random.fold_in(key, 21)
    second_key = jax.random.fold_in(key, 22)
    third_key = jax.random.fold_in(key, 23)
    fourth_key = jax.random.fold_in(key, 24)
    groups = N_WALK
    remaining = W_TOT - W_CAP
    base_count = remaining // (groups - 1)
    leftover = remaining - base_count * (groups - 1)
    full_group = jax.random.randint(first_key, (), 0, groups)
    others = jnp.full((groups - 1,), base_count, jnp.int32).at[0].add(leftover)
    donor = jax.random.randint(second_key, (), 0, groups - 1)
    stride = jax.random.randint(third_key, (), 1, groups - 1)
    taker = (donor + stride) % (groups - 1)
    moved = jax.random.randint(fourth_key, (), 0, base_count + 1)
    others = others.at[donor].add(-moved).at[taker].add(moved)
    group_ids = jnp.arange(groups, dtype=jnp.int32)
    placed = others[(group_ids - full_group - 1) % groups]
    return jnp.where(group_ids == full_group, W_CAP, placed).astype(jnp.int32)


def levels(stream_key, dims, split, least, high):
    def one(dim, shards_of):
        heights = jax.random.uniform(jax.random.fold_in(jax.random.fold_in(stream_key, 6), dim), (shards_of,), jnp.float32, least / len(split), high / len(split))
        return jnp.repeat(jnp.exp(heights), dims[dim] // shards_of).reshape((-1,) + (1,) * (len(dims) - dim - 1))

    gain = one(*split[0])
    for cut in split[1:]:
        gain = gain * one(*cut)
    return gain


def noise(stream_key, extent, spread, bound, shards=(), kind=jnp.bfloat16):
    drawn = jax.random.normal(stream_key, extent, jnp.float32) * spread
    if len(shards) > 0:
        drawn = levels(stream_key, extent, shards, -0.22, 0.18) * drawn
    return jnp.clip(drawn, min=-bound, max=bound).astype(kind)


def setup_inputs(seed: int = 0) -> dict:
    key_list = jax.random.split(jax.random.key(seed), 9)
    return {
        "green_rows": noise(key_list[0], (M, W_TOT, N), 0.02, 0.119628906, ((0, 8), (1, 4))),
        "cholesky_rot": noise(key_list[1], (NCHOL, N, M), M ** -0.5, 0.125, ((0, 8),)),
        "one_body": noise(key_list[2], (M, N), (M // 4) ** -0.5, 0.25, ((0, 8),)),
        "fields": noise(key_list[3], (NCHOL, W_SLOTS), 1.0, 5.0, ((0, 8), (1, 4)), jnp.float32),
        "weights": jnp.clip(jnp.exp(math.log(3.0) - 2.3025851 * jax.random.uniform(key_list[4], (W_TOT,), jnp.float32) ** levels(key_list[4], (W_TOT,), ((0, 4),), -0.2, 0.2)), 0.3, 3.0),
        "sources": draw_sources(jax.random.fold_in(key_list[8], 71), 0),
        "counts": draw_counts(jax.random.fold_in(key_list[8], 71), 0),
        "owners": jax.random.permutation(key_list[7], N_WALK).astype(jnp.int32),
    }


time_step = 0.02
root_step = 0.02 ** 0.5


def reference(green_rows, cholesky_rot, one_body, fields, weights, sources, counts, owners):
    theta = green_rows.astype(jnp.float32)
    blocks = cholesky_rot.reshape(NCHOL // CHOL_DEV, CHOL_DEV, N, M)

    def measure(block):
        tensor = jnp.einsum("cim,mbj->cibj", block.astype(jnp.float32), theta, precision=lax.Precision.HIGHEST)
        traces = jnp.sum(jnp.diagonal(tensor, axis1=1, axis2=3), axis=-1)
        exchange = jnp.einsum("cibj,cjbi->b", tensor, tensor, precision=lax.Precision.HIGHEST)
        return traces, exchange

    trace_blocks, exchange_blocks = lax.map(measure, blocks)
    traces = trace_blocks.reshape(NCHOL, W_TOT)
    exchange = jnp.sum(exchange_blocks, axis=0)
    squares = jnp.sum(traces * traces, axis=0)
    onebody = jnp.einsum("mbn,mn->b", theta, one_body.astype(jnp.float32), precision=lax.Precision.HIGHEST)
    slot_ids = jnp.arange(W_SLOTS, dtype=jnp.int32)
    live = (slot_ids % W_CAP < counts[slot_ids // W_CAP]).astype(jnp.float32)
    raw_energy = onebody[sources] + 0.5 * squares[sources] - 0.5 * exchange[sources]
    energies = live * raw_energy
    drive = -root_step * jnp.sum(fields * traces[:, sources], axis=0)
    mean_weight = jnp.sum(weights) / W_TOT
    new_weights = live * mean_weight * jnp.exp(drive - 0.5 * time_step * squares[sources] - time_step * raw_energy)
    pick = (sources[:, None] == jnp.arange(W_TOT, dtype=jnp.int32)[None, :]).astype(jnp.float32)
    summed = jnp.dot(new_weights, pick, precision=lax.Precision.HIGHEST)
    density = jnp.einsum("b,mbj->mj", summed, theta, precision=lax.Precision.HIGHEST) / jnp.sum(new_weights)
    panels = density.reshape(M, N_WALK, N // N_WALK)
    onehot = (owners[None, :] == jnp.arange(N_WALK, dtype=jnp.int32)[:, None]).astype(jnp.float32)
    arranged = jnp.einsum("kp,mpc->kmc", onehot, panels, precision=lax.Precision.HIGHEST)
    return energies, new_weights, arranged.reshape(N_WALK, M * N // N_WALK)
```

```python
import functools

import jax
import jax.numpy as jnp
from jax import lax
from jax.experimental import pallas as pl
from jax.experimental.pallas import tpu as pltpu
from jax.sharding import PartitionSpec as P

time_step = 0.02
root_step = 0.02**0.5
LANES = 128
VMEM_LIMIT = 48 * 1024 * 1024
RING_LIMIT = 16


def params(**more):
    return pltpu.CompilerParams(vmem_limit_bytes=VMEM_LIMIT, **more)


def vmem():
    return pl.BlockSpec(memory_space=pltpu.VMEM)


def smem():
    return pl.BlockSpec(memory_space=pltpu.SMEM)


def ring_order(size):
    return [2 * q if q < size // 2 else 2 * (size - 1 - q) + 1 for q in range(size)]


def ring_place(index, size):
    return jnp.where(index % 2 == 0, index // 2, size - 1 - index // 2)


def ring_owner(place, size):
    return jnp.where(place < size // 2, 2 * place, 2 * (size - 1 - place) + 1)


def split_walkers(green_rows):
    rows, walkers, orbitals = green_rows.shape

    def kernel(green_ref, *outs):
        for b in range(walkers):
            outs[b][...] = green_ref[:, b, :]

    return pl.pallas_call(
        kernel,
        name="split_walkers",
        out_shape=[jax.ShapeDtypeStruct((rows, orbitals), green_rows.dtype)] * walkers,
        in_specs=[vmem()],
        out_specs=[vmem()] * walkers,
        compiler_params=params(),
        cost_estimate=pl.CostEstimate(flops=0, bytes_accessed=4 * rows * walkers * orbitals, transcendentals=0),
    )(green_rows)


def gather_rows(blocks):
    size = lax.axis_size("chol")
    if size > RING_LIMIT or size % 2:
        return [(None, [lax.all_gather(x, "chol", axis=0, tiled=True) for x in blocks])]
    order = ring_order(size)
    ahead = [(order[q], order[(q + 1) % size]) for q in range(size)]
    back = [(order[q], order[(q - 1) % size]) for q in range(size)]
    parts = [(0, blocks)]
    right, left = blocks, blocks
    half = len(blocks) // 2
    for step in range(1, size // 2):
        right = [lax.ppermute(x, "chol", ahead) for x in right]
        left = [lax.ppermute(x, "chol", back) for x in left]
        parts.append((-step, right))
        parts.append((step, left))
    last = [lax.ppermute(x, "chol", ahead) for x in right[:half]]
    last += [lax.ppermute(x, "chol", back) for x in left[half:]]
    parts.append((size // 2, last))
    return parts


def pack(blocks, one_body, fields, weights, sources, owners):
    rows, orbitals = blocks[0].shape
    walk_size = lax.axis_size("walk")
    walkers = len(blocks)
    width = orbitals // walk_size
    pair = LANES // width
    vectors, slots = fields.shape
    table_rows = -(-(vectors + 2) // 8) * 8

    def kernel(*refs):
        green = refs[:walkers]
        body_ref, fields_ref, weights_ref, sources_ref, owners_ref = refs[walkers : walkers + 5]
        panels = refs[walkers + 5 : walkers + 5 + walk_size]
        onebody_ref, table_ref = refs[walkers + 5 + walk_size :]
        walk = lax.axis_index("walk")
        lane = lax.broadcasted_iota(jnp.int32, (1, LANES), 1)
        body = body_ref[...].astype(jnp.float32)
        onebody_ref[...] = jnp.zeros_like(onebody_ref)
        for b in range(walkers):
            total = jnp.sum(green[b][...].astype(jnp.float32) * body, axis=0, keepdims=True)
            folded = total[:, :LANES]
            for start in range(LANES, orbitals, LANES):
                folded = folded + total[:, start : start + LANES]
            onebody_ref[b : b + 1, :] = folded
        r = lax.broadcasted_iota(jnp.int32, (rows // pair, rows), 0)
        m = lax.broadcasted_iota(jnp.int32, (rows // pair, rows), 1)
        k = lax.broadcasted_iota(jnp.int32, (orbitals, LANES), 0)
        c = lax.broadcasted_iota(jnp.int32, (orbitals, LANES), 1)
        thinned = []
        for b in range(walkers):
            values = green[b][...]
            thinned.append(
                [
                    jnp.dot(
                        (m == r * pair + h).astype(jnp.bfloat16), values, preferred_element_type=jnp.float32
                    ).astype(jnp.bfloat16)
                    for h in range(pair)
                ]
            )
        for d in range(walk_size):
            target = lax.rem(walk + d, walk_size)
            panel = jnp.int32(0)
            for p in range(walk_size):
                panel = jnp.where(owners_ref[p] == target, p, panel)
            for b in range(walkers):
                total = jnp.zeros((rows // pair, LANES), jnp.float32)
                for h in range(pair):
                    take = (k == panel * width + c - h * width) & (c >= h * width) & (c < (h + 1) * width)
                    total += jnp.dot(
                        thinned[b][h], take.astype(jnp.bfloat16), preferred_element_type=jnp.float32
                    )
                panels[d][b] = total.astype(jnp.bfloat16)
        spread = jnp.zeros((vectors, LANES), jnp.float32)
        source = jnp.zeros((1, LANES), jnp.float32)
        for j in range(slots):
            mine = lane % slots == j
            spread += jnp.where(mine, fields_ref[:, j : j + 1], 0.0)
            source += jnp.where(mine, sources_ref[j].astype(jnp.float32), 0.0)
        weight = weights_ref[0]
        for j in range(1, weights.shape[0]):
            weight = weight + weights_ref[j]
        table_ref[...] = jnp.zeros_like(table_ref)
        table_ref[:vectors, :] = spread
        table_ref[vectors : vectors + 1, :] = source
        table_ref[vectors + 1 : vectors + 2, :] = jnp.zeros((1, LANES), jnp.float32) + weight

    out = pl.pallas_call(
        kernel,
        name="pack",
        out_shape=[jax.ShapeDtypeStruct((walkers, rows // pair, LANES), jnp.bfloat16)] * walk_size
        + [jax.ShapeDtypeStruct((8, LANES), jnp.float32), jax.ShapeDtypeStruct((table_rows, LANES), jnp.float32)],
        in_specs=[vmem()] * (walkers + 2) + [smem()] * 3,
        out_specs=[vmem()] * (walk_size + 2),
        compiler_params=params(),
        cost_estimate=pl.CostEstimate(flops=10**8, bytes_accessed=10**6, transcendentals=0),
    )(*blocks, one_body, fields, weights, sources, owners)
    return out[:walk_size], out[walk_size], out[walk_size + 1]


def shifted(x, d):
    size = lax.axis_size("walk")
    return lax.ppermute(x, "walk", [(q, (q + d) % size) for q in range(size)])


def merge_tables(tables, rows, walk, walk_size, slots, lane):
    total = jnp.zeros((rows, LANES), jnp.float32)
    for d, table in enumerate(tables):
        group = lax.rem(walk - d + walk_size, walk_size)
        total += jnp.where(lane // slots == group, table[:rows, :], 0.0)
    return total


def measure(cholesky_rot, parts, tables, onebody, slots):
    vectors, orbitals, basis = cholesky_rot.shape
    walkers = len(parts[0][1])
    walk_size = len(tables)
    chol_size = lax.axis_size("chol")
    shards = [x for _, arrays in parts for x in arrays]
    spots = [(shift, b) for shift, _ in parts for b in range(walkers)]
    eye_blocks = orbitals // LANES

    def kernel(*refs):
        chol_ref = refs[0]
        table_refs = refs[1 : 1 + walk_size]
        onebody_ref = refs[1 + walk_size]
        shard_refs = refs[2 + walk_size : 2 + walk_size + len(shards)]
        out_ref, rows_scr, exchange_scr, small_scr, sem = refs[2 + walk_size + len(shards) :]
        g = pl.program_id(0)
        walk = lax.axis_index("walk")
        chol = lax.axis_index("chol")
        lane = lax.broadcasted_iota(jnp.int32, (1, LANES), 1)
        tables_here = merge_tables([t[...] for t in table_refs], vectors + 1, walk, walk_size, slots, lane)
        picks = [
            jnp.where(
                (lane < slots * walk_size) & (tables_here[vectors : vectors + 1, :] == (walk * walkers + b).astype(jnp.float32)),
                1.0,
                0.0,
            )
            for b in range(walkers)
        ]

        @pl.when(g == 0)
        def _():
            place = ring_place(chol, chol_size)
            copies = []
            for n, (shard, (shift, b)) in enumerate(zip(shard_refs, spots)):
                rows = shard.shape[0]
                if shift is None:
                    start = 0
                else:
                    owner = ring_owner(lax.rem(place + shift + chol_size, chol_size), chol_size)
                    start = pl.multiple_of(owner * rows, rows)
                copies.append(
                    pltpu.make_async_copy(
                        shard,
                        rows_scr.at[pl.ds(start, rows), pl.ds(b * orbitals, orbitals)],
                        sem.at[n],
                    )
                )
            for copy in copies:
                copy.start()
            exchange_scr[...] = jnp.zeros_like(exchange_scr)
            small_scr[...] = jnp.zeros_like(small_scr)
            for copy in copies:
                copy.wait()

        tensor = jnp.dot(chol_ref[0], rows_scr[...], preferred_element_type=jnp.float32)
        row = lax.broadcasted_iota(jnp.int32, (LANES, LANES), 0)
        col = lax.broadcasted_iota(jnp.int32, (LANES, LANES), 1)
        eye = row == col
        field = jnp.sum(
            jnp.where(
                lax.broadcasted_iota(jnp.int32, (vectors, LANES), 0) == g, tables_here[:vectors, :], 0.0
            ),
            axis=0,
            keepdims=True,
        )
        drive = small_scr[walkers : walkers + 1, :]
        for b in range(walkers):
            block = tensor[:, b * orbitals : (b + 1) * orbitals]
            exchange_scr[b : b + 1, :] += jnp.sum(block * block.T, axis=0, keepdims=True)
            diagonal = jnp.zeros((1, LANES), jnp.float32)
            for q in range(eye_blocks):
                piece = block[q * LANES : (q + 1) * LANES, q * LANES : (q + 1) * LANES]
                diagonal += jnp.sum(jnp.where(eye, piece, 0.0), axis=0, keepdims=True)
            trace = jnp.sum(diagonal, axis=1, keepdims=True)
            small_scr[b : b + 1, :] += jnp.broadcast_to(trace * trace, (1, LANES))
            drive = drive - root_step * picks[b] * field * trace
        small_scr[walkers : walkers + 1, :] = drive

        @pl.when(g == vectors - 1)
        def _():
            raw = jnp.zeros((1, LANES), jnp.float32)
            squares = jnp.zeros((1, LANES), jnp.float32)
            for b in range(walkers):
                exchange = jnp.sum(exchange_scr[b : b + 1, :], axis=1, keepdims=True)
                single = jnp.sum(onebody_ref[b : b + 1, :], axis=1, keepdims=True)
                square = small_scr[b : b + 1, :]
                raw += picks[b] * (single + 0.5 * square - 0.5 * exchange)
                squares += picks[b] * square
            power = drive - 0.5 * time_step * squares - time_step * raw
            out_ref[...] = raw + pltpu.roll(power, slots * walk_size, 1)

    return pl.pallas_call(
        kernel,
        name="measure",
        grid=(vectors,),
        out_shape=jax.ShapeDtypeStruct((1, LANES), jnp.float32),
        in_specs=[pl.BlockSpec((1, orbitals, basis), lambda g: (g, 0, 0))]
        + [vmem()] * (walk_size + 1)
        + [pl.BlockSpec(memory_space=pl.ANY)] * len(shards),
        out_specs=vmem(),
        scratch_shapes=[
            pltpu.VMEM((basis, walkers * orbitals), jnp.bfloat16),
            pltpu.VMEM((8, orbitals), jnp.float32),
            pltpu.VMEM((8, LANES), jnp.float32),
            pltpu.SemaphoreType.DMA((len(shards),)),
        ],
        compiler_params=params(dimension_semantics=("arbitrary",)),
        cost_estimate=pl.CostEstimate(
            flops=2 * vectors * orbitals * basis * walkers * orbitals,
            bytes_accessed=2 * vectors * orbitals * basis,
            transcendentals=0,
        ),
    )(cholesky_rot, *tables, onebody, *shards)


def finish(stats, tables, panels, counts, vectors, slots):
    walk_size = len(tables)
    walkers, rows, _ = panels[0].shape

    def kernel(stats_ref, counts_ref, *refs):
        table_refs = refs[:walk_size]
        panel_refs = refs[walk_size : 2 * walk_size]
        energies_ref, weights_ref, density_ref = refs[2 * walk_size :]
        walk = lax.axis_index("walk")
        lane = lax.broadcasted_iota(jnp.int32, (1, LANES), 1)
        all_slots = slots * walk_size
        source = merge_tables(
            [t[vectors : vectors + 1, :] for t in table_refs], 1, walk, walk_size, slots, lane
        )
        total_weight = table_refs[0][vectors + 1 : vectors + 2, :]
        for t in table_refs[1:]:
            total_weight = total_weight + t[vectors + 1 : vectors + 2, :]
        mean_weight = total_weight / (walkers * walk_size)
        total = jnp.sum(stats_ref[...], axis=0, keepdims=True)
        power = pltpu.roll(total, LANES - all_slots, 1)
        live_count = jnp.zeros((1, LANES), jnp.int32)
        for q in range(walk_size):
            live_count = jnp.where(lane // slots == q, counts_ref[q], live_count)
        live = (lane < all_slots) & (lane % slots < live_count)
        energies = jnp.where(live, total, 0.0)
        new_weights = jnp.where(live, mean_weight * jnp.exp(jnp.where(live, power, 0.0)), 0.0)
        norm = jnp.sum(new_weights, axis=1, keepdims=True)
        density = jnp.zeros((rows, LANES), jnp.float32)
        for d in range(walk_size):
            group = lax.rem(walk - d + walk_size, walk_size)
            for b in range(walkers):
                walker = (group * walkers + b).astype(jnp.float32)
                share = jnp.sum(jnp.where(source == walker, new_weights, 0.0), axis=1, keepdims=True) / norm
                density += share * panel_refs[d][b].astype(jnp.float32)
        density_ref[...] = density
        first = lax.rem(LANES - walk * slots, LANES)
        energies_ref[...] = pltpu.roll(jnp.broadcast_to(energies, (8, LANES)), first, 1)[:1, :slots]
        weights_ref[...] = pltpu.roll(jnp.broadcast_to(new_weights, (8, LANES)), first, 1)[:1, :slots]

    return pl.pallas_call(
        kernel,
        name="finish",
        out_shape=[
            jax.ShapeDtypeStruct((1, slots), jnp.float32),
            jax.ShapeDtypeStruct((1, slots), jnp.float32),
            jax.ShapeDtypeStruct((rows, LANES), jnp.float32),
        ],
        in_specs=[vmem(), smem()] + [vmem()] * (2 * walk_size),
        out_specs=[vmem()] * 3,
        compiler_params=params(),
        cost_estimate=pl.CostEstimate(flops=10**6, bytes_accessed=6 * 10**5, transcendentals=128),
    )(stats, counts, *tables, *panels)


def per_device(green_rows, cholesky_rot, one_body, fields, weights, sources, counts, owners):
    walk_size = lax.axis_size("walk")
    vectors, slots = fields.shape
    blocks = split_walkers(green_rows)
    parts = gather_rows(blocks)
    panels, onebody, table = pack(blocks, one_body, fields, weights, sources, owners)
    panels = [panels[0]] + [shifted(panels[d], d) for d in range(1, walk_size)]
    tables = [table] + [shifted(table, d) for d in range(1, walk_size)]
    stats = measure(cholesky_rot, parts, tables, onebody, slots)
    stats = lax.all_gather(stats, ("chol", "walk"), axis=0, tiled=True)
    energies, new_weights, density = finish(stats, tables, panels, counts, vectors, slots)
    return energies.reshape(slots), new_weights.reshape(slots), density.reshape(1, density.size)


def solution(mesh):
    return jax.shard_map(
        per_device,
        mesh=mesh,
        in_specs=(
            P("chol", "walk", None),
            P("chol", None, None),
            P("chol", None),
            P("chol", "walk"),
            P("walk"),
            P("walk"),
            P(),
            P(),
        ),
        out_specs=(P("walk"), P("walk"), P("walk", "chol")),
        check_vma=False,
    )
```

```python
import functools

import jax
import jax.numpy as jnp
from jax import lax
from jax.experimental import pallas as pl
from jax.experimental.pallas import tpu as pltpu
from jax.sharding import PartitionSpec as P

time_step = 0.02
root_step = 0.02**0.5
LANES = 128
VMEM_LIMIT = 16 * 1024 * 1024
RING_LIMIT = 16


def params(**more):
    return pltpu.CompilerParams(vmem_limit_bytes=VMEM_LIMIT, **more)


def vmem():
    return pl.BlockSpec(memory_space=pltpu.VMEM)


def smem():
    return pl.BlockSpec(memory_space=pltpu.SMEM)


def ring_order(size):
    return [2 * q if q < size // 2 else 2 * (size - 1 - q) + 1 for q in range(size)]


def ring_place(index, size):
    return jnp.where(index % 2 == 0, index // 2, size - 1 - index // 2)


def ring_owner(place, size):
    return jnp.where(place < size // 2, 2 * place, 2 * (size - 1 - place) + 1)


def split_walkers(green_rows):
    rows, walkers, orbitals = green_rows.shape
    steps = 4 if rows % 64 == 0 else 1

    def kernel(green_ref, out_ref):
        for b in range(walkers):
            out_ref[:, b * orbitals : (b + 1) * orbitals] = green_ref[:, b, :]

    return pl.pallas_call(
        kernel,
        name="split_walkers",
        grid=(steps,),
        out_shape=jax.ShapeDtypeStruct((rows, walkers * orbitals), green_rows.dtype),
        in_specs=[pl.BlockSpec((rows // steps, walkers, orbitals), lambda n: (n, 0, 0))],
        out_specs=pl.BlockSpec((rows // steps, walkers * orbitals), lambda n: (n, 0)),
        compiler_params=params(),
        cost_estimate=pl.CostEstimate(flops=0, bytes_accessed=4 * rows * walkers * orbitals, transcendentals=0),
    )(green_rows)


def column_start(shift, rows):
    size = lax.axis_size("chol")
    place = ring_place(lax.axis_index("chol"), size)
    owner = ring_owner(lax.rem(place + shift + size, size), size)
    return pl.multiple_of(owner * rows, rows)


def accumulate(cholesky_rot, parts, total, mark, fetch):
    vectors, orbitals, _ = cholesky_rot.shape
    rows, columns = parts[0][1].shape
    shifts = [shift for shift, _ in parts]
    count = len(parts)
    fresh = total is None

    def kernel(chol_ref, *refs):
        ins = refs[: len(arrays)]
        outs = refs[len(arrays) : len(arrays) + len(shapes)]
        blocks_scr, sems = refs[len(arrays) + len(shapes) :][:2]
        copies = []
        for n, shift in enumerate(shifts):
            start = column_start(shift, rows)
            copies.append(
                [
                    pltpu.make_async_copy(
                        chol_ref.at[g, :, pl.ds(start, rows)], blocks_scr.at[n, g], sems.at[n, g]
                    )
                    for g in range(vectors)
                ]
            )
        for g in range(vectors):
            for n in range(count):
                copies[n][g].start()
        if fetch is not None:
            ahead = pltpu.make_async_copy(
                chol_ref.at[:, :, pl.ds(column_start(fetch, rows), rows)], outs[2], refs[-1]
            )
            ahead.start()
        outs[1][...] = jnp.zeros_like(outs[1])
        for g in range(vectors):
            value = None if fresh else ins[count + 1][g]
            for n in range(count):
                copies[n][g].wait()
                term = jnp.dot(blocks_scr[n, g], ins[n][...], preferred_element_type=jnp.float32)
                value = term if value is None else value + term
            outs[0][g] = value
        if fetch is not None:
            ahead.wait()

    arrays = [x for _, x in parts] + [mark] + ([] if fresh else [total])
    shapes = [
        jax.ShapeDtypeStruct((vectors, orbitals, columns), jnp.float32),
        jax.ShapeDtypeStruct((8, LANES), jnp.float32),
    ]
    if fetch is not None:
        shapes.append(jax.ShapeDtypeStruct((vectors, orbitals, rows), cholesky_rot.dtype))
    return pl.pallas_call(
        kernel,
        name="accumulate",
        out_shape=shapes,
        in_specs=[pl.BlockSpec(memory_space=pl.ANY)] + [vmem()] * len(arrays),
        out_specs=[vmem()] * len(shapes),
        scratch_shapes=[
            pltpu.VMEM((count, vectors, orbitals, rows), cholesky_rot.dtype),
            pltpu.SemaphoreType.DMA((count, vectors)),
        ]
        + ([] if fetch is None else [pltpu.SemaphoreType.DMA]),
        compiler_params=params(),
        cost_estimate=pl.CostEstimate(
            flops=2 * count * vectors * orbitals * rows * columns,
            bytes_accessed=2 * count * vectors * orbitals * rows,
            transcendentals=0,
        ),
    )(cholesky_rot, *arrays)


def tie(*arrays):
    return lax.optimization_barrier(arrays)


def ring(cholesky_rot, own, packed):
    size = lax.axis_size("chol")
    rows, _ = own.shape
    order = ring_order(size)
    ahead = [(order[q], order[(q + 1) % size]) for q in range(size)]
    back = [(order[q], order[(q - 1) % size]) for q in range(size)]
    right = left = own
    parts = [(0, own)]
    total = None
    mark = packed[-1]
    steps = size // 2
    for step in range(1, steps):
        next_right = lax.ppermute(right, "chol", ahead)
        next_left = lax.ppermute(left, "chol", back)
        total, mark = accumulate(cholesky_rot, parts, total, mark, None)
        if step == 1:
            others = [shifted(packed[d], d) for d in range(1, len(packed) - 1)]
        if step == min(2, steps - 1):
            right, left, mark, *others = tie(next_right, next_left, mark, *others)
        else:
            right, left, mark = tie(next_right, next_left, mark)
        parts = [(-step, right), (step, left)]
    first = lax.ppermute(right[: rows // 2], "chol", ahead)
    second = lax.ppermute(left[rows // 2 :], "chol", back)
    total, _, block = accumulate(cholesky_rot, parts, total, mark, steps)
    return total, block, [first, second], [packed[0]] + others


def table_height(vectors):
    return -(-(vectors + 2) // 16) * 16


def pack(own, one_body, fields, weights, sources, owners):
    rows, orbitals = one_body.shape
    walk_size = lax.axis_size("walk")
    walkers = own.shape[1] // orbitals
    width = orbitals // walk_size
    pair = LANES // width
    vectors, slots = fields.shape
    table_rows = table_height(vectors)
    height = walkers * (rows // pair) + 3 * table_rows

    def kernel(*refs):
        own_ref, body_ref, fields_ref, weights_ref, sources_ref, owners_ref = refs[:6]
        packs = refs[6 : 6 + walk_size]
        onebody_ref, table_scr = refs[6 + walk_size :]
        green = [own_ref[:, b * orbitals : (b + 1) * orbitals] for b in range(walkers)]
        walk = lax.axis_index("walk")
        lane = lax.broadcasted_iota(jnp.int32, (1, LANES), 1)
        body = body_ref[...].astype(jnp.float32)
        onebody_ref[...] = jnp.zeros_like(onebody_ref)
        for b in range(walkers):
            total = jnp.sum(green[b].astype(jnp.float32) * body, axis=0, keepdims=True)
            folded = total[:, :LANES]
            for start in range(LANES, orbitals, LANES):
                folded = folded + total[:, start : start + LANES]
            onebody_ref[b : b + 1, :] = folded
        r = lax.broadcasted_iota(jnp.int32, (rows // pair, rows), 0)
        m = lax.broadcasted_iota(jnp.int32, (rows // pair, rows), 1)
        k = lax.broadcasted_iota(jnp.int32, (orbitals, LANES), 0)
        c = lax.broadcasted_iota(jnp.int32, (orbitals, LANES), 1)
        thinned = []
        for b in range(walkers):
            values = green[b]
            thinned.append(
                [
                    jnp.dot(
                        (m == r * pair + h).astype(jnp.bfloat16), values, preferred_element_type=jnp.float32
                    ).astype(jnp.bfloat16)
                    for h in range(pair)
                ]
            )
        for d in range(walk_size):
            target = lax.rem(walk + d, walk_size)
            panel = jnp.int32(0)
            for p in range(walk_size):
                panel = jnp.where(owners_ref[p] == target, p, panel)
            for b in range(walkers):
                total = jnp.zeros((rows // pair, LANES), jnp.float32)
                for h in range(pair):
                    take = (k == panel * width + c - h * width) & (c >= h * width) & (c < (h + 1) * width)
                    total += jnp.dot(
                        thinned[b][h], take.astype(jnp.bfloat16), preferred_element_type=jnp.float32
                    )
                packs[d][b * (rows // pair) : (b + 1) * (rows // pair), :] = total.astype(jnp.bfloat16)
        spread = jnp.zeros((vectors, LANES), jnp.float32)
        source = jnp.zeros((1, LANES), jnp.float32)
        for j in range(slots):
            mine = lane % slots == j
            spread += jnp.where(mine, fields_ref[:, j : j + 1], 0.0)
            source += jnp.where(mine, sources_ref[j].astype(jnp.float32), 0.0)
        weight = weights_ref[0]
        for j in range(1, weights.shape[0]):
            weight = weight + weights_ref[j]
        table_scr[...] = jnp.zeros_like(table_scr)
        table_scr[:vectors, :] = spread
        table_scr[vectors : vectors + 1, :] = source
        table_scr[vectors + 1 : vectors + 2, :] = jnp.zeros((1, LANES), jnp.float32) + weight
        rest = table_scr[...]
        for n in range(3):
            piece = rest.astype(jnp.bfloat16)
            rest = rest - piece.astype(jnp.float32)
            at = walkers * (rows // pair) + n * table_rows
            for d in range(walk_size):
                packs[d][at : at + table_rows, :] = piece

    out = pl.pallas_call(
        kernel,
        name="pack",
        out_shape=[jax.ShapeDtypeStruct((height, LANES), jnp.bfloat16)] * walk_size
        + [jax.ShapeDtypeStruct((8, LANES), jnp.float32)],
        in_specs=[vmem()] * 3 + [smem()] * 3,
        out_specs=[vmem()] * (walk_size + 1),
        scratch_shapes=[pltpu.VMEM((table_rows, LANES), jnp.float32)],
        compiler_params=params(),
        cost_estimate=pl.CostEstimate(flops=10**8, bytes_accessed=10**6, transcendentals=0),
    )(own, one_body, fields, weights, sources, owners)
    return out


def shifted(x, d):
    size = lax.axis_size("walk")
    return lax.ppermute(x, "walk", [(q, (q + d) % size) for q in range(size)])


def read_table(ref, vectors):
    height = table_height(vectors)
    start = ref.shape[0] - 3 * height
    parts = [ref[start + n * height : start + (n + 1) * height, :].astype(jnp.float32) for n in range(3)]
    return parts[0] + (parts[1] + parts[2])


def merge_tables(tables, walk, walk_size, slots, lane):
    total = jnp.zeros_like(tables[0])
    for d, table in enumerate(tables):
        group = lax.rem(walk - d + walk_size, walk_size)
        total += jnp.where(lane // slots == group, table, 0.0)
    return total


def measure(block, total, last, packs, onebody, slots):
    vectors, orbitals, depth = block.shape
    columns = last[0].shape[1]
    walkers = columns // orbitals
    walk_size = len(packs)
    devices = walk_size * lax.axis_size("chol")
    whole = total is None
    quads = orbitals // LANES

    def fold(x):
        return jnp.sum(x.reshape(-1, 8, LANES), axis=0)

    def kernel(*refs):
        block_ref, onebody_ref = refs[:2]
        pack_refs = refs[2 : 2 + walk_size]
        last_refs = refs[2 + walk_size : 2 + walk_size + len(last)]
        out_ref, depth_scr, tensor_scr = refs[-3:]
        walk = lax.axis_index("walk")
        lane = lax.broadcasted_iota(jnp.int32, (1, LANES), 1)
        table = merge_tables([read_table(x, vectors) for x in pack_refs], walk, walk_size, slots, lane)
        picks = [
            jnp.where(
                (lane < slots * walk_size) & (table[vectors : vectors + 1, :] == (walk * walkers + b).astype(jnp.float32)),
                1.0,
                0.0,
            )
            for b in range(walkers)
        ]
        at = 0
        for x in last_refs:
            depth_scr[at : at + x.shape[0], :] = x[...]
            at += x.shape[0]
        eye = lax.broadcasted_iota(jnp.int32, (LANES, LANES), 0) == lax.broadcasted_iota(
            jnp.int32, (LANES, LANES), 1
        )
        exchange = [jnp.zeros((8, LANES), jnp.float32) for _ in range(walkers)]
        squares = [jnp.zeros((1, 1), jnp.float32) for _ in range(walkers)]
        drive = jnp.zeros((1, LANES), jnp.float32)
        for g in range(vectors):
            value = jnp.dot(block_ref[g], depth_scr[...], preferred_element_type=jnp.float32)
            if not whole:
                value = value + refs[2 + walk_size + len(last)][g]
            tensor_scr[g % 2] = value
            for b in range(walkers):
                diagonal = jnp.zeros((LANES, LANES), jnp.float32)
                for q in range(quads):
                    for p in range(q + 1):
                        one = tensor_scr[
                            g % 2,
                            q * LANES : (q + 1) * LANES,
                            b * orbitals + p * LANES : b * orbitals + (p + 1) * LANES,
                        ]
                        if p == q:
                            exchange[b] = exchange[b] + fold(one * one.T)
                            diagonal = diagonal + one
                        else:
                            two = tensor_scr[
                                g % 2,
                                p * LANES : (p + 1) * LANES,
                                b * orbitals + q * LANES : b * orbitals + (q + 1) * LANES,
                            ]
                            exchange[b] = exchange[b] + 2.0 * fold(two * one.T)
                trace = jnp.sum(fold(jnp.where(eye, diagonal, 0.0)), axis=0, keepdims=True)
                trace = jnp.sum(trace, axis=1, keepdims=True)
                squares[b] = squares[b] + trace * trace
                drive = drive - root_step * picks[b] * table[g : g + 1, :] * trace
        raw = jnp.zeros((1, LANES), jnp.float32)
        square = jnp.zeros((1, LANES), jnp.float32)
        for b in range(walkers):
            swapped = jnp.sum(jnp.sum(exchange[b], axis=0, keepdims=True), axis=1, keepdims=True)
            single = jnp.sum(onebody_ref[b : b + 1, :], axis=1, keepdims=True)
            raw += picks[b] * (single + 0.5 * squares[b] - 0.5 * swapped)
            square += picks[b] * squares[b]
        power = drive - 0.5 * time_step * square - time_step * raw
        out_ref[...] = jnp.broadcast_to(raw + pltpu.roll(power, slots * walk_size, 1), (devices, LANES))

    arrays = list(last) + ([] if whole else [total])
    return pl.pallas_call(
        kernel,
        name="measure",
        out_shape=jax.ShapeDtypeStruct((devices, LANES), jnp.float32),
        in_specs=[vmem()] * (2 + walk_size + len(arrays)),
        out_specs=vmem(),
        scratch_shapes=[
            pltpu.VMEM((depth, columns), jnp.bfloat16),
            pltpu.VMEM((2, orbitals, columns), jnp.float32),
        ],
        compiler_params=params(),
        cost_estimate=pl.CostEstimate(
            flops=2 * vectors * orbitals * depth * columns,
            bytes_accessed=4 * vectors * orbitals * columns,
            transcendentals=0,
        ),
    )(block, onebody, *packs, *arrays)


def finish(stats, packs, counts, vectors, slots, walkers):
    walk_size = len(packs)
    rows = (packs[0].shape[0] - 3 * table_height(vectors)) // walkers

    def kernel(stats_ref, counts_ref, *refs):
        pack_refs = refs[:walk_size]
        energies_ref, weights_ref, density_ref = refs[walk_size:]
        walk = lax.axis_index("walk")
        lane = lax.broadcasted_iota(jnp.int32, (1, LANES), 1)
        all_slots = slots * walk_size
        tables = [read_table(x, vectors) for x in pack_refs]
        source = merge_tables([t[vectors : vectors + 1, :] for t in tables], walk, walk_size, slots, lane)
        total_weight = tables[0][vectors + 1 : vectors + 2, :]
        for t in tables[1:]:
            total_weight = total_weight + t[vectors + 1 : vectors + 2, :]
        mean_weight = total_weight / (walkers * walk_size)
        total = jnp.sum(stats_ref[...], axis=0, keepdims=True)
        power = pltpu.roll(total, LANES - all_slots, 1)
        live_count = jnp.zeros((1, LANES), jnp.int32)
        for q in range(walk_size):
            live_count = jnp.where(lane // slots == q, counts_ref[q], live_count)
        live = (lane < all_slots) & (lane % slots < live_count)
        energies = jnp.where(live, total, 0.0)
        new_weights = jnp.where(live, mean_weight * jnp.exp(jnp.where(live, power, 0.0)), 0.0)
        norm = jnp.sum(new_weights, axis=1, keepdims=True)
        density = jnp.zeros((rows, LANES), jnp.float32)
        for d in range(walk_size):
            group = lax.rem(walk - d + walk_size, walk_size)
            for b in range(walkers):
                walker = (group * walkers + b).astype(jnp.float32)
                share = jnp.sum(jnp.where(source == walker, new_weights, 0.0), axis=1, keepdims=True) / norm
                density += share * pack_refs[d][b * rows : (b + 1) * rows, :].astype(jnp.float32)
        density_ref[...] = density
        first = lax.rem(LANES - walk * slots, LANES)
        energies_ref[...] = pltpu.roll(jnp.broadcast_to(energies, (8, LANES)), first, 1)[:1, :slots]
        weights_ref[...] = pltpu.roll(jnp.broadcast_to(new_weights, (8, LANES)), first, 1)[:1, :slots]

    return pl.pallas_call(
        kernel,
        name="finish",
        out_shape=[
            jax.ShapeDtypeStruct((1, slots), jnp.float32),
            jax.ShapeDtypeStruct((1, slots), jnp.float32),
            jax.ShapeDtypeStruct((rows, LANES), jnp.float32),
        ],
        in_specs=[vmem(), smem()] + [vmem()] * walk_size,
        out_specs=[vmem()] * 3,
        compiler_params=params(),
        cost_estimate=pl.CostEstimate(flops=10**6, bytes_accessed=6 * 10**5, transcendentals=128),
    )(stats, counts, *packs)


def per_device(green_rows, cholesky_rot, one_body, fields, weights, sources, counts, owners):
    chol_size = lax.axis_size("chol")
    walk_size = lax.axis_size("walk")
    vectors, slots = fields.shape
    own = split_walkers(green_rows)
    packed = pack(own, one_body, fields, weights, sources, owners)
    if chol_size > RING_LIMIT or chol_size % 2:
        packs = [packed[0]] + [shifted(packed[d], d) for d in range(1, walk_size)]
        total, block, last = None, cholesky_rot, [lax.all_gather(own, "chol", axis=0, tiled=True)]
    else:
        total, block, last, packs = ring(cholesky_rot, own, packed)
    stats = measure(block, total, last, packs, packed[-1], slots)
    stats = lax.all_to_all(stats, ("chol", "walk"), split_axis=0, concat_axis=0, tiled=True)
    energies, new_weights, density = finish(stats, packs, counts, vectors, slots, green_rows.shape[1])
    return energies.reshape(slots), new_weights.reshape(slots), density.reshape(1, density.size)


def solution(mesh):
    return jax.shard_map(
        per_device,
        mesh=mesh,
        in_specs=(
            P("chol", "walk", None),
            P("chol", None, None),
            P("chol", None),
            P("chol", "walk"),
            P("walk"),
            P("walk"),
            P(),
            P(),
        ),
        out_specs=(P("walk"), P("walk"), P("walk", "chol")),
        check_vma=False,
    )
```

```python
import functools

import jax
import jax.numpy as jnp
from jax import lax
from jax.experimental import pallas as pl
from jax.experimental.pallas import tpu as pltpu
from jax.sharding import PartitionSpec as P

time_step = 0.02
root_step = 0.02**0.5
LANES = 128
VMEM_LIMIT = 16 * 1024 * 1024
PACK_LIMIT = 54 * 1024 * 1024
FETCH_LIMIT = 42 * 1024 * 1024
RING_LIMIT = 16


def params(limit=VMEM_LIMIT):
    return pltpu.CompilerParams(vmem_limit_bytes=limit)


def vmem():
    return pl.BlockSpec(memory_space=pltpu.VMEM)


def smem():
    return pl.BlockSpec(memory_space=pltpu.SMEM)


def ring_order(size):
    return [2 * q if q < size // 2 else 2 * (size - 1 - q) + 1 for q in range(size)]


def ring_place(index, size):
    return jnp.where(index % 2 == 0, index // 2, size - 1 - index // 2)


def ring_owner(place, size):
    return jnp.where(place < size // 2, 2 * place, 2 * (size - 1 - place) + 1)


def column_start(shift, rows):
    size = lax.axis_size("chol")
    place = ring_place(lax.axis_index("chol"), size)
    owner = ring_owner(lax.rem(place + shift + size, size), size)
    return pl.multiple_of(owner * rows, rows)


def accumulate(blocks, first, parts, total, mark):
    size, width = blocks.shape
    rows, walkers, orbitals = parts[0].shape
    count = len(parts)
    fresh = total is None
    arrays = list(parts) + [mark] + ([] if fresh else [total])

    def kernel(blocks_ref, *refs):
        shards = refs[:count]
        total_ref, mark_ref = refs[len(arrays) :]
        mark_ref[...] = jnp.zeros_like(mark_ref)
        lhs = blocks_ref[:, first * rows : (first + count) * rows]
        for b in range(walkers):
            rhs = jnp.concatenate([x[:, b, :] for x in shards], axis=0)
            value = jnp.dot(lhs, rhs, preferred_element_type=jnp.float32)
            total_ref[b] = value if fresh else refs[count + 1][b] + value

    return pl.pallas_call(
        kernel,
        name="accumulate",
        out_shape=[
            jax.ShapeDtypeStruct((walkers, size, orbitals), jnp.float32),
            jax.ShapeDtypeStruct((8, LANES), jnp.float32),
        ],
        in_specs=[vmem()] * (1 + len(arrays)),
        out_specs=[vmem()] * 2,
        compiler_params=params(),
        cost_estimate=pl.CostEstimate(
            flops=2 * count * size * rows * walkers * orbitals,
            bytes_accessed=2 * count * size * rows,
            transcendentals=0,
        ),
    )(blocks, *arrays)


def tie(*arrays):
    return lax.optimization_barrier(arrays)


def arrival_shifts(size):
    shifts = [0]
    for step in range(1, size // 2):
        shifts += [-step, step]
    return shifts + [size // 2]


def ring(own, cholesky_rot, onebody, packed):
    size = lax.axis_size("chol")
    rows = own.shape[0]
    order = ring_order(size)
    ahead = [(order[q], order[(q + 1) % size]) for q in range(size)]
    back = [(order[q], order[(q - 1) % size]) for q in range(size)]
    right = left = own
    parts = [own]
    first = 0
    total = None
    steps = size // 2
    blocks, mark = fetch(cholesky_rot, arrival_shifts(size))
    for step in range(1, steps):
        next_right = lax.ppermute(right, "chol", ahead)
        next_left = lax.ppermute(left, "chol", back)
        if step > 1:
            total, mark = accumulate(blocks, first, parts, total, mark)
            first += len(parts)
            parts = []
        if step == 1:
            others = [shifted(packed[d], d) for d in range(1, len(packed))]
        if step == 1:
            right, left, mark, onebody = tie(next_right, next_left, mark, onebody)
        elif step == 2:
            right, left, mark, *others = tie(next_right, next_left, mark, *others)
        else:
            right, left, mark = tie(next_right, next_left, mark)
        parts = parts + [right, left]
    last = [lax.ppermute(right[: rows // 2], "chol", ahead), lax.ppermute(left[rows // 2 :], "chol", back)]
    total, _ = accumulate(blocks, first, parts, total, mark)
    return blocks, onebody, total, last, [packed[0]] + others


def table_height(vectors):
    return -(-(vectors + 2) // 16) * 16


def fetch(cholesky_rot, shifts):
    vectors, orbitals, basis = cholesky_rot.shape
    rows = basis // len(shifts)

    def kernel(chol_any, blocks_ref, mark_ref, sems):
        mark_ref[...] = jnp.zeros_like(mark_ref)
        copies = []
        for n, shift in enumerate(shifts):
            start = 0 if shift is None else column_start(shift, rows)
            for g in range(vectors):
                copies.append(
                    pltpu.make_async_copy(
                        chol_any.at[g, :, pl.ds(start, rows)],
                        blocks_ref.at[pl.ds(g * orbitals, orbitals), pl.ds(n * rows, rows)],
                        sems.at[n, g],
                    )
                )
        for copy in copies:
            copy.start()
        for copy in copies:
            copy.wait()

    return pl.pallas_call(
        kernel,
        name="fetch",
        out_shape=[
            jax.ShapeDtypeStruct((vectors * orbitals, basis), cholesky_rot.dtype),
            jax.ShapeDtypeStruct((8, LANES), jnp.float32),
        ],
        in_specs=[pl.BlockSpec(memory_space=pl.ANY)],
        out_specs=[vmem()] * 2,
        scratch_shapes=[pltpu.SemaphoreType.DMA((len(shifts), vectors))],
        compiler_params=params(FETCH_LIMIT),
        cost_estimate=pl.CostEstimate(flops=0, bytes_accessed=2 * cholesky_rot.size, transcendentals=0),
    )(cholesky_rot)


def pack(own, one_body, fields, weights, sources, owners):
    rows, walkers, orbitals = own.shape
    walk_size = lax.axis_size("walk")
    width = orbitals // walk_size
    pair = LANES // width
    vectors, slots = fields.shape
    table_rows = table_height(vectors)
    height = walkers * (rows // pair) + 3 * table_rows

    def kernel(own_any, body_any, fields_any, weights_any, sources_any, owners_any, *refs):
        onebody_ref = refs[0]
        packs = refs[1 : 1 + walk_size]
        own_ref, body_ref, fields_ref, weights_ref, sources_ref, owners_ref, table_scr, sems = refs[1 + walk_size :]
        places = [
            (own_any, own_ref),
            (body_any, body_ref),
            (fields_any, fields_ref),
            (weights_any, weights_ref),
            (sources_any, sources_ref),
            (owners_any, owners_ref),
        ]
        small = [pltpu.make_async_copy(a, b, sems.at[n]) for n, (a, b) in enumerate(places)]
        for copy in small:
            copy.start()
        for copy in small:
            copy.wait()
        green = [own_ref[:, b, :] for b in range(walkers)]
        walk = lax.axis_index("walk")
        lane = lax.broadcasted_iota(jnp.int32, (1, LANES), 1)
        body = body_ref[...].astype(jnp.float32)
        onebody_ref[...] = jnp.zeros_like(onebody_ref)
        for b in range(walkers):
            total = jnp.sum(green[b].astype(jnp.float32) * body, axis=0, keepdims=True)
            folded = total[:, :LANES]
            for start in range(LANES, orbitals, LANES):
                folded = folded + total[:, start : start + LANES]
            onebody_ref[b : b + 1, :] = folded
        r = lax.broadcasted_iota(jnp.int32, (rows // pair, rows), 0)
        m = lax.broadcasted_iota(jnp.int32, (rows // pair, rows), 1)
        k = lax.broadcasted_iota(jnp.int32, (orbitals, LANES), 0)
        c = lax.broadcasted_iota(jnp.int32, (orbitals, LANES), 1)
        thinned = []
        for b in range(walkers):
            values = green[b]
            thinned.append(
                [
                    jnp.dot(
                        (m == r * pair + h).astype(jnp.bfloat16), values, preferred_element_type=jnp.float32
                    ).astype(jnp.bfloat16)
                    for h in range(pair)
                ]
            )
        for d in range(walk_size):
            target = lax.rem(walk + d, walk_size)
            panel = jnp.int32(0)
            for p in range(walk_size):
                panel = jnp.where(owners_ref[p] == target, p, panel)
            for b in range(walkers):
                total = jnp.zeros((rows // pair, LANES), jnp.float32)
                for h in range(pair):
                    take = (k == panel * width + c - h * width) & (c >= h * width) & (c < (h + 1) * width)
                    total += jnp.dot(
                        thinned[b][h], take.astype(jnp.bfloat16), preferred_element_type=jnp.float32
                    )
                packs[d][b * (rows // pair) : (b + 1) * (rows // pair), :] = total.astype(jnp.bfloat16)
        spread = jnp.zeros((vectors, LANES), jnp.float32)
        source = jnp.zeros((1, LANES), jnp.float32)
        corner = lax.broadcasted_iota(jnp.int32, (vectors, vectors), 0) == lax.broadcasted_iota(
            jnp.int32, (vectors, vectors), 1
        )
        for j in range(slots):
            mine = lane % slots == j
            upright = jnp.sum(jnp.where(corner, fields_ref[j : j + 1, :], 0.0), axis=1, keepdims=True)
            spread += jnp.where(mine, upright, 0.0)
            source += jnp.where(mine, sources_ref[j].astype(jnp.float32), 0.0)
        weight = weights_ref[0]
        for j in range(1, weights.shape[0]):
            weight = weight + weights_ref[j]
        table_scr[...] = jnp.zeros_like(table_scr)
        table_scr[:vectors, :] = spread
        table_scr[vectors : vectors + 1, :] = source
        table_scr[vectors + 1 : vectors + 2, :] = jnp.zeros((1, LANES), jnp.float32) + weight
        rest = table_scr[...]
        for n in range(3):
            piece = rest.astype(jnp.bfloat16)
            rest = rest - piece.astype(jnp.float32)
            at = walkers * (rows // pair) + n * table_rows
            for d in range(walk_size):
                packs[d][at : at + table_rows, :] = piece

    return pl.pallas_call(
        kernel,
        name="pack",
        out_shape=[
            jax.ShapeDtypeStruct((8, LANES), jnp.float32),
        ]
        + [jax.ShapeDtypeStruct((height, LANES), jnp.bfloat16)] * walk_size,
        in_specs=[pl.BlockSpec(memory_space=pl.ANY)] * 6,
        out_specs=[vmem()] * (walk_size + 1),
        scratch_shapes=[
            pltpu.VMEM(own.shape, own.dtype),
            pltpu.VMEM(one_body.shape, one_body.dtype),
            pltpu.VMEM((slots, vectors), jnp.float32),
            pltpu.SMEM(weights.shape, weights.dtype),
            pltpu.SMEM(sources.shape, sources.dtype),
            pltpu.SMEM(owners.shape, owners.dtype),
            pltpu.VMEM((table_rows, LANES), jnp.float32),
            pltpu.SemaphoreType.DMA((6,)),
        ],
        compiler_params=params(PACK_LIMIT),
        cost_estimate=pl.CostEstimate(flops=10**8, bytes_accessed=10**6, transcendentals=0),
    )(own, one_body, fields.T, weights, sources, owners)


def shifted(x, d):
    size = lax.axis_size("walk")
    return lax.ppermute(x, "walk", [(q, (q + d) % size) for q in range(size)])


def read_table(ref, vectors):
    height = table_height(vectors)
    start = ref.shape[0] - 3 * height
    parts = [ref[start + n * height : start + (n + 1) * height, :].astype(jnp.float32) for n in range(3)]
    return parts[0] + (parts[1] + parts[2])


def merge_tables(tables, walk, walk_size, slots, lane):
    total = jnp.zeros_like(tables[0])
    for d, table in enumerate(tables):
        group = lax.rem(walk - d + walk_size, walk_size)
        total += jnp.where(lane // slots == group, table, 0.0)
    return total


def measure(blocks, first, total, last, packs, onebody, vectors, slots):
    _, walkers, orbitals = last[0].shape
    depth = sum(x.shape[0] for x in last)
    walk_size = len(packs)
    targets = lax.axis_size("chol")
    whole = total is None
    quads = orbitals // LANES

    def fold(x):
        return jnp.sum(x.reshape(-1, 8, LANES), axis=0)

    def kernel(*refs):
        blocks_ref, onebody_ref = refs[:2]
        pack_refs = refs[2 : 2 + walk_size]
        last_refs = refs[2 + walk_size : 2 + walk_size + len(last)]
        out_ref, tensor_scr = refs[-2:]
        walk = lax.axis_index("walk")
        lane = lax.broadcasted_iota(jnp.int32, (1, LANES), 1)
        table = merge_tables([read_table(x, vectors) for x in pack_refs], walk, walk_size, slots, lane)
        picks = [
            jnp.where(
                (lane < slots * walk_size) & (table[vectors : vectors + 1, :] == (walk * walkers + b).astype(jnp.float32)),
                1.0,
                0.0,
            )
            for b in range(walkers)
        ]
        rhs = [jnp.concatenate([x[:, b, :] for x in last_refs], axis=0) for b in range(walkers)]
        eye = lax.broadcasted_iota(jnp.int32, (LANES, LANES), 0) == lax.broadcasted_iota(
            jnp.int32, (LANES, LANES), 1
        )
        exchange = [jnp.zeros((8, LANES), jnp.float32) for _ in range(walkers)]
        squares = [jnp.zeros((1, 1), jnp.float32) for _ in range(walkers)]
        drive = jnp.zeros((1, LANES), jnp.float32)
        for b in range(walkers):
            value = jnp.dot(
                blocks_ref[:, first * depth : (first + 1) * depth], rhs[b], preferred_element_type=jnp.float32
            )
            tensor_scr[b] = value if whole else refs[2 + walk_size + len(last)][b] + value
        for g in range(vectors):
            top = g * orbitals
            for b in range(walkers):
                diagonal = jnp.zeros((LANES, LANES), jnp.float32)
                for q in range(quads):
                    for p in range(q + 1):
                        one = tensor_scr[
                            b, top + q * LANES : top + (q + 1) * LANES, p * LANES : (p + 1) * LANES
                        ]
                        if p == q:
                            exchange[b] = exchange[b] + fold(one * one.T)
                            diagonal = diagonal + one
                        else:
                            two = tensor_scr[
                                b, top + p * LANES : top + (p + 1) * LANES, q * LANES : (q + 1) * LANES
                            ]
                            exchange[b] = exchange[b] + 2.0 * fold(two * one.T)
                trace = jnp.sum(fold(jnp.where(eye, diagonal, 0.0)), axis=0, keepdims=True)
                trace = jnp.sum(trace, axis=1, keepdims=True)
                squares[b] = squares[b] + trace * trace
                drive = drive - root_step * picks[b] * table[g : g + 1, :] * trace
        raw = jnp.zeros((1, LANES), jnp.float32)
        square = jnp.zeros((1, LANES), jnp.float32)
        for b in range(walkers):
            swapped = jnp.sum(jnp.sum(exchange[b], axis=0, keepdims=True), axis=1, keepdims=True)
            single = jnp.sum(onebody_ref[b : b + 1, :], axis=1, keepdims=True)
            raw += picks[b] * (single + 0.5 * squares[b] - 0.5 * swapped)
            square += picks[b] * squares[b]
        power = drive - 0.5 * time_step * square - time_step * raw
        out_ref[...] = jnp.broadcast_to(raw + pltpu.roll(power, slots * walk_size, 1), (targets, LANES))

    arrays = list(last) + ([] if whole else [total])
    return pl.pallas_call(
        kernel,
        name="measure",
        out_shape=jax.ShapeDtypeStruct((targets, LANES), jnp.float32),
        in_specs=[vmem()] * (2 + walk_size + len(arrays)),
        out_specs=vmem(),
        scratch_shapes=[
            pltpu.VMEM((walkers, vectors * orbitals, orbitals), jnp.float32),
        ],
        compiler_params=params(),
        cost_estimate=pl.CostEstimate(
            flops=2 * vectors * orbitals * depth * walkers * orbitals,
            bytes_accessed=2 * vectors * orbitals * depth,
            transcendentals=0,
        ),
    )(blocks, onebody, *packs, *arrays)


def add_up(stats, targets):
    def kernel(stats_ref, out_ref):
        out_ref[...] = jnp.broadcast_to(jnp.sum(stats_ref[...], axis=0, keepdims=True), out_ref.shape)

    return pl.pallas_call(
        kernel,
        name="add_up",
        out_shape=jax.ShapeDtypeStruct((targets, LANES), jnp.float32),
        in_specs=[vmem()],
        out_specs=vmem(),
        compiler_params=params(),
    )(stats)


def finish(stats, packs, counts, vectors, slots, walkers):
    walk_size = len(packs)
    rows = (packs[0].shape[0] - 3 * table_height(vectors)) // walkers

    def kernel(stats_ref, counts_ref, *refs):
        pack_refs = refs[:walk_size]
        energies_ref, weights_ref, density_ref = refs[walk_size:]
        walk = lax.axis_index("walk")
        lane = lax.broadcasted_iota(jnp.int32, (1, LANES), 1)
        all_slots = slots * walk_size
        tables = [read_table(x, vectors) for x in pack_refs]
        source = merge_tables([t[vectors : vectors + 1, :] for t in tables], walk, walk_size, slots, lane)
        total_weight = tables[0][vectors + 1 : vectors + 2, :]
        for t in tables[1:]:
            total_weight = total_weight + t[vectors + 1 : vectors + 2, :]
        mean_weight = total_weight / (walkers * walk_size)
        total = jnp.sum(stats_ref[...], axis=0, keepdims=True)
        power = pltpu.roll(total, LANES - all_slots, 1)
        live_count = jnp.zeros((1, LANES), jnp.int32)
        for q in range(walk_size):
            live_count = jnp.where(lane // slots == q, counts_ref[q], live_count)
        live = (lane < all_slots) & (lane % slots < live_count)
        energies = jnp.where(live, total, 0.0)
        new_weights = jnp.where(live, mean_weight * jnp.exp(jnp.where(live, power, 0.0)), 0.0)
        norm = jnp.sum(new_weights, axis=1, keepdims=True)
        density = jnp.zeros((rows, LANES), jnp.float32)
        for d in range(walk_size):
            group = lax.rem(walk - d + walk_size, walk_size)
            for b in range(walkers):
                walker = (group * walkers + b).astype(jnp.float32)
                share = jnp.sum(jnp.where(source == walker, new_weights, 0.0), axis=1, keepdims=True) / norm
                density += share * pack_refs[d][b * rows : (b + 1) * rows, :].astype(jnp.float32)
        density_ref[...] = density
        first = lax.rem(LANES - walk * slots, LANES)
        energies_ref[...] = pltpu.roll(jnp.broadcast_to(energies, (8, LANES)), first, 1)[:1, :slots]
        weights_ref[...] = pltpu.roll(jnp.broadcast_to(new_weights, (8, LANES)), first, 1)[:1, :slots]

    return pl.pallas_call(
        kernel,
        name="finish",
        out_shape=[
            jax.ShapeDtypeStruct((1, slots), jnp.float32),
            jax.ShapeDtypeStruct((1, slots), jnp.float32),
            jax.ShapeDtypeStruct((rows, LANES), jnp.float32),
        ],
        in_specs=[vmem(), smem()] + [vmem()] * walk_size,
        out_specs=[vmem()] * 3,
        compiler_params=params(),
        cost_estimate=pl.CostEstimate(flops=10**6, bytes_accessed=6 * 10**5, transcendentals=128),
    )(stats, counts, *packs)


def per_device(green_rows, cholesky_rot, one_body, fields, weights, sources, counts, owners):
    chol_size = lax.axis_size("chol")
    walk_size = lax.axis_size("walk")
    vectors, slots = fields.shape
    walkers = green_rows.shape[1]
    onebody, *packed = pack(green_rows, one_body, fields, weights, sources, owners)
    if chol_size > RING_LIMIT or chol_size % 2 or chol_size < 6:
        blocks, first = fetch(cholesky_rot, [None])[0], 0
        packs = [packed[0]] + [shifted(packed[d], d) for d in range(1, walk_size)]
        total, last = None, [lax.all_gather(green_rows, "chol", axis=0, tiled=True)]
    else:
        blocks, onebody, total, last, packs = ring(green_rows, cholesky_rot, onebody, packed)
        first = chol_size - 1
    stats = measure(blocks, first, total, last, packs, onebody, vectors, slots)
    stats = lax.all_to_all(stats, "chol", split_axis=0, concat_axis=0, tiled=True)
    stats = add_up(stats, walk_size)
    stats = lax.all_to_all(stats, "walk", split_axis=0, concat_axis=0, tiled=True)
    energies, new_weights, density = finish(stats, packs, counts, vectors, slots, walkers)
    return energies.reshape(slots), new_weights.reshape(slots), density.reshape(1, density.size)


def solution(mesh):
    return jax.shard_map(
        per_device,
        mesh=mesh,
        in_specs=(
            P("chol", "walk", None),
            P("chol", None, None),
            P("chol", None),
            P("chol", "walk"),
            P("walk"),
            P("walk"),
            P(),
            P(),
        ),
        out_specs=(P("walk"), P("walk"), P("walk", "chol")),
        check_vma=False,
    )
```

```python
import functools

import jax
import jax.numpy as jnp
from jax import lax
from jax.experimental import pallas as pl
from jax.experimental.pallas import tpu as pltpu
from jax.sharding import PartitionSpec as P

time_step = 0.02
root_step = 0.02**0.5
LANES = 128
VMEM_LIMIT = 16 * 1024 * 1024
PACK_LIMIT = 54 * 1024 * 1024
ACCUMULATE_LIMIT = 43 * 1024 * 1024
RING_LIMIT = 16


def params(limit=VMEM_LIMIT):
    return pltpu.CompilerParams(vmem_limit_bytes=limit)


def vmem():
    return pl.BlockSpec(memory_space=pltpu.VMEM)


def smem():
    return pl.BlockSpec(memory_space=pltpu.SMEM)


def ring_order(size):
    return [2 * q if q < size // 2 else 2 * (size - 1 - q) + 1 for q in range(size)]


def ring_place(index, size):
    return jnp.where(index % 2 == 0, index // 2, size - 1 - index // 2)


def ring_owner(place, size):
    return jnp.where(place < size // 2, 2 * place, 2 * (size - 1 - place) + 1)


def column_start(shift, rows):
    size = lax.axis_size("chol")
    place = ring_place(lax.axis_index("chol"), size)
    owner = ring_owner(lax.rem(place + shift + size, size), size)
    return pl.multiple_of(owner * rows, rows)


def accumulate(cholesky_rot, shifts, parts, total, mark, ahead):
    vectors, orbitals, _ = cholesky_rot.shape
    rows, walkers, _ = parts[0].shape
    count = len(parts)
    size = vectors * orbitals
    chunks = vectors // 2 if vectors % 2 == 0 else vectors
    each = vectors // chunks
    arrays = list(parts) + ([] if mark is None else [mark]) + ([] if total is None else [total])
    shapes = [
        jax.ShapeDtypeStruct((walkers, size, orbitals), jnp.float32),
        jax.ShapeDtypeStruct((8, LANES), jnp.float32),
    ]
    if ahead is not None:
        shapes.append(jax.ShapeDtypeStruct((size, rows), cholesky_rot.dtype))

    def kernel(chol_any, *refs):
        ins = refs[: len(arrays)]
        outs = refs[len(arrays) : len(arrays) + len(shapes)]
        blocks_scr, sems = refs[len(arrays) + len(shapes) :]

        def columns(shift, g, target):
            return chol_any.at[g, :, pl.ds(column_start(shift, rows), rows)], target

        copies = []
        for g in range(vectors):
            for n, shift in enumerate(shifts):
                copies.append(
                    pltpu.make_async_copy(
                        *columns(
                            shift, g, blocks_scr.at[pl.ds(g * orbitals, orbitals), pl.ds(n * rows, rows)]
                        ),
                        sems.at[g * (count + 1) + n],
                    )
                )
        for copy in copies:
            copy.start()
        later = []
        if ahead is not None:
            for g in range(vectors):
                later.append(
                    pltpu.make_async_copy(
                        *columns(ahead, g, outs[2].at[pl.ds(g * orbitals, orbitals), :]),
                        sems.at[g * (count + 1) + count],
                    )
                )
            for copy in later:
                copy.start()
        outs[1][...] = jnp.zeros_like(outs[1])
        rhs = [jnp.concatenate([x[:, b, :] for x in ins[:count]], axis=0) for b in range(walkers)]
        for q in range(chunks):
            for copy in copies[q * each * count : (q + 1) * each * count]:
                copy.wait()
            at = slice(q * each * orbitals, (q + 1) * each * orbitals)
            for b in range(walkers):
                value = jnp.dot(blocks_scr[at, :], rhs[b], preferred_element_type=jnp.float32)
                outs[0][b, at, :] = value if total is None else ins[-1][b, at, :] + value
        for copy in later:
            copy.wait()

    return pl.pallas_call(
        kernel,
        name="accumulate",
        out_shape=shapes,
        in_specs=[pl.BlockSpec(memory_space=pl.ANY)] + [vmem()] * len(arrays),
        out_specs=[vmem()] * len(shapes),
        scratch_shapes=[
            pltpu.VMEM((size, count * rows), cholesky_rot.dtype),
            pltpu.SemaphoreType.DMA((vectors * (count + 1),)),
        ],
        compiler_params=params(ACCUMULATE_LIMIT),
        cost_estimate=pl.CostEstimate(
            flops=2 * count * size * rows * walkers * orbitals,
            bytes_accessed=2 * count * size * rows,
            transcendentals=0,
        ),
    )(cholesky_rot, *arrays)


def tie(*arrays):
    return lax.optimization_barrier(arrays)


def ring(own, cholesky_rot, onebody, packed):
    size = lax.axis_size("chol")
    rows = own.shape[0]
    order = ring_order(size)
    ahead = [(order[q], order[(q + 1) % size]) for q in range(size)]
    back = [(order[q], order[(q - 1) % size]) for q in range(size)]
    steps = size // 2
    right, left = lax.ppermute(own, "chol", ahead), lax.ppermute(own, "chol", back)
    right, onebody = tie(right, onebody)
    left, onebody = tie(left, onebody)
    next_right, next_left = lax.ppermute(right, "chol", ahead), lax.ppermute(left, "chol", back)
    total, mark = accumulate(cholesky_rot, [0, -1, 1], [own, right, left], None, None, None)
    right, mark = tie(next_right, mark)
    left, mark = tie(next_left, mark)
    others = packed[1:]
    for step in range(3, steps):
        next_right, next_left = lax.ppermute(right, "chol", ahead), lax.ppermute(left, "chol", back)
        if step == 3:
            *others, mark = tie(*others, mark)
            others = [shifted(x, d + 1) for d, x in enumerate(others)]
        total, mark = accumulate(cholesky_rot, [1 - step, step - 1], [right, left], total, mark, None)
        right, mark = tie(next_right, mark)
        left, mark, *others = tie(next_left, mark, *others)
    last = [lax.ppermute(right[: rows // 2], "chol", ahead), lax.ppermute(left[rows // 2 :], "chol", back)]
    total, _, block = accumulate(cholesky_rot, [1 - steps, steps - 1], [right, left], total, mark, steps)
    return block, onebody, total, last, [packed[0]] + others


def table_height(vectors):
    return -(-(vectors + 2) // 16) * 16


def pack(own, one_body, fields, weights, sources, owners):
    rows, walkers, orbitals = own.shape
    walk_size = lax.axis_size("walk")
    width = orbitals // walk_size
    pair = LANES // width
    vectors, slots = fields.shape
    table_rows = table_height(vectors)
    height = walkers * (rows // pair) + 3 * table_rows

    def kernel(own_any, body_any, fields_any, weights_any, sources_any, owners_any, *refs):
        onebody_ref = refs[0]
        packs = refs[1 : 1 + walk_size]
        own_ref, body_ref, fields_ref, weights_ref, sources_ref, owners_ref, table_scr, sems = refs[1 + walk_size :]
        places = [
            (own_any, own_ref),
            (body_any, body_ref),
            (fields_any, fields_ref),
            (weights_any, weights_ref),
            (sources_any, sources_ref),
            (owners_any, owners_ref),
        ]
        small = [pltpu.make_async_copy(a, b, sems.at[n]) for n, (a, b) in enumerate(places)]
        for copy in small:
            copy.start()
        for copy in small:
            copy.wait()
        green = [own_ref[:, b, :] for b in range(walkers)]
        walk = lax.axis_index("walk")
        lane = lax.broadcasted_iota(jnp.int32, (1, LANES), 1)
        body = body_ref[...].astype(jnp.float32)
        onebody_ref[...] = jnp.zeros_like(onebody_ref)
        for b in range(walkers):
            total = jnp.sum(green[b].astype(jnp.float32) * body, axis=0, keepdims=True)
            folded = total[:, :LANES]
            for start in range(LANES, orbitals, LANES):
                folded = folded + total[:, start : start + LANES]
            onebody_ref[b : b + 1, :] = folded
        r = lax.broadcasted_iota(jnp.int32, (rows // pair, rows), 0)
        m = lax.broadcasted_iota(jnp.int32, (rows // pair, rows), 1)
        k = lax.broadcasted_iota(jnp.int32, (orbitals, LANES), 0)
        c = lax.broadcasted_iota(jnp.int32, (orbitals, LANES), 1)
        thinned = []
        for b in range(walkers):
            values = green[b]
            thinned.append(
                [
                    jnp.dot(
                        (m == r * pair + h).astype(jnp.bfloat16), values, preferred_element_type=jnp.float32
                    ).astype(jnp.bfloat16)
                    for h in range(pair)
                ]
            )
        for d in range(walk_size):
            target = lax.rem(walk + d, walk_size)
            panel = jnp.int32(0)
            for p in range(walk_size):
                panel = jnp.where(owners_ref[p] == target, p, panel)
            for b in range(walkers):
                total = jnp.zeros((rows // pair, LANES), jnp.float32)
                for h in range(pair):
                    take = (k == panel * width + c - h * width) & (c >= h * width) & (c < (h + 1) * width)
                    total += jnp.dot(
                        thinned[b][h], take.astype(jnp.bfloat16), preferred_element_type=jnp.float32
                    )
                packs[d][b * (rows // pair) : (b + 1) * (rows // pair), :] = total.astype(jnp.bfloat16)
        spread = jnp.zeros((vectors, LANES), jnp.float32)
        source = jnp.zeros((1, LANES), jnp.float32)
        corner = lax.broadcasted_iota(jnp.int32, (vectors, vectors), 0) == lax.broadcasted_iota(
            jnp.int32, (vectors, vectors), 1
        )
        for j in range(slots):
            mine = lane % slots == j
            upright = jnp.sum(jnp.where(corner, fields_ref[j : j + 1, :], 0.0), axis=1, keepdims=True)
            spread += jnp.where(mine, upright, 0.0)
            source += jnp.where(mine, sources_ref[j].astype(jnp.float32), 0.0)
        weight = weights_ref[0]
        for j in range(1, weights.shape[0]):
            weight = weight + weights_ref[j]
        table_scr[...] = jnp.zeros_like(table_scr)
        table_scr[:vectors, :] = spread
        table_scr[vectors : vectors + 1, :] = source
        table_scr[vectors + 1 : vectors + 2, :] = jnp.zeros((1, LANES), jnp.float32) + weight
        rest = table_scr[...]
        for n in range(3):
            piece = rest.astype(jnp.bfloat16)
            rest = rest - piece.astype(jnp.float32)
            at = walkers * (rows // pair) + n * table_rows
            for d in range(walk_size):
                packs[d][at : at + table_rows, :] = piece

    return pl.pallas_call(
        kernel,
        name="pack",
        out_shape=[
            jax.ShapeDtypeStruct((8, LANES), jnp.float32),
        ]
        + [jax.ShapeDtypeStruct((height, LANES), jnp.bfloat16)] * walk_size,
        in_specs=[pl.BlockSpec(memory_space=pl.ANY)] * 6,
        out_specs=[vmem()] * (walk_size + 1),
        scratch_shapes=[
            pltpu.VMEM(own.shape, own.dtype),
            pltpu.VMEM(one_body.shape, one_body.dtype),
            pltpu.VMEM((slots, vectors), jnp.float32),
            pltpu.SMEM(weights.shape, weights.dtype),
            pltpu.SMEM(sources.shape, sources.dtype),
            pltpu.SMEM(owners.shape, owners.dtype),
            pltpu.VMEM((table_rows, LANES), jnp.float32),
            pltpu.SemaphoreType.DMA((6,)),
        ],
        compiler_params=params(PACK_LIMIT),
        cost_estimate=pl.CostEstimate(flops=10**8, bytes_accessed=10**6, transcendentals=0),
    )(own, one_body, fields.T, weights, sources, owners)


def shifted(x, d):
    size = lax.axis_size("walk")
    return lax.ppermute(x, "walk", [(q, (q + d) % size) for q in range(size)])


def read_table(ref, vectors):
    height = table_height(vectors)
    start = ref.shape[0] - 3 * height
    parts = [ref[start + n * height : start + (n + 1) * height, :].astype(jnp.float32) for n in range(3)]
    return parts[0] + (parts[1] + parts[2])


def merge_tables(tables, walk, walk_size, slots, lane):
    total = jnp.zeros_like(tables[0])
    for d, table in enumerate(tables):
        group = lax.rem(walk - d + walk_size, walk_size)
        total += jnp.where(lane // slots == group, table, 0.0)
    return total


def measure(block, total, last, packs, onebody, vectors, slots):
    _, walkers, orbitals = last[0].shape
    depth = sum(x.shape[0] for x in last)
    walk_size = len(packs)
    targets = walk_size * lax.axis_size("chol")
    whole = total is None
    quads = orbitals // LANES

    def fold(x):
        return jnp.sum(x.reshape(-1, 8, LANES), axis=0)

    def kernel(*refs):
        block_ref, onebody_ref = refs[:2]
        pack_refs = refs[2 : 2 + walk_size]
        last_refs = refs[2 + walk_size : 2 + walk_size + len(last)]
        out_ref, tensor_scr = refs[-2:]
        walk = lax.axis_index("walk")
        lane = lax.broadcasted_iota(jnp.int32, (1, LANES), 1)
        table = merge_tables([read_table(x, vectors) for x in pack_refs], walk, walk_size, slots, lane)
        picks = [
            jnp.where(
                (lane < slots * walk_size) & (table[vectors : vectors + 1, :] == (walk * walkers + b).astype(jnp.float32)),
                1.0,
                0.0,
            )
            for b in range(walkers)
        ]
        rhs = [jnp.concatenate([x[:, b, :] for x in last_refs], axis=0) for b in range(walkers)]
        eye = lax.broadcasted_iota(jnp.int32, (LANES, LANES), 0) == lax.broadcasted_iota(
            jnp.int32, (LANES, LANES), 1
        )
        exchange = [jnp.zeros((8, LANES), jnp.float32) for _ in range(walkers)]
        squares = [jnp.zeros((1, 1), jnp.float32) for _ in range(walkers)]
        drive = jnp.zeros((1, LANES), jnp.float32)
        for b in range(walkers):
            value = jnp.dot(block_ref[...], rhs[b], preferred_element_type=jnp.float32)
            tensor_scr[b] = value if whole else refs[2 + walk_size + len(last)][b] + value
        for g in range(vectors):
            top = g * orbitals
            for b in range(walkers):
                diagonal = jnp.zeros((LANES, LANES), jnp.float32)
                for q in range(quads):
                    for p in range(q + 1):
                        one = tensor_scr[
                            b, top + q * LANES : top + (q + 1) * LANES, p * LANES : (p + 1) * LANES
                        ]
                        if p == q:
                            exchange[b] = exchange[b] + fold(one * one.T)
                            diagonal = diagonal + one
                        else:
                            two = tensor_scr[
                                b, top + p * LANES : top + (p + 1) * LANES, q * LANES : (q + 1) * LANES
                            ]
                            exchange[b] = exchange[b] + 2.0 * fold(two * one.T)
                trace = jnp.sum(fold(jnp.where(eye, diagonal, 0.0)), axis=0, keepdims=True)
                trace = jnp.sum(trace, axis=1, keepdims=True)
                squares[b] = squares[b] + trace * trace
                drive = drive - root_step * picks[b] * table[g : g + 1, :] * trace
        raw = jnp.zeros((1, LANES), jnp.float32)
        square = jnp.zeros((1, LANES), jnp.float32)
        for b in range(walkers):
            swapped = jnp.sum(jnp.sum(exchange[b], axis=0, keepdims=True), axis=1, keepdims=True)
            single = jnp.sum(onebody_ref[b : b + 1, :], axis=1, keepdims=True)
            raw += picks[b] * (single + 0.5 * squares[b] - 0.5 * swapped)
            square += picks[b] * squares[b]
        power = drive - 0.5 * time_step * square - time_step * raw
        out_ref[...] = jnp.broadcast_to(raw + pltpu.roll(power, slots * walk_size, 1), (targets, LANES))

    arrays = list(last) + ([] if whole else [total])
    return pl.pallas_call(
        kernel,
        name="measure",
        out_shape=jax.ShapeDtypeStruct((targets, LANES), jnp.float32),
        in_specs=[vmem()] * (2 + walk_size + len(arrays)),
        out_specs=vmem(),
        scratch_shapes=[
            pltpu.VMEM((walkers, vectors * orbitals, orbitals), jnp.float32),
        ],
        compiler_params=params(),
        cost_estimate=pl.CostEstimate(
            flops=2 * vectors * orbitals * depth * walkers * orbitals,
            bytes_accessed=2 * vectors * orbitals * depth,
            transcendentals=0,
        ),
    )(block, onebody, *packs, *arrays)


def finish(stats, packs, counts, vectors, slots, walkers):
    walk_size = len(packs)
    rows = (packs[0].shape[0] - 3 * table_height(vectors)) // walkers

    def kernel(stats_ref, counts_ref, *refs):
        pack_refs = refs[:walk_size]
        energies_ref, weights_ref, density_ref = refs[walk_size:]
        walk = lax.axis_index("walk")
        lane = lax.broadcasted_iota(jnp.int32, (1, LANES), 1)
        all_slots = slots * walk_size
        tables = [read_table(x, vectors) for x in pack_refs]
        source = merge_tables([t[vectors : vectors + 1, :] for t in tables], walk, walk_size, slots, lane)
        total_weight = tables[0][vectors + 1 : vectors + 2, :]
        for t in tables[1:]:
            total_weight = total_weight + t[vectors + 1 : vectors + 2, :]
        mean_weight = total_weight / (walkers * walk_size)
        total = jnp.sum(stats_ref[...], axis=0, keepdims=True)
        power = pltpu.roll(total, LANES - all_slots, 1)
        live_count = jnp.zeros((1, LANES), jnp.int32)
        for q in range(walk_size):
            live_count = jnp.where(lane // slots == q, counts_ref[q], live_count)
        live = (lane < all_slots) & (lane % slots < live_count)
        energies = jnp.where(live, total, 0.0)
        new_weights = jnp.where(live, mean_weight * jnp.exp(jnp.where(live, power, 0.0)), 0.0)
        norm = jnp.sum(new_weights, axis=1, keepdims=True)
        density = jnp.zeros((rows, LANES), jnp.float32)
        for d in range(walk_size):
            group = lax.rem(walk - d + walk_size, walk_size)
            for b in range(walkers):
                walker = (group * walkers + b).astype(jnp.float32)
                share = jnp.sum(jnp.where(source == walker, new_weights, 0.0), axis=1, keepdims=True) / norm
                density += share * pack_refs[d][b * rows : (b + 1) * rows, :].astype(jnp.float32)
        density_ref[...] = density
        first = lax.rem(LANES - walk * slots, LANES)
        energies_ref[...] = pltpu.roll(jnp.broadcast_to(energies, (8, LANES)), first, 1)[:1, :slots]
        weights_ref[...] = pltpu.roll(jnp.broadcast_to(new_weights, (8, LANES)), first, 1)[:1, :slots]

    return pl.pallas_call(
        kernel,
        name="finish",
        out_shape=[
            jax.ShapeDtypeStruct((1, slots), jnp.float32),
            jax.ShapeDtypeStruct((1, slots), jnp.float32),
            jax.ShapeDtypeStruct((rows, LANES), jnp.float32),
        ],
        in_specs=[vmem(), smem()] + [vmem()] * walk_size,
        out_specs=[vmem()] * 3,
        compiler_params=params(),
        cost_estimate=pl.CostEstimate(flops=10**6, bytes_accessed=6 * 10**5, transcendentals=128),
    )(stats, counts, *packs)


def per_device(green_rows, cholesky_rot, one_body, fields, weights, sources, counts, owners):
    chol_size = lax.axis_size("chol")
    walk_size = lax.axis_size("walk")
    vectors, slots = fields.shape
    walkers = green_rows.shape[1]
    onebody, *packed = pack(green_rows, one_body, fields, weights, sources, owners)
    if chol_size > RING_LIMIT or chol_size % 2 or chol_size < 8:
        block = cholesky_rot.reshape(-1, cholesky_rot.shape[2])
        packs = [packed[0]] + [shifted(packed[d], d) for d in range(1, walk_size)]
        total, last = None, [lax.all_gather(green_rows, "chol", axis=0, tiled=True)]
    else:
        block, onebody, total, last, packs = ring(green_rows, cholesky_rot, onebody, packed)
    stats = measure(block, total, last, packs, onebody, vectors, slots)
    stats = lax.all_to_all(stats, ("chol", "walk"), split_axis=0, concat_axis=0, tiled=True)
    energies, new_weights, density = finish(stats, packs, counts, vectors, slots, walkers)
    return energies.reshape(slots), new_weights.reshape(slots), density.reshape(1, density.size)


def solution(mesh):
    return jax.shard_map(
        per_device,
        mesh=mesh,
        in_specs=(
            P("chol", "walk", None),
            P("chol", None, None),
            P("chol", None),
            P("chol", "walk"),
            P("walk"),
            P("walk"),
            P(),
            P(),
        ),
        out_specs=(P("walk"), P("walk"), P("walk", "chol")),
        check_vma=False,
    )
```

```python
import jax
import jax.numpy as jnp
from jax import lax
from jax.experimental import pallas as pl
from jax.experimental.pallas import tpu as pltpu
from jax.sharding import PartitionSpec as P

time_step = 0.02
root_step = 0.02**0.5
LANES = 128
VMEM_LIMIT = 16 * 1024 * 1024
PACK_LIMIT = 54 * 1024 * 1024
ACCUMULATE_LIMIT = 40 * 1024 * 1024
FETCH_LIMIT = 48 * 1024 * 1024
RING_LIMIT = 16


def params(limit=VMEM_LIMIT):
    return pltpu.CompilerParams(vmem_limit_bytes=limit)


def vmem():
    return pl.BlockSpec(memory_space=pltpu.VMEM)


def smem():
    return pl.BlockSpec(memory_space=pltpu.SMEM)


def ring_order(size):
    return [2 * q if q < size // 2 else 2 * (size - 1 - q) + 1 for q in range(size)]


def ring_place(index, size):
    return jnp.where(index % 2 == 0, index // 2, size - 1 - index // 2)


def ring_owner(place, size):
    return jnp.where(place < size // 2, 2 * place, 2 * (size - 1 - place) + 1)


def column_start(shift, rows):
    size = lax.axis_size("chol")
    place = ring_place(lax.axis_index("chol"), size)
    owner = ring_owner(lax.rem(place + shift + size, size), size)
    return pl.multiple_of(owner * rows, rows)


def start_columns(chol_any, shifts, rows, target, sems):
    vectors, orbitals, _ = chol_any.shape
    copies = []
    for g in range(vectors):
        for n, shift in enumerate(shifts):
            copies.append(
                pltpu.make_async_copy(
                    chol_any.at[g, :, pl.ds(column_start(shift, rows), rows)],
                    target.at[pl.ds(g * orbitals, orbitals), pl.ds(n * rows, rows)],
                    sems.at[g * len(shifts) + n],
                )
            )
    for copy in copies:
        copy.start()
    return copies


def fetch(cholesky_rot, shifts, rows):
    vectors, orbitals, _ = cholesky_rot.shape

    def kernel(chol_any, blocks_ref, mark_ref, sems):
        copies = start_columns(chol_any, shifts, rows, blocks_ref, sems)
        mark_ref[...] = jnp.zeros_like(mark_ref)
        for copy in copies:
            copy.wait()

    return pl.pallas_call(
        kernel,
        name="fetch",
        out_shape=[
            jax.ShapeDtypeStruct((vectors * orbitals, len(shifts) * rows), cholesky_rot.dtype),
            jax.ShapeDtypeStruct((8, LANES), jnp.float32),
        ],
        in_specs=[pl.BlockSpec(memory_space=pl.ANY)],
        out_specs=[vmem()] * 2,
        scratch_shapes=[pltpu.SemaphoreType.DMA((vectors * len(shifts),))],
        compiler_params=params(FETCH_LIMIT),
        cost_estimate=pl.CostEstimate(
            flops=0, bytes_accessed=4 * vectors * orbitals * len(shifts) * rows, transcendentals=0
        ),
    )(cholesky_rot)


def accumulate(cholesky_rot, blocks, parts, total, mark, ahead):
    vectors, orbitals, _ = cholesky_rot.shape
    rows, walkers, _ = parts[0].shape
    size = vectors * orbitals
    arrays = [blocks] + list(parts) + [mark] + ([] if total is None else [total])

    def kernel(chol_any, *refs):
        blocks_ref = refs[0]
        shards = refs[1 : 1 + len(parts)]
        total_ref, mark_ref, ahead_ref, sems = refs[len(arrays) :]
        copies = start_columns(chol_any, ahead, rows, ahead_ref, sems)
        mark_ref[...] = jnp.zeros_like(mark_ref)
        for b in range(walkers):
            rhs = jnp.concatenate([x[:, b, :] for x in shards], axis=0)
            value = jnp.dot(blocks_ref[...], rhs, preferred_element_type=jnp.float32)
            total_ref[b] = value if total is None else refs[len(arrays) - 1][b] + value
        for copy in copies:
            copy.wait()

    return pl.pallas_call(
        kernel,
        name="accumulate",
        out_shape=[
            jax.ShapeDtypeStruct((walkers, size, orbitals), jnp.float32),
            jax.ShapeDtypeStruct((8, LANES), jnp.float32),
            jax.ShapeDtypeStruct((size, len(ahead) * rows), cholesky_rot.dtype),
        ],
        in_specs=[pl.BlockSpec(memory_space=pl.ANY)] + [vmem()] * len(arrays),
        out_specs=[vmem()] * 3,
        scratch_shapes=[pltpu.SemaphoreType.DMA((vectors * len(ahead),))],
        compiler_params=params(ACCUMULATE_LIMIT),
        cost_estimate=pl.CostEstimate(
            flops=2 * len(parts) * size * rows * walkers * orbitals,
            bytes_accessed=4 * len(ahead) * size * rows,
            transcendentals=0,
        ),
    )(cholesky_rot, *arrays)


def tie(*arrays):
    return lax.optimization_barrier(arrays)


def ring(own, cholesky_rot, onebody, packed):
    size = lax.axis_size("chol")
    rows = own.shape[0]
    order = ring_order(size)
    ahead = [(order[q], order[(q + 1) % size]) for q in range(size)]
    back = [(order[q], order[(q - 1) % size]) for q in range(size)]
    steps = size // 2
    right = left = own
    parts = [own]
    total = None
    for step in range(1, steps):
        next_right, next_left = lax.ppermute(right, "chol", ahead), lax.ppermute(left, "chol", back)
        if step == 1:
            blocks, mark = fetch(cholesky_rot, [0, -1, 1], rows)
            right, onebody = tie(next_right, onebody)
            left, mark, *packed = tie(next_left, mark, *packed)
        else:
            total, mark, blocks = accumulate(cholesky_rot, blocks, parts, total, mark, [-step, step])
            parts = []
            if step == 2:
                far = exchange_far(packed)
                right, mark = tie(next_right, mark)
                left, far = tie(next_left, far)
            elif step == 3:
                near = exchange_near(packed, far)
                right, mark = tie(next_right, mark)
                left, *near = tie(next_left, *near)
            else:
                right, mark = tie(next_right, mark)
                left = next_left
        parts = parts + [right, left]
    last = [lax.ppermute(right[: rows // 2], "chol", ahead), lax.ppermute(left[rows // 2 :], "chol", back)]
    total, _, blocks = accumulate(cholesky_rot, blocks, parts, total, mark, [steps])
    return blocks, onebody, total, last, [packed[0], far] + near


def table_height(vectors):
    return -(-(vectors + 2) // 16) * 16


def pack(own, one_body, fields, weights, sources, owners):
    rows, walkers, orbitals = own.shape
    walk_size = lax.axis_size("walk")
    width = orbitals // walk_size
    pair = LANES // width
    vectors, slots = fields.shape
    table_rows = table_height(vectors)
    panel_rows = walkers * (rows // pair)
    both = panel_rows + 3 * table_rows
    if walk_size == 4:
        heights = [both, both + panel_rows, both]
        spots = [(0, 0), (2, 0), (1, 0), (1, both)]
    else:
        heights = [both] * walk_size
        spots = [(d, 0) for d in range(walk_size)]

    def kernel(own_any, body_any, fields_any, weights_any, sources_any, owners_any, *refs):
        onebody_ref = refs[0]
        packs = refs[1 : 1 + len(heights)]
        own_ref, body_ref, fields_ref, weights_ref, sources_ref, owners_ref, table_scr, sems = refs[1 + len(heights) :]
        places = [
            (own_any, own_ref),
            (body_any, body_ref),
            (fields_any, fields_ref),
            (weights_any, weights_ref),
            (sources_any, sources_ref),
            (owners_any, owners_ref),
        ]
        small = [pltpu.make_async_copy(a, b, sems.at[n]) for n, (a, b) in enumerate(places)]
        for copy in small:
            copy.start()
        for copy in small:
            copy.wait()
        green = [own_ref[:, b, :] for b in range(walkers)]
        walk = lax.axis_index("walk")
        lane = lax.broadcasted_iota(jnp.int32, (1, LANES), 1)
        body = body_ref[...].astype(jnp.float32)
        onebody_ref[...] = jnp.zeros_like(onebody_ref)
        for b in range(walkers):
            total = jnp.sum(green[b].astype(jnp.float32) * body, axis=0, keepdims=True)
            folded = total[:, :LANES]
            for start in range(LANES, orbitals, LANES):
                folded = folded + total[:, start : start + LANES]
            onebody_ref[b : b + 1, :] = folded
        r = lax.broadcasted_iota(jnp.int32, (rows // pair, rows), 0)
        m = lax.broadcasted_iota(jnp.int32, (rows // pair, rows), 1)
        k = lax.broadcasted_iota(jnp.int32, (orbitals, LANES), 0)
        c = lax.broadcasted_iota(jnp.int32, (orbitals, LANES), 1)
        thinned = []
        for b in range(walkers):
            values = green[b]
            thinned.append(
                [
                    jnp.dot(
                        (m == r * pair + h).astype(jnp.bfloat16), values, preferred_element_type=jnp.float32
                    ).astype(jnp.bfloat16)
                    for h in range(pair)
                ]
            )
        for d in range(walk_size):
            target = walk_partner(walk, d, walk_size, False)
            out, top = spots[d]
            panel = jnp.int32(0)
            for p in range(walk_size):
                panel = jnp.where(owners_ref[p] == target, p, panel)
            for b in range(walkers):
                total = jnp.zeros((rows // pair, LANES), jnp.float32)
                for h in range(pair):
                    take = (k == panel * width + c - h * width) & (c >= h * width) & (c < (h + 1) * width)
                    total += jnp.dot(
                        thinned[b][h], take.astype(jnp.bfloat16), preferred_element_type=jnp.float32
                    )
                packs[out][top + b * (rows // pair) : top + (b + 1) * (rows // pair), :] = total.astype(jnp.bfloat16)
        spread = jnp.zeros((vectors, LANES), jnp.float32)
        source = jnp.zeros((1, LANES), jnp.float32)
        corner = lax.broadcasted_iota(jnp.int32, (vectors, vectors), 0) == lax.broadcasted_iota(
            jnp.int32, (vectors, vectors), 1
        )
        for j in range(slots):
            mine = lane % slots == j
            upright = jnp.sum(jnp.where(corner, fields_ref[j : j + 1, :], 0.0), axis=1, keepdims=True)
            spread += jnp.where(mine, upright, 0.0)
            source += jnp.where(mine, sources_ref[j].astype(jnp.float32), 0.0)
        weight = weights_ref[0]
        for j in range(1, weights.shape[0]):
            weight = weight + weights_ref[j]
        table_scr[...] = jnp.zeros_like(table_scr)
        table_scr[:vectors, :] = spread
        table_scr[vectors : vectors + 1, :] = source
        table_scr[vectors + 1 : vectors + 2, :] = jnp.zeros((1, LANES), jnp.float32) + weight
        rest = table_scr[...]
        for n in range(3):
            piece = rest.astype(jnp.bfloat16)
            rest = rest - piece.astype(jnp.float32)
            at = panel_rows + n * table_rows
            for d in range(len(heights)):
                packs[d][at : at + table_rows, :] = piece

    return pl.pallas_call(
        kernel,
        name="pack",
        out_shape=[
            jax.ShapeDtypeStruct((8, LANES), jnp.float32),
        ]
        + [jax.ShapeDtypeStruct((height, LANES), jnp.bfloat16) for height in heights],
        in_specs=[pl.BlockSpec(memory_space=pl.ANY)] * 6,
        out_specs=[vmem()] * (len(heights) + 1),
        scratch_shapes=[
            pltpu.VMEM(own.shape, own.dtype),
            pltpu.VMEM(one_body.shape, one_body.dtype),
            pltpu.VMEM((slots, vectors), jnp.float32),
            pltpu.SMEM(weights.shape, weights.dtype),
            pltpu.SMEM(sources.shape, sources.dtype),
            pltpu.SMEM(owners.shape, owners.dtype),
            pltpu.VMEM((table_rows, LANES), jnp.float32),
            pltpu.SemaphoreType.DMA((6,)),
        ],
        compiler_params=params(PACK_LIMIT),
        cost_estimate=pl.CostEstimate(flops=10**8, bytes_accessed=10**6, transcendentals=0),
    )(own, one_body, fields.T, weights, sources, owners)


def walk_partner(walk, d, size, back):
    if size == 4:
        return lax.bitwise_xor(walk, d)
    return lax.rem(walk + (size - d if back else d), size)


def exchange_far(packed):
    size = lax.axis_size("walk")
    if size != 4:
        return lax.ppermute(packed[1], "walk", [(q, (q + 1) % size) for q in range(size)])
    return lax.ppermute(packed[1], "walk", [(q, q ^ 2) for q in range(size)])


def exchange_near(packed, far):
    size = lax.axis_size("walk")
    if size != 4:
        return [
            lax.ppermute(packed[d], "walk", [(q, (q + d) % size) for q in range(size)]) for d in range(2, size)
        ]
    keep, _, near = packed
    panel = far.shape[0] - keep.shape[0]
    return [lax.ppermute(jnp.concatenate([near, far[panel:]], axis=0), "walk", [(q, q ^ 1) for q in range(size)])]


def walk_places(panel, table, size):
    if size != 4:
        return [(d, 0, panel) for d in range(size)]
    return [(0, 0, panel), (2, 0, panel), (1, 0, panel), (2, panel + 2 * table, panel + table)]


def read_table(ref, at, vectors):
    height = table_height(vectors)
    parts = [ref[at + n * height : at + (n + 1) * height, :].astype(jnp.float32) for n in range(3)]
    return parts[0] + (parts[1] + parts[2])


def merge_tables(tables, walk, walk_size, slots, lane):
    total = jnp.zeros_like(tables[0])
    for d, table in enumerate(tables):
        group = walk_partner(walk, d, walk_size, True)
        total += jnp.where(lane // slots == group, table, 0.0)
    return total


def measure(block, total, last, packs, places, onebody, vectors, slots):
    _, walkers, orbitals = last[0].shape
    depth = sum(x.shape[0] for x in last)
    walk_size = len(places)
    targets = walk_size * lax.axis_size("chol")
    whole = total is None
    quads = orbitals // LANES

    def fold(x):
        return jnp.sum(x.reshape(-1, 8, LANES), axis=0)

    def kernel(*refs):
        block_ref, onebody_ref = refs[:2]
        pack_refs = refs[2 : 2 + len(packs)]
        last_refs = refs[2 + len(packs) : 2 + len(packs) + len(last)]
        out_ref, tensor_scr = refs[-2:]
        walk = lax.axis_index("walk")
        lane = lax.broadcasted_iota(jnp.int32, (1, LANES), 1)
        table = merge_tables(
            [read_table(pack_refs[n], at, vectors) for n, _, at in places], walk, walk_size, slots, lane
        )
        picks = [
            jnp.where(
                (lane < slots * walk_size) & (table[vectors : vectors + 1, :] == (walk * walkers + b).astype(jnp.float32)),
                1.0,
                0.0,
            )
            for b in range(walkers)
        ]
        rhs = [jnp.concatenate([x[:, b, :] for x in last_refs], axis=0) for b in range(walkers)]
        eye = lax.broadcasted_iota(jnp.int32, (LANES, LANES), 0) == lax.broadcasted_iota(
            jnp.int32, (LANES, LANES), 1
        )
        exchange = [jnp.zeros((8, LANES), jnp.float32) for _ in range(walkers)]
        squares = [jnp.zeros((1, 1), jnp.float32) for _ in range(walkers)]
        drive = jnp.zeros((1, LANES), jnp.float32)
        for b in range(walkers):
            value = jnp.dot(block_ref[...], rhs[b], preferred_element_type=jnp.float32)
            tensor_scr[b] = value if whole else refs[2 + len(packs) + len(last)][b] + value
        for g in range(vectors):
            top = g * orbitals
            for b in range(walkers):
                diagonal = jnp.zeros((LANES, LANES), jnp.float32)
                for q in range(quads):
                    for p in range(q + 1):
                        one = tensor_scr[
                            b, top + q * LANES : top + (q + 1) * LANES, p * LANES : (p + 1) * LANES
                        ]
                        if p == q:
                            exchange[b] = exchange[b] + fold(one * one.T)
                            diagonal = diagonal + one
                        else:
                            two = tensor_scr[
                                b, top + p * LANES : top + (p + 1) * LANES, q * LANES : (q + 1) * LANES
                            ]
                            exchange[b] = exchange[b] + 2.0 * fold(two * one.T)
                trace = jnp.sum(fold(jnp.where(eye, diagonal, 0.0)), axis=0, keepdims=True)
                trace = jnp.sum(trace, axis=1, keepdims=True)
                squares[b] = squares[b] + trace * trace
                drive = drive - root_step * picks[b] * table[g : g + 1, :] * trace
        raw = jnp.zeros((1, LANES), jnp.float32)
        square = jnp.zeros((1, LANES), jnp.float32)
        for b in range(walkers):
            swapped = jnp.sum(jnp.sum(exchange[b], axis=0, keepdims=True), axis=1, keepdims=True)
            single = jnp.sum(onebody_ref[b : b + 1, :], axis=1, keepdims=True)
            raw += picks[b] * (single + 0.5 * squares[b] - 0.5 * swapped)
            square += picks[b] * squares[b]
        power = drive - 0.5 * time_step * square - time_step * raw
        out_ref[...] = jnp.broadcast_to(raw + pltpu.roll(power, slots * walk_size, 1), (targets, LANES))

    arrays = list(last) + ([] if whole else [total])
    return pl.pallas_call(
        kernel,
        name="measure",
        out_shape=jax.ShapeDtypeStruct((targets, LANES), jnp.float32),
        in_specs=[vmem()] * (2 + len(packs) + len(arrays)),
        out_specs=vmem(),
        scratch_shapes=[
            pltpu.VMEM((walkers, vectors * orbitals, orbitals), jnp.float32),
        ],
        compiler_params=params(),
        cost_estimate=pl.CostEstimate(
            flops=2 * vectors * orbitals * depth * walkers * orbitals,
            bytes_accessed=2 * vectors * orbitals * depth,
            transcendentals=0,
        ),
    )(block, onebody, *packs, *arrays)


def finish(stats, packs, places, counts, vectors, slots, walkers):
    walk_size = len(places)
    rows = (packs[0].shape[0] - 3 * table_height(vectors)) // walkers

    def kernel(stats_ref, counts_ref, *refs):
        pack_refs = refs[: len(packs)]
        energies_ref, weights_ref, density_ref = refs[len(packs) :]
        walk = lax.axis_index("walk")
        lane = lax.broadcasted_iota(jnp.int32, (1, LANES), 1)
        all_slots = slots * walk_size
        tables = [read_table(pack_refs[n], at, vectors) for n, _, at in places]
        source = merge_tables([t[vectors : vectors + 1, :] for t in tables], walk, walk_size, slots, lane)
        total_weight = tables[0][vectors + 1 : vectors + 2, :]
        for t in tables[1:]:
            total_weight = total_weight + t[vectors + 1 : vectors + 2, :]
        mean_weight = total_weight / (walkers * walk_size)
        total = jnp.sum(stats_ref[...], axis=0, keepdims=True)
        power = pltpu.roll(total, LANES - all_slots, 1)
        live_count = jnp.zeros((1, LANES), jnp.int32)
        for q in range(walk_size):
            live_count = jnp.where(lane // slots == q, counts_ref[q], live_count)
        live = (lane < all_slots) & (lane % slots < live_count)
        energies = jnp.where(live, total, 0.0)
        new_weights = jnp.where(live, mean_weight * jnp.exp(jnp.where(live, power, 0.0)), 0.0)
        norm = jnp.sum(new_weights, axis=1, keepdims=True)
        density = jnp.zeros((rows, LANES), jnp.float32)
        for d, (n, top, _) in enumerate(places):
            group = walk_partner(walk, d, walk_size, True)
            for b in range(walkers):
                walker = (group * walkers + b).astype(jnp.float32)
                share = jnp.sum(jnp.where(source == walker, new_weights, 0.0), axis=1, keepdims=True) / norm
                density += share * pack_refs[n][top + b * rows : top + (b + 1) * rows, :].astype(jnp.float32)
        density_ref[...] = density
        first = lax.rem(LANES - walk * slots, LANES)
        energies_ref[...] = pltpu.roll(jnp.broadcast_to(energies, (8, LANES)), first, 1)[:1, :slots]
        weights_ref[...] = pltpu.roll(jnp.broadcast_to(new_weights, (8, LANES)), first, 1)[:1, :slots]

    return pl.pallas_call(
        kernel,
        name="finish",
        out_shape=[
            jax.ShapeDtypeStruct((1, slots), jnp.float32),
            jax.ShapeDtypeStruct((1, slots), jnp.float32),
            jax.ShapeDtypeStruct((rows, LANES), jnp.float32),
        ],
        in_specs=[vmem(), smem()] + [vmem()] * len(packs),
        out_specs=[vmem()] * 3,
        compiler_params=params(),
        cost_estimate=pl.CostEstimate(flops=10**6, bytes_accessed=6 * 10**5, transcendentals=128),
    )(stats, counts, *packs)


def per_device(green_rows, cholesky_rot, one_body, fields, weights, sources, counts, owners):
    chol_size = lax.axis_size("chol")
    walk_size = lax.axis_size("walk")
    vectors, slots = fields.shape
    walkers = green_rows.shape[1]
    onebody, *packed = pack(green_rows, one_body, fields, weights, sources, owners)
    if chol_size > RING_LIMIT or chol_size % 2 or chol_size < 8:
        block = cholesky_rot.reshape(-1, cholesky_rot.shape[2])
        far = exchange_far(packed)
        packs = [packed[0], far] + exchange_near(packed, far)
        total, last = None, [lax.all_gather(green_rows, "chol", axis=0, tiled=True)]
    else:
        block, onebody, total, last, packs = ring(green_rows, cholesky_rot, onebody, packed)
    table = 3 * table_height(vectors)
    places = walk_places(packs[0].shape[0] - table, table, walk_size)
    stats = measure(block, total, last, packs, places, onebody, vectors, slots)
    stats = lax.all_to_all(stats, ("chol", "walk"), split_axis=0, concat_axis=0, tiled=True)
    energies, new_weights, density = finish(stats, packs, places, counts, vectors, slots, walkers)
    return energies.reshape(slots), new_weights.reshape(slots), density.reshape(1, density.size)


def solution(mesh):
    return jax.shard_map(
        per_device,
        mesh=mesh,
        in_specs=(
            P("chol", "walk", None),
            P("chol", None, None),
            P("chol", None),
            P("chol", "walk"),
            P("walk"),
            P("walk"),
            P(),
            P(),
        ),
        out_specs=(P("walk"), P("walk"), P("walk", "chol")),
        check_vma=False,
    )
```

```python
import jax
import jax.numpy as jnp
from jax import lax
from jax.experimental import pallas as pl
from jax.experimental.pallas import tpu as pltpu
from jax.sharding import PartitionSpec as P

time_step = 0.02
root_step = 0.02**0.5
LANES = 128
VMEM_LIMIT = 16 * 1024 * 1024
PACK_LIMIT = 54 * 1024 * 1024
ACCUMULATE_LIMIT = 40 * 1024 * 1024
FETCH_LIMIT = 48 * 1024 * 1024
RING_LIMIT = 16


def params(limit=VMEM_LIMIT):
    return pltpu.CompilerParams(vmem_limit_bytes=limit)


def vmem():
    return pl.BlockSpec(memory_space=pltpu.VMEM)


def smem():
    return pl.BlockSpec(memory_space=pltpu.SMEM)


def ring_order(size):
    return [2 * q if q < size // 2 else 2 * (size - 1 - q) + 1 for q in range(size)]


def ring_place(index, size):
    return jnp.where(index % 2 == 0, index // 2, size - 1 - index // 2)


def ring_owner(place, size):
    return jnp.where(place < size // 2, 2 * place, 2 * (size - 1 - place) + 1)


def column_start(shift, rows):
    size = lax.axis_size("chol")
    place = ring_place(lax.axis_index("chol"), size)
    shift = jnp.where(lax.axis_index("walk") % 2 == 0, shift, -shift)
    owner = ring_owner(lax.rem(place + shift + size, size), size)
    return pl.multiple_of(owner * rows, rows)


def start_columns(chol_any, shifts, rows, target, sems):
    copies = [
        pltpu.make_async_copy(
            chol_any.at[:, :, pl.ds(column_start(shift, rows), rows)],
            target.at[:, :, pl.ds(n * rows, rows)],
            sems.at[n],
        )
        for n, shift in enumerate(shifts)
    ]
    for copy in copies:
        copy.start()
    return copies


def fetch(cholesky_rot, shifts, rows, mark):
    vectors, orbitals, _ = cholesky_rot.shape

    def kernel(chol_any, mark_any, blocks_ref, mark_ref, sems):
        copies = start_columns(chol_any, shifts, rows, blocks_ref, sems)
        mark_ref[...] = jnp.zeros_like(mark_ref)
        for copy in copies:
            copy.wait()

    return pl.pallas_call(
        kernel,
        name="fetch",
        out_shape=[
            jax.ShapeDtypeStruct((vectors, orbitals, len(shifts) * rows), cholesky_rot.dtype),
            jax.ShapeDtypeStruct((8, LANES), jnp.float32),
        ],
        in_specs=[pl.BlockSpec(memory_space=pl.ANY)] * 2,
        out_specs=[vmem()] * 2,
        scratch_shapes=[pltpu.SemaphoreType.DMA((len(shifts),))],
        compiler_params=params(FETCH_LIMIT),
        cost_estimate=pl.CostEstimate(
            flops=0, bytes_accessed=4 * vectors * orbitals * len(shifts) * rows, transcendentals=0
        ),
    )(cholesky_rot, mark)


def accumulate(cholesky_rot, blocks, parts, total, mark, ahead):
    vectors, orbitals, _ = cholesky_rot.shape
    rows, walkers, _ = parts[0].shape
    size = vectors * orbitals
    arrays = [blocks] + list(parts) + [mark] + ([] if total is None else [total])

    def kernel(chol_any, *refs):
        blocks_ref = refs[0]
        shards = refs[1 : 1 + len(parts)]
        total_ref, mark_ref, ahead_ref, sems = refs[len(arrays) :]
        copies = start_columns(chol_any, ahead, rows, ahead_ref, sems)
        mark_ref[...] = jnp.zeros_like(mark_ref)
        for b in range(walkers):
            rhs = jnp.concatenate([x[:, b, :] for x in shards], axis=0)
            value = jnp.dot(
                blocks_ref[...].reshape(size, -1), rhs, preferred_element_type=jnp.float32
            )
            total_ref[b] = value if total is None else refs[len(arrays) - 1][b] + value
        for copy in copies:
            copy.wait()

    return pl.pallas_call(
        kernel,
        name="accumulate",
        out_shape=[
            jax.ShapeDtypeStruct((walkers, size, orbitals), jnp.float32),
            jax.ShapeDtypeStruct((8, LANES), jnp.float32),
            jax.ShapeDtypeStruct((vectors, orbitals, len(ahead) * rows), cholesky_rot.dtype),
        ],
        in_specs=[pl.BlockSpec(memory_space=pl.ANY)] + [vmem()] * len(arrays),
        out_specs=[vmem()] * 3,
        scratch_shapes=[pltpu.SemaphoreType.DMA((len(ahead),))],
        compiler_params=params(ACCUMULATE_LIMIT),
        cost_estimate=pl.CostEstimate(
            flops=2 * len(parts) * size * rows * walkers * orbitals,
            bytes_accessed=4 * len(ahead) * size * rows,
            transcendentals=0,
        ),
    )(cholesky_rot, *arrays)


def tie(*arrays):
    return lax.optimization_barrier(arrays)


def ring(own, cholesky_rot, onebody, packed):
    size = lax.axis_size("chol")
    walk_size = lax.axis_size("walk")
    rows = own.shape[0]
    order = ring_order(size)
    pairs = [[], []]
    for q in range(size):
        for w in range(walk_size):
            for n, turn in enumerate((1 - 2 * (w % 2), 2 * (w % 2) - 1)):
                pairs[n].append((order[q] * walk_size + w, order[(q + turn) % size] * walk_size + w))

    def send(x, n):
        return lax.ppermute(x, ("chol", "walk"), pairs[n])

    steps = size // 2
    one = send(own, 0)
    other, onebody = tie(own, onebody)
    other = send(other, 1)
    blocks, mark = fetch(cholesky_rot, [0, -1, 1], rows, onebody)
    held = [own]
    total = None
    for step in range(1, steps):
        final = step == steps - 1
        one, mark = tie(one, mark)
        next_one = send(one[: rows // 2] if final else one, 0)
        if step == 1:
            *packed, mark = tie(*packed, mark)
            far = exchange_far(packed)
        else:
            total, mark, blocks = accumulate(cholesky_rot, blocks, held, total, mark, [-step, step])
            held = []
        if step == 2:
            other, mark, far = tie(other, mark, far)
            near = exchange_near(packed, far)
        elif step == 3:
            other, mark, *near = tie(other, mark, *near)
        else:
            other, mark = tie(other, mark)
        next_other = send(other[rows // 2 :] if final else other, 1)
        held = held + [one, other]
        one, other = next_one, next_other
    total, _, blocks = accumulate(cholesky_rot, blocks, held, total, mark, [steps])
    return blocks, onebody, total, [one, other], [packed[0], far] + near


def table_height(vectors):
    return -(-(vectors + 2) // 16) * 16


def pack(own, one_body, fields, weights, sources, owners):
    rows, walkers, orbitals = own.shape
    walk_size = lax.axis_size("walk")
    width = orbitals // walk_size
    pair = LANES // width
    vectors, slots = fields.shape
    table_rows = table_height(vectors)
    panel_rows = walkers * (rows // pair)
    both = panel_rows + 3 * table_rows
    if walk_size == 4:
        heights = [both, both + panel_rows, both]
        spots = [(0, 0), (2, 0), (1, 0), (1, both)]
    else:
        heights = [both] * walk_size
        spots = [(d, 0) for d in range(walk_size)]

    def kernel(own_any, body_any, fields_any, weights_any, sources_any, owners_any, *refs):
        onebody_ref = refs[0]
        packs = refs[1 : 1 + len(heights)]
        own_ref, body_ref, fields_ref, weights_ref, sources_ref, owners_ref, table_scr, sems = refs[1 + len(heights) :]
        places = [
            (own_any, own_ref),
            (body_any, body_ref),
            (fields_any, fields_ref),
            (weights_any, weights_ref),
            (sources_any, sources_ref),
            (owners_any, owners_ref),
        ]
        small = [pltpu.make_async_copy(a, b, sems.at[n]) for n, (a, b) in enumerate(places)]
        for copy in small:
            copy.start()
        for copy in small:
            copy.wait()
        green = [own_ref[:, b, :] for b in range(walkers)]
        walk = lax.axis_index("walk")
        lane = lax.broadcasted_iota(jnp.int32, (1, LANES), 1)
        body = body_ref[...].astype(jnp.float32)
        onebody_ref[...] = jnp.zeros_like(onebody_ref)
        for b in range(walkers):
            total = jnp.sum(green[b].astype(jnp.float32) * body, axis=0, keepdims=True)
            folded = total[:, :LANES]
            for start in range(LANES, orbitals, LANES):
                folded = folded + total[:, start : start + LANES]
            onebody_ref[b : b + 1, :] = folded
        r = lax.broadcasted_iota(jnp.int32, (rows // pair, rows), 0)
        m = lax.broadcasted_iota(jnp.int32, (rows // pair, rows), 1)
        k = lax.broadcasted_iota(jnp.int32, (orbitals, LANES), 0)
        c = lax.broadcasted_iota(jnp.int32, (orbitals, LANES), 1)
        thinned = []
        for b in range(walkers):
            values = green[b]
            thinned.append(
                [
                    jnp.dot(
                        (m == r * pair + h).astype(jnp.bfloat16), values, preferred_element_type=jnp.float32
                    ).astype(jnp.bfloat16)
                    for h in range(pair)
                ]
            )
        for d in range(walk_size):
            target = walk_partner(walk, d, walk_size, False)
            out, top = spots[d]
            panel = jnp.int32(0)
            for p in range(walk_size):
                panel = jnp.where(owners_ref[p] == target, p, panel)
            for b in range(walkers):
                total = jnp.zeros((rows // pair, LANES), jnp.float32)
                for h in range(pair):
                    take = (k == panel * width + c - h * width) & (c >= h * width) & (c < (h + 1) * width)
                    total += jnp.dot(
                        thinned[b][h], take.astype(jnp.bfloat16), preferred_element_type=jnp.float32
                    )
                packs[out][top + b * (rows // pair) : top + (b + 1) * (rows // pair), :] = total.astype(jnp.bfloat16)
        spread = jnp.zeros((vectors, LANES), jnp.float32)
        source = jnp.zeros((1, LANES), jnp.float32)
        corner = lax.broadcasted_iota(jnp.int32, (vectors, vectors), 0) == lax.broadcasted_iota(
            jnp.int32, (vectors, vectors), 1
        )
        for j in range(slots):
            mine = lane % slots == j
            upright = jnp.sum(jnp.where(corner, fields_ref[j : j + 1, :], 0.0), axis=1, keepdims=True)
            spread += jnp.where(mine, upright, 0.0)
            source += jnp.where(mine, sources_ref[j].astype(jnp.float32), 0.0)
        weight = weights_ref[0]
        for j in range(1, weights.shape[0]):
            weight = weight + weights_ref[j]
        table_scr[...] = jnp.zeros_like(table_scr)
        table_scr[:vectors, :] = spread
        table_scr[vectors : vectors + 1, :] = source
        table_scr[vectors + 1 : vectors + 2, :] = jnp.zeros((1, LANES), jnp.float32) + weight
        rest = table_scr[...]
        for n in range(3):
            piece = rest.astype(jnp.bfloat16)
            rest = rest - piece.astype(jnp.float32)
            at = panel_rows + n * table_rows
            for d in range(len(heights)):
                packs[d][at : at + table_rows, :] = piece

    return pl.pallas_call(
        kernel,
        name="pack",
        out_shape=[
            jax.ShapeDtypeStruct((8, LANES), jnp.float32),
        ]
        + [jax.ShapeDtypeStruct((height, LANES), jnp.bfloat16) for height in heights],
        in_specs=[pl.BlockSpec(memory_space=pl.ANY)] * 6,
        out_specs=[vmem()] * (len(heights) + 1),
        scratch_shapes=[
            pltpu.VMEM(own.shape, own.dtype),
            pltpu.VMEM(one_body.shape, one_body.dtype),
            pltpu.VMEM((slots, vectors), jnp.float32),
            pltpu.SMEM(weights.shape, weights.dtype),
            pltpu.SMEM(sources.shape, sources.dtype),
            pltpu.SMEM(owners.shape, owners.dtype),
            pltpu.VMEM((table_rows, LANES), jnp.float32),
            pltpu.SemaphoreType.DMA((6,)),
        ],
        compiler_params=params(PACK_LIMIT),
        cost_estimate=pl.CostEstimate(flops=10**8, bytes_accessed=10**6, transcendentals=0),
    )(own, one_body, fields.T, weights, sources, owners)


def walk_partner(walk, d, size, back):
    if size == 4:
        return lax.bitwise_xor(walk, d)
    return lax.rem(walk + (size - d if back else d), size)


def exchange_far(packed):
    size = lax.axis_size("walk")
    if size != 4:
        return lax.ppermute(packed[1], "walk", [(q, (q + 1) % size) for q in range(size)])
    return lax.ppermute(packed[1], "walk", [(q, q ^ 2) for q in range(size)])


def exchange_near(packed, far):
    size = lax.axis_size("walk")
    if size != 4:
        return [
            lax.ppermute(packed[d], "walk", [(q, (q + d) % size) for q in range(size)]) for d in range(2, size)
        ]
    keep, _, near = packed
    panel = far.shape[0] - keep.shape[0]
    return [lax.ppermute(jnp.concatenate([near, far[panel:]], axis=0), "walk", [(q, q ^ 1) for q in range(size)])]


def walk_places(panel, table, size):
    if size != 4:
        return [(d, 0, panel) for d in range(size)]
    return [(0, 0, panel), (2, 0, panel), (1, 0, panel), (2, panel + 2 * table, panel + table)]


def read_table(ref, at, vectors):
    height = table_height(vectors)
    parts = [ref[at + n * height : at + (n + 1) * height, :].astype(jnp.float32) for n in range(3)]
    return parts[0] + (parts[1] + parts[2])


def merge_tables(tables, walk, walk_size, slots, lane):
    total = jnp.zeros_like(tables[0])
    for d, table in enumerate(tables):
        group = walk_partner(walk, d, walk_size, True)
        total += jnp.where(lane // slots == group, table, 0.0)
    return total


def measure(block, total, last, packs, places, onebody, vectors, slots):
    _, walkers, orbitals = last[0].shape
    depth = sum(x.shape[0] for x in last)
    walk_size = len(places)
    targets = walk_size * lax.axis_size("chol")
    whole = total is None
    quads = orbitals // LANES

    def fold(x):
        return jnp.sum(x.reshape(-1, 8, LANES), axis=0)

    def kernel(*refs):
        block_ref, onebody_ref = refs[:2]
        pack_refs = refs[2 : 2 + len(packs)]
        last_refs = refs[2 + len(packs) : 2 + len(packs) + len(last)]
        out_ref, tensor_scr = refs[-2:]
        walk = lax.axis_index("walk")
        lane = lax.broadcasted_iota(jnp.int32, (1, LANES), 1)
        table = merge_tables(
            [read_table(pack_refs[n], at, vectors) for n, _, at in places], walk, walk_size, slots, lane
        )
        picks = [
            jnp.where(
                (lane < slots * walk_size) & (table[vectors : vectors + 1, :] == (walk * walkers + b).astype(jnp.float32)),
                1.0,
                0.0,
            )
            for b in range(walkers)
        ]
        rhs = [jnp.concatenate([x[:, b, :] for x in last_refs], axis=0) for b in range(walkers)]
        eye = lax.broadcasted_iota(jnp.int32, (LANES, LANES), 0) == lax.broadcasted_iota(
            jnp.int32, (LANES, LANES), 1
        )
        exchange = [jnp.zeros((8, LANES), jnp.float32) for _ in range(walkers)]
        squares = [jnp.zeros((1, 1), jnp.float32) for _ in range(walkers)]
        drive = jnp.zeros((1, LANES), jnp.float32)
        for b in range(walkers):
            value = jnp.dot(
                block_ref[...].reshape(vectors * orbitals, depth), rhs[b], preferred_element_type=jnp.float32
            )
            tensor_scr[b] = value if whole else refs[2 + len(packs) + len(last)][b] + value
        for g in range(vectors):
            top = g * orbitals
            for b in range(walkers):
                diagonal = jnp.zeros((LANES, LANES), jnp.float32)
                for q in range(quads):
                    for p in range(q + 1):
                        one = tensor_scr[
                            b, top + q * LANES : top + (q + 1) * LANES, p * LANES : (p + 1) * LANES
                        ]
                        if p == q:
                            exchange[b] = exchange[b] + fold(one * one.T)
                            diagonal = diagonal + one
                        else:
                            two = tensor_scr[
                                b, top + p * LANES : top + (p + 1) * LANES, q * LANES : (q + 1) * LANES
                            ]
                            exchange[b] = exchange[b] + 2.0 * fold(two * one.T)
                trace = jnp.sum(fold(jnp.where(eye, diagonal, 0.0)), axis=0, keepdims=True)
                trace = jnp.sum(trace, axis=1, keepdims=True)
                squares[b] = squares[b] + trace * trace
                drive = drive - root_step * picks[b] * table[g : g + 1, :] * trace
        raw = jnp.zeros((1, LANES), jnp.float32)
        square = jnp.zeros((1, LANES), jnp.float32)
        for b in range(walkers):
            swapped = jnp.sum(jnp.sum(exchange[b], axis=0, keepdims=True), axis=1, keepdims=True)
            single = jnp.sum(onebody_ref[b : b + 1, :], axis=1, keepdims=True)
            raw += picks[b] * (single + 0.5 * squares[b] - 0.5 * swapped)
            square += picks[b] * squares[b]
        power = drive - 0.5 * time_step * square - time_step * raw
        out_ref[...] = jnp.broadcast_to(raw + pltpu.roll(power, slots * walk_size, 1), (targets, LANES))

    arrays = list(last) + ([] if whole else [total])
    return pl.pallas_call(
        kernel,
        name="measure",
        out_shape=jax.ShapeDtypeStruct((targets, LANES), jnp.float32),
        in_specs=[vmem()] * (2 + len(packs) + len(arrays)),
        out_specs=vmem(),
        scratch_shapes=[
            pltpu.VMEM((walkers, vectors * orbitals, orbitals), jnp.float32),
        ],
        compiler_params=params(),
        cost_estimate=pl.CostEstimate(
            flops=2 * vectors * orbitals * depth * walkers * orbitals,
            bytes_accessed=2 * vectors * orbitals * depth,
            transcendentals=0,
        ),
    )(block, onebody, *packs, *arrays)


def finish(stats, packs, places, counts, vectors, slots, walkers):
    walk_size = len(places)
    rows = (packs[0].shape[0] - 3 * table_height(vectors)) // walkers

    def kernel(stats_ref, counts_ref, *refs):
        pack_refs = refs[: len(packs)]
        energies_ref, weights_ref, density_ref = refs[len(packs) :]
        walk = lax.axis_index("walk")
        lane = lax.broadcasted_iota(jnp.int32, (1, LANES), 1)
        all_slots = slots * walk_size
        tables = [read_table(pack_refs[n], at, vectors) for n, _, at in places]
        source = merge_tables([t[vectors : vectors + 1, :] for t in tables], walk, walk_size, slots, lane)
        total_weight = tables[0][vectors + 1 : vectors + 2, :]
        for t in tables[1:]:
            total_weight = total_weight + t[vectors + 1 : vectors + 2, :]
        mean_weight = total_weight / (walkers * walk_size)
        total = jnp.sum(stats_ref[...], axis=0, keepdims=True)
        power = pltpu.roll(total, LANES - all_slots, 1)
        live_count = jnp.zeros((1, LANES), jnp.int32)
        for q in range(walk_size):
            live_count = jnp.where(lane // slots == q, counts_ref[q], live_count)
        live = (lane < all_slots) & (lane % slots < live_count)
        energies = jnp.where(live, total, 0.0)
        new_weights = jnp.where(live, mean_weight * jnp.exp(jnp.where(live, power, 0.0)), 0.0)
        norm = jnp.sum(new_weights, axis=1, keepdims=True)
        density = jnp.zeros((rows, LANES), jnp.float32)
        for d, (n, top, _) in enumerate(places):
            group = walk_partner(walk, d, walk_size, True)
            for b in range(walkers):
                walker = (group * walkers + b).astype(jnp.float32)
                share = jnp.sum(jnp.where(source == walker, new_weights, 0.0), axis=1, keepdims=True) / norm
                density += share * pack_refs[n][top + b * rows : top + (b + 1) * rows, :].astype(jnp.float32)
        density_ref[...] = density
        first = lax.rem(LANES - walk * slots, LANES)
        energies_ref[...] = pltpu.roll(jnp.broadcast_to(energies, (8, LANES)), first, 1)[:1, :slots]
        weights_ref[...] = pltpu.roll(jnp.broadcast_to(new_weights, (8, LANES)), first, 1)[:1, :slots]

    return pl.pallas_call(
        kernel,
        name="finish",
        out_shape=[
            jax.ShapeDtypeStruct((1, slots), jnp.float32),
            jax.ShapeDtypeStruct((1, slots), jnp.float32),
            jax.ShapeDtypeStruct((rows, LANES), jnp.float32),
        ],
        in_specs=[vmem(), smem()] + [vmem()] * len(packs),
        out_specs=[vmem()] * 3,
        compiler_params=params(),
        cost_estimate=pl.CostEstimate(flops=10**6, bytes_accessed=6 * 10**5, transcendentals=128),
    )(stats, counts, *packs)


def per_device(green_rows, cholesky_rot, one_body, fields, weights, sources, counts, owners):
    chol_size = lax.axis_size("chol")
    walk_size = lax.axis_size("walk")
    vectors, slots = fields.shape
    walkers = green_rows.shape[1]
    onebody, *packed = pack(green_rows, one_body, fields, weights, sources, owners)
    if chol_size > RING_LIMIT or chol_size % 2 or chol_size < 8:
        block = cholesky_rot
        far = exchange_far(packed)
        packs = [packed[0], far] + exchange_near(packed, far)
        total, last = None, [lax.all_gather(green_rows, "chol", axis=0, tiled=True)]
    else:
        block, onebody, total, last, packs = ring(green_rows, cholesky_rot, onebody, packed)
    table = 3 * table_height(vectors)
    places = walk_places(packs[0].shape[0] - table, table, walk_size)
    stats = measure(block, total, last, packs, places, onebody, vectors, slots)
    stats = lax.all_to_all(stats, ("chol", "walk"), split_axis=0, concat_axis=0, tiled=True)
    energies, new_weights, density = finish(stats, packs, places, counts, vectors, slots, walkers)
    return energies.reshape(slots), new_weights.reshape(slots), density.reshape(1, density.size)


def solution(mesh):
    return jax.shard_map(
        per_device,
        mesh=mesh,
        in_specs=(
            P("chol", "walk", None),
            P("chol", None, None),
            P("chol", None),
            P("chol", "walk"),
            P("walk"),
            P("walk"),
            P(),
            P(),
        ),
        out_specs=(P("walk"), P("walk"), P("walk", "chol")),
        check_vma=False,
    )
```

```python
import jax
import jax.numpy as jnp
from jax import lax
from jax.experimental import pallas as pl
from jax.experimental.pallas import tpu as pltpu
from jax.sharding import PartitionSpec as P

time_step = 0.02
root_step = 0.02**0.5
LANES = 128
VMEM_LIMIT = 16 * 1024 * 1024
PACK_LIMIT = 54 * 1024 * 1024
ACCUMULATE_LIMIT = 24 * 1024 * 1024
RING_LIMIT = 16


def params(limit=VMEM_LIMIT):
    return pltpu.CompilerParams(vmem_limit_bytes=limit)


def vmem():
    return pl.BlockSpec(memory_space=pltpu.VMEM)


def smem():
    return pl.BlockSpec(memory_space=pltpu.SMEM)


def ring_order(size):
    return [2 * q if q < size // 2 else 2 * (size - 1 - q) + 1 for q in range(size)]


def ring_place(index, size):
    return jnp.where(index % 2 == 0, index // 2, size - 1 - index // 2)


def ring_owner(place, size):
    return jnp.where(place < size // 2, 2 * place, 2 * (size - 1 - place) + 1)


def column_start(shift, rows):
    size = lax.axis_size("chol")
    place = ring_place(lax.axis_index("chol"), size)
    owner = ring_owner(lax.rem(place + shift + size, size), size)
    return pl.multiple_of(owner * rows, rows)


def accumulate(cholesky_rot, shifts, parts, total, mark):
    vectors, orbitals, _ = cholesky_rot.shape
    rows, walkers, _ = parts[0].shape
    size = vectors * orbitals
    arrays = list(parts) + ([] if mark is None else [mark]) + ([] if total is None else [total])

    def kernel(chol_ref, *refs):
        shards = refs[: len(parts)]
        total_ref, mark_ref = refs[len(arrays) :]
        mark_ref[...] = jnp.zeros_like(mark_ref)
        lhs = jnp.concatenate(
            [chol_ref[:, :, pl.ds(column_start(shift, rows), rows)].reshape(size, rows) for shift in shifts], axis=1
        )
        for b in range(walkers):
            rhs = jnp.concatenate([x[:, b, :] for x in shards], axis=0)
            value = jnp.dot(lhs, rhs, preferred_element_type=jnp.float32)
            total_ref[b] = value if total is None else refs[len(arrays) - 1][b] + value

    return pl.pallas_call(
        kernel,
        name="accumulate",
        out_shape=[
            jax.ShapeDtypeStruct((walkers, size, orbitals), jnp.float32),
            jax.ShapeDtypeStruct((8, LANES), jnp.float32),
        ],
        in_specs=[vmem()] * (1 + len(arrays)),
        out_specs=[vmem()] * 2,
        compiler_params=params(ACCUMULATE_LIMIT),
        cost_estimate=pl.CostEstimate(
            flops=2 * len(parts) * size * rows * walkers * orbitals,
            bytes_accessed=2 * len(parts) * size * rows,
            transcendentals=0,
        ),
    )(cholesky_rot, *arrays)


def tie(*arrays):
    return lax.optimization_barrier(arrays)


def ring(own, cholesky_rot, onebody, packed):
    size = lax.axis_size("chol")
    rows = own.shape[0]
    order = ring_order(size)
    ahead = [(order[q], order[(q + 1) % size]) for q in range(size)]
    back = [(order[q], order[(q - 1) % size]) for q in range(size)]
    steps = size // 2
    right = left = own
    shifts, parts = [0], [own]
    total = mark = None
    for step in range(1, steps):
        next_right, next_left = lax.ppermute(right, "chol", ahead), lax.ppermute(left, "chol", back)
        if step == 1:
            right, onebody = tie(next_right, onebody)
            left, *packed = tie(next_left, *packed)
        elif step == 2:
            far = exchange_far(packed)
            right = next_right
            left, far = tie(next_left, far)
        else:
            if step == 3:
                near = exchange_near(packed, far)
            total, mark = accumulate(cholesky_rot, shifts[:-2], parts[:-2], total, mark)
            shifts, parts = shifts[-2:], parts[-2:]
            right, mark = tie(next_right, mark)
            if step == 3:
                left, mark, *near = tie(next_left, mark, *near)
            else:
                left, mark = tie(next_left, mark)
        shifts += [-step, step]
        parts = parts + [right, left]
    last = [lax.ppermute(right[: rows // 2], "chol", ahead), lax.ppermute(left[rows // 2 :], "chol", back)]
    total, _ = accumulate(cholesky_rot, shifts, parts, total, mark)
    return onebody, total, last, [packed[0], far] + near


def table_height(vectors):
    return -(-(vectors + 2) // 16) * 16


def pack(own, one_body, fields, weights, sources, owners, cholesky_rot):
    rows, walkers, orbitals = own.shape
    walk_size = lax.axis_size("walk")
    width = orbitals // walk_size
    pair = LANES // width
    vectors, slots = fields.shape
    table_rows = table_height(vectors)
    panel_rows = walkers * (rows // pair)
    both = panel_rows + 3 * table_rows
    if walk_size == 4:
        heights = [both, both + panel_rows, both]
        spots = [(0, 0), (2, 0), (1, 0), (1, both)]
    else:
        heights = [both] * walk_size
        spots = [(d, 0) for d in range(walk_size)]

    def kernel(own_any, body_any, fields_any, weights_any, sources_any, owners_any, chol_any, *refs):
        onebody_ref = refs[0]
        packs = refs[1 : 1 + len(heights)]
        own_ref, body_ref, fields_ref, weights_ref, sources_ref, owners_ref, table_scr, sems = refs[1 + len(heights) :]
        places = [
            (own_any, own_ref),
            (body_any, body_ref),
            (fields_any, fields_ref),
            (weights_any, weights_ref),
            (sources_any, sources_ref),
            (owners_any, owners_ref),
        ]
        small = [pltpu.make_async_copy(a, b, sems.at[n]) for n, (a, b) in enumerate(places)]
        for copy in small:
            copy.start()
        for copy in small:
            copy.wait()
        green = [own_ref[:, b, :] for b in range(walkers)]
        walk = lax.axis_index("walk")
        lane = lax.broadcasted_iota(jnp.int32, (1, LANES), 1)
        body = body_ref[...].astype(jnp.float32)
        onebody_ref[...] = jnp.zeros_like(onebody_ref)
        for b in range(walkers):
            total = jnp.sum(green[b].astype(jnp.float32) * body, axis=0, keepdims=True)
            folded = total[:, :LANES]
            for start in range(LANES, orbitals, LANES):
                folded = folded + total[:, start : start + LANES]
            onebody_ref[b : b + 1, :] = folded
        r = lax.broadcasted_iota(jnp.int32, (rows // pair, rows), 0)
        m = lax.broadcasted_iota(jnp.int32, (rows // pair, rows), 1)
        k = lax.broadcasted_iota(jnp.int32, (orbitals, LANES), 0)
        c = lax.broadcasted_iota(jnp.int32, (orbitals, LANES), 1)
        thinned = []
        for b in range(walkers):
            values = green[b]
            thinned.append(
                [
                    jnp.dot(
                        (m == r * pair + h).astype(jnp.bfloat16), values, preferred_element_type=jnp.float32
                    ).astype(jnp.bfloat16)
                    for h in range(pair)
                ]
            )
        for d in range(walk_size):
            target = walk_partner(walk, d, walk_size, False)
            out, top = spots[d]
            panel = jnp.int32(0)
            for p in range(walk_size):
                panel = jnp.where(owners_ref[p] == target, p, panel)
            for b in range(walkers):
                total = jnp.zeros((rows // pair, LANES), jnp.float32)
                for h in range(pair):
                    take = (k == panel * width + c - h * width) & (c >= h * width) & (c < (h + 1) * width)
                    total += jnp.dot(
                        thinned[b][h], take.astype(jnp.bfloat16), preferred_element_type=jnp.float32
                    )
                packs[out][top + b * (rows // pair) : top + (b + 1) * (rows // pair), :] = total.astype(jnp.bfloat16)
        spread = jnp.zeros((vectors, LANES), jnp.float32)
        source = jnp.zeros((1, LANES), jnp.float32)
        corner = lax.broadcasted_iota(jnp.int32, (vectors, vectors), 0) == lax.broadcasted_iota(
            jnp.int32, (vectors, vectors), 1
        )
        for j in range(slots):
            mine = lane % slots == j
            upright = jnp.sum(jnp.where(corner, fields_ref[j : j + 1, :], 0.0), axis=1, keepdims=True)
            spread += jnp.where(mine, upright, 0.0)
            source += jnp.where(mine, sources_ref[j].astype(jnp.float32), 0.0)
        weight = weights_ref[0]
        for j in range(1, weights.shape[0]):
            weight = weight + weights_ref[j]
        table_scr[...] = jnp.zeros_like(table_scr)
        table_scr[:vectors, :] = spread
        table_scr[vectors : vectors + 1, :] = source
        table_scr[vectors + 1 : vectors + 2, :] = jnp.zeros((1, LANES), jnp.float32) + weight
        rest = table_scr[...]
        for n in range(3):
            piece = rest.astype(jnp.bfloat16)
            rest = rest - piece.astype(jnp.float32)
            at = panel_rows + n * table_rows
            for d in range(len(heights)):
                packs[d][at : at + table_rows, :] = piece

    return pl.pallas_call(
        kernel,
        name="pack",
        out_shape=[
            jax.ShapeDtypeStruct((8, LANES), jnp.float32),
        ]
        + [jax.ShapeDtypeStruct((height, LANES), jnp.bfloat16) for height in heights],
        in_specs=[pl.BlockSpec(memory_space=pl.ANY)] * 7,
        out_specs=[vmem()] * (len(heights) + 1),
        scratch_shapes=[
            pltpu.VMEM(own.shape, own.dtype),
            pltpu.VMEM(one_body.shape, one_body.dtype),
            pltpu.VMEM((slots, vectors), jnp.float32),
            pltpu.SMEM(weights.shape, weights.dtype),
            pltpu.SMEM(sources.shape, sources.dtype),
            pltpu.SMEM(owners.shape, owners.dtype),
            pltpu.VMEM((table_rows, LANES), jnp.float32),
            pltpu.SemaphoreType.DMA((6,)),
        ],
        compiler_params=params(PACK_LIMIT),
        cost_estimate=pl.CostEstimate(flops=10**8, bytes_accessed=10**6, transcendentals=0),
    )(own, one_body, fields.T, weights, sources, owners, cholesky_rot)


def walk_partner(walk, d, size, back):
    if size == 4:
        return lax.bitwise_xor(walk, d)
    return lax.rem(walk + (size - d if back else d), size)


def exchange_far(packed):
    size = lax.axis_size("walk")
    if size != 4:
        return lax.ppermute(packed[1], "walk", [(q, (q + 1) % size) for q in range(size)])
    return lax.ppermute(packed[1], "walk", [(q, q ^ 2) for q in range(size)])


def exchange_near(packed, far):
    size = lax.axis_size("walk")
    if size != 4:
        return [
            lax.ppermute(packed[d], "walk", [(q, (q + d) % size) for q in range(size)]) for d in range(2, size)
        ]
    keep, _, near = packed
    panel = far.shape[0] - keep.shape[0]
    return [lax.ppermute(jnp.concatenate([near, far[panel:]], axis=0), "walk", [(q, q ^ 1) for q in range(size)])]


def walk_places(panel, table, size):
    if size != 4:
        return [(d, 0, panel) for d in range(size)]
    return [(0, 0, panel), (2, 0, panel), (1, 0, panel), (2, panel + 2 * table, panel + table)]


def read_table(ref, at, vectors):
    height = table_height(vectors)
    parts = [ref[at + n * height : at + (n + 1) * height, :].astype(jnp.float32) for n in range(3)]
    return parts[0] + (parts[1] + parts[2])


def merge_tables(tables, walk, walk_size, slots, lane):
    total = jnp.zeros_like(tables[0])
    for d, table in enumerate(tables):
        group = walk_partner(walk, d, walk_size, True)
        total += jnp.where(lane // slots == group, table, 0.0)
    return total


def measure(cholesky_rot, total, last, packs, places, onebody, vectors, slots):
    _, walkers, orbitals = last[0].shape
    depth = sum(x.shape[0] for x in last)
    walk_size = len(places)
    targets = walk_size * lax.axis_size("chol")
    whole = total is None
    quads = orbitals // LANES

    def fold(x):
        return jnp.sum(x.reshape(-1, 8, LANES), axis=0)

    def kernel(*refs):
        chol_ref, onebody_ref = refs[:2]
        pack_refs = refs[2 : 2 + len(packs)]
        last_refs = refs[2 + len(packs) : 2 + len(packs) + len(last)]
        out_ref, tensor_scr = refs[-2:]
        walk = lax.axis_index("walk")
        lane = lax.broadcasted_iota(jnp.int32, (1, LANES), 1)
        table = merge_tables(
            [read_table(pack_refs[n], at, vectors) for n, _, at in places], walk, walk_size, slots, lane
        )
        picks = [
            jnp.where(
                (lane < slots * walk_size) & (table[vectors : vectors + 1, :] == (walk * walkers + b).astype(jnp.float32)),
                1.0,
                0.0,
            )
            for b in range(walkers)
        ]
        rhs = [jnp.concatenate([x[:, b, :] for x in last_refs], axis=0) for b in range(walkers)]
        eye = lax.broadcasted_iota(jnp.int32, (LANES, LANES), 0) == lax.broadcasted_iota(
            jnp.int32, (LANES, LANES), 1
        )
        exchange = [jnp.zeros((8, LANES), jnp.float32) for _ in range(walkers)]
        squares = [jnp.zeros((1, 1), jnp.float32) for _ in range(walkers)]
        drive = jnp.zeros((1, LANES), jnp.float32)
        start = 0 if whole else column_start(lax.axis_size("chol") // 2, depth)
        lhs = chol_ref[:, :, pl.ds(start, depth)].reshape(vectors * orbitals, depth)
        for b in range(walkers):
            value = jnp.dot(lhs, rhs[b], preferred_element_type=jnp.float32)
            tensor_scr[b] = value if whole else refs[2 + len(packs) + len(last)][b] + value
        for g in range(vectors):
            top = g * orbitals
            for b in range(walkers):
                diagonal = jnp.zeros((LANES, LANES), jnp.float32)
                for q in range(quads):
                    for p in range(q + 1):
                        one = tensor_scr[
                            b, top + q * LANES : top + (q + 1) * LANES, p * LANES : (p + 1) * LANES
                        ]
                        if p == q:
                            exchange[b] = exchange[b] + fold(one * one.T)
                            diagonal = diagonal + one
                        else:
                            two = tensor_scr[
                                b, top + p * LANES : top + (p + 1) * LANES, q * LANES : (q + 1) * LANES
                            ]
                            exchange[b] = exchange[b] + 2.0 * fold(two * one.T)
                trace = jnp.sum(fold(jnp.where(eye, diagonal, 0.0)), axis=0, keepdims=True)
                trace = jnp.sum(trace, axis=1, keepdims=True)
                squares[b] = squares[b] + trace * trace
                drive = drive - root_step * picks[b] * table[g : g + 1, :] * trace
        raw = jnp.zeros((1, LANES), jnp.float32)
        square = jnp.zeros((1, LANES), jnp.float32)
        for b in range(walkers):
            swapped = jnp.sum(jnp.sum(exchange[b], axis=0, keepdims=True), axis=1, keepdims=True)
            single = jnp.sum(onebody_ref[b : b + 1, :], axis=1, keepdims=True)
            raw += picks[b] * (single + 0.5 * squares[b] - 0.5 * swapped)
            square += picks[b] * squares[b]
        power = drive - 0.5 * time_step * square - time_step * raw
        out_ref[...] = jnp.broadcast_to(raw + pltpu.roll(power, slots * walk_size, 1), (targets, LANES))

    arrays = list(last) + ([] if whole else [total])
    return pl.pallas_call(
        kernel,
        name="measure",
        out_shape=jax.ShapeDtypeStruct((targets, LANES), jnp.float32),
        in_specs=[vmem()] * (2 + len(packs) + len(arrays)),
        out_specs=vmem(),
        scratch_shapes=[
            pltpu.VMEM((walkers, vectors * orbitals, orbitals), jnp.float32),
        ],
        compiler_params=params(),
        cost_estimate=pl.CostEstimate(
            flops=2 * vectors * orbitals * depth * walkers * orbitals,
            bytes_accessed=2 * vectors * orbitals * depth,
            transcendentals=0,
        ),
    )(cholesky_rot, onebody, *packs, *arrays)


def finish(stats, packs, places, counts, vectors, slots, walkers):
    walk_size = len(places)
    rows = (packs[0].shape[0] - 3 * table_height(vectors)) // walkers

    def kernel(stats_ref, counts_ref, *refs):
        pack_refs = refs[: len(packs)]
        energies_ref, weights_ref, density_ref = refs[len(packs) :]
        walk = lax.axis_index("walk")
        lane = lax.broadcasted_iota(jnp.int32, (1, LANES), 1)
        all_slots = slots * walk_size
        tables = [read_table(pack_refs[n], at, vectors) for n, _, at in places]
        source = merge_tables([t[vectors : vectors + 1, :] for t in tables], walk, walk_size, slots, lane)
        total_weight = tables[0][vectors + 1 : vectors + 2, :]
        for t in tables[1:]:
            total_weight = total_weight + t[vectors + 1 : vectors + 2, :]
        mean_weight = total_weight / (walkers * walk_size)
        total = jnp.sum(stats_ref[...], axis=0, keepdims=True)
        power = pltpu.roll(total, LANES - all_slots, 1)
        live_count = jnp.zeros((1, LANES), jnp.int32)
        for q in range(walk_size):
            live_count = jnp.where(lane // slots == q, counts_ref[q], live_count)
        live = (lane < all_slots) & (lane % slots < live_count)
        energies = jnp.where(live, total, 0.0)
        new_weights = jnp.where(live, mean_weight * jnp.exp(jnp.where(live, power, 0.0)), 0.0)
        norm = jnp.sum(new_weights, axis=1, keepdims=True)
        density = jnp.zeros((rows, LANES), jnp.float32)
        for d, (n, top, _) in enumerate(places):
            group = walk_partner(walk, d, walk_size, True)
            for b in range(walkers):
                walker = (group * walkers + b).astype(jnp.float32)
                share = jnp.sum(jnp.where(source == walker, new_weights, 0.0), axis=1, keepdims=True) / norm
                density += share * pack_refs[n][top + b * rows : top + (b + 1) * rows, :].astype(jnp.float32)
        density_ref[...] = density
        first = lax.rem(LANES - walk * slots, LANES)
        energies_ref[...] = pltpu.roll(jnp.broadcast_to(energies, (8, LANES)), first, 1)[:1, :slots]
        weights_ref[...] = pltpu.roll(jnp.broadcast_to(new_weights, (8, LANES)), first, 1)[:1, :slots]

    return pl.pallas_call(
        kernel,
        name="finish",
        out_shape=[
            jax.ShapeDtypeStruct((1, slots), jnp.float32),
            jax.ShapeDtypeStruct((1, slots), jnp.float32),
            jax.ShapeDtypeStruct((rows, LANES), jnp.float32),
        ],
        in_specs=[vmem(), smem()] + [vmem()] * len(packs),
        out_specs=[vmem()] * 3,
        compiler_params=params(),
        cost_estimate=pl.CostEstimate(flops=10**6, bytes_accessed=6 * 10**5, transcendentals=128),
    )(stats, counts, *packs)


def per_device(green_rows, cholesky_rot, one_body, fields, weights, sources, counts, owners):
    chol_size = lax.axis_size("chol")
    walk_size = lax.axis_size("walk")
    vectors, slots = fields.shape
    walkers = green_rows.shape[1]
    onebody, *packed = pack(green_rows, one_body, fields, weights, sources, owners, cholesky_rot)
    if chol_size > RING_LIMIT or chol_size % 2 or chol_size < 8:
        far = exchange_far(packed)
        packs = [packed[0], far] + exchange_near(packed, far)
        total, last = None, [lax.all_gather(green_rows, "chol", axis=0, tiled=True)]
    else:
        onebody, total, last, packs = ring(green_rows, cholesky_rot, onebody, packed)
    table = 3 * table_height(vectors)
    places = walk_places(packs[0].shape[0] - table, table, walk_size)
    stats = measure(cholesky_rot, total, last, packs, places, onebody, vectors, slots)
    stats = lax.all_to_all(stats, ("chol", "walk"), split_axis=0, concat_axis=0, tiled=True)
    energies, new_weights, density = finish(stats, packs, places, counts, vectors, slots, walkers)
    return energies.reshape(slots), new_weights.reshape(slots), density.reshape(1, density.size)


def solution(mesh):
    return jax.shard_map(
        per_device,
        mesh=mesh,
        in_specs=(
            P("chol", "walk", None),
            P("chol", None, None),
            P("chol", None),
            P("chol", "walk"),
            P("walk"),
            P("walk"),
            P(),
            P(),
        ),
        out_specs=(P("walk"), P("walk"), P("walk", "chol")),
        check_vma=False,
    )
```

```python
import jax
import jax.numpy as jnp
from jax import lax
from jax.experimental import pallas as pl
from jax.experimental.pallas import tpu as pltpu
from jax.sharding import PartitionSpec as P

time_step = 0.02
root_step = 0.02**0.5
LANES = 128
VMEM_LIMIT = 16 * 1024 * 1024
PACK_LIMIT = 54 * 1024 * 1024
ACCUMULATE_LIMIT = 24 * 1024 * 1024
RING_LIMIT = 16


def params(limit=VMEM_LIMIT):
    return pltpu.CompilerParams(vmem_limit_bytes=limit)


def vmem():
    return pl.BlockSpec(memory_space=pltpu.VMEM)


def smem():
    return pl.BlockSpec(memory_space=pltpu.SMEM)


def ring_order(size):
    return [2 * q if q < size // 2 else 2 * (size - 1 - q) + 1 for q in range(size)]


def ring_place(index, size):
    return jnp.where(index % 2 == 0, index // 2, size - 1 - index // 2)


def ring_owner(place, size):
    return jnp.where(place < size // 2, 2 * place, 2 * (size - 1 - place) + 1)


def column_start(shift, rows):
    size = lax.axis_size("chol")
    place = ring_place(lax.axis_index("chol"), size)
    owner = ring_owner(lax.rem(place + shift + size, size), size)
    return pl.multiple_of(owner * rows, rows)


def accumulate(cholesky_rot, shifts, parts, total, mark):
    vectors, orbitals, _ = cholesky_rot.shape
    rows, walkers, _ = parts[0].shape
    size = vectors * orbitals
    arrays = list(parts) + ([] if mark is None else [mark]) + ([] if total is None else [total])

    def kernel(chol_ref, *refs):
        shards = refs[: len(parts)]
        total_ref, mark_ref = refs[len(arrays) :]
        mark_ref[...] = jnp.zeros_like(mark_ref)
        lhs = jnp.concatenate(
            [chol_ref[:, :, pl.ds(column_start(shift, rows), rows)].reshape(size, rows) for shift in shifts], axis=1
        )
        for b in range(walkers):
            rhs = jnp.concatenate([x[:, b, :] for x in shards], axis=0)
            value = jnp.dot(lhs, rhs, preferred_element_type=jnp.float32)
            total_ref[b] = value if total is None else refs[len(arrays) - 1][b] + value

    return pl.pallas_call(
        kernel,
        name="accumulate",
        out_shape=[
            jax.ShapeDtypeStruct((walkers, size, orbitals), jnp.float32),
            jax.ShapeDtypeStruct((8, LANES), jnp.float32),
        ],
        in_specs=[vmem()] * (1 + len(arrays)),
        out_specs=[vmem()] * 2,
        compiler_params=params(ACCUMULATE_LIMIT),
        cost_estimate=pl.CostEstimate(
            flops=2 * len(parts) * size * rows * walkers * orbitals,
            bytes_accessed=2 * len(parts) * size * rows,
            transcendentals=0,
        ),
    )(cholesky_rot, *arrays)


def tie(*arrays):
    return lax.optimization_barrier(arrays)


def ring(own, cholesky_rot, onebody, packed):
    size = lax.axis_size("chol")
    order = ring_order(size)

    def send(x, places):
        return lax.ppermute(x, "chol", [(order[q], order[(q + places) % size]) for q in range(size)])

    steps = size // 2 - 1
    right, left = send(own, 1), send(own, -1)
    opposite = send(own, size // 2)
    right, onebody = tie(right, onebody)
    left, *packed = tie(left, *packed)
    shifts, parts = [0, -1, 1], [own, right, left]
    total = mark = None
    for step in range(2, steps + 1):
        next_right, next_left = send(right, 1), send(left, -1)
        if step == 2:
            far = exchange_far(packed)
        elif step == 3:
            near = exchange_near(packed, far)
        if step == steps:
            opposite, mark = tie(opposite, mark)
            shifts, parts = shifts + [size // 2], parts + [opposite]
        total, mark = accumulate(cholesky_rot, shifts, parts, total, mark)
        right, mark = tie(next_right, mark)
        if step == 2:
            left, mark, far = tie(next_left, mark, far)
        else:
            left, mark = tie(next_left, mark)
        shifts, parts = [-step, step], [right, left]
    return onebody, total, shifts, parts, [packed[0], far] + near


def table_height(vectors):
    return -(-(vectors + 2) // 16) * 16


def pack(own, one_body, fields, weights, sources, owners, cholesky_rot):
    rows, walkers, orbitals = own.shape
    walk_size = lax.axis_size("walk")
    width = orbitals // walk_size
    pair = LANES // width
    vectors, slots = fields.shape
    table_rows = table_height(vectors)
    panel_rows = walkers * (rows // pair)
    both = panel_rows + 3 * table_rows
    if walk_size == 4:
        heights = [both, both + panel_rows, both]
        spots = [(0, 0), (2, 0), (1, 0), (1, both)]
    else:
        heights = [both] * walk_size
        spots = [(d, 0) for d in range(walk_size)]

    def kernel(own_any, body_any, fields_any, weights_any, sources_any, owners_any, chol_any, *refs):
        onebody_ref = refs[0]
        packs = refs[1 : 1 + len(heights)]
        own_ref, body_ref, fields_ref, weights_ref, sources_ref, owners_ref, table_scr, sems = refs[1 + len(heights) :]
        places = [
            (own_any, own_ref),
            (body_any, body_ref),
            (fields_any, fields_ref),
            (weights_any, weights_ref),
            (sources_any, sources_ref),
            (owners_any, owners_ref),
        ]
        small = [pltpu.make_async_copy(a, b, sems.at[n]) for n, (a, b) in enumerate(places)]
        for copy in small:
            copy.start()
        for copy in small:
            copy.wait()
        green = [own_ref[:, b, :] for b in range(walkers)]
        walk = lax.axis_index("walk")
        lane = lax.broadcasted_iota(jnp.int32, (1, LANES), 1)
        body = body_ref[...].astype(jnp.float32)
        onebody_ref[...] = jnp.zeros_like(onebody_ref)
        for b in range(walkers):
            total = jnp.sum(green[b].astype(jnp.float32) * body, axis=0, keepdims=True)
            folded = total[:, :LANES]
            for start in range(LANES, orbitals, LANES):
                folded = folded + total[:, start : start + LANES]
            onebody_ref[b : b + 1, :] = folded
        r = lax.broadcasted_iota(jnp.int32, (rows // pair, rows), 0)
        m = lax.broadcasted_iota(jnp.int32, (rows // pair, rows), 1)
        k = lax.broadcasted_iota(jnp.int32, (orbitals, LANES), 0)
        c = lax.broadcasted_iota(jnp.int32, (orbitals, LANES), 1)
        thinned = []
        for b in range(walkers):
            values = green[b]
            thinned.append(
                [
                    jnp.dot(
                        (m == r * pair + h).astype(jnp.bfloat16), values, preferred_element_type=jnp.float32
                    ).astype(jnp.bfloat16)
                    for h in range(pair)
                ]
            )
        for d in range(walk_size):
            target = walk_partner(walk, d, walk_size, False)
            out, top = spots[d]
            panel = jnp.int32(0)
            for p in range(walk_size):
                panel = jnp.where(owners_ref[p] == target, p, panel)
            for b in range(walkers):
                total = jnp.zeros((rows // pair, LANES), jnp.float32)
                for h in range(pair):
                    take = (k == panel * width + c - h * width) & (c >= h * width) & (c < (h + 1) * width)
                    total += jnp.dot(
                        thinned[b][h], take.astype(jnp.bfloat16), preferred_element_type=jnp.float32
                    )
                packs[out][top + b * (rows // pair) : top + (b + 1) * (rows // pair), :] = total.astype(jnp.bfloat16)
        spread = jnp.zeros((vectors, LANES), jnp.float32)
        source = jnp.zeros((1, LANES), jnp.float32)
        corner = lax.broadcasted_iota(jnp.int32, (vectors, vectors), 0) == lax.broadcasted_iota(
            jnp.int32, (vectors, vectors), 1
        )
        for j in range(slots):
            mine = lane % slots == j
            upright = jnp.sum(jnp.where(corner, fields_ref[j : j + 1, :], 0.0), axis=1, keepdims=True)
            spread += jnp.where(mine, upright, 0.0)
            source += jnp.where(mine, sources_ref[j].astype(jnp.float32), 0.0)
        weight = weights_ref[0]
        for j in range(1, weights.shape[0]):
            weight = weight + weights_ref[j]
        table_scr[...] = jnp.zeros_like(table_scr)
        table_scr[:vectors, :] = spread
        table_scr[vectors : vectors + 1, :] = source
        table_scr[vectors + 1 : vectors + 2, :] = jnp.zeros((1, LANES), jnp.float32) + weight
        rest = table_scr[...]
        for n in range(3):
            piece = rest.astype(jnp.bfloat16)
            rest = rest - piece.astype(jnp.float32)
            at = panel_rows + n * table_rows
            for d in range(len(heights)):
                packs[d][at : at + table_rows, :] = piece

    return pl.pallas_call(
        kernel,
        name="pack",
        out_shape=[
            jax.ShapeDtypeStruct((8, LANES), jnp.float32),
        ]
        + [jax.ShapeDtypeStruct((height, LANES), jnp.bfloat16) for height in heights],
        in_specs=[pl.BlockSpec(memory_space=pl.ANY)] * 7,
        out_specs=[vmem()] * (len(heights) + 1),
        scratch_shapes=[
            pltpu.VMEM(own.shape, own.dtype),
            pltpu.VMEM(one_body.shape, one_body.dtype),
            pltpu.VMEM((slots, vectors), jnp.float32),
            pltpu.SMEM(weights.shape, weights.dtype),
            pltpu.SMEM(sources.shape, sources.dtype),
            pltpu.SMEM(owners.shape, owners.dtype),
            pltpu.VMEM((table_rows, LANES), jnp.float32),
            pltpu.SemaphoreType.DMA((6,)),
        ],
        compiler_params=params(PACK_LIMIT),
        cost_estimate=pl.CostEstimate(flops=10**8, bytes_accessed=10**6, transcendentals=0),
    )(own, one_body, fields.T, weights, sources, owners, cholesky_rot)


def walk_partner(walk, d, size, back):
    if size == 4:
        return lax.bitwise_xor(walk, d)
    return lax.rem(walk + (size - d if back else d), size)


def exchange_far(packed):
    size = lax.axis_size("walk")
    if size != 4:
        return lax.ppermute(packed[1], "walk", [(q, (q + 1) % size) for q in range(size)])
    return lax.ppermute(packed[1], "walk", [(q, q ^ 2) for q in range(size)])


def exchange_near(packed, far):
    size = lax.axis_size("walk")
    if size != 4:
        return [
            lax.ppermute(packed[d], "walk", [(q, (q + d) % size) for q in range(size)]) for d in range(2, size)
        ]
    keep, _, near = packed
    panel = far.shape[0] - keep.shape[0]
    return [lax.ppermute(jnp.concatenate([near, far[panel:]], axis=0), "walk", [(q, q ^ 1) for q in range(size)])]


def walk_places(panel, table, size):
    if size != 4:
        return [(d, 0, panel) for d in range(size)]
    return [(0, 0, panel), (2, 0, panel), (1, 0, panel), (2, panel + 2 * table, panel + table)]


def read_table(ref, at, vectors):
    height = table_height(vectors)
    parts = [ref[at + n * height : at + (n + 1) * height, :].astype(jnp.float32) for n in range(3)]
    return parts[0] + (parts[1] + parts[2])


def merge_tables(tables, walk, walk_size, slots, lane):
    total = jnp.zeros_like(tables[0])
    for d, table in enumerate(tables):
        group = walk_partner(walk, d, walk_size, True)
        total += jnp.where(lane // slots == group, table, 0.0)
    return total


def measure(cholesky_rot, total, shifts, last, packs, places, onebody, vectors, slots):
    _, walkers, orbitals = last[0].shape
    rows = last[0].shape[0]
    depth = rows * len(last)
    walk_size = len(places)
    targets = walk_size * lax.axis_size("chol")
    whole = total is None
    quads = orbitals // LANES

    def fold(x):
        return jnp.sum(x.reshape(-1, 8, LANES), axis=0)

    def kernel(*refs):
        chol_ref, onebody_ref = refs[:2]
        pack_refs = refs[2 : 2 + len(packs)]
        last_refs = refs[2 + len(packs) : 2 + len(packs) + len(last)]
        out_ref, tensor_scr = refs[-2:]
        walk = lax.axis_index("walk")
        lane = lax.broadcasted_iota(jnp.int32, (1, LANES), 1)
        table = merge_tables(
            [read_table(pack_refs[n], at, vectors) for n, _, at in places], walk, walk_size, slots, lane
        )
        picks = [
            jnp.where(
                (lane < slots * walk_size) & (table[vectors : vectors + 1, :] == (walk * walkers + b).astype(jnp.float32)),
                1.0,
                0.0,
            )
            for b in range(walkers)
        ]
        rhs = [jnp.concatenate([x[:, b, :] for x in last_refs], axis=0) for b in range(walkers)]
        eye = lax.broadcasted_iota(jnp.int32, (LANES, LANES), 0) == lax.broadcasted_iota(
            jnp.int32, (LANES, LANES), 1
        )
        exchange = [jnp.zeros((8, LANES), jnp.float32) for _ in range(walkers)]
        squares = [jnp.zeros((1, 1), jnp.float32) for _ in range(walkers)]
        drive = jnp.zeros((1, LANES), jnp.float32)
        starts = [0 if shift is None else column_start(shift, rows) for shift in shifts]
        blocks = [chol_ref[:, :, pl.ds(start, rows)].reshape(vectors * orbitals, rows) for start in starts]
        lhs = jnp.concatenate(blocks, axis=1)
        for b in range(walkers):
            value = jnp.dot(lhs, rhs[b], preferred_element_type=jnp.float32)
            tensor_scr[b] = value if whole else refs[2 + len(packs) + len(last)][b] + value
        for g in range(vectors):
            top = g * orbitals
            for b in range(walkers):
                diagonal = jnp.zeros((LANES, LANES), jnp.float32)
                for q in range(quads):
                    for p in range(q + 1):
                        one = tensor_scr[
                            b, top + q * LANES : top + (q + 1) * LANES, p * LANES : (p + 1) * LANES
                        ]
                        if p == q:
                            exchange[b] = exchange[b] + fold(one * one.T)
                            diagonal = diagonal + one
                        else:
                            two = tensor_scr[
                                b, top + p * LANES : top + (p + 1) * LANES, q * LANES : (q + 1) * LANES
                            ]
                            exchange[b] = exchange[b] + 2.0 * fold(two * one.T)
                trace = jnp.sum(fold(jnp.where(eye, diagonal, 0.0)), axis=0, keepdims=True)
                trace = jnp.sum(trace, axis=1, keepdims=True)
                squares[b] = squares[b] + trace * trace
                drive = drive - root_step * picks[b] * table[g : g + 1, :] * trace
        raw = jnp.zeros((1, LANES), jnp.float32)
        square = jnp.zeros((1, LANES), jnp.float32)
        for b in range(walkers):
            swapped = jnp.sum(jnp.sum(exchange[b], axis=0, keepdims=True), axis=1, keepdims=True)
            single = jnp.sum(onebody_ref[b : b + 1, :], axis=1, keepdims=True)
            raw += picks[b] * (single + 0.5 * squares[b] - 0.5 * swapped)
            square += picks[b] * squares[b]
        power = drive - 0.5 * time_step * square - time_step * raw
        out_ref[...] = jnp.broadcast_to(raw + pltpu.roll(power, slots * walk_size, 1), (targets, LANES))

    arrays = list(last) + ([] if whole else [total])
    return pl.pallas_call(
        kernel,
        name="measure",
        out_shape=jax.ShapeDtypeStruct((targets, LANES), jnp.float32),
        in_specs=[vmem()] * (2 + len(packs) + len(arrays)),
        out_specs=vmem(),
        scratch_shapes=[
            pltpu.VMEM((walkers, vectors * orbitals, orbitals), jnp.float32),
        ],
        compiler_params=params(),
        cost_estimate=pl.CostEstimate(
            flops=2 * vectors * orbitals * depth * walkers * orbitals,
            bytes_accessed=2 * vectors * orbitals * depth,
            transcendentals=0,
        ),
    )(cholesky_rot, onebody, *packs, *arrays)


def finish(stats, packs, places, counts, vectors, slots, walkers):
    walk_size = len(places)
    rows = (packs[0].shape[0] - 3 * table_height(vectors)) // walkers

    def kernel(stats_ref, counts_ref, *refs):
        pack_refs = refs[: len(packs)]
        energies_ref, weights_ref, density_ref = refs[len(packs) :]
        walk = lax.axis_index("walk")
        lane = lax.broadcasted_iota(jnp.int32, (1, LANES), 1)
        all_slots = slots * walk_size
        tables = [read_table(pack_refs[n], at, vectors) for n, _, at in places]
        source = merge_tables([t[vectors : vectors + 1, :] for t in tables], walk, walk_size, slots, lane)
        total_weight = tables[0][vectors + 1 : vectors + 2, :]
        for t in tables[1:]:
            total_weight = total_weight + t[vectors + 1 : vectors + 2, :]
        mean_weight = total_weight / (walkers * walk_size)
        total = jnp.sum(stats_ref[...], axis=0, keepdims=True)
        power = pltpu.roll(total, LANES - all_slots, 1)
        live_count = jnp.zeros((1, LANES), jnp.int32)
        for q in range(walk_size):
            live_count = jnp.where(lane // slots == q, counts_ref[q], live_count)
        live = (lane < all_slots) & (lane % slots < live_count)
        energies = jnp.where(live, total, 0.0)
        new_weights = jnp.where(live, mean_weight * jnp.exp(jnp.where(live, power, 0.0)), 0.0)
        norm = jnp.sum(new_weights, axis=1, keepdims=True)
        density = jnp.zeros((rows, LANES), jnp.float32)
        for d, (n, top, _) in enumerate(places):
            group = walk_partner(walk, d, walk_size, True)
            for b in range(walkers):
                walker = (group * walkers + b).astype(jnp.float32)
                share = jnp.sum(jnp.where(source == walker, new_weights, 0.0), axis=1, keepdims=True) / norm
                density += share * pack_refs[n][top + b * rows : top + (b + 1) * rows, :].astype(jnp.float32)
        density_ref[...] = density
        first = lax.rem(LANES - walk * slots, LANES)
        energies_ref[...] = pltpu.roll(jnp.broadcast_to(energies, (8, LANES)), first, 1)[:1, :slots]
        weights_ref[...] = pltpu.roll(jnp.broadcast_to(new_weights, (8, LANES)), first, 1)[:1, :slots]

    return pl.pallas_call(
        kernel,
        name="finish",
        out_shape=[
            jax.ShapeDtypeStruct((1, slots), jnp.float32),
            jax.ShapeDtypeStruct((1, slots), jnp.float32),
            jax.ShapeDtypeStruct((rows, LANES), jnp.float32),
        ],
        in_specs=[vmem(), smem()] + [vmem()] * len(packs),
        out_specs=[vmem()] * 3,
        compiler_params=params(),
        cost_estimate=pl.CostEstimate(flops=10**6, bytes_accessed=6 * 10**5, transcendentals=128),
    )(stats, counts, *packs)


def per_device(green_rows, cholesky_rot, one_body, fields, weights, sources, counts, owners):
    chol_size = lax.axis_size("chol")
    walk_size = lax.axis_size("walk")
    vectors, slots = fields.shape
    walkers = green_rows.shape[1]
    onebody, *packed = pack(green_rows, one_body, fields, weights, sources, owners, cholesky_rot)
    if chol_size > RING_LIMIT or chol_size % 2 or chol_size < 8:
        far = exchange_far(packed)
        packs = [packed[0], far] + exchange_near(packed, far)
        total, shifts, last = None, [None], [lax.all_gather(green_rows, "chol", axis=0, tiled=True)]
    else:
        onebody, total, shifts, last, packs = ring(green_rows, cholesky_rot, onebody, packed)
    table = 3 * table_height(vectors)
    places = walk_places(packs[0].shape[0] - table, table, walk_size)
    stats = measure(cholesky_rot, total, shifts, last, packs, places, onebody, vectors, slots)
    stats = lax.all_to_all(stats, ("chol", "walk"), split_axis=0, concat_axis=0, tiled=True)
    energies, new_weights, density = finish(stats, packs, places, counts, vectors, slots, walkers)
    return energies.reshape(slots), new_weights.reshape(slots), density.reshape(1, density.size)


def solution(mesh):
    return jax.shard_map(
        per_device,
        mesh=mesh,
        in_specs=(
            P("chol", "walk", None),
            P("chol", None, None),
            P("chol", None),
            P("chol", "walk"),
            P("walk"),
            P("walk"),
            P(),
            P(),
        ),
        out_specs=(P("walk"), P("walk"), P("walk", "chol")),
        check_vma=False,
    )
```

```python
import jax
import jax.numpy as jnp
from jax import lax
from jax.experimental import pallas as pl
from jax.experimental.pallas import tpu as pltpu
from jax.sharding import PartitionSpec as P

time_step = 0.02
root_step = 0.02**0.5
LANES = 128
VMEM_LIMIT = 16 * 1024 * 1024
PACK_LIMIT = 54 * 1024 * 1024
ACCUMULATE_LIMIT = 24 * 1024 * 1024
RING_LIMIT = 16


def params(limit=VMEM_LIMIT):
    return pltpu.CompilerParams(vmem_limit_bytes=limit)


def vmem():
    return pl.BlockSpec(memory_space=pltpu.VMEM)


def smem():
    return pl.BlockSpec(memory_space=pltpu.SMEM)


def ring_order(size):
    return [2 * q if q < size // 2 else 2 * (size - 1 - q) + 1 for q in range(size)]


def ring_place(index, size):
    return jnp.where(index % 2 == 0, index // 2, size - 1 - index // 2)


def ring_owner(place, size):
    return jnp.where(place < size // 2, 2 * place, 2 * (size - 1 - place) + 1)


def column_start(shift, rows):
    size = lax.axis_size("chol")
    place = ring_place(lax.axis_index("chol"), size)
    owner = ring_owner(lax.rem(place + shift + size, size), size)
    return pl.multiple_of(owner * rows, rows)


def accumulate(cholesky_rot, shifts, parts, total, mark):
    vectors, orbitals, _ = cholesky_rot.shape
    rows, walkers, _ = parts[0].shape
    size = vectors * orbitals
    arrays = list(parts) + ([] if mark is None else [mark]) + ([] if total is None else [total])

    def kernel(chol_ref, *refs):
        shards = refs[: len(parts)]
        total_ref, mark_ref = refs[len(arrays) :]
        mark_ref[...] = jnp.zeros_like(mark_ref)
        lhs = jnp.concatenate(
            [chol_ref[:, :, pl.ds(column_start(shift, rows), rows)].reshape(size, rows) for shift in shifts], axis=1
        )
        for b in range(walkers):
            rhs = jnp.concatenate([x[:, b, :] for x in shards], axis=0)
            value = jnp.dot(lhs, rhs, preferred_element_type=jnp.float32)
            total_ref[b] = value if total is None else refs[len(arrays) - 1][b] + value

    return pl.pallas_call(
        kernel,
        name="accumulate",
        out_shape=[
            jax.ShapeDtypeStruct((walkers, size, orbitals), jnp.float32),
            jax.ShapeDtypeStruct((8, LANES), jnp.float32),
        ],
        in_specs=[vmem()] * (1 + len(arrays)),
        out_specs=[vmem()] * 2,
        compiler_params=params(ACCUMULATE_LIMIT),
        cost_estimate=pl.CostEstimate(
            flops=2 * len(parts) * size * rows * walkers * orbitals,
            bytes_accessed=2 * len(parts) * size * rows,
            transcendentals=0,
        ),
    )(cholesky_rot, *arrays)


def tie(*arrays):
    return lax.optimization_barrier(arrays)


def ring(own, cholesky_rot, onebody, packed):
    size = lax.axis_size("chol")
    rows = own.shape[0]
    order = ring_order(size)
    ahead = [(order[q], order[(q + 1) % size]) for q in range(size)]
    back = [(order[q], order[(q - 1) % size]) for q in range(size)]
    steps = size // 2
    right = left = own
    shifts, parts = [0], [own]
    total = mark = None
    for step in range(1, steps):
        next_right, next_left = lax.ppermute(right, "chol", ahead), lax.ppermute(left, "chol", back)
        if step == 1:
            right, onebody = tie(next_right, onebody)
            left, *packed = tie(next_left, *packed)
        else:
            if step == 2:
                far = exchange_far(packed)
            elif step == 3:
                near = exchange_near(packed, far)
            total, mark = accumulate(cholesky_rot, shifts, parts, total, mark)
            shifts, parts = [], []
            right, mark = tie(next_right, mark)
            left, mark = tie(next_left, mark)
        shifts += [-step, step]
        parts = parts + [right, left]
    last = [lax.ppermute(right[: rows // 2], "chol", ahead), lax.ppermute(left[rows // 2 :], "chol", back)]
    mark, *near = tie(mark, *near)
    total, _ = accumulate(cholesky_rot, shifts, parts, total, mark)
    return onebody, total, last, [packed[0], far] + near


def table_height(vectors):
    return -(-(vectors + 2) // 16) * 16


def pack(own, one_body, fields, weights, sources, owners, cholesky_rot):
    rows, walkers, orbitals = own.shape
    walk_size = lax.axis_size("walk")
    width = orbitals // walk_size
    pair = LANES // width
    vectors, slots = fields.shape
    table_rows = table_height(vectors)
    panel_rows = walkers * (rows // pair)
    both = panel_rows + 3 * table_rows
    if walk_size == 4:
        heights = [both, both + panel_rows, both]
        spots = [(0, 0), (2, 0), (1, 0), (1, both)]
    else:
        heights = [both] * walk_size
        spots = [(d, 0) for d in range(walk_size)]

    def kernel(own_any, body_any, fields_any, weights_any, sources_any, owners_any, chol_any, *refs):
        onebody_ref = refs[0]
        packs = refs[1 : 1 + len(heights)]
        own_ref, body_ref, fields_ref, weights_ref, sources_ref, owners_ref, table_scr, sems = refs[1 + len(heights) :]
        places = [
            (own_any, own_ref),
            (body_any, body_ref),
            (fields_any, fields_ref),
            (weights_any, weights_ref),
            (sources_any, sources_ref),
            (owners_any, owners_ref),
        ]
        small = [pltpu.make_async_copy(a, b, sems.at[n]) for n, (a, b) in enumerate(places)]
        for copy in small:
            copy.start()
        for copy in small:
            copy.wait()
        green = [own_ref[:, b, :] for b in range(walkers)]
        walk = lax.axis_index("walk")
        lane = lax.broadcasted_iota(jnp.int32, (1, LANES), 1)
        body = body_ref[...].astype(jnp.float32)
        onebody_ref[...] = jnp.zeros_like(onebody_ref)
        for b in range(walkers):
            total = jnp.sum(green[b].astype(jnp.float32) * body, axis=0, keepdims=True)
            folded = total[:, :LANES]
            for start in range(LANES, orbitals, LANES):
                folded = folded + total[:, start : start + LANES]
            onebody_ref[b : b + 1, :] = folded
        r = lax.broadcasted_iota(jnp.int32, (rows // pair, rows), 0)
        m = lax.broadcasted_iota(jnp.int32, (rows // pair, rows), 1)
        k = lax.broadcasted_iota(jnp.int32, (orbitals, LANES), 0)
        c = lax.broadcasted_iota(jnp.int32, (orbitals, LANES), 1)
        thinned = []
        for b in range(walkers):
            values = green[b]
            thinned.append(
                [
                    jnp.dot(
                        (m == r * pair + h).astype(jnp.bfloat16), values, preferred_element_type=jnp.float32
                    ).astype(jnp.bfloat16)
                    for h in range(pair)
                ]
            )
        for d in range(walk_size):
            target = walk_partner(walk, d, walk_size, False)
            out, top = spots[d]
            panel = jnp.int32(0)
            for p in range(walk_size):
                panel = jnp.where(owners_ref[p] == target, p, panel)
            for b in range(walkers):
                total = jnp.zeros((rows // pair, LANES), jnp.float32)
                for h in range(pair):
                    take = (k == panel * width + c - h * width) & (c >= h * width) & (c < (h + 1) * width)
                    total += jnp.dot(
                        thinned[b][h], take.astype(jnp.bfloat16), preferred_element_type=jnp.float32
                    )
                packs[out][top + b * (rows // pair) : top + (b + 1) * (rows // pair), :] = total.astype(jnp.bfloat16)
        spread = jnp.zeros((vectors, LANES), jnp.float32)
        source = jnp.zeros((1, LANES), jnp.float32)
        corner = lax.broadcasted_iota(jnp.int32, (vectors, vectors), 0) == lax.broadcasted_iota(
            jnp.int32, (vectors, vectors), 1
        )
        for j in range(slots):
            mine = lane % slots == j
            upright = jnp.sum(jnp.where(corner, fields_ref[j : j + 1, :], 0.0), axis=1, keepdims=True)
            spread += jnp.where(mine, upright, 0.0)
            source += jnp.where(mine, sources_ref[j].astype(jnp.float32), 0.0)
        weight = weights_ref[0]
        for j in range(1, weights.shape[0]):
            weight = weight + weights_ref[j]
        table_scr[...] = jnp.zeros_like(table_scr)
        table_scr[:vectors, :] = spread
        table_scr[vectors : vectors + 1, :] = source
        table_scr[vectors + 1 : vectors + 2, :] = jnp.zeros((1, LANES), jnp.float32) + weight
        rest = table_scr[...]
        for n in range(3):
            piece = rest.astype(jnp.bfloat16)
            rest = rest - piece.astype(jnp.float32)
            at = panel_rows + n * table_rows
            for d in range(len(heights)):
                packs[d][at : at + table_rows, :] = piece

    return pl.pallas_call(
        kernel,
        name="pack",
        out_shape=[
            jax.ShapeDtypeStruct((8, LANES), jnp.float32),
        ]
        + [jax.ShapeDtypeStruct((height, LANES), jnp.bfloat16) for height in heights],
        in_specs=[pl.BlockSpec(memory_space=pl.ANY)] * 7,
        out_specs=[vmem()] * (len(heights) + 1),
        scratch_shapes=[
            pltpu.VMEM(own.shape, own.dtype),
            pltpu.VMEM(one_body.shape, one_body.dtype),
            pltpu.VMEM((slots, vectors), jnp.float32),
            pltpu.SMEM(weights.shape, weights.dtype),
            pltpu.SMEM(sources.shape, sources.dtype),
            pltpu.SMEM(owners.shape, owners.dtype),
            pltpu.VMEM((table_rows, LANES), jnp.float32),
            pltpu.SemaphoreType.DMA((6,)),
        ],
        compiler_params=params(PACK_LIMIT),
        cost_estimate=pl.CostEstimate(flops=10**8, bytes_accessed=10**6, transcendentals=0),
    )(own, one_body, fields.T, weights, sources, owners, cholesky_rot)


def walk_partner(walk, d, size, back):
    if size == 4:
        return lax.bitwise_xor(walk, d)
    return lax.rem(walk + (size - d if back else d), size)


def exchange_far(packed):
    size = lax.axis_size("walk")
    if size != 4:
        return lax.ppermute(packed[1], "walk", [(q, (q + 1) % size) for q in range(size)])
    return lax.ppermute(packed[1], "walk", [(q, q ^ 2) for q in range(size)])


def exchange_near(packed, far):
    size = lax.axis_size("walk")
    if size != 4:
        return [
            lax.ppermute(packed[d], "walk", [(q, (q + d) % size) for q in range(size)]) for d in range(2, size)
        ]
    keep, _, near = packed
    panel = far.shape[0] - keep.shape[0]
    return [lax.ppermute(jnp.concatenate([near, far[panel:]], axis=0), "walk", [(q, q ^ 1) for q in range(size)])]


def walk_places(panel, table, size):
    if size != 4:
        return [(d, 0, panel) for d in range(size)]
    return [(0, 0, panel), (2, 0, panel), (1, 0, panel), (2, panel + 2 * table, panel + table)]


def read_table(ref, at, vectors):
    height = table_height(vectors)
    parts = [ref[at + n * height : at + (n + 1) * height, :].astype(jnp.float32) for n in range(3)]
    return parts[0] + (parts[1] + parts[2])


def merge_tables(tables, walk, walk_size, slots, lane):
    total = jnp.zeros_like(tables[0])
    for d, table in enumerate(tables):
        group = walk_partner(walk, d, walk_size, True)
        total += jnp.where(lane // slots == group, table, 0.0)
    return total


def measure(cholesky_rot, total, last, packs, places, onebody, vectors, slots):
    _, walkers, orbitals = last[0].shape
    depth = sum(x.shape[0] for x in last)
    walk_size = len(places)
    targets = walk_size * lax.axis_size("chol")
    whole = total is None
    quads = orbitals // LANES

    def fold(x):
        return jnp.sum(x.reshape(-1, 8, LANES), axis=0)

    def kernel(*refs):
        chol_ref, onebody_ref = refs[:2]
        pack_refs = refs[2 : 2 + len(packs)]
        last_refs = refs[2 + len(packs) : 2 + len(packs) + len(last)]
        out_ref, tensor_scr = refs[-2:]
        walk = lax.axis_index("walk")
        lane = lax.broadcasted_iota(jnp.int32, (1, LANES), 1)
        table = merge_tables(
            [read_table(pack_refs[n], at, vectors) for n, _, at in places], walk, walk_size, slots, lane
        )
        picks = [
            jnp.where(
                (lane < slots * walk_size) & (table[vectors : vectors + 1, :] == (walk * walkers + b).astype(jnp.float32)),
                1.0,
                0.0,
            )
            for b in range(walkers)
        ]
        rhs = [jnp.concatenate([x[:, b, :] for x in last_refs], axis=0) for b in range(walkers)]
        eye = lax.broadcasted_iota(jnp.int32, (LANES, LANES), 0) == lax.broadcasted_iota(
            jnp.int32, (LANES, LANES), 1
        )
        exchange = [jnp.zeros((8, LANES), jnp.float32) for _ in range(walkers)]
        squares = [jnp.zeros((1, 1), jnp.float32) for _ in range(walkers)]
        drive = jnp.zeros((1, LANES), jnp.float32)
        start = 0 if whole else column_start(lax.axis_size("chol") // 2, depth)
        lhs = chol_ref[:, :, pl.ds(start, depth)].reshape(vectors * orbitals, depth)
        for b in range(walkers):
            value = jnp.dot(lhs, rhs[b], preferred_element_type=jnp.float32)
            tensor_scr[b] = value if whole else refs[2 + len(packs) + len(last)][b] + value
        for g in range(vectors):
            top = g * orbitals
            for b in range(walkers):
                diagonal = jnp.zeros((LANES, LANES), jnp.float32)
                for q in range(quads):
                    for p in range(q + 1):
                        one = tensor_scr[
                            b, top + q * LANES : top + (q + 1) * LANES, p * LANES : (p + 1) * LANES
                        ]
                        if p == q:
                            exchange[b] = exchange[b] + fold(one * one.T)
                            diagonal = diagonal + one
                        else:
                            two = tensor_scr[
                                b, top + p * LANES : top + (p + 1) * LANES, q * LANES : (q + 1) * LANES
                            ]
                            exchange[b] = exchange[b] + 2.0 * fold(two * one.T)
                trace = jnp.sum(fold(jnp.where(eye, diagonal, 0.0)), axis=0, keepdims=True)
                trace = jnp.sum(trace, axis=1, keepdims=True)
                squares[b] = squares[b] + trace * trace
                drive = drive - root_step * picks[b] * table[g : g + 1, :] * trace
        raw = jnp.zeros((1, LANES), jnp.float32)
        square = jnp.zeros((1, LANES), jnp.float32)
        for b in range(walkers):
            swapped = jnp.sum(jnp.sum(exchange[b], axis=0, keepdims=True), axis=1, keepdims=True)
            single = jnp.sum(onebody_ref[b : b + 1, :], axis=1, keepdims=True)
            raw += picks[b] * (single + 0.5 * squares[b] - 0.5 * swapped)
            square += picks[b] * squares[b]
        power = drive - 0.5 * time_step * square - time_step * raw
        out_ref[...] = jnp.broadcast_to(raw + pltpu.roll(power, slots * walk_size, 1), (targets, LANES))

    arrays = list(last) + ([] if whole else [total])
    return pl.pallas_call(
        kernel,
        name="measure",
        out_shape=jax.ShapeDtypeStruct((targets, LANES), jnp.float32),
        in_specs=[vmem()] * (2 + len(packs) + len(arrays)),
        out_specs=vmem(),
        scratch_shapes=[
            pltpu.VMEM((walkers, vectors * orbitals, orbitals), jnp.float32),
        ],
        compiler_params=params(),
        cost_estimate=pl.CostEstimate(
            flops=2 * vectors * orbitals * depth * walkers * orbitals,
            bytes_accessed=2 * vectors * orbitals * depth,
            transcendentals=0,
        ),
    )(cholesky_rot, onebody, *packs, *arrays)


def finish(stats, packs, places, counts, vectors, slots, walkers):
    walk_size = len(places)
    rows = (packs[0].shape[0] - 3 * table_height(vectors)) // walkers

    def kernel(stats_ref, counts_ref, *refs):
        pack_refs = refs[: len(packs)]
        energies_ref, weights_ref, density_ref = refs[len(packs) :]
        walk = lax.axis_index("walk")
        lane = lax.broadcasted_iota(jnp.int32, (1, LANES), 1)
        all_slots = slots * walk_size
        tables = [read_table(pack_refs[n], at, vectors) for n, _, at in places]
        source = merge_tables([t[vectors : vectors + 1, :] for t in tables], walk, walk_size, slots, lane)
        total_weight = tables[0][vectors + 1 : vectors + 2, :]
        for t in tables[1:]:
            total_weight = total_weight + t[vectors + 1 : vectors + 2, :]
        mean_weight = total_weight / (walkers * walk_size)
        total = jnp.sum(stats_ref[...], axis=0, keepdims=True)
        power = pltpu.roll(total, LANES - all_slots, 1)
        live_count = jnp.zeros((1, LANES), jnp.int32)
        for q in range(walk_size):
            live_count = jnp.where(lane // slots == q, counts_ref[q], live_count)
        live = (lane < all_slots) & (lane % slots < live_count)
        energies = jnp.where(live, total, 0.0)
        new_weights = jnp.where(live, mean_weight * jnp.exp(jnp.where(live, power, 0.0)), 0.0)
        norm = jnp.sum(new_weights, axis=1, keepdims=True)
        density = jnp.zeros((rows, LANES), jnp.float32)
        for d, (n, top, _) in enumerate(places):
            group = walk_partner(walk, d, walk_size, True)
            for b in range(walkers):
                walker = (group * walkers + b).astype(jnp.float32)
                share = jnp.sum(jnp.where(source == walker, new_weights, 0.0), axis=1, keepdims=True) / norm
                density += share * pack_refs[n][top + b * rows : top + (b + 1) * rows, :].astype(jnp.float32)
        density_ref[...] = density
        first = lax.rem(LANES - walk * slots, LANES)
        energies_ref[...] = pltpu.roll(jnp.broadcast_to(energies, (8, LANES)), first, 1)[:1, :slots]
        weights_ref[...] = pltpu.roll(jnp.broadcast_to(new_weights, (8, LANES)), first, 1)[:1, :slots]

    return pl.pallas_call(
        kernel,
        name="finish",
        out_shape=[
            jax.ShapeDtypeStruct((1, slots), jnp.float32),
            jax.ShapeDtypeStruct((1, slots), jnp.float32),
            jax.ShapeDtypeStruct((rows, LANES), jnp.float32),
        ],
        in_specs=[vmem(), smem()] + [vmem()] * len(packs),
        out_specs=[vmem()] * 3,
        compiler_params=params(),
        cost_estimate=pl.CostEstimate(flops=10**6, bytes_accessed=6 * 10**5, transcendentals=128),
    )(stats, counts, *packs)


def per_device(green_rows, cholesky_rot, one_body, fields, weights, sources, counts, owners):
    chol_size = lax.axis_size("chol")
    walk_size = lax.axis_size("walk")
    vectors, slots = fields.shape
    walkers = green_rows.shape[1]
    onebody, *packed = pack(green_rows, one_body, fields, weights, sources, owners, cholesky_rot)
    if chol_size > RING_LIMIT or chol_size % 2 or chol_size < 8:
        far = exchange_far(packed)
        packs = [packed[0], far] + exchange_near(packed, far)
        total, last = None, [lax.all_gather(green_rows, "chol", axis=0, tiled=True)]
    else:
        onebody, total, last, packs = ring(green_rows, cholesky_rot, onebody, packed)
    table = 3 * table_height(vectors)
    places = walk_places(packs[0].shape[0] - table, table, walk_size)
    stats = measure(cholesky_rot, total, last, packs, places, onebody, vectors, slots)
    turned = [list(range(stats.shape[0]))[::-1]]
    stats = lax.all_to_all(
        stats, ("chol", "walk"), split_axis=0, concat_axis=0, axis_index_groups=turned, tiled=True
    )
    energies, new_weights, density = finish(stats, packs, places, counts, vectors, slots, walkers)
    return energies.reshape(slots), new_weights.reshape(slots), density.reshape(1, density.size)


def solution(mesh):
    return jax.shard_map(
        per_device,
        mesh=mesh,
        in_specs=(
            P("chol", "walk", None),
            P("chol", None, None),
            P("chol", None),
            P("chol", "walk"),
            P("walk"),
            P("walk"),
            P(),
            P(),
        ),
        out_specs=(P("walk"), P("walk"), P("walk", "chol")),
        check_vma=False,
    )
```

```python
import jax
import jax.numpy as jnp
from jax import lax
from jax.experimental import pallas as pl
from jax.experimental.pallas import tpu as pltpu
from jax.sharding import PartitionSpec as P

time_step = 0.02
root_step = 0.02**0.5
LANES = 128
VMEM_LIMIT = 16 * 1024 * 1024
PACK_LIMIT = 54 * 1024 * 1024
ACCUMULATE_LIMIT = 24 * 1024 * 1024
RING_LIMIT = 16


def params(limit=VMEM_LIMIT):
    return pltpu.CompilerParams(vmem_limit_bytes=limit)


def vmem():
    return pl.BlockSpec(memory_space=pltpu.VMEM)


def smem():
    return pl.BlockSpec(memory_space=pltpu.SMEM)


def ring_order(size):
    return [2 * q if q < size // 2 else 2 * (size - 1 - q) + 1 for q in range(size)]


def ring_place(index, size):
    return jnp.where(index % 2 == 0, index // 2, size - 1 - index // 2)


def ring_owner(place, size):
    return jnp.where(place < size // 2, 2 * place, 2 * (size - 1 - place) + 1)


def column_start(shift, rows):
    size = lax.axis_size("chol")
    place = ring_place(lax.axis_index("chol"), size)
    owner = ring_owner(lax.rem(place + shift + size, size), size)
    return pl.multiple_of(owner * rows, rows)


def accumulate(cholesky_rot, shifts, parts, total, mark):
    vectors, orbitals, _ = cholesky_rot.shape
    walkers = parts[0].shape[1]
    rows = sum(x.shape[0] for x in parts) // len(shifts)
    size = vectors * orbitals
    arrays = list(parts) + ([] if mark is None else [mark]) + ([] if total is None else [total])

    def kernel(chol_ref, *refs):
        shards = refs[: len(parts)]
        total_ref, mark_ref = refs[len(arrays) :]
        mark_ref[...] = jnp.zeros_like(mark_ref)
        lhs = jnp.concatenate(
            [chol_ref[:, :, pl.ds(column_start(shift, rows), rows)].reshape(size, rows) for shift in shifts], axis=1
        )
        for b in range(walkers):
            rhs = jnp.concatenate([x[:, b, :] for x in shards], axis=0)
            value = jnp.dot(lhs, rhs, preferred_element_type=jnp.float32)
            total_ref[b] = value if total is None else refs[len(arrays) - 1][b] + value

    return pl.pallas_call(
        kernel,
        name="accumulate",
        out_shape=[
            jax.ShapeDtypeStruct((walkers, size, orbitals), jnp.float32),
            jax.ShapeDtypeStruct((8, LANES), jnp.float32),
        ],
        in_specs=[vmem()] * (1 + len(arrays)),
        out_specs=[vmem()] * 2,
        compiler_params=params(ACCUMULATE_LIMIT),
        cost_estimate=pl.CostEstimate(
            flops=2 * len(parts) * size * rows * walkers * orbitals,
            bytes_accessed=2 * len(parts) * size * rows,
            transcendentals=0,
        ),
    )(cholesky_rot, *arrays)


def tie(*arrays):
    return lax.optimization_barrier(arrays)


def ring(own, cholesky_rot, onebody, packed):
    size = lax.axis_size("chol")
    half = own.shape[0] // 2
    order = ring_order(size)

    def send(x, places):
        return lax.ppermute(x, "chol", [(order[q], order[(q + places) % size]) for q in range(size)])

    steps = size // 2
    right, back = send(own, 1), send(own, -1)
    right, onebody = tie(right, onebody)
    upper, lower = send(right[:half], 1), send(right[half:], 1)
    back, *packed = tie(back, *packed)
    next_back = send(back, -1)
    far = exchange_far(packed)
    total, mark = accumulate(cholesky_rot, [0, -1, 1], [own, right, back], None, None)
    back = next_back
    shifts, parts = [], []
    for step in range(2, steps):
        upper, mark = tie(upper, mark)
        next_upper = send(upper, 1)
        lower, mark = tie(lower, mark)
        next_lower = send(lower, 1)
        shifts, parts = shifts + [-step], parts + [upper, lower]
        if step < steps - 1:
            back, mark = tie(back, mark)
            next_back = send(back, -1)
            shifts, parts = shifts + [step], parts + [back]
            back = next_back
        if step == 2:
            near = exchange_near(packed, far)
        total, mark = accumulate(cholesky_rot, shifts, parts, total, mark)
        shifts, parts = [], []
        upper, lower = next_upper, next_lower
    return onebody, total, [-steps, steps - 1], [upper, lower, back], [packed[0], far] + near


def table_height(vectors):
    return -(-(vectors + 2) // 16) * 16


def pack(own, one_body, fields, weights, sources, owners, cholesky_rot):
    rows, walkers, orbitals = own.shape
    walk_size = lax.axis_size("walk")
    width = orbitals // walk_size
    pair = LANES // width
    vectors, slots = fields.shape
    table_rows = table_height(vectors)
    panel_rows = walkers * (rows // pair)
    both = panel_rows + 3 * table_rows
    if walk_size == 4:
        heights = [both, both + panel_rows, both]
        spots = [(0, 0), (2, 0), (1, 0), (1, both)]
    else:
        heights = [both] * walk_size
        spots = [(d, 0) for d in range(walk_size)]

    def kernel(own_any, body_any, fields_any, weights_any, sources_any, owners_any, chol_any, *refs):
        onebody_ref = refs[0]
        packs = refs[1 : 1 + len(heights)]
        own_ref, body_ref, fields_ref, weights_ref, sources_ref, owners_ref, table_scr, sems = refs[1 + len(heights) :]
        places = [
            (own_any, own_ref),
            (body_any, body_ref),
            (fields_any, fields_ref),
            (weights_any, weights_ref),
            (sources_any, sources_ref),
            (owners_any, owners_ref),
        ]
        small = [pltpu.make_async_copy(a, b, sems.at[n]) for n, (a, b) in enumerate(places)]
        for copy in small:
            copy.start()
        for copy in small:
            copy.wait()
        green = [own_ref[:, b, :] for b in range(walkers)]
        walk = lax.axis_index("walk")
        lane = lax.broadcasted_iota(jnp.int32, (1, LANES), 1)
        body = body_ref[...].astype(jnp.float32)
        onebody_ref[...] = jnp.zeros_like(onebody_ref)
        for b in range(walkers):
            total = jnp.sum(green[b].astype(jnp.float32) * body, axis=0, keepdims=True)
            folded = total[:, :LANES]
            for start in range(LANES, orbitals, LANES):
                folded = folded + total[:, start : start + LANES]
            onebody_ref[b : b + 1, :] = folded
        r = lax.broadcasted_iota(jnp.int32, (rows // pair, rows), 0)
        m = lax.broadcasted_iota(jnp.int32, (rows // pair, rows), 1)
        k = lax.broadcasted_iota(jnp.int32, (orbitals, LANES), 0)
        c = lax.broadcasted_iota(jnp.int32, (orbitals, LANES), 1)
        thinned = []
        for b in range(walkers):
            values = green[b]
            thinned.append(
                [
                    jnp.dot(
                        (m == r * pair + h).astype(jnp.bfloat16), values, preferred_element_type=jnp.float32
                    ).astype(jnp.bfloat16)
                    for h in range(pair)
                ]
            )
        for d in range(walk_size):
            target = walk_partner(walk, d, walk_size, False)
            out, top = spots[d]
            panel = jnp.int32(0)
            for p in range(walk_size):
                panel = jnp.where(owners_ref[p] == target, p, panel)
            for b in range(walkers):
                total = jnp.zeros((rows // pair, LANES), jnp.float32)
                for h in range(pair):
                    take = (k == panel * width + c - h * width) & (c >= h * width) & (c < (h + 1) * width)
                    total += jnp.dot(
                        thinned[b][h], take.astype(jnp.bfloat16), preferred_element_type=jnp.float32
                    )
                packs[out][top + b * (rows // pair) : top + (b + 1) * (rows // pair), :] = total.astype(jnp.bfloat16)
        spread = jnp.zeros((vectors, LANES), jnp.float32)
        source = jnp.zeros((1, LANES), jnp.float32)
        corner = lax.broadcasted_iota(jnp.int32, (vectors, vectors), 0) == lax.broadcasted_iota(
            jnp.int32, (vectors, vectors), 1
        )
        for j in range(slots):
            mine = lane % slots == j
            upright = jnp.sum(jnp.where(corner, fields_ref[j : j + 1, :], 0.0), axis=1, keepdims=True)
            spread += jnp.where(mine, upright, 0.0)
            source += jnp.where(mine, sources_ref[j].astype(jnp.float32), 0.0)
        weight = weights_ref[0]
        for j in range(1, weights.shape[0]):
            weight = weight + weights_ref[j]
        table_scr[...] = jnp.zeros_like(table_scr)
        table_scr[:vectors, :] = spread
        table_scr[vectors : vectors + 1, :] = source
        table_scr[vectors + 1 : vectors + 2, :] = jnp.zeros((1, LANES), jnp.float32) + weight
        rest = table_scr[...]
        for n in range(3):
            piece = rest.astype(jnp.bfloat16)
            rest = rest - piece.astype(jnp.float32)
            at = panel_rows + n * table_rows
            for d in range(len(heights)):
                packs[d][at : at + table_rows, :] = piece

    return pl.pallas_call(
        kernel,
        name="pack",
        out_shape=[
            jax.ShapeDtypeStruct((8, LANES), jnp.float32),
        ]
        + [jax.ShapeDtypeStruct((height, LANES), jnp.bfloat16) for height in heights],
        in_specs=[pl.BlockSpec(memory_space=pl.ANY)] * 7,
        out_specs=[vmem()] * (len(heights) + 1),
        scratch_shapes=[
            pltpu.VMEM(own.shape, own.dtype),
            pltpu.VMEM(one_body.shape, one_body.dtype),
            pltpu.VMEM((slots, vectors), jnp.float32),
            pltpu.SMEM(weights.shape, weights.dtype),
            pltpu.SMEM(sources.shape, sources.dtype),
            pltpu.SMEM(owners.shape, owners.dtype),
            pltpu.VMEM((table_rows, LANES), jnp.float32),
            pltpu.SemaphoreType.DMA((6,)),
        ],
        compiler_params=params(PACK_LIMIT),
        cost_estimate=pl.CostEstimate(flops=10**8, bytes_accessed=10**6, transcendentals=0),
    )(own, one_body, fields.T, weights, sources, owners, cholesky_rot)


def walk_partner(walk, d, size, back):
    if size == 4:
        return lax.bitwise_xor(walk, d)
    return lax.rem(walk + (size - d if back else d), size)


def exchange_far(packed):
    size = lax.axis_size("walk")
    if size != 4:
        return lax.ppermute(packed[1], "walk", [(q, (q + 1) % size) for q in range(size)])
    return lax.ppermute(packed[1], "walk", [(q, q ^ 2) for q in range(size)])


def exchange_near(packed, far):
    size = lax.axis_size("walk")
    if size != 4:
        return [
            lax.ppermute(packed[d], "walk", [(q, (q + d) % size) for q in range(size)]) for d in range(2, size)
        ]
    keep, _, near = packed
    panel = far.shape[0] - keep.shape[0]
    return [lax.ppermute(jnp.concatenate([near, far[panel:]], axis=0), "walk", [(q, q ^ 1) for q in range(size)])]


def walk_places(panel, table, size):
    if size != 4:
        return [(d, 0, panel) for d in range(size)]
    return [(0, 0, panel), (2, 0, panel), (1, 0, panel), (2, panel + 2 * table, panel + table)]


def read_table(ref, at, vectors):
    height = table_height(vectors)
    parts = [ref[at + n * height : at + (n + 1) * height, :].astype(jnp.float32) for n in range(3)]
    return parts[0] + (parts[1] + parts[2])


def merge_tables(tables, walk, walk_size, slots, lane):
    total = jnp.zeros_like(tables[0])
    for d, table in enumerate(tables):
        group = walk_partner(walk, d, walk_size, True)
        total += jnp.where(lane // slots == group, table, 0.0)
    return total


def measure(cholesky_rot, total, shifts, last, packs, places, onebody, vectors, slots):
    _, walkers, orbitals = last[0].shape
    rows = sum(x.shape[0] for x in last) // len(shifts)
    walk_size = len(places)
    targets = walk_size * lax.axis_size("chol")
    whole = total is None
    quads = orbitals // LANES

    def fold(x):
        return jnp.sum(x.reshape(-1, 8, LANES), axis=0)

    def kernel(*refs):
        chol_ref, onebody_ref = refs[:2]
        pack_refs = refs[2 : 2 + len(packs)]
        last_refs = refs[2 + len(packs) : 2 + len(packs) + len(last)]
        out_ref, tensor_scr = refs[-2:]
        walk = lax.axis_index("walk")
        lane = lax.broadcasted_iota(jnp.int32, (1, LANES), 1)
        table = merge_tables(
            [read_table(pack_refs[n], at, vectors) for n, _, at in places], walk, walk_size, slots, lane
        )
        picks = [
            jnp.where(
                (lane < slots * walk_size) & (table[vectors : vectors + 1, :] == (walk * walkers + b).astype(jnp.float32)),
                1.0,
                0.0,
            )
            for b in range(walkers)
        ]
        rhs = [jnp.concatenate([x[:, b, :] for x in last_refs], axis=0) for b in range(walkers)]
        eye = lax.broadcasted_iota(jnp.int32, (LANES, LANES), 0) == lax.broadcasted_iota(
            jnp.int32, (LANES, LANES), 1
        )
        exchange = [jnp.zeros((8, LANES), jnp.float32) for _ in range(walkers)]
        squares = [jnp.zeros((1, 1), jnp.float32) for _ in range(walkers)]
        drive = jnp.zeros((1, LANES), jnp.float32)
        starts = [0 if shift is None else column_start(shift, rows) for shift in shifts]
        blocks = [chol_ref[:, :, pl.ds(start, rows)].reshape(vectors * orbitals, rows) for start in starts]
        lhs = jnp.concatenate(blocks, axis=1)
        for b in range(walkers):
            value = jnp.dot(lhs, rhs[b], preferred_element_type=jnp.float32)
            tensor_scr[b] = value if whole else refs[2 + len(packs) + len(last)][b] + value
        for g in range(vectors):
            top = g * orbitals
            for b in range(walkers):
                diagonal = jnp.zeros((LANES, LANES), jnp.float32)
                for q in range(quads):
                    for p in range(q + 1):
                        one = tensor_scr[
                            b, top + q * LANES : top + (q + 1) * LANES, p * LANES : (p + 1) * LANES
                        ]
                        if p == q:
                            exchange[b] = exchange[b] + fold(one * one.T)
                            diagonal = diagonal + one
                        else:
                            two = tensor_scr[
                                b, top + p * LANES : top + (p + 1) * LANES, q * LANES : (q + 1) * LANES
                            ]
                            exchange[b] = exchange[b] + 2.0 * fold(two * one.T)
                trace = jnp.sum(fold(jnp.where(eye, diagonal, 0.0)), axis=0, keepdims=True)
                trace = jnp.sum(trace, axis=1, keepdims=True)
                squares[b] = squares[b] + trace * trace
                drive = drive - root_step * picks[b] * table[g : g + 1, :] * trace
        raw = jnp.zeros((1, LANES), jnp.float32)
        square = jnp.zeros((1, LANES), jnp.float32)
        for b in range(walkers):
            swapped = jnp.sum(jnp.sum(exchange[b], axis=0, keepdims=True), axis=1, keepdims=True)
            single = jnp.sum(onebody_ref[b : b + 1, :], axis=1, keepdims=True)
            raw += picks[b] * (single + 0.5 * squares[b] - 0.5 * swapped)
            square += picks[b] * squares[b]
        power = drive - 0.5 * time_step * square - time_step * raw
        out_ref[...] = jnp.broadcast_to(raw + pltpu.roll(power, slots * walk_size, 1), (targets, LANES))

    arrays = list(last) + ([] if whole else [total])
    return pl.pallas_call(
        kernel,
        name="measure",
        out_shape=jax.ShapeDtypeStruct((targets, LANES), jnp.float32),
        in_specs=[vmem()] * (2 + len(packs) + len(arrays)),
        out_specs=vmem(),
        scratch_shapes=[
            pltpu.VMEM((walkers, vectors * orbitals, orbitals), jnp.float32),
        ],
        compiler_params=params(),
        cost_estimate=pl.CostEstimate(
            flops=2 * vectors * orbitals * rows * len(shifts) * walkers * orbitals,
            bytes_accessed=2 * vectors * orbitals * rows * len(shifts),
            transcendentals=0,
        ),
    )(cholesky_rot, onebody, *packs, *arrays)


def finish(stats, packs, places, counts, vectors, slots, walkers):
    walk_size = len(places)
    rows = (packs[0].shape[0] - 3 * table_height(vectors)) // walkers

    def kernel(stats_ref, counts_ref, *refs):
        pack_refs = refs[: len(packs)]
        energies_ref, weights_ref, density_ref = refs[len(packs) :]
        walk = lax.axis_index("walk")
        lane = lax.broadcasted_iota(jnp.int32, (1, LANES), 1)
        all_slots = slots * walk_size
        tables = [read_table(pack_refs[n], at, vectors) for n, _, at in places]
        source = merge_tables([t[vectors : vectors + 1, :] for t in tables], walk, walk_size, slots, lane)
        total_weight = tables[0][vectors + 1 : vectors + 2, :]
        for t in tables[1:]:
            total_weight = total_weight + t[vectors + 1 : vectors + 2, :]
        mean_weight = total_weight / (walkers * walk_size)
        total = jnp.sum(stats_ref[...], axis=0, keepdims=True)
        power = pltpu.roll(total, LANES - all_slots, 1)
        live_count = jnp.zeros((1, LANES), jnp.int32)
        for q in range(walk_size):
            live_count = jnp.where(lane // slots == q, counts_ref[q], live_count)
        live = (lane < all_slots) & (lane % slots < live_count)
        energies = jnp.where(live, total, 0.0)
        new_weights = jnp.where(live, mean_weight * jnp.exp(jnp.where(live, power, 0.0)), 0.0)
        norm = jnp.sum(new_weights, axis=1, keepdims=True)
        density = jnp.zeros((rows, LANES), jnp.float32)
        for d, (n, top, _) in enumerate(places):
            group = walk_partner(walk, d, walk_size, True)
            for b in range(walkers):
                walker = (group * walkers + b).astype(jnp.float32)
                share = jnp.sum(jnp.where(source == walker, new_weights, 0.0), axis=1, keepdims=True) / norm
                density += share * pack_refs[n][top + b * rows : top + (b + 1) * rows, :].astype(jnp.float32)
        density_ref[...] = density
        first = lax.rem(LANES - walk * slots, LANES)
        energies_ref[...] = pltpu.roll(jnp.broadcast_to(energies, (8, LANES)), first, 1)[:1, :slots]
        weights_ref[...] = pltpu.roll(jnp.broadcast_to(new_weights, (8, LANES)), first, 1)[:1, :slots]

    return pl.pallas_call(
        kernel,
        name="finish",
        out_shape=[
            jax.ShapeDtypeStruct((1, slots), jnp.float32),
            jax.ShapeDtypeStruct((1, slots), jnp.float32),
            jax.ShapeDtypeStruct((rows, LANES), jnp.float32),
        ],
        in_specs=[vmem(), smem()] + [vmem()] * len(packs),
        out_specs=[vmem()] * 3,
        compiler_params=params(),
        cost_estimate=pl.CostEstimate(flops=10**6, bytes_accessed=6 * 10**5, transcendentals=128),
    )(stats, counts, *packs)


def per_device(green_rows, cholesky_rot, one_body, fields, weights, sources, counts, owners):
    chol_size = lax.axis_size("chol")
    walk_size = lax.axis_size("walk")
    vectors, slots = fields.shape
    walkers = green_rows.shape[1]
    onebody, *packed = pack(green_rows, one_body, fields, weights, sources, owners, cholesky_rot)
    if chol_size > RING_LIMIT or chol_size % 2 or chol_size < 8:
        far = exchange_far(packed)
        packs = [packed[0], far] + exchange_near(packed, far)
        total, shifts, last = None, [None], [lax.all_gather(green_rows, "chol", axis=0, tiled=True)]
    else:
        onebody, total, shifts, last, packs = ring(green_rows, cholesky_rot, onebody, packed)
    table = 3 * table_height(vectors)
    places = walk_places(packs[0].shape[0] - table, table, walk_size)
    stats = measure(cholesky_rot, total, shifts, last, packs, places, onebody, vectors, slots)
    stats = lax.all_to_all(stats, ("chol", "walk"), split_axis=0, concat_axis=0, tiled=True)
    energies, new_weights, density = finish(stats, packs, places, counts, vectors, slots, walkers)
    return energies.reshape(slots), new_weights.reshape(slots), density.reshape(1, density.size)


def solution(mesh):
    return jax.shard_map(
        per_device,
        mesh=mesh,
        in_specs=(
            P("chol", "walk", None),
            P("chol", None, None),
            P("chol", None),
            P("chol", "walk"),
            P("walk"),
            P("walk"),
            P(),
            P(),
        ),
        out_specs=(P("walk"), P("walk"), P("walk", "chol")),
        check_vma=False,
    )
```

```python
import jax
import jax.numpy as jnp
from jax import lax
from jax.experimental import pallas as pl
from jax.experimental.pallas import tpu as pltpu
from jax.sharding import PartitionSpec as P

time_step = 0.02
root_step = 0.02**0.5
LANES = 128
VMEM_LIMIT = 16 * 1024 * 1024
PACK_LIMIT = 54 * 1024 * 1024
ACCUMULATE_LIMIT = 24 * 1024 * 1024
RING_LIMIT = 16


def params(limit=VMEM_LIMIT):
    return pltpu.CompilerParams(vmem_limit_bytes=limit)


def vmem():
    return pl.BlockSpec(memory_space=pltpu.VMEM)


def smem():
    return pl.BlockSpec(memory_space=pltpu.SMEM)


def ring_order(size):
    return [2 * q if q < size // 2 else 2 * (size - 1 - q) + 1 for q in range(size)]


def ring_place(index, size):
    return jnp.where(index % 2 == 0, index // 2, size - 1 - index // 2)


def ring_owner(place, size):
    return jnp.where(place < size // 2, 2 * place, 2 * (size - 1 - place) + 1)


def column_start(shift, rows):
    size = lax.axis_size("chol")
    place = ring_place(lax.axis_index("chol"), size)
    owner = ring_owner(lax.rem(place + shift + size, size), size)
    return pl.multiple_of(owner * rows, rows)


def accumulate(cholesky_rot, shifts, parts, total, mark):
    vectors, orbitals, _ = cholesky_rot.shape
    rows, walkers, _ = parts[0].shape
    size = vectors * orbitals
    arrays = list(parts) + ([] if mark is None else [mark]) + ([] if total is None else [total])

    def kernel(chol_ref, *refs):
        shards = refs[: len(parts)]
        total_ref, mark_ref = refs[len(arrays) :]
        mark_ref[...] = jnp.zeros_like(mark_ref)
        lhs = jnp.concatenate(
            [chol_ref[:, :, pl.ds(column_start(shift, rows), rows)].reshape(size, rows) for shift in shifts], axis=1
        )
        for b in range(walkers):
            rhs = jnp.concatenate([x[:, b, :] for x in shards], axis=0)
            value = jnp.dot(lhs, rhs, preferred_element_type=jnp.float32)
            total_ref[b] = value if total is None else refs[len(arrays) - 1][b] + value

    return pl.pallas_call(
        kernel,
        name="accumulate",
        out_shape=[
            jax.ShapeDtypeStruct((walkers, size, orbitals), jnp.float32),
            jax.ShapeDtypeStruct((8, LANES), jnp.float32),
        ],
        in_specs=[vmem()] * (1 + len(arrays)),
        out_specs=[vmem()] * 2,
        compiler_params=params(ACCUMULATE_LIMIT),
        cost_estimate=pl.CostEstimate(
            flops=2 * len(parts) * size * rows * walkers * orbitals,
            bytes_accessed=2 * len(parts) * size * rows,
            transcendentals=0,
        ),
    )(cholesky_rot, *arrays)


def tie(*arrays):
    return lax.optimization_barrier(arrays)


def ring(own, cholesky_rot, onebody, packed, do_prepare):
    size = lax.axis_size("chol")
    rows = own.shape[0]
    order = ring_order(size)
    ahead = [(order[q], order[(q + 1) % size]) for q in range(size)]
    back = [(order[q], order[(q - 1) % size]) for q in range(size)]
    steps = size // 2
    right = left = own
    shifts, parts = [0], [own]
    total = mark = None
    for step in range(1, steps):
        next_right, next_left = lax.ppermute(right, "chol", ahead), lax.ppermute(left, "chol", back)
        if step == 1:
            right, onebody = tie(next_right, onebody)
            left, *packed = tie(next_left, *packed)
        else:
            if step == 2:
                far = exchange_far(packed)
            elif step == 3:
                near = exchange_near(packed, far)
            total, mark = accumulate(cholesky_rot, shifts, parts, total, mark)
            shifts, parts = [], []
            right, mark = tie(next_right, mark)
            left, mark = tie(next_left, mark)
        shifts += [-step, step]
        parts = parts + [right, left]
    last = [lax.ppermute(right[: rows // 2], "chol", ahead), lax.ppermute(left[rows // 2 :], "chol", back)]
    mark, *near = tie(mark, *near)
    packs = [packed[0], far] + near
    plan = do_prepare(packs)
    mark, plan = tie(mark, plan)
    total, _ = accumulate(cholesky_rot, shifts, parts, total, mark)
    return total, last, packs, plan


def table_height(vectors):
    return -(-(vectors + 2) // 16) * 16


def pack(own, one_body, fields, weights, sources, owners, cholesky_rot):
    rows, walkers, orbitals = own.shape
    walk_size = lax.axis_size("walk")
    width = orbitals // walk_size
    pair = LANES // width
    vectors, slots = fields.shape
    table_rows = table_height(vectors)
    panel_rows = walkers * (rows // pair)
    both = panel_rows + 3 * table_rows
    if walk_size == 4:
        heights = [both, both + panel_rows, both]
        spots = [(0, 0), (2, 0), (1, 0), (1, both)]
    else:
        heights = [both] * walk_size
        spots = [(d, 0) for d in range(walk_size)]

    def kernel(own_any, body_any, fields_any, weights_any, sources_any, owners_any, chol_any, *refs):
        onebody_ref = refs[0]
        packs = refs[1 : 1 + len(heights)]
        own_ref, body_ref, fields_ref, weights_ref, sources_ref, owners_ref, table_scr, sems = refs[1 + len(heights) :]
        places = [
            (own_any, own_ref),
            (body_any, body_ref),
            (fields_any, fields_ref),
            (weights_any, weights_ref),
            (sources_any, sources_ref),
            (owners_any, owners_ref),
        ]
        small = [pltpu.make_async_copy(a, b, sems.at[n]) for n, (a, b) in enumerate(places)]
        for copy in small:
            copy.start()
        for copy in small:
            copy.wait()
        green = [own_ref[:, b, :] for b in range(walkers)]
        walk = lax.axis_index("walk")
        lane = lax.broadcasted_iota(jnp.int32, (1, LANES), 1)
        body = body_ref[...].astype(jnp.float32)
        onebody_ref[...] = jnp.zeros_like(onebody_ref)
        for b in range(walkers):
            total = jnp.sum(green[b].astype(jnp.float32) * body, axis=0, keepdims=True)
            folded = total[:, :LANES]
            for start in range(LANES, orbitals, LANES):
                folded = folded + total[:, start : start + LANES]
            onebody_ref[b : b + 1, :] = folded
        r = lax.broadcasted_iota(jnp.int32, (rows // pair, rows), 0)
        m = lax.broadcasted_iota(jnp.int32, (rows // pair, rows), 1)
        k = lax.broadcasted_iota(jnp.int32, (orbitals, LANES), 0)
        c = lax.broadcasted_iota(jnp.int32, (orbitals, LANES), 1)
        thinned = []
        for b in range(walkers):
            values = green[b]
            thinned.append(
                [
                    jnp.dot(
                        (m == r * pair + h).astype(jnp.bfloat16), values, preferred_element_type=jnp.float32
                    ).astype(jnp.bfloat16)
                    for h in range(pair)
                ]
            )
        for d in range(walk_size):
            target = walk_partner(walk, d, walk_size, False)
            out, top = spots[d]
            panel = jnp.int32(0)
            for p in range(walk_size):
                panel = jnp.where(owners_ref[p] == target, p, panel)
            for b in range(walkers):
                total = jnp.zeros((rows // pair, LANES), jnp.float32)
                for h in range(pair):
                    take = (k == panel * width + c - h * width) & (c >= h * width) & (c < (h + 1) * width)
                    total += jnp.dot(
                        thinned[b][h], take.astype(jnp.bfloat16), preferred_element_type=jnp.float32
                    )
                packs[out][top + b * (rows // pair) : top + (b + 1) * (rows // pair), :] = total.astype(jnp.bfloat16)
        spread = jnp.zeros((vectors, LANES), jnp.float32)
        source = jnp.zeros((1, LANES), jnp.float32)
        corner = lax.broadcasted_iota(jnp.int32, (vectors, vectors), 0) == lax.broadcasted_iota(
            jnp.int32, (vectors, vectors), 1
        )
        for j in range(slots):
            mine = lane % slots == j
            upright = jnp.sum(jnp.where(corner, fields_ref[j : j + 1, :], 0.0), axis=1, keepdims=True)
            spread += jnp.where(mine, upright, 0.0)
            source += jnp.where(mine, sources_ref[j].astype(jnp.float32), 0.0)
        weight = weights_ref[0]
        for j in range(1, weights.shape[0]):
            weight = weight + weights_ref[j]
        table_scr[...] = jnp.zeros_like(table_scr)
        table_scr[:vectors, :] = spread
        table_scr[vectors : vectors + 1, :] = source
        table_scr[vectors + 1 : vectors + 2, :] = jnp.zeros((1, LANES), jnp.float32) + weight
        rest = table_scr[...]
        for n in range(3):
            piece = rest.astype(jnp.bfloat16)
            rest = rest - piece.astype(jnp.float32)
            at = panel_rows + n * table_rows
            for d in range(len(heights)):
                packs[d][at : at + table_rows, :] = piece

    return pl.pallas_call(
        kernel,
        name="pack",
        out_shape=[
            jax.ShapeDtypeStruct((8, LANES), jnp.float32),
        ]
        + [jax.ShapeDtypeStruct((height, LANES), jnp.bfloat16) for height in heights],
        in_specs=[pl.BlockSpec(memory_space=pl.ANY)] * 7,
        out_specs=[vmem()] * (len(heights) + 1),
        scratch_shapes=[
            pltpu.VMEM(own.shape, own.dtype),
            pltpu.VMEM(one_body.shape, one_body.dtype),
            pltpu.VMEM((slots, vectors), jnp.float32),
            pltpu.SMEM(weights.shape, weights.dtype),
            pltpu.SMEM(sources.shape, sources.dtype),
            pltpu.SMEM(owners.shape, owners.dtype),
            pltpu.VMEM((table_rows, LANES), jnp.float32),
            pltpu.SemaphoreType.DMA((6,)),
        ],
        compiler_params=params(PACK_LIMIT),
        cost_estimate=pl.CostEstimate(flops=10**8, bytes_accessed=10**6, transcendentals=0),
    )(own, one_body, fields.T, weights, sources, owners, cholesky_rot)


def walk_partner(walk, d, size, back):
    if size == 4:
        return lax.bitwise_xor(walk, d)
    return lax.rem(walk + (size - d if back else d), size)


def exchange_far(packed):
    size = lax.axis_size("walk")
    if size != 4:
        return lax.ppermute(packed[1], "walk", [(q, (q + 1) % size) for q in range(size)])
    return lax.ppermute(packed[1], "walk", [(q, q ^ 2) for q in range(size)])


def exchange_near(packed, far):
    size = lax.axis_size("walk")
    if size != 4:
        return [
            lax.ppermute(packed[d], "walk", [(q, (q + d) % size) for q in range(size)]) for d in range(2, size)
        ]
    keep, _, near = packed
    panel = far.shape[0] - keep.shape[0]
    return [lax.ppermute(jnp.concatenate([near, far[panel:]], axis=0), "walk", [(q, q ^ 1) for q in range(size)])]


def walk_places(panel, table, size):
    if size != 4:
        return [(d, 0, panel) for d in range(size)]
    return [(0, 0, panel), (2, 0, panel), (1, 0, panel), (2, panel + 2 * table, panel + table)]


def read_table(ref, at, vectors):
    height = table_height(vectors)
    parts = [ref[at + n * height : at + (n + 1) * height, :].astype(jnp.float32) for n in range(3)]
    return parts[0] + (parts[1] + parts[2])


def merge_tables(tables, walk, walk_size, slots, lane):
    total = jnp.zeros_like(tables[0])
    for d, table in enumerate(tables):
        group = walk_partner(walk, d, walk_size, True)
        total += jnp.where(lane // slots == group, table, 0.0)
    return total


def plan_rows(vectors, walkers, walk_size):
    shares = walkers * vectors
    picks = shares + walkers * walk_size
    single = picks + walkers
    return 0, shares, picks, single, single + 1, single + 2, -(-(single + 3) // 8) * 8


def prepare(packs, places, onebody, counts, vectors, slots, walkers):
    walk_size = len(places)
    at_drive, at_share, at_pick, at_single, at_live, at_mean, height = plan_rows(vectors, walkers, walk_size)

    def kernel(counts_ref, onebody_ref, *refs):
        pack_refs, plan_ref = refs[:-1], refs[-1]
        walk = lax.axis_index("walk")
        lane = lax.broadcasted_iota(jnp.int32, (1, LANES), 1)
        all_slots = slots * walk_size
        tables = [read_table(pack_refs[n], at, vectors) for n, _, at in places]
        table = merge_tables(tables, walk, walk_size, slots, lane)
        source = jnp.where(lane < all_slots, table[vectors : vectors + 1, :], -1.0)
        total_weight = tables[0][vectors + 1 : vectors + 2, :]
        for t in tables[1:]:
            total_weight = total_weight + t[vectors + 1 : vectors + 2, :]
        live_count = jnp.zeros((1, LANES), jnp.int32)
        for q in range(walk_size):
            live_count = jnp.where(lane // slots == q, counts_ref[q], live_count)
        live = (lane < all_slots) & (lane % slots < live_count)
        plan_ref[...] = jnp.zeros_like(plan_ref)
        single = jnp.zeros((1, LANES), jnp.float32)
        for b in range(walkers):
            pick = jnp.where(source == (walk * walkers + b).astype(jnp.float32), 1.0, 0.0)
            plan_ref[at_pick + b : at_pick + b + 1, :] = pick
            plan_ref[at_drive + b * vectors : at_drive + (b + 1) * vectors, :] = -root_step * pick * table[:vectors, :]
            single += pick * jnp.sum(onebody_ref[b : b + 1, :], axis=1, keepdims=True)
        plan_ref[at_single : at_single + 1, :] = single
        for d in range(walk_size):
            group = walk_partner(walk, d, walk_size, True)
            for b in range(walkers):
                row = at_share + d * walkers + b
                plan_ref[row : row + 1, :] = jnp.where(
                    source == (group * walkers + b).astype(jnp.float32), 1.0, 0.0
                )
        plan_ref[at_live : at_live + 1, :] = jnp.where(live, 1.0, 0.0)
        plan_ref[at_mean : at_mean + 1, :] = total_weight / (walkers * walk_size)

    return pl.pallas_call(
        kernel,
        name="prepare",
        out_shape=jax.ShapeDtypeStruct((height, LANES), jnp.float32),
        in_specs=[smem()] + [vmem()] * (1 + len(packs)),
        out_specs=vmem(),
        compiler_params=params(),
        cost_estimate=pl.CostEstimate(flops=10**8, bytes_accessed=10**6, transcendentals=0),
    )(counts, onebody, *packs)


def measure(cholesky_rot, total, last, plan, vectors, walk_size):
    _, walkers, orbitals = last[0].shape
    depth = sum(x.shape[0] for x in last)
    targets = walk_size * lax.axis_size("chol")
    whole = total is None
    quads = orbitals // LANES
    at_drive, _, at_pick, at_single, _, _, _ = plan_rows(vectors, walkers, walk_size)

    def fold(x):
        return jnp.sum(x.reshape(-1, 8, LANES), axis=0)

    def kernel(*refs):
        chol_ref, plan_ref = refs[:2]
        last_refs = refs[2 : 2 + len(last)]
        out_ref, tensor_scr = refs[-2:]
        rhs = [jnp.concatenate([x[:, b, :] for x in last_refs], axis=0) for b in range(walkers)]
        eye = lax.broadcasted_iota(jnp.int32, (LANES, LANES), 0) == lax.broadcasted_iota(
            jnp.int32, (LANES, LANES), 1
        )
        exchange = [jnp.zeros((8, LANES), jnp.float32) for _ in range(walkers)]
        squares = [jnp.zeros((1, 1), jnp.float32) for _ in range(walkers)]
        drive = jnp.zeros((1, LANES), jnp.float32)
        start = 0 if whole else column_start(lax.axis_size("chol") // 2, depth)
        lhs = chol_ref[:, :, pl.ds(start, depth)].reshape(vectors * orbitals, depth)
        for b in range(walkers):
            value = jnp.dot(lhs, rhs[b], preferred_element_type=jnp.float32)
            tensor_scr[b] = value if whole else refs[2 + len(last)][b] + value
        for g in range(vectors):
            top = g * orbitals
            for b in range(walkers):
                diagonal = jnp.zeros((LANES, LANES), jnp.float32)
                for q in range(quads):
                    for p in range(q + 1):
                        one = tensor_scr[
                            b, top + q * LANES : top + (q + 1) * LANES, p * LANES : (p + 1) * LANES
                        ]
                        if p == q:
                            exchange[b] = exchange[b] + fold(one * one.T)
                            diagonal = diagonal + one
                        else:
                            two = tensor_scr[
                                b, top + p * LANES : top + (p + 1) * LANES, q * LANES : (q + 1) * LANES
                            ]
                            exchange[b] = exchange[b] + 2.0 * fold(two * one.T)
                trace = jnp.sum(fold(jnp.where(eye, diagonal, 0.0)), axis=0, keepdims=True)
                trace = jnp.sum(trace, axis=1, keepdims=True)
                squares[b] = squares[b] + trace * trace
                row = at_drive + b * vectors + g
                drive = drive + plan_ref[row : row + 1, :] * trace
        raw = plan_ref[at_single : at_single + 1, :]
        square = jnp.zeros((1, LANES), jnp.float32)
        for b in range(walkers):
            swapped = jnp.sum(jnp.sum(exchange[b], axis=0, keepdims=True), axis=1, keepdims=True)
            pick = plan_ref[at_pick + b : at_pick + b + 1, :]
            raw += pick * (0.5 * squares[b] - 0.5 * swapped)
            square += pick * squares[b]
        power = drive - 0.5 * time_step * square - time_step * raw
        out_ref[...] = jnp.broadcast_to(raw + pltpu.roll(power, LANES // 2, 1), (targets, LANES))

    arrays = list(last) + ([] if whole else [total])
    return pl.pallas_call(
        kernel,
        name="measure",
        out_shape=jax.ShapeDtypeStruct((targets, LANES), jnp.float32),
        in_specs=[vmem()] * (2 + len(arrays)),
        out_specs=vmem(),
        scratch_shapes=[
            pltpu.VMEM((walkers, vectors * orbitals, orbitals), jnp.float32),
        ],
        compiler_params=params(),
        cost_estimate=pl.CostEstimate(
            flops=2 * vectors * orbitals * depth * walkers * orbitals,
            bytes_accessed=2 * vectors * orbitals * depth,
            transcendentals=0,
        ),
    )(cholesky_rot, plan, *arrays)


def finish(stats, plan, packs, places, vectors, slots, walkers):
    walk_size = len(places)
    rows = (packs[0].shape[0] - 3 * table_height(vectors)) // walkers
    _, at_share, at_pick, _, at_live, at_mean, _ = plan_rows(vectors, walkers, walk_size)

    def kernel(stats_ref, plan_ref, *refs):
        pack_refs = refs[: len(packs)]
        energies_ref, weights_ref, density_ref = refs[len(packs) :]
        walk = lax.axis_index("walk")
        total = jnp.sum(stats_ref[...], axis=0, keepdims=True)
        power = pltpu.roll(total, LANES // 2, 1)
        live = plan_ref[at_live : at_live + 1, :] > 0.0
        energies = jnp.where(live, total, 0.0)
        new_weights = jnp.where(
            live, plan_ref[at_mean : at_mean + 1, :] * jnp.exp(jnp.where(live, power, 0.0)), 0.0
        )
        norm = jnp.sum(new_weights, axis=1, keepdims=True)
        shares = jnp.sum(plan_ref[at_share:at_pick, :] * new_weights, axis=1, keepdims=True) / norm
        density = jnp.zeros((rows, LANES), jnp.float32)
        for d, (n, top, _) in enumerate(places):
            for b in range(walkers):
                share = shares[d * walkers + b : d * walkers + b + 1, :]
                density += share * pack_refs[n][top + b * rows : top + (b + 1) * rows, :].astype(jnp.float32)
        density_ref[...] = density
        first = lax.rem(LANES - walk * slots, LANES)
        energies_ref[...] = pltpu.roll(jnp.broadcast_to(energies, (8, LANES)), first, 1)[:1, :slots]
        weights_ref[...] = pltpu.roll(jnp.broadcast_to(new_weights, (8, LANES)), first, 1)[:1, :slots]

    return pl.pallas_call(
        kernel,
        name="finish",
        out_shape=[
            jax.ShapeDtypeStruct((1, slots), jnp.float32),
            jax.ShapeDtypeStruct((1, slots), jnp.float32),
            jax.ShapeDtypeStruct((rows, LANES), jnp.float32),
        ],
        in_specs=[vmem()] * (2 + len(packs)),
        out_specs=[vmem()] * 3,
        compiler_params=params(),
        cost_estimate=pl.CostEstimate(flops=10**6, bytes_accessed=6 * 10**5, transcendentals=128),
    )(stats, plan, *packs)


def per_device(green_rows, cholesky_rot, one_body, fields, weights, sources, counts, owners):
    chol_size = lax.axis_size("chol")
    walk_size = lax.axis_size("walk")
    vectors, slots = fields.shape
    walkers = green_rows.shape[1]
    onebody, *packed = pack(green_rows, one_body, fields, weights, sources, owners, cholesky_rot)
    table = 3 * table_height(vectors)
    places = walk_places(packed[0].shape[0] - table, table, walk_size)

    def do_prepare(packs):
        return prepare(packs, places, onebody, counts, vectors, slots, walkers)

    if chol_size > RING_LIMIT or chol_size % 2 or chol_size < 8:
        far = exchange_far(packed)
        packs = [packed[0], far] + exchange_near(packed, far)
        plan = do_prepare(packs)
        total, last = None, [lax.all_gather(green_rows, "chol", axis=0, tiled=True)]
    else:
        total, last, packs, plan = ring(green_rows, cholesky_rot, onebody, packed, do_prepare)
    stats = measure(cholesky_rot, total, last, plan, vectors, walk_size)
    stats = lax.all_to_all(stats, ("chol", "walk"), split_axis=0, concat_axis=0, tiled=True)
    energies, new_weights, density = finish(stats, plan, packs, places, vectors, slots, walkers)
    return energies.reshape(slots), new_weights.reshape(slots), density.reshape(1, density.size)


def solution(mesh):
    return jax.shard_map(
        per_device,
        mesh=mesh,
        in_specs=(
            P("chol", "walk", None),
            P("chol", None, None),
            P("chol", None),
            P("chol", "walk"),
            P("walk"),
            P("walk"),
            P(),
            P(),
        ),
        out_specs=(P("walk"), P("walk"), P("walk", "chol")),
        check_vma=False,
    )
```

```python
import jax
import jax.numpy as jnp
from jax import lax
from jax.experimental import pallas as pl
from jax.experimental.pallas import tpu as pltpu
from jax.sharding import PartitionSpec as P

time_step = 0.02
root_step = 0.02**0.5
LANES = 128
VMEM_LIMIT = 16 * 1024 * 1024
PACK_LIMIT = 54 * 1024 * 1024
ACCUMULATE_LIMIT = 24 * 1024 * 1024
RING_LIMIT = 16


def params(limit=VMEM_LIMIT):
    return pltpu.CompilerParams(vmem_limit_bytes=limit)


def vmem():
    return pl.BlockSpec(memory_space=pltpu.VMEM)


def smem():
    return pl.BlockSpec(memory_space=pltpu.SMEM)


def ring_order(size):
    return [2 * q if q < size // 2 else 2 * (size - 1 - q) + 1 for q in range(size)]


def ring_place(index, size):
    return jnp.where(index % 2 == 0, index // 2, size - 1 - index // 2)


def ring_owner(place, size):
    return jnp.where(place < size // 2, 2 * place, 2 * (size - 1 - place) + 1)


def column_start(shift, rows):
    size = lax.axis_size("chol")
    place = ring_place(lax.axis_index("chol"), size)
    owner = ring_owner(lax.rem(place + shift + size, size), size)
    return pl.multiple_of(owner * rows, rows)


def accumulate(cholesky_rot, shifts, parts, total, mark):
    vectors, orbitals, _ = cholesky_rot.shape
    walkers = parts[0].shape[1]
    rows = sum(x.shape[0] for x in parts) // len(shifts)
    size = vectors * orbitals
    arrays = list(parts) + ([] if mark is None else [mark]) + ([] if total is None else [total])

    def kernel(chol_ref, *refs):
        shards = refs[: len(parts)]
        total_ref, mark_ref = refs[len(arrays) :]
        mark_ref[...] = jnp.zeros_like(mark_ref)
        lhs = jnp.concatenate(
            [chol_ref[:, :, pl.ds(column_start(shift, rows), rows)].reshape(size, rows) for shift in shifts], axis=1
        )
        for b in range(walkers):
            rhs = jnp.concatenate([x[:, b, :] for x in shards], axis=0)
            value = jnp.dot(lhs, rhs, preferred_element_type=jnp.float32)
            total_ref[b] = value if total is None else refs[len(arrays) - 1][b] + value

    return pl.pallas_call(
        kernel,
        name="accumulate",
        out_shape=[
            jax.ShapeDtypeStruct((walkers, size, orbitals), jnp.float32),
            jax.ShapeDtypeStruct((8, LANES), jnp.float32),
        ],
        in_specs=[vmem()] * (1 + len(arrays)),
        out_specs=[vmem()] * 2,
        compiler_params=params(ACCUMULATE_LIMIT),
        cost_estimate=pl.CostEstimate(
            flops=2 * len(shifts) * size * rows * walkers * orbitals,
            bytes_accessed=2 * len(shifts) * size * rows,
            transcendentals=0,
        ),
    )(cholesky_rot, *arrays)


def tie(*arrays):
    return lax.optimization_barrier(arrays)


def ring(own, cholesky_rot, onebody, packed, do_prepare):
    size = lax.axis_size("chol")
    rows = own.shape[0]
    order = ring_order(size)
    ahead = [(order[q], order[(q + 1) % size]) for q in range(size)]
    back = [(order[q], order[(q - 1) % size]) for q in range(size)]
    steps = size // 2
    half = rows // 2
    right = left = own
    shifts, parts = [0], [own]
    total = mark = None
    for step in range(1, steps - 1):
        next_right, next_left = lax.ppermute(right, "chol", ahead), lax.ppermute(left, "chol", back)
        if step == 1:
            right, onebody = tie(next_right, onebody)
            far = exchange_far(packed)
            left = next_left
        else:
            total, mark = accumulate(cholesky_rot, shifts, parts, total, mark)
            shifts, parts = [], []
            if step == 2:
                far, mark = tie(far, mark)
                near = exchange_near(packed, far)
            right, mark = tie(next_right, mark)
            left, mark = tie(next_left, mark)
        shifts += [-step, step]
        parts = parts + [right, left]
    upper = lax.ppermute(right[:half], "chol", ahead)
    lower = lax.ppermute(left[half:], "chol", back)
    rest = [lax.ppermute(right[half:], "chol", ahead), lax.ppermute(left[:half], "chol", back)]
    total, mark = accumulate(cholesky_rot, shifts, parts, total, mark)
    upper, mark = tie(upper, mark)
    lower, mark = tie(lower, mark)
    last = [lax.ppermute(upper, "chol", ahead), lax.ppermute(lower, "chol", back)]
    mark, *near = tie(mark, *near)
    packs = [packed[0], far] + near
    plan = do_prepare(packs)
    mark, plan, *rest = tie(mark, plan, *rest)
    parts = [upper, rest[0], rest[1], lower]
    total, _ = accumulate(cholesky_rot, [1 - steps, steps - 1], parts, total, mark)
    return total, last, packs, plan


def table_height(vectors):
    return -(-(vectors + 2) // 16) * 16


def pack(own, one_body, fields, weights, sources, owners, cholesky_rot):
    rows, walkers, orbitals = own.shape
    walk_size = lax.axis_size("walk")
    width = orbitals // walk_size
    pair = LANES // width
    vectors, slots = fields.shape
    table_rows = table_height(vectors)
    panel_rows = walkers * (rows // pair)
    both = panel_rows + 3 * table_rows
    if walk_size == 4:
        heights = [both, both + panel_rows, both]
        spots = [(0, 0), (2, 0), (1, 0), (1, both)]
    else:
        heights = [both] * walk_size
        spots = [(d, 0) for d in range(walk_size)]

    def kernel(own_any, body_any, fields_any, weights_any, sources_any, owners_any, chol_any, *refs):
        onebody_ref = refs[0]
        packs = refs[1 : 1 + len(heights)]
        own_ref, body_ref, fields_ref, weights_ref, sources_ref, owners_ref, table_scr, sems = refs[1 + len(heights) :]
        places = [
            (own_any, own_ref),
            (body_any, body_ref),
            (fields_any, fields_ref),
            (weights_any, weights_ref),
            (sources_any, sources_ref),
            (owners_any, owners_ref),
        ]
        small = [pltpu.make_async_copy(a, b, sems.at[n]) for n, (a, b) in enumerate(places)]
        for copy in small:
            copy.start()
        for copy in small:
            copy.wait()
        green = [own_ref[:, b, :] for b in range(walkers)]
        walk = lax.axis_index("walk")
        lane = lax.broadcasted_iota(jnp.int32, (1, LANES), 1)
        body = body_ref[...].astype(jnp.float32)
        onebody_ref[...] = jnp.zeros_like(onebody_ref)
        for b in range(walkers):
            total = jnp.sum(green[b].astype(jnp.float32) * body, axis=0, keepdims=True)
            folded = total[:, :LANES]
            for start in range(LANES, orbitals, LANES):
                folded = folded + total[:, start : start + LANES]
            onebody_ref[b : b + 1, :] = folded
        r = lax.broadcasted_iota(jnp.int32, (rows // pair, rows), 0)
        m = lax.broadcasted_iota(jnp.int32, (rows // pair, rows), 1)
        k = lax.broadcasted_iota(jnp.int32, (orbitals, LANES), 0)
        c = lax.broadcasted_iota(jnp.int32, (orbitals, LANES), 1)
        thinned = []
        for b in range(walkers):
            values = green[b]
            thinned.append(
                [
                    jnp.dot(
                        (m == r * pair + h).astype(jnp.bfloat16), values, preferred_element_type=jnp.float32
                    ).astype(jnp.bfloat16)
                    for h in range(pair)
                ]
            )
        for d in range(walk_size):
            target = walk_partner(walk, d, walk_size, False)
            out, top = spots[d]
            panel = jnp.int32(0)
            for p in range(walk_size):
                panel = jnp.where(owners_ref[p] == target, p, panel)
            for b in range(walkers):
                total = jnp.zeros((rows // pair, LANES), jnp.float32)
                for h in range(pair):
                    take = (k == panel * width + c - h * width) & (c >= h * width) & (c < (h + 1) * width)
                    total += jnp.dot(
                        thinned[b][h], take.astype(jnp.bfloat16), preferred_element_type=jnp.float32
                    )
                packs[out][top + b * (rows // pair) : top + (b + 1) * (rows // pair), :] = total.astype(jnp.bfloat16)
        spread = jnp.zeros((vectors, LANES), jnp.float32)
        source = jnp.zeros((1, LANES), jnp.float32)
        corner = lax.broadcasted_iota(jnp.int32, (vectors, vectors), 0) == lax.broadcasted_iota(
            jnp.int32, (vectors, vectors), 1
        )
        for j in range(slots):
            mine = lane % slots == j
            upright = jnp.sum(jnp.where(corner, fields_ref[j : j + 1, :], 0.0), axis=1, keepdims=True)
            spread += jnp.where(mine, upright, 0.0)
            source += jnp.where(mine, sources_ref[j].astype(jnp.float32), 0.0)
        weight = weights_ref[0]
        for j in range(1, weights.shape[0]):
            weight = weight + weights_ref[j]
        table_scr[...] = jnp.zeros_like(table_scr)
        table_scr[:vectors, :] = spread
        table_scr[vectors : vectors + 1, :] = source
        table_scr[vectors + 1 : vectors + 2, :] = jnp.zeros((1, LANES), jnp.float32) + weight
        rest = table_scr[...]
        for n in range(3):
            piece = rest.astype(jnp.bfloat16)
            rest = rest - piece.astype(jnp.float32)
            at = panel_rows + n * table_rows
            for d in range(len(heights)):
                packs[d][at : at + table_rows, :] = piece

    return pl.pallas_call(
        kernel,
        name="pack",
        out_shape=[
            jax.ShapeDtypeStruct((8, LANES), jnp.float32),
        ]
        + [jax.ShapeDtypeStruct((height, LANES), jnp.bfloat16) for height in heights],
        in_specs=[pl.BlockSpec(memory_space=pl.ANY)] * 7,
        out_specs=[vmem()] * (len(heights) + 1),
        scratch_shapes=[
            pltpu.VMEM(own.shape, own.dtype),
            pltpu.VMEM(one_body.shape, one_body.dtype),
            pltpu.VMEM((slots, vectors), jnp.float32),
            pltpu.SMEM(weights.shape, weights.dtype),
            pltpu.SMEM(sources.shape, sources.dtype),
            pltpu.SMEM(owners.shape, owners.dtype),
            pltpu.VMEM((table_rows, LANES), jnp.float32),
            pltpu.SemaphoreType.DMA((6,)),
        ],
        compiler_params=params(PACK_LIMIT),
        cost_estimate=pl.CostEstimate(flops=10**8, bytes_accessed=10**6, transcendentals=0),
    )(own, one_body, fields.T, weights, sources, owners, cholesky_rot)


def walk_partner(walk, d, size, back):
    if size == 4:
        return lax.bitwise_xor(walk, d)
    return lax.rem(walk + (size - d if back else d), size)


def exchange_far(packed):
    size = lax.axis_size("walk")
    if size != 4:
        return lax.ppermute(packed[1], "walk", [(q, (q + 1) % size) for q in range(size)])
    return lax.ppermute(packed[1], "walk", [(q, q ^ 2) for q in range(size)])


def exchange_near(packed, far):
    size = lax.axis_size("walk")
    if size != 4:
        return [
            lax.ppermute(packed[d], "walk", [(q, (q + d) % size) for q in range(size)]) for d in range(2, size)
        ]
    keep, _, near = packed
    panel = far.shape[0] - keep.shape[0]
    return [lax.ppermute(jnp.concatenate([near, far[panel:]], axis=0), "walk", [(q, q ^ 1) for q in range(size)])]


def walk_places(panel, table, size):
    if size != 4:
        return [(d, 0, panel) for d in range(size)]
    return [(0, 0, panel), (2, 0, panel), (1, 0, panel), (2, panel + 2 * table, panel + table)]


def read_table(ref, at, vectors):
    height = table_height(vectors)
    parts = [ref[at + n * height : at + (n + 1) * height, :].astype(jnp.float32) for n in range(3)]
    return parts[0] + (parts[1] + parts[2])


def merge_tables(tables, walk, walk_size, slots, lane):
    total = jnp.zeros_like(tables[0])
    for d, table in enumerate(tables):
        group = walk_partner(walk, d, walk_size, True)
        total += jnp.where(lane // slots == group, table, 0.0)
    return total


def plan_rows(vectors, walkers, walk_size):
    shares = walkers * vectors
    picks = shares + walkers * walk_size
    single = picks + walkers
    return 0, shares, picks, single, single + 1, single + 2, -(-(single + 3) // 8) * 8


def prepare(packs, places, onebody, counts, vectors, slots, walkers):
    walk_size = len(places)
    at_drive, at_share, at_pick, at_single, at_live, at_mean, height = plan_rows(vectors, walkers, walk_size)

    def kernel(counts_ref, onebody_ref, *refs):
        pack_refs, plan_ref = refs[:-1], refs[-1]
        walk = lax.axis_index("walk")
        lane = lax.broadcasted_iota(jnp.int32, (1, LANES), 1)
        all_slots = slots * walk_size
        tables = [read_table(pack_refs[n], at, vectors) for n, _, at in places]
        table = merge_tables(tables, walk, walk_size, slots, lane)
        source = jnp.where(lane < all_slots, table[vectors : vectors + 1, :], -1.0)
        total_weight = tables[0][vectors + 1 : vectors + 2, :]
        for t in tables[1:]:
            total_weight = total_weight + t[vectors + 1 : vectors + 2, :]
        live_count = jnp.zeros((1, LANES), jnp.int32)
        for q in range(walk_size):
            live_count = jnp.where(lane // slots == q, counts_ref[q], live_count)
        live = (lane < all_slots) & (lane % slots < live_count)
        plan_ref[...] = jnp.zeros_like(plan_ref)
        single = jnp.zeros((1, LANES), jnp.float32)
        for b in range(walkers):
            pick = jnp.where(source == (walk * walkers + b).astype(jnp.float32), 1.0, 0.0)
            plan_ref[at_pick + b : at_pick + b + 1, :] = pick
            plan_ref[at_drive + b * vectors : at_drive + (b + 1) * vectors, :] = -root_step * pick * table[:vectors, :]
            single += pick * jnp.sum(onebody_ref[b : b + 1, :], axis=1, keepdims=True)
        plan_ref[at_single : at_single + 1, :] = single
        for d in range(walk_size):
            group = walk_partner(walk, d, walk_size, True)
            for b in range(walkers):
                row = at_share + d * walkers + b
                plan_ref[row : row + 1, :] = jnp.where(
                    source == (group * walkers + b).astype(jnp.float32), 1.0, 0.0
                )
        plan_ref[at_live : at_live + 1, :] = jnp.where(live, 1.0, 0.0)
        plan_ref[at_mean : at_mean + 1, :] = total_weight / (walkers * walk_size)

    return pl.pallas_call(
        kernel,
        name="prepare",
        out_shape=jax.ShapeDtypeStruct((height, LANES), jnp.float32),
        in_specs=[smem()] + [vmem()] * (1 + len(packs)),
        out_specs=vmem(),
        compiler_params=params(),
        cost_estimate=pl.CostEstimate(flops=10**8, bytes_accessed=10**6, transcendentals=0),
    )(counts, onebody, *packs)


def measure(cholesky_rot, total, last, plan, vectors, walk_size):
    _, walkers, orbitals = last[0].shape
    depth = sum(x.shape[0] for x in last)
    targets = walk_size * lax.axis_size("chol")
    whole = total is None
    quads = orbitals // LANES
    at_drive, _, at_pick, at_single, _, _, _ = plan_rows(vectors, walkers, walk_size)

    def fold(x):
        return jnp.sum(x.reshape(-1, 8, LANES), axis=0)

    def kernel(*refs):
        chol_ref, plan_ref = refs[:2]
        last_refs = refs[2 : 2 + len(last)]
        out_ref, tensor_scr = refs[-2:]
        rhs = [jnp.concatenate([x[:, b, :] for x in last_refs], axis=0) for b in range(walkers)]
        eye = lax.broadcasted_iota(jnp.int32, (LANES, LANES), 0) == lax.broadcasted_iota(
            jnp.int32, (LANES, LANES), 1
        )
        exchange = [jnp.zeros((8, LANES), jnp.float32) for _ in range(walkers)]
        squares = [jnp.zeros((1, 1), jnp.float32) for _ in range(walkers)]
        drive = jnp.zeros((1, LANES), jnp.float32)
        start = 0 if whole else column_start(lax.axis_size("chol") // 2, depth)
        lhs = chol_ref[:, :, pl.ds(start, depth)].reshape(vectors * orbitals, depth)
        for b in range(walkers):
            value = jnp.dot(lhs, rhs[b], preferred_element_type=jnp.float32)
            tensor_scr[b] = value if whole else refs[2 + len(last)][b] + value
        for g in range(vectors):
            top = g * orbitals
            for b in range(walkers):
                diagonal = jnp.zeros((LANES, LANES), jnp.float32)
                for q in range(quads):
                    for p in range(q + 1):
                        one = tensor_scr[
                            b, top + q * LANES : top + (q + 1) * LANES, p * LANES : (p + 1) * LANES
                        ]
                        if p == q:
                            exchange[b] = exchange[b] + fold(one * one.T)
                            diagonal = diagonal + one
                        else:
                            two = tensor_scr[
                                b, top + p * LANES : top + (p + 1) * LANES, q * LANES : (q + 1) * LANES
                            ]
                            exchange[b] = exchange[b] + 2.0 * fold(two * one.T)
                trace = jnp.sum(fold(jnp.where(eye, diagonal, 0.0)), axis=0, keepdims=True)
                trace = jnp.sum(trace, axis=1, keepdims=True)
                squares[b] = squares[b] + trace * trace
                row = at_drive + b * vectors + g
                drive = drive + plan_ref[row : row + 1, :] * trace
        raw = plan_ref[at_single : at_single + 1, :]
        square = jnp.zeros((1, LANES), jnp.float32)
        for b in range(walkers):
            swapped = jnp.sum(jnp.sum(exchange[b], axis=0, keepdims=True), axis=1, keepdims=True)
            pick = plan_ref[at_pick + b : at_pick + b + 1, :]
            raw += pick * (0.5 * squares[b] - 0.5 * swapped)
            square += pick * squares[b]
        power = drive - 0.5 * time_step * square - time_step * raw
        out_ref[...] = jnp.broadcast_to(raw + pltpu.roll(power, LANES // 2, 1), (targets, LANES))

    arrays = list(last) + ([] if whole else [total])
    return pl.pallas_call(
        kernel,
        name="measure",
        out_shape=jax.ShapeDtypeStruct((targets, LANES), jnp.float32),
        in_specs=[vmem()] * (2 + len(arrays)),
        out_specs=vmem(),
        scratch_shapes=[
            pltpu.VMEM((walkers, vectors * orbitals, orbitals), jnp.float32),
        ],
        compiler_params=params(),
        cost_estimate=pl.CostEstimate(
            flops=2 * vectors * orbitals * depth * walkers * orbitals,
            bytes_accessed=2 * vectors * orbitals * depth,
            transcendentals=0,
        ),
    )(cholesky_rot, plan, *arrays)


def finish(stats, plan, packs, places, vectors, slots, walkers):
    walk_size = len(places)
    rows = (packs[0].shape[0] - 3 * table_height(vectors)) // walkers
    _, at_share, at_pick, _, at_live, at_mean, _ = plan_rows(vectors, walkers, walk_size)

    def kernel(stats_ref, plan_ref, *refs):
        pack_refs = refs[: len(packs)]
        energies_ref, weights_ref, density_ref = refs[len(packs) :]
        walk = lax.axis_index("walk")
        total = jnp.sum(stats_ref[...], axis=0, keepdims=True)
        power = pltpu.roll(total, LANES // 2, 1)
        live = plan_ref[at_live : at_live + 1, :] > 0.0
        energies = jnp.where(live, total, 0.0)
        new_weights = jnp.where(
            live, plan_ref[at_mean : at_mean + 1, :] * jnp.exp(jnp.where(live, power, 0.0)), 0.0
        )
        norm = jnp.sum(new_weights, axis=1, keepdims=True)
        shares = jnp.sum(plan_ref[at_share:at_pick, :] * new_weights, axis=1, keepdims=True) / norm
        density = jnp.zeros((rows, LANES), jnp.float32)
        for d, (n, top, _) in enumerate(places):
            for b in range(walkers):
                share = shares[d * walkers + b : d * walkers + b + 1, :]
                density += share * pack_refs[n][top + b * rows : top + (b + 1) * rows, :].astype(jnp.float32)
        density_ref[...] = density
        first = lax.rem(LANES - walk * slots, LANES)
        energies_ref[...] = pltpu.roll(jnp.broadcast_to(energies, (8, LANES)), first, 1)[:1, :slots]
        weights_ref[...] = pltpu.roll(jnp.broadcast_to(new_weights, (8, LANES)), first, 1)[:1, :slots]

    return pl.pallas_call(
        kernel,
        name="finish",
        out_shape=[
            jax.ShapeDtypeStruct((1, slots), jnp.float32),
            jax.ShapeDtypeStruct((1, slots), jnp.float32),
            jax.ShapeDtypeStruct((rows, LANES), jnp.float32),
        ],
        in_specs=[vmem()] * (2 + len(packs)),
        out_specs=[vmem()] * 3,
        compiler_params=params(),
        cost_estimate=pl.CostEstimate(flops=10**6, bytes_accessed=6 * 10**5, transcendentals=128),
    )(stats, plan, *packs)


def per_device(green_rows, cholesky_rot, one_body, fields, weights, sources, counts, owners):
    chol_size = lax.axis_size("chol")
    walk_size = lax.axis_size("walk")
    vectors, slots = fields.shape
    walkers = green_rows.shape[1]
    onebody, *packed = pack(green_rows, one_body, fields, weights, sources, owners, cholesky_rot)
    table = 3 * table_height(vectors)
    places = walk_places(packed[0].shape[0] - table, table, walk_size)

    def do_prepare(packs):
        return prepare(packs, places, onebody, counts, vectors, slots, walkers)

    if chol_size > RING_LIMIT or chol_size % 2 or chol_size < 8:
        far = exchange_far(packed)
        packs = [packed[0], far] + exchange_near(packed, far)
        plan = do_prepare(packs)
        total, last = None, [lax.all_gather(green_rows, "chol", axis=0, tiled=True)]
    else:
        total, last, packs, plan = ring(green_rows, cholesky_rot, onebody, packed, do_prepare)
    stats = measure(cholesky_rot, total, last, plan, vectors, walk_size)
    stats = lax.all_to_all(stats, ("chol", "walk"), split_axis=0, concat_axis=0, tiled=True)
    energies, new_weights, density = finish(stats, plan, packs, places, vectors, slots, walkers)
    return energies.reshape(slots), new_weights.reshape(slots), density.reshape(1, density.size)


def solution(mesh):
    return jax.shard_map(
        per_device,
        mesh=mesh,
        in_specs=(
            P("chol", "walk", None),
            P("chol", None, None),
            P("chol", None),
            P("chol", "walk"),
            P("walk"),
            P("walk"),
            P(),
            P(),
        ),
        out_specs=(P("walk"), P("walk"), P("walk", "chol")),
        check_vma=False,
    )
```

```python
import jax
import jax.numpy as jnp
from jax import lax
from jax.experimental import pallas as pl
from jax.experimental.pallas import tpu as pltpu
from jax.sharding import PartitionSpec as P

time_step = 0.02
root_step = 0.02**0.5
LANES = 128
VMEM_LIMIT = 16 * 1024 * 1024
PACK_LIMIT = 54 * 1024 * 1024
ACCUMULATE_LIMIT = 24 * 1024 * 1024
RING_LIMIT = 16


def params(limit=VMEM_LIMIT):
    return pltpu.CompilerParams(vmem_limit_bytes=limit)


def vmem():
    return pl.BlockSpec(memory_space=pltpu.VMEM)


def smem():
    return pl.BlockSpec(memory_space=pltpu.SMEM)


def ring_order(size):
    return [2 * q if q < size // 2 else 2 * (size - 1 - q) + 1 for q in range(size)]


def ring_place(index, size):
    return jnp.where(index % 2 == 0, index // 2, size - 1 - index // 2)


def ring_owner(place, size):
    return jnp.where(place < size // 2, 2 * place, 2 * (size - 1 - place) + 1)


def column_start(shift, rows):
    size = lax.axis_size("chol")
    place = ring_place(lax.axis_index("chol"), size)
    owner = ring_owner(lax.rem(place + shift + size, size), size)
    return pl.multiple_of(owner * rows, rows)


def accumulate(cholesky_rot, shifts, parts, total, mark):
    vectors, orbitals, _ = cholesky_rot.shape
    rows, walkers, _ = parts[0].shape
    size = vectors * orbitals
    arrays = list(parts) + ([] if mark is None else [mark]) + ([] if total is None else [total])

    def kernel(chol_ref, *refs):
        shards = refs[: len(parts)]
        total_ref, mark_ref = refs[len(arrays) :]
        mark_ref[...] = jnp.zeros_like(mark_ref)
        lhs = jnp.concatenate(
            [chol_ref[:, :, pl.ds(column_start(shift, rows), rows)].reshape(size, rows) for shift in shifts], axis=1
        )
        for b in range(walkers):
            rhs = jnp.concatenate([x[:, b, :] for x in shards], axis=0)
            value = jnp.dot(lhs, rhs, preferred_element_type=jnp.float32)
            total_ref[b] = value if total is None else refs[len(arrays) - 1][b] + value

    return pl.pallas_call(
        kernel,
        name="accumulate",
        out_shape=[
            jax.ShapeDtypeStruct((walkers, size, orbitals), jnp.float32),
            jax.ShapeDtypeStruct((8, LANES), jnp.float32),
        ],
        in_specs=[vmem()] * (1 + len(arrays)),
        out_specs=[vmem()] * 2,
        compiler_params=params(ACCUMULATE_LIMIT),
        cost_estimate=pl.CostEstimate(
            flops=2 * len(parts) * size * rows * walkers * orbitals,
            bytes_accessed=2 * len(parts) * size * rows,
            transcendentals=0,
        ),
    )(cholesky_rot, *arrays)


def tie(*arrays):
    return lax.optimization_barrier(arrays)


def ring(own, cholesky_rot, onebody, packed, do_prepare):
    size = lax.axis_size("chol")
    rows = own.shape[0]
    order = ring_order(size)
    ahead = [(order[q], order[(q + 1) % size]) for q in range(size)]
    back = [(order[q], order[(q - 1) % size]) for q in range(size)]
    steps = size // 2
    right = left = own
    shifts, parts = [0], [own]
    total = mark = None
    for step in range(1, steps):
        next_right, next_left = lax.ppermute(right, "chol", ahead), lax.ppermute(left, "chol", back)
        if step == 1:
            right, onebody = tie(next_right, onebody)
            left, *packed = tie(next_left, *packed)
        else:
            if step == 2:
                far = exchange_far(packed)
            elif step == 3:
                near = exchange_near(packed, far)
            total, mark = accumulate(cholesky_rot, shifts, parts, total, mark)
            shifts, parts = [], []
            right, mark = tie(next_right, mark)
            left, mark = tie(next_left, mark)
        shifts += [-step, step]
        parts = parts + [right, left]
    last = [lax.ppermute(right[: rows // 2], "chol", ahead), lax.ppermute(left[rows // 2 :], "chol", back)]
    mark, *near = tie(mark, *near)
    packs = [packed[0], far] + near
    plan = do_prepare(packs)
    mark, plan = tie(mark, plan)
    total, _ = accumulate(cholesky_rot, shifts, parts, total, mark)
    return total, last, packs, plan


def table_height(vectors):
    return -(-(vectors + 2) // 16) * 16


def pack(own, one_body, fields, weights, sources, owners, cholesky_rot):
    rows, walkers, orbitals = own.shape
    walk_size = lax.axis_size("walk")
    width = orbitals // walk_size
    pair = LANES // width
    vectors, slots = fields.shape
    table_rows = table_height(vectors)
    panel_rows = walkers * (rows // pair)
    both = panel_rows + 3 * table_rows
    if walk_size == 4:
        heights = [both, both + panel_rows, both]
        spots = [(0, 0), (2, 0), (1, 0), (1, both)]
    else:
        heights = [both] * walk_size
        spots = [(d, 0) for d in range(walk_size)]

    def kernel(own_any, body_any, fields_any, weights_any, sources_any, owners_any, chol_any, *refs):
        onebody_ref = refs[0]
        packs = refs[1 : 1 + len(heights)]
        own_ref, body_ref, fields_ref, weights_ref, sources_ref, owners_ref, table_scr, sems = refs[1 + len(heights) :]
        places = [
            (own_any, own_ref),
            (body_any, body_ref),
            (fields_any, fields_ref),
            (weights_any, weights_ref),
            (sources_any, sources_ref),
            (owners_any, owners_ref),
        ]
        small = [pltpu.make_async_copy(a, b, sems.at[n]) for n, (a, b) in enumerate(places)]
        for copy in small:
            copy.start()
        for copy in small:
            copy.wait()
        green = [own_ref[:, b, :] for b in range(walkers)]
        walk = lax.axis_index("walk")
        lane = lax.broadcasted_iota(jnp.int32, (1, LANES), 1)
        body = body_ref[...].astype(jnp.float32)
        onebody_ref[...] = jnp.zeros_like(onebody_ref)
        for b in range(walkers):
            total = jnp.sum(green[b].astype(jnp.float32) * body, axis=0, keepdims=True)
            folded = total[:, :LANES]
            for start in range(LANES, orbitals, LANES):
                folded = folded + total[:, start : start + LANES]
            onebody_ref[b : b + 1, :] = folded
        r = lax.broadcasted_iota(jnp.int32, (rows // pair, rows), 0)
        m = lax.broadcasted_iota(jnp.int32, (rows // pair, rows), 1)
        k = lax.broadcasted_iota(jnp.int32, (orbitals, LANES), 0)
        c = lax.broadcasted_iota(jnp.int32, (orbitals, LANES), 1)
        thinned = []
        for b in range(walkers):
            values = green[b]
            thinned.append(
                [
                    jnp.dot(
                        (m == r * pair + h).astype(jnp.bfloat16), values, preferred_element_type=jnp.float32
                    ).astype(jnp.bfloat16)
                    for h in range(pair)
                ]
            )
        for d in range(walk_size):
            target = walk_partner(walk, d, walk_size, False)
            out, top = spots[d]
            panel = jnp.int32(0)
            for p in range(walk_size):
                panel = jnp.where(owners_ref[p] == target, p, panel)
            for b in range(walkers):
                total = jnp.zeros((rows // pair, LANES), jnp.float32)
                for h in range(pair):
                    take = (k == panel * width + c - h * width) & (c >= h * width) & (c < (h + 1) * width)
                    total += jnp.dot(
                        thinned[b][h], take.astype(jnp.bfloat16), preferred_element_type=jnp.float32
                    )
                packs[out][top + b * (rows // pair) : top + (b + 1) * (rows // pair), :] = total.astype(jnp.bfloat16)
        spread = jnp.zeros((vectors, LANES), jnp.float32)
        source = jnp.zeros((1, LANES), jnp.float32)
        corner = lax.broadcasted_iota(jnp.int32, (vectors, vectors), 0) == lax.broadcasted_iota(
            jnp.int32, (vectors, vectors), 1
        )
        for j in range(slots):
            mine = lane % slots == j
            upright = jnp.sum(jnp.where(corner, fields_ref[j : j + 1, :], 0.0), axis=1, keepdims=True)
            spread += jnp.where(mine, upright, 0.0)
            source += jnp.where(mine, sources_ref[j].astype(jnp.float32), 0.0)
        weight = weights_ref[0]
        for j in range(1, weights.shape[0]):
            weight = weight + weights_ref[j]
        table_scr[...] = jnp.zeros_like(table_scr)
        table_scr[:vectors, :] = spread
        table_scr[vectors : vectors + 1, :] = source
        table_scr[vectors + 1 : vectors + 2, :] = jnp.zeros((1, LANES), jnp.float32) + weight
        rest = table_scr[...]
        for n in range(3):
            piece = rest.astype(jnp.bfloat16)
            rest = rest - piece.astype(jnp.float32)
            at = panel_rows + n * table_rows
            for d in range(len(heights)):
                packs[d][at : at + table_rows, :] = piece

    return pl.pallas_call(
        kernel,
        name="pack",
        out_shape=[
            jax.ShapeDtypeStruct((8, LANES), jnp.float32),
        ]
        + [jax.ShapeDtypeStruct((height, LANES), jnp.bfloat16) for height in heights],
        in_specs=[pl.BlockSpec(memory_space=pl.ANY)] * 7,
        out_specs=[vmem()] * (len(heights) + 1),
        scratch_shapes=[
            pltpu.VMEM(own.shape, own.dtype),
            pltpu.VMEM(one_body.shape, one_body.dtype),
            pltpu.VMEM((slots, vectors), jnp.float32),
            pltpu.SMEM(weights.shape, weights.dtype),
            pltpu.SMEM(sources.shape, sources.dtype),
            pltpu.SMEM(owners.shape, owners.dtype),
            pltpu.VMEM((table_rows, LANES), jnp.float32),
            pltpu.SemaphoreType.DMA((6,)),
        ],
        compiler_params=params(PACK_LIMIT),
        cost_estimate=pl.CostEstimate(flops=10**8, bytes_accessed=10**6, transcendentals=0),
    )(own, one_body, fields.T, weights, sources, owners, cholesky_rot)


def walk_partner(walk, d, size, back):
    if size == 4:
        return lax.bitwise_xor(walk, d)
    return lax.rem(walk + (size - d if back else d), size)


def exchange_far(packed):
    size = lax.axis_size("walk")
    if size != 4:
        return lax.ppermute(packed[1], "walk", [(q, (q + 1) % size) for q in range(size)])
    return lax.ppermute(packed[1], "walk", [(q, q ^ 2) for q in range(size)])


def exchange_near(packed, far):
    size = lax.axis_size("walk")
    if size != 4:
        return [
            lax.ppermute(packed[d], "walk", [(q, (q + d) % size) for q in range(size)]) for d in range(2, size)
        ]
    keep, _, near = packed
    panel = far.shape[0] - keep.shape[0]
    return [lax.ppermute(jnp.concatenate([near, far[panel:]], axis=0), "walk", [(q, q ^ 1) for q in range(size)])]


def walk_places(panel, table, size):
    if size != 4:
        return [(d, 0, panel) for d in range(size)]
    return [(0, 0, panel), (2, 0, panel), (1, 0, panel), (2, panel + 2 * table, panel + table)]


def read_table(ref, at, vectors):
    height = table_height(vectors)
    parts = [ref[at + n * height : at + (n + 1) * height, :].astype(jnp.float32) for n in range(3)]
    return parts[0] + (parts[1] + parts[2])


def merge_tables(tables, walk, walk_size, slots, lane):
    total = jnp.zeros_like(tables[0])
    for d, table in enumerate(tables):
        group = walk_partner(walk, d, walk_size, True)
        total += jnp.where(lane // slots == group, table, 0.0)
    return total


def plan_rows(vectors, walkers, walk_size):
    shares = walkers * vectors
    picks = shares + walkers * walk_size
    single = picks + walkers
    return 0, shares, picks, single, single + 1, single + 2, -(-(single + 3) // 8) * 8


def prepare(packs, places, onebody, counts, vectors, slots, walkers):
    walk_size = len(places)
    at_drive, at_share, at_pick, at_single, at_live, at_mean, height = plan_rows(vectors, walkers, walk_size)

    def kernel(counts_ref, onebody_ref, *refs):
        pack_refs, plan_ref = refs[:-1], refs[-1]
        walk = lax.axis_index("walk")
        lane = lax.broadcasted_iota(jnp.int32, (1, LANES), 1)
        all_slots = slots * walk_size
        tables = [read_table(pack_refs[n], at, vectors) for n, _, at in places]
        table = merge_tables(tables, walk, walk_size, slots, lane)
        source = jnp.where(lane < all_slots, table[vectors : vectors + 1, :], -1.0)
        total_weight = tables[0][vectors + 1 : vectors + 2, :]
        for t in tables[1:]:
            total_weight = total_weight + t[vectors + 1 : vectors + 2, :]
        live_count = jnp.zeros((1, LANES), jnp.int32)
        for q in range(walk_size):
            live_count = jnp.where(lane // slots == q, counts_ref[q], live_count)
        live = (lane < all_slots) & (lane % slots < live_count)
        plan_ref[...] = jnp.zeros_like(plan_ref)
        single = jnp.zeros((1, LANES), jnp.float32)
        for b in range(walkers):
            pick = jnp.where(source == (walk * walkers + b).astype(jnp.float32), 1.0, 0.0)
            plan_ref[at_pick + b : at_pick + b + 1, :] = pick
            plan_ref[at_drive + b * vectors : at_drive + (b + 1) * vectors, :] = -root_step * pick * table[:vectors, :]
            single += pick * jnp.sum(onebody_ref[b : b + 1, :], axis=1, keepdims=True)
        plan_ref[at_single : at_single + 1, :] = single
        for d in range(walk_size):
            group = walk_partner(walk, d, walk_size, True)
            for b in range(walkers):
                row = at_share + d * walkers + b
                plan_ref[row : row + 1, :] = jnp.where(
                    source == (group * walkers + b).astype(jnp.float32), 1.0, 0.0
                )
        plan_ref[at_live : at_live + 1, :] = jnp.where(live, 1.0, 0.0)
        plan_ref[at_mean : at_mean + 1, :] = total_weight / (walkers * walk_size)

    return pl.pallas_call(
        kernel,
        name="prepare",
        out_shape=jax.ShapeDtypeStruct((height, LANES), jnp.float32),
        in_specs=[smem()] + [vmem()] * (1 + len(packs)),
        out_specs=vmem(),
        compiler_params=params(),
        cost_estimate=pl.CostEstimate(flops=10**8, bytes_accessed=10**6, transcendentals=0),
    )(counts, onebody, *packs)


def measure(cholesky_rot, total, last, plan, vectors, walk_size):
    _, walkers, orbitals = last[0].shape
    depth = sum(x.shape[0] for x in last)
    targets = walk_size * lax.axis_size("chol")
    whole = total is None
    quads = orbitals // LANES
    at_drive, _, at_pick, at_single, _, _, _ = plan_rows(vectors, walkers, walk_size)

    def fold(x):
        return jnp.sum(x.reshape(-1, 8, LANES), axis=0)

    def kernel(*refs):
        chol_ref, plan_ref = refs[:2]
        last_refs = refs[2 : 2 + len(last)]
        out_ref, tensor_scr = refs[-2:]
        rhs = [jnp.concatenate([x[:, b, :] for x in last_refs], axis=0) for b in range(walkers)]
        eye = lax.broadcasted_iota(jnp.int32, (LANES, LANES), 0) == lax.broadcasted_iota(
            jnp.int32, (LANES, LANES), 1
        )
        exchange = [jnp.zeros((8, LANES), jnp.float32) for _ in range(walkers)]
        squares = [jnp.zeros((1, 1), jnp.float32) for _ in range(walkers)]
        drive = jnp.zeros((1, LANES), jnp.float32)
        start = 0 if whole else column_start(lax.axis_size("chol") // 2, depth)
        for g in range(vectors):
            lhs = chol_ref[g, :, pl.ds(start, depth)]
            top = g * orbitals
            for b in range(walkers):
                value = jnp.dot(lhs, rhs[b], preferred_element_type=jnp.float32)
                if not whole:
                    value = value + refs[2 + len(last)][b, top : top + orbitals, :]
                tensor_scr[g % 2, b] = value
            for b in range(walkers):
                diagonal = jnp.zeros((LANES, LANES), jnp.float32)
                for q in range(quads):
                    for p in range(q + 1):
                        one = tensor_scr[
                            g % 2, b, q * LANES : (q + 1) * LANES, p * LANES : (p + 1) * LANES
                        ]
                        if p == q:
                            exchange[b] = exchange[b] + fold(one * one.T)
                            diagonal = diagonal + one
                        else:
                            two = tensor_scr[
                                g % 2, b, p * LANES : (p + 1) * LANES, q * LANES : (q + 1) * LANES
                            ]
                            exchange[b] = exchange[b] + 2.0 * fold(two * one.T)
                trace = jnp.sum(fold(jnp.where(eye, diagonal, 0.0)), axis=0, keepdims=True)
                trace = jnp.sum(trace, axis=1, keepdims=True)
                squares[b] = squares[b] + trace * trace
                row = at_drive + b * vectors + g
                drive = drive + plan_ref[row : row + 1, :] * trace
        raw = plan_ref[at_single : at_single + 1, :]
        square = jnp.zeros((1, LANES), jnp.float32)
        for b in range(walkers):
            swapped = jnp.sum(jnp.sum(exchange[b], axis=0, keepdims=True), axis=1, keepdims=True)
            pick = plan_ref[at_pick + b : at_pick + b + 1, :]
            raw += pick * (0.5 * squares[b] - 0.5 * swapped)
            square += pick * squares[b]
        power = drive - 0.5 * time_step * square - time_step * raw
        out_ref[...] = jnp.broadcast_to(raw + pltpu.roll(power, LANES // 2, 1), (targets, LANES))

    arrays = list(last) + ([] if whole else [total])
    return pl.pallas_call(
        kernel,
        name="measure",
        out_shape=jax.ShapeDtypeStruct((targets, LANES), jnp.float32),
        in_specs=[vmem()] * (2 + len(arrays)),
        out_specs=vmem(),
        scratch_shapes=[
            pltpu.VMEM((2, walkers, orbitals, orbitals), jnp.float32),
        ],
        compiler_params=params(),
        cost_estimate=pl.CostEstimate(
            flops=2 * vectors * orbitals * depth * walkers * orbitals,
            bytes_accessed=2 * vectors * orbitals * depth,
            transcendentals=0,
        ),
    )(cholesky_rot, plan, *arrays)


def finish(stats, plan, packs, places, vectors, slots, walkers):
    walk_size = len(places)
    rows = (packs[0].shape[0] - 3 * table_height(vectors)) // walkers
    _, at_share, at_pick, _, at_live, at_mean, _ = plan_rows(vectors, walkers, walk_size)

    def kernel(stats_ref, plan_ref, *refs):
        pack_refs = refs[: len(packs)]
        energies_ref, weights_ref, density_ref = refs[len(packs) :]
        walk = lax.axis_index("walk")
        total = jnp.sum(stats_ref[...], axis=0, keepdims=True)
        power = pltpu.roll(total, LANES // 2, 1)
        live = plan_ref[at_live : at_live + 1, :] > 0.0
        energies = jnp.where(live, total, 0.0)
        new_weights = jnp.where(
            live, plan_ref[at_mean : at_mean + 1, :] * jnp.exp(jnp.where(live, power, 0.0)), 0.0
        )
        norm = jnp.sum(new_weights, axis=1, keepdims=True)
        shares = jnp.sum(plan_ref[at_share:at_pick, :] * new_weights, axis=1, keepdims=True) / norm
        density = jnp.zeros((rows, LANES), jnp.float32)
        for d, (n, top, _) in enumerate(places):
            for b in range(walkers):
                share = shares[d * walkers + b : d * walkers + b + 1, :]
                density += share * pack_refs[n][top + b * rows : top + (b + 1) * rows, :].astype(jnp.float32)
        density_ref[...] = density
        first = lax.rem(LANES - walk * slots, LANES)
        energies_ref[...] = pltpu.roll(jnp.broadcast_to(energies, (8, LANES)), first, 1)[:1, :slots]
        weights_ref[...] = pltpu.roll(jnp.broadcast_to(new_weights, (8, LANES)), first, 1)[:1, :slots]

    return pl.pallas_call(
        kernel,
        name="finish",
        out_shape=[
            jax.ShapeDtypeStruct((1, slots), jnp.float32),
            jax.ShapeDtypeStruct((1, slots), jnp.float32),
            jax.ShapeDtypeStruct((rows, LANES), jnp.float32),
        ],
        in_specs=[vmem()] * (2 + len(packs)),
        out_specs=[vmem()] * 3,
        compiler_params=params(),
        cost_estimate=pl.CostEstimate(flops=10**6, bytes_accessed=6 * 10**5, transcendentals=128),
    )(stats, plan, *packs)


def per_device(green_rows, cholesky_rot, one_body, fields, weights, sources, counts, owners):
    chol_size = lax.axis_size("chol")
    walk_size = lax.axis_size("walk")
    vectors, slots = fields.shape
    walkers = green_rows.shape[1]
    onebody, *packed = pack(green_rows, one_body, fields, weights, sources, owners, cholesky_rot)
    table = 3 * table_height(vectors)
    places = walk_places(packed[0].shape[0] - table, table, walk_size)

    def do_prepare(packs):
        return prepare(packs, places, onebody, counts, vectors, slots, walkers)

    if chol_size > RING_LIMIT or chol_size % 2 or chol_size < 8:
        far = exchange_far(packed)
        packs = [packed[0], far] + exchange_near(packed, far)
        plan = do_prepare(packs)
        total, last = None, [lax.all_gather(green_rows, "chol", axis=0, tiled=True)]
    else:
        total, last, packs, plan = ring(green_rows, cholesky_rot, onebody, packed, do_prepare)
    stats = measure(cholesky_rot, total, last, plan, vectors, walk_size)
    stats = lax.all_to_all(stats, ("walk", "chol"), split_axis=0, concat_axis=0, tiled=True)
    energies, new_weights, density = finish(stats, plan, packs, places, vectors, slots, walkers)
    return energies.reshape(slots), new_weights.reshape(slots), density.reshape(1, density.size)


def solution(mesh):
    return jax.shard_map(
        per_device,
        mesh=mesh,
        in_specs=(
            P("chol", "walk", None),
            P("chol", None, None),
            P("chol", None),
            P("chol", "walk"),
            P("walk"),
            P("walk"),
            P(),
            P(),
        ),
        out_specs=(P("walk"), P("walk"), P("walk", "chol")),
        check_vma=False,
    )
```

```python
import jax
import jax.numpy as jnp
from jax import lax
from jax.experimental import pallas as pl
from jax.experimental.pallas import tpu as pltpu
from jax.sharding import PartitionSpec as P

time_step = 0.02
root_step = 0.02**0.5
LANES = 128
VMEM_LIMIT = 16 * 1024 * 1024
PACK_LIMIT = 54 * 1024 * 1024
ACCUMULATE_LIMIT = 24 * 1024 * 1024
RING_LIMIT = 16


def params(limit=VMEM_LIMIT):
    return pltpu.CompilerParams(vmem_limit_bytes=limit)


def vmem():
    return pl.BlockSpec(memory_space=pltpu.VMEM)


def smem():
    return pl.BlockSpec(memory_space=pltpu.SMEM)


def ring_order(size):
    return [2 * q if q < size // 2 else 2 * (size - 1 - q) + 1 for q in range(size)]


def ring_place(index, size):
    return jnp.where(index % 2 == 0, index // 2, size - 1 - index // 2)


def ring_owner(place, size):
    return jnp.where(place < size // 2, 2 * place, 2 * (size - 1 - place) + 1)


def column_start(shift, rows):
    size = lax.axis_size("chol")
    place = ring_place(lax.axis_index("chol"), size)
    owner = ring_owner(lax.rem(place + shift + size, size), size)
    return pl.multiple_of(owner * rows, rows)


def accumulate(cholesky_rot, shifts, parts, total, mark):
    vectors, orbitals, _ = cholesky_rot.shape
    rows, walkers, _ = parts[0].shape
    size = vectors * orbitals
    arrays = list(parts) + ([] if mark is None else [mark]) + ([] if total is None else [total])

    def kernel(chol_ref, *refs):
        shards = refs[: len(parts)]
        total_ref, mark_ref = refs[len(arrays) :]
        mark_ref[...] = jnp.zeros_like(mark_ref)
        lhs = jnp.concatenate(
            [chol_ref[:, :, pl.ds(column_start(shift, rows), rows)].reshape(size, rows) for shift in shifts], axis=1
        )
        for b in range(walkers):
            rhs = jnp.concatenate([x[:, b, :] for x in shards], axis=0)
            value = jnp.dot(lhs, rhs, preferred_element_type=jnp.float32)
            total_ref[b] = value if total is None else refs[len(arrays) - 1][b] + value

    return pl.pallas_call(
        kernel,
        name="accumulate",
        out_shape=[
            jax.ShapeDtypeStruct((walkers, size, orbitals), jnp.float32),
            jax.ShapeDtypeStruct((8, LANES), jnp.float32),
        ],
        in_specs=[vmem()] * (1 + len(arrays)),
        out_specs=[vmem()] * 2,
        compiler_params=params(ACCUMULATE_LIMIT),
        cost_estimate=pl.CostEstimate(
            flops=2 * len(parts) * size * rows * walkers * orbitals,
            bytes_accessed=2 * len(parts) * size * rows,
            transcendentals=0,
        ),
    )(cholesky_rot, *arrays)


def tie(*arrays):
    return lax.optimization_barrier(arrays)


def ring(own, cholesky_rot, onebody, packed, do_prepare):
    size = lax.axis_size("chol")
    rows = own.shape[0]
    order = ring_order(size)
    ahead = [(order[q], order[(q + 1) % size]) for q in range(size)]
    back = [(order[q], order[(q - 1) % size]) for q in range(size)]
    steps = size // 2
    right = left = own
    shifts, parts = [0], [own]
    total = mark = None
    for step in range(1, steps):
        next_left, next_right = lax.ppermute(left, "chol", back), lax.ppermute(right, "chol", ahead)
        if step == 1:
            left, onebody = tie(next_left, onebody)
            right, *packed = tie(next_right, *packed)
        else:
            if step == 2:
                far = exchange_far(packed)
            elif step == 3:
                near = exchange_near(packed, far)
            total, mark = accumulate(cholesky_rot, shifts, parts, total, mark)
            shifts, parts = [], []
            left, mark = tie(next_left, mark)
            right, mark = tie(next_right, mark)
        shifts += [-step, step]
        parts = parts + [right, left]
    lower = lax.ppermute(left[rows // 2 :], "chol", back)
    last = [lax.ppermute(right[: rows // 2], "chol", ahead), lower]
    mark, *near = tie(mark, *near)
    packs = [packed[0], far] + near
    plan = do_prepare(packs)
    mark, plan = tie(mark, plan)
    total, _ = accumulate(cholesky_rot, shifts, parts, total, mark)
    return total, last, packs, plan


def table_height(vectors):
    return -(-(vectors + 2) // 16) * 16


def pack(own, one_body, fields, weights, sources, owners, cholesky_rot):
    rows, walkers, orbitals = own.shape
    walk_size = lax.axis_size("walk")
    width = orbitals // walk_size
    pair = LANES // width
    vectors, slots = fields.shape
    table_rows = table_height(vectors)
    panel_rows = walkers * (rows // pair)
    both = panel_rows + 3 * table_rows
    if walk_size == 4:
        heights = [both, both + panel_rows, both]
        spots = [(0, 0), (2, 0), (1, 0), (1, both)]
    else:
        heights = [both] * walk_size
        spots = [(d, 0) for d in range(walk_size)]

    def kernel(own_any, body_any, fields_any, weights_any, sources_any, owners_any, chol_any, *refs):
        onebody_ref = refs[0]
        packs = refs[1 : 1 + len(heights)]
        own_ref, body_ref, fields_ref, weights_ref, sources_ref, owners_ref, table_scr, sems = refs[1 + len(heights) :]
        places = [
            (own_any, own_ref),
            (body_any, body_ref),
            (fields_any, fields_ref),
            (weights_any, weights_ref),
            (sources_any, sources_ref),
            (owners_any, owners_ref),
        ]
        small = [pltpu.make_async_copy(a, b, sems.at[n]) for n, (a, b) in enumerate(places)]
        for copy in small:
            copy.start()
        for copy in small:
            copy.wait()
        green = [own_ref[:, b, :] for b in range(walkers)]
        walk = lax.axis_index("walk")
        lane = lax.broadcasted_iota(jnp.int32, (1, LANES), 1)
        body = body_ref[...].astype(jnp.float32)
        onebody_ref[...] = jnp.zeros_like(onebody_ref)
        for b in range(walkers):
            total = jnp.sum(green[b].astype(jnp.float32) * body, axis=0, keepdims=True)
            folded = total[:, :LANES]
            for start in range(LANES, orbitals, LANES):
                folded = folded + total[:, start : start + LANES]
            onebody_ref[b : b + 1, :] = folded
        r = lax.broadcasted_iota(jnp.int32, (rows // pair, rows), 0)
        m = lax.broadcasted_iota(jnp.int32, (rows // pair, rows), 1)
        k = lax.broadcasted_iota(jnp.int32, (orbitals, LANES), 0)
        c = lax.broadcasted_iota(jnp.int32, (orbitals, LANES), 1)
        thinned = []
        for b in range(walkers):
            values = green[b]
            thinned.append(
                [
                    jnp.dot(
                        (m == r * pair + h).astype(jnp.bfloat16), values, preferred_element_type=jnp.float32
                    ).astype(jnp.bfloat16)
                    for h in range(pair)
                ]
            )
        for d in range(walk_size):
            target = walk_partner(walk, d, walk_size, False)
            out, top = spots[d]
            panel = jnp.int32(0)
            for p in range(walk_size):
                panel = jnp.where(owners_ref[p] == target, p, panel)
            for b in range(walkers):
                total = jnp.zeros((rows // pair, LANES), jnp.float32)
                for h in range(pair):
                    take = (k == panel * width + c - h * width) & (c >= h * width) & (c < (h + 1) * width)
                    total += jnp.dot(
                        thinned[b][h], take.astype(jnp.bfloat16), preferred_element_type=jnp.float32
                    )
                packs[out][top + b * (rows // pair) : top + (b + 1) * (rows // pair), :] = total.astype(jnp.bfloat16)
        spread = jnp.zeros((vectors, LANES), jnp.float32)
        source = jnp.zeros((1, LANES), jnp.float32)
        corner = lax.broadcasted_iota(jnp.int32, (vectors, vectors), 0) == lax.broadcasted_iota(
            jnp.int32, (vectors, vectors), 1
        )
        for j in range(slots):
            mine = lane % slots == j
            upright = jnp.sum(jnp.where(corner, fields_ref[j : j + 1, :], 0.0), axis=1, keepdims=True)
            spread += jnp.where(mine, upright, 0.0)
            source += jnp.where(mine, sources_ref[j].astype(jnp.float32), 0.0)
        weight = weights_ref[0]
        for j in range(1, weights.shape[0]):
            weight = weight + weights_ref[j]
        table_scr[...] = jnp.zeros_like(table_scr)
        table_scr[:vectors, :] = spread
        table_scr[vectors : vectors + 1, :] = source
        table_scr[vectors + 1 : vectors + 2, :] = jnp.zeros((1, LANES), jnp.float32) + weight
        rest = table_scr[...]
        for n in range(3):
            piece = rest.astype(jnp.bfloat16)
            rest = rest - piece.astype(jnp.float32)
            at = panel_rows + n * table_rows
            for d in range(len(heights)):
                packs[d][at : at + table_rows, :] = piece

    return pl.pallas_call(
        kernel,
        name="pack",
        out_shape=[
            jax.ShapeDtypeStruct((8, LANES), jnp.float32),
        ]
        + [jax.ShapeDtypeStruct((height, LANES), jnp.bfloat16) for height in heights],
        in_specs=[pl.BlockSpec(memory_space=pl.ANY)] * 7,
        out_specs=[vmem()] * (len(heights) + 1),
        scratch_shapes=[
            pltpu.VMEM(own.shape, own.dtype),
            pltpu.VMEM(one_body.shape, one_body.dtype),
            pltpu.VMEM((slots, vectors), jnp.float32),
            pltpu.SMEM(weights.shape, weights.dtype),
            pltpu.SMEM(sources.shape, sources.dtype),
            pltpu.SMEM(owners.shape, owners.dtype),
            pltpu.VMEM((table_rows, LANES), jnp.float32),
            pltpu.SemaphoreType.DMA((6,)),
        ],
        compiler_params=params(PACK_LIMIT),
        cost_estimate=pl.CostEstimate(flops=10**8, bytes_accessed=10**6, transcendentals=0),
    )(own, one_body, fields.T, weights, sources, owners, cholesky_rot)


def walk_partner(walk, d, size, back):
    if size == 4:
        return lax.bitwise_xor(walk, d)
    return lax.rem(walk + (size - d if back else d), size)


def exchange_far(packed):
    size = lax.axis_size("walk")
    if size != 4:
        return lax.ppermute(packed[1], "walk", [(q, (q + 1) % size) for q in range(size)])
    return lax.ppermute(packed[1], "walk", [(q, q ^ 2) for q in range(size)])


def exchange_near(packed, far):
    size = lax.axis_size("walk")
    if size != 4:
        return [
            lax.ppermute(packed[d], "walk", [(q, (q + d) % size) for q in range(size)]) for d in range(2, size)
        ]
    keep, _, near = packed
    panel = far.shape[0] - keep.shape[0]
    return [lax.ppermute(jnp.concatenate([near, far[panel:]], axis=0), "walk", [(q, q ^ 1) for q in range(size)])]


def walk_places(panel, table, size):
    if size != 4:
        return [(d, 0, panel) for d in range(size)]
    return [(0, 0, panel), (2, 0, panel), (1, 0, panel), (2, panel + 2 * table, panel + table)]


def read_table(ref, at, vectors):
    height = table_height(vectors)
    parts = [ref[at + n * height : at + (n + 1) * height, :].astype(jnp.float32) for n in range(3)]
    return parts[0] + (parts[1] + parts[2])


def merge_tables(tables, walk, walk_size, slots, lane):
    total = jnp.zeros_like(tables[0])
    for d, table in enumerate(tables):
        group = walk_partner(walk, d, walk_size, True)
        total += jnp.where(lane // slots == group, table, 0.0)
    return total


def plan_rows(vectors, walkers, walk_size):
    shares = walkers * vectors
    picks = shares + walkers * walk_size
    single = picks + walkers
    return 0, shares, picks, single, single + 1, single + 2, -(-(single + 3) // 8) * 8


def prepare(packs, places, onebody, counts, vectors, slots, walkers):
    walk_size = len(places)
    at_drive, at_share, at_pick, at_single, at_live, at_mean, height = plan_rows(vectors, walkers, walk_size)

    def kernel(counts_ref, onebody_ref, *refs):
        pack_refs, plan_ref = refs[:-1], refs[-1]
        walk = lax.axis_index("walk")
        lane = lax.broadcasted_iota(jnp.int32, (1, LANES), 1)
        all_slots = slots * walk_size
        tables = [read_table(pack_refs[n], at, vectors) for n, _, at in places]
        table = merge_tables(tables, walk, walk_size, slots, lane)
        source = jnp.where(lane < all_slots, table[vectors : vectors + 1, :], -1.0)
        total_weight = tables[0][vectors + 1 : vectors + 2, :]
        for t in tables[1:]:
            total_weight = total_weight + t[vectors + 1 : vectors + 2, :]
        live_count = jnp.zeros((1, LANES), jnp.int32)
        for q in range(walk_size):
            live_count = jnp.where(lane // slots == q, counts_ref[q], live_count)
        live = (lane < all_slots) & (lane % slots < live_count)
        plan_ref[...] = jnp.zeros_like(plan_ref)
        single = jnp.zeros((1, LANES), jnp.float32)
        for b in range(walkers):
            pick = jnp.where(source == (walk * walkers + b).astype(jnp.float32), 1.0, 0.0)
            plan_ref[at_pick + b : at_pick + b + 1, :] = pick
            plan_ref[at_drive + b * vectors : at_drive + (b + 1) * vectors, :] = -root_step * pick * table[:vectors, :]
            single += pick * jnp.sum(onebody_ref[b : b + 1, :], axis=1, keepdims=True)
        plan_ref[at_single : at_single + 1, :] = single
        for d in range(walk_size):
            group = walk_partner(walk, d, walk_size, True)
            for b in range(walkers):
                row = at_share + d * walkers + b
                plan_ref[row : row + 1, :] = jnp.where(
                    source == (group * walkers + b).astype(jnp.float32), 1.0, 0.0
                )
        plan_ref[at_live : at_live + 1, :] = jnp.where(live, 1.0, 0.0)
        plan_ref[at_mean : at_mean + 1, :] = total_weight / (walkers * walk_size)

    return pl.pallas_call(
        kernel,
        name="prepare",
        out_shape=jax.ShapeDtypeStruct((height, LANES), jnp.float32),
        in_specs=[smem()] + [vmem()] * (1 + len(packs)),
        out_specs=vmem(),
        compiler_params=params(),
        cost_estimate=pl.CostEstimate(flops=10**8, bytes_accessed=10**6, transcendentals=0),
    )(counts, onebody, *packs)


def measure(cholesky_rot, total, last, plan, vectors, walk_size):
    _, walkers, orbitals = last[0].shape
    depth = sum(x.shape[0] for x in last)
    targets = walk_size * lax.axis_size("chol")
    whole = total is None
    quads = orbitals // LANES
    at_drive, _, at_pick, at_single, _, _, _ = plan_rows(vectors, walkers, walk_size)

    def fold(x):
        return jnp.sum(x.reshape(-1, 8, LANES), axis=0)

    def kernel(*refs):
        chol_ref, plan_ref = refs[:2]
        last_refs = refs[2 : 2 + len(last)]
        out_ref, tensor_scr = refs[-2:]
        rhs = [jnp.concatenate([x[:, b, :] for x in last_refs], axis=0) for b in range(walkers)]
        eye = lax.broadcasted_iota(jnp.int32, (LANES, LANES), 0) == lax.broadcasted_iota(
            jnp.int32, (LANES, LANES), 1
        )
        exchange = [jnp.zeros((8, LANES), jnp.float32) for _ in range(walkers)]
        squares = [jnp.zeros((1, 1), jnp.float32) for _ in range(walkers)]
        drive = jnp.zeros((1, LANES), jnp.float32)
        start = 0 if whole else column_start(lax.axis_size("chol") // 2, depth)
        lhs = chol_ref[:, :, pl.ds(start, depth)].reshape(vectors * orbitals, depth)
        for b in range(walkers):
            value = jnp.dot(lhs, rhs[b], preferred_element_type=jnp.float32)
            tensor_scr[b] = value if whole else refs[2 + len(last)][b] + value
        for g in range(vectors):
            top = g * orbitals
            for b in range(walkers):
                diagonal = jnp.zeros((LANES, LANES), jnp.float32)
                for q in range(quads):
                    for p in range(q + 1):
                        one = tensor_scr[
                            b, top + q * LANES : top + (q + 1) * LANES, p * LANES : (p + 1) * LANES
                        ]
                        if p == q:
                            exchange[b] = exchange[b] + fold(one * one.T)
                            diagonal = diagonal + one
                        else:
                            two = tensor_scr[
                                b, top + p * LANES : top + (p + 1) * LANES, q * LANES : (q + 1) * LANES
                            ]
                            exchange[b] = exchange[b] + 2.0 * fold(two * one.T)
                trace = jnp.sum(fold(jnp.where(eye, diagonal, 0.0)), axis=0, keepdims=True)
                trace = jnp.sum(trace, axis=1, keepdims=True)
                squares[b] = squares[b] + trace * trace
                row = at_drive + b * vectors + g
                drive = drive + plan_ref[row : row + 1, :] * trace
        raw = plan_ref[at_single : at_single + 1, :]
        square = jnp.zeros((1, LANES), jnp.float32)
        for b in range(walkers):
            swapped = jnp.sum(jnp.sum(exchange[b], axis=0, keepdims=True), axis=1, keepdims=True)
            pick = plan_ref[at_pick + b : at_pick + b + 1, :]
            raw += pick * (0.5 * squares[b] - 0.5 * swapped)
            square += pick * squares[b]
        power = drive - 0.5 * time_step * square - time_step * raw
        out_ref[...] = jnp.broadcast_to(raw + pltpu.roll(power, LANES // 2, 1), (targets, LANES))

    arrays = list(last) + ([] if whole else [total])
    return pl.pallas_call(
        kernel,
        name="measure",
        out_shape=jax.ShapeDtypeStruct((targets, LANES), jnp.float32),
        in_specs=[vmem()] * (2 + len(arrays)),
        out_specs=vmem(),
        scratch_shapes=[
            pltpu.VMEM((walkers, vectors * orbitals, orbitals), jnp.float32),
        ],
        compiler_params=params(),
        cost_estimate=pl.CostEstimate(
            flops=2 * vectors * orbitals * depth * walkers * orbitals,
            bytes_accessed=2 * vectors * orbitals * depth,
            transcendentals=0,
        ),
    )(cholesky_rot, plan, *arrays)


def finish(stats, plan, packs, places, vectors, slots, walkers):
    walk_size = len(places)
    rows = (packs[0].shape[0] - 3 * table_height(vectors)) // walkers
    _, at_share, at_pick, _, at_live, at_mean, _ = plan_rows(vectors, walkers, walk_size)

    def kernel(stats_ref, plan_ref, *refs):
        pack_refs = refs[: len(packs)]
        energies_ref, weights_ref, density_ref = refs[len(packs) :]
        walk = lax.axis_index("walk")
        total = jnp.sum(stats_ref[...], axis=0, keepdims=True)
        power = pltpu.roll(total, LANES // 2, 1)
        live = plan_ref[at_live : at_live + 1, :] > 0.0
        energies = jnp.where(live, total, 0.0)
        new_weights = jnp.where(
            live, plan_ref[at_mean : at_mean + 1, :] * jnp.exp(jnp.where(live, power, 0.0)), 0.0
        )
        norm = jnp.sum(new_weights, axis=1, keepdims=True)
        shares = jnp.sum(plan_ref[at_share:at_pick, :] * new_weights, axis=1, keepdims=True) / norm
        density = jnp.zeros((rows, LANES), jnp.float32)
        for d, (n, top, _) in enumerate(places):
            for b in range(walkers):
                share = shares[d * walkers + b : d * walkers + b + 1, :]
                density += share * pack_refs[n][top + b * rows : top + (b + 1) * rows, :].astype(jnp.float32)
        density_ref[...] = density
        first = lax.rem(LANES - walk * slots, LANES)
        energies_ref[...] = pltpu.roll(jnp.broadcast_to(energies, (8, LANES)), first, 1)[:1, :slots]
        weights_ref[...] = pltpu.roll(jnp.broadcast_to(new_weights, (8, LANES)), first, 1)[:1, :slots]

    return pl.pallas_call(
        kernel,
        name="finish",
        out_shape=[
            jax.ShapeDtypeStruct((1, slots), jnp.float32),
            jax.ShapeDtypeStruct((1, slots), jnp.float32),
            jax.ShapeDtypeStruct((rows, LANES), jnp.float32),
        ],
        in_specs=[vmem()] * (2 + len(packs)),
        out_specs=[vmem()] * 3,
        compiler_params=params(),
        cost_estimate=pl.CostEstimate(flops=10**6, bytes_accessed=6 * 10**5, transcendentals=128),
    )(stats, plan, *packs)


def per_device(green_rows, cholesky_rot, one_body, fields, weights, sources, counts, owners):
    chol_size = lax.axis_size("chol")
    walk_size = lax.axis_size("walk")
    vectors, slots = fields.shape
    walkers = green_rows.shape[1]
    onebody, *packed = pack(green_rows, one_body, fields, weights, sources, owners, cholesky_rot)
    table = 3 * table_height(vectors)
    places = walk_places(packed[0].shape[0] - table, table, walk_size)

    def do_prepare(packs):
        return prepare(packs, places, onebody, counts, vectors, slots, walkers)

    if chol_size > RING_LIMIT or chol_size % 2 or chol_size < 8:
        far = exchange_far(packed)
        packs = [packed[0], far] + exchange_near(packed, far)
        plan = do_prepare(packs)
        total, last = None, [lax.all_gather(green_rows, "chol", axis=0, tiled=True)]
    else:
        total, last, packs, plan = ring(green_rows, cholesky_rot, onebody, packed, do_prepare)
    stats = measure(cholesky_rot, total, last, plan, vectors, walk_size)
    stats = lax.all_to_all(stats, ("chol", "walk"), split_axis=0, concat_axis=0, tiled=True)
    energies, new_weights, density = finish(stats, plan, packs, places, vectors, slots, walkers)
    return energies.reshape(slots), new_weights.reshape(slots), density.reshape(1, density.size)


def solution(mesh):
    return jax.shard_map(
        per_device,
        mesh=mesh,
        in_specs=(
            P("chol", "walk", None),
            P("chol", None, None),
            P("chol", None),
            P("chol", "walk"),
            P("walk"),
            P("walk"),
            P(),
            P(),
        ),
        out_specs=(P("walk"), P("walk"), P("walk", "chol")),
        check_vma=False,
    )
```

```python
import jax
import jax.numpy as jnp
from jax import lax
from jax.experimental import pallas as pl
from jax.experimental.pallas import tpu as pltpu
from jax.sharding import PartitionSpec as P

time_step = 0.02
root_step = 0.02**0.5
LANES = 128
VMEM_LIMIT = 16 * 1024 * 1024
PACK_LIMIT = 54 * 1024 * 1024
ACCUMULATE_LIMIT = 24 * 1024 * 1024
RING_LIMIT = 16


def params(limit=VMEM_LIMIT):
    return pltpu.CompilerParams(vmem_limit_bytes=limit)


def vmem():
    return pl.BlockSpec(memory_space=pltpu.VMEM)


def smem():
    return pl.BlockSpec(memory_space=pltpu.SMEM)


def ring_order(size):
    return [2 * q if q < size // 2 else 2 * (size - 1 - q) + 1 for q in range(size)]


def ring_place(index, size):
    return jnp.where(index % 2 == 0, index // 2, size - 1 - index // 2)


def ring_owner(place, size):
    return jnp.where(place < size // 2, 2 * place, 2 * (size - 1 - place) + 1)


def column_start(shift, rows):
    size = lax.axis_size("chol")
    place = ring_place(lax.axis_index("chol"), size)
    owner = ring_owner(lax.rem(place + shift + size, size), size)
    return pl.multiple_of(owner * rows, rows)


def accumulate(cholesky_rot, shifts, parts, total, mark):
    vectors, orbitals, _ = cholesky_rot.shape
    rows, walkers, _ = parts[0].shape
    size = vectors * orbitals
    arrays = list(parts) + ([] if mark is None else [mark]) + ([] if total is None else [total])

    def kernel(chol_ref, *refs):
        shards = refs[: len(parts)]
        total_ref, mark_ref = refs[len(arrays) :]
        mark_ref[...] = jnp.zeros_like(mark_ref)
        lhs = jnp.concatenate(
            [chol_ref[:, :, pl.ds(column_start(shift, rows), rows)].reshape(size, rows) for shift in shifts], axis=1
        )
        for b in range(walkers):
            rhs = jnp.concatenate([x[:, b, :] for x in shards], axis=0)
            value = jnp.dot(lhs, rhs, preferred_element_type=jnp.float32)
            total_ref[b] = value if total is None else refs[len(arrays) - 1][b] + value

    return pl.pallas_call(
        kernel,
        name="accumulate",
        out_shape=[
            jax.ShapeDtypeStruct((walkers, size, orbitals), jnp.float32),
            jax.ShapeDtypeStruct((8, LANES), jnp.float32),
        ],
        in_specs=[vmem()] * (1 + len(arrays)),
        out_specs=[vmem()] * 2,
        compiler_params=params(ACCUMULATE_LIMIT),
        cost_estimate=pl.CostEstimate(
            flops=2 * len(parts) * size * rows * walkers * orbitals,
            bytes_accessed=2 * len(parts) * size * rows,
            transcendentals=0,
        ),
    )(cholesky_rot, *arrays)


def tie(*arrays):
    return lax.optimization_barrier(arrays)


def ring(own, cholesky_rot, onebody, packed, do_prepare):
    size = lax.axis_size("chol")
    rows = own.shape[0]
    order = ring_order(size)
    ahead = [(order[q], order[(q + 1) % size]) for q in range(size)]
    back = [(order[q], order[(q - 1) % size]) for q in range(size)]
    steps = size // 2
    right = left = own
    shifts, parts = [0], [own]
    total = mark = None
    for step in range(1, steps):
        next_right, next_left = lax.ppermute(right, "chol", ahead), lax.ppermute(left, "chol", back)
        if step == 1:
            right, onebody = tie(next_right, onebody)
            left, *packed = tie(next_left, *packed)
        else:
            if step == 2:
                far = exchange_far(packed)
            elif step == 3:
                near = exchange_near(packed, far)
            total, mark = accumulate(cholesky_rot, shifts, parts, total, mark)
            shifts, parts = [], []
            right, mark = tie(next_right, mark)
            left, mark = tie(next_left, mark)
        shifts += [-step, step]
        parts = parts + [right, left]
    last = [lax.ppermute(right[: rows // 2], "chol", ahead), lax.ppermute(left[rows // 2 :], "chol", back)]
    mark, *near = tie(mark, *near)
    packs = [packed[0], far] + near
    plan = do_prepare(packs)
    mark, plan = tie(mark, plan)
    total, _ = accumulate(cholesky_rot, shifts, parts, total, mark)
    return total, last, packs, plan


def table_height(vectors):
    return -(-(vectors + 2) // 16) * 16


def pack(own, one_body, fields, weights, sources, owners, cholesky_rot):
    rows, walkers, orbitals = own.shape
    walk_size = lax.axis_size("walk")
    width = orbitals // walk_size
    pair = LANES // width
    vectors, slots = fields.shape
    table_rows = table_height(vectors)
    panel_rows = walkers * (rows // pair)
    both = panel_rows + 3 * table_rows
    if walk_size == 4:
        heights = [both, both + panel_rows, both]
        spots = [(0, 0), (2, 0), (1, 0), (1, both)]
    else:
        heights = [both] * walk_size
        spots = [(d, 0) for d in range(walk_size)]

    def kernel(own_any, body_any, fields_any, weights_any, sources_any, owners_any, chol_any, *refs):
        onebody_ref = refs[0]
        packs = refs[1 : 1 + len(heights)]
        own_ref, body_ref, fields_ref, weights_ref, sources_ref, owners_ref, table_scr, sems = refs[1 + len(heights) :]
        places = [
            (own_any, own_ref),
            (body_any, body_ref),
            (fields_any, fields_ref),
            (weights_any, weights_ref),
            (sources_any, sources_ref),
            (owners_any, owners_ref),
        ]
        small = [pltpu.make_async_copy(a, b, sems.at[n]) for n, (a, b) in enumerate(places)]
        for copy in small:
            copy.start()
        for copy in small:
            copy.wait()
        green = [own_ref[:, b, :] for b in range(walkers)]
        walk = lax.axis_index("walk")
        lane = lax.broadcasted_iota(jnp.int32, (1, LANES), 1)
        body = body_ref[...].astype(jnp.float32)
        onebody_ref[...] = jnp.zeros_like(onebody_ref)
        for b in range(walkers):
            total = jnp.sum(green[b].astype(jnp.float32) * body, axis=0, keepdims=True)
            folded = total[:, :LANES]
            for start in range(LANES, orbitals, LANES):
                folded = folded + total[:, start : start + LANES]
            onebody_ref[b : b + 1, :] = folded
        r = lax.broadcasted_iota(jnp.int32, (rows // pair, rows), 0)
        m = lax.broadcasted_iota(jnp.int32, (rows // pair, rows), 1)
        k = lax.broadcasted_iota(jnp.int32, (orbitals, LANES), 0)
        c = lax.broadcasted_iota(jnp.int32, (orbitals, LANES), 1)
        thinned = []
        for b in range(walkers):
            values = green[b]
            thinned.append(
                [
                    jnp.dot(
                        (m == r * pair + h).astype(jnp.bfloat16), values, preferred_element_type=jnp.float32
                    ).astype(jnp.bfloat16)
                    for h in range(pair)
                ]
            )
        for d in range(walk_size):
            target = walk_partner(walk, d, walk_size, False)
            out, top = spots[d]
            panel = jnp.int32(0)
            for p in range(walk_size):
                panel = jnp.where(owners_ref[p] == target, p, panel)
            for b in range(walkers):
                total = jnp.zeros((rows // pair, LANES), jnp.float32)
                for h in range(pair):
                    take = (k == panel * width + c - h * width) & (c >= h * width) & (c < (h + 1) * width)
                    total += jnp.dot(
                        thinned[b][h], take.astype(jnp.bfloat16), preferred_element_type=jnp.float32
                    )
                packs[out][top + b * (rows // pair) : top + (b + 1) * (rows // pair), :] = total.astype(jnp.bfloat16)
        spread = jnp.zeros((vectors, LANES), jnp.float32)
        source = jnp.zeros((1, LANES), jnp.float32)
        corner = lax.broadcasted_iota(jnp.int32, (vectors, vectors), 0) == lax.broadcasted_iota(
            jnp.int32, (vectors, vectors), 1
        )
        for j in range(slots):
            mine = lane % slots == j
            upright = jnp.sum(jnp.where(corner, fields_ref[j : j + 1, :], 0.0), axis=1, keepdims=True)
            spread += jnp.where(mine, upright, 0.0)
            source += jnp.where(mine, sources_ref[j].astype(jnp.float32), 0.0)
        weight = weights_ref[0]
        for j in range(1, weights.shape[0]):
            weight = weight + weights_ref[j]
        table_scr[...] = jnp.zeros_like(table_scr)
        table_scr[:vectors, :] = spread
        table_scr[vectors : vectors + 1, :] = source
        table_scr[vectors + 1 : vectors + 2, :] = jnp.zeros((1, LANES), jnp.float32) + weight
        rest = table_scr[...]
        for n in range(3):
            piece = rest.astype(jnp.bfloat16)
            rest = rest - piece.astype(jnp.float32)
            at = panel_rows + n * table_rows
            for d in range(len(heights)):
                packs[d][at : at + table_rows, :] = piece

    return pl.pallas_call(
        kernel,
        name="pack",
        out_shape=[
            jax.ShapeDtypeStruct((8, LANES), jnp.float32),
        ]
        + [jax.ShapeDtypeStruct((height, LANES), jnp.bfloat16) for height in heights],
        in_specs=[pl.BlockSpec(memory_space=pl.ANY)] * 7,
        out_specs=[vmem()] * (len(heights) + 1),
        scratch_shapes=[
            pltpu.VMEM(own.shape, own.dtype),
            pltpu.VMEM(one_body.shape, one_body.dtype),
            pltpu.VMEM((slots, vectors), jnp.float32),
            pltpu.SMEM(weights.shape, weights.dtype),
            pltpu.SMEM(sources.shape, sources.dtype),
            pltpu.SMEM(owners.shape, owners.dtype),
            pltpu.VMEM((table_rows, LANES), jnp.float32),
            pltpu.SemaphoreType.DMA((6,)),
        ],
        compiler_params=params(PACK_LIMIT),
        cost_estimate=pl.CostEstimate(flops=10**8, bytes_accessed=10**6, transcendentals=0),
    )(own, one_body, fields.T, weights, sources, owners, cholesky_rot)


def walk_partner(walk, d, size, back):
    if size == 4:
        return lax.bitwise_xor(walk, d)
    return lax.rem(walk + (size - d if back else d), size)


def exchange_far(packed):
    size = lax.axis_size("walk")
    if size != 4:
        return lax.ppermute(packed[1], "walk", [(q, (q + 1) % size) for q in range(size)])
    return lax.ppermute(packed[1], "walk", [(q, q ^ 2) for q in range(size)])


def exchange_near(packed, far):
    size = lax.axis_size("walk")
    if size != 4:
        return [
            lax.ppermute(packed[d], "walk", [(q, (q + d) % size) for q in range(size)]) for d in range(2, size)
        ]
    keep, _, near = packed
    panel = far.shape[0] - keep.shape[0]
    return [lax.ppermute(jnp.concatenate([near, far[panel:]], axis=0), "walk", [(q, q ^ 1) for q in range(size)])]


def walk_places(panel, table, size):
    if size != 4:
        return [(d, 0, panel) for d in range(size)]
    return [(0, 0, panel), (2, 0, panel), (1, 0, panel), (2, panel + 2 * table, panel + table)]


def read_table(ref, at, vectors):
    height = table_height(vectors)
    parts = [ref[at + n * height : at + (n + 1) * height, :].astype(jnp.float32) for n in range(3)]
    return parts[0] + (parts[1] + parts[2])


def merge_tables(tables, walk, walk_size, slots, lane):
    total = jnp.zeros_like(tables[0])
    for d, table in enumerate(tables):
        group = walk_partner(walk, d, walk_size, True)
        total += jnp.where(lane // slots == group, table, 0.0)
    return total


def plan_rows(vectors, walkers, walk_size):
    shares = walkers * vectors
    picks = shares + walkers * walk_size
    single = picks + walkers
    return 0, shares, picks, single, single + 1, single + 2, -(-(single + 3) // 8) * 8


def prepare(packs, places, onebody, counts, vectors, slots, walkers):
    walk_size = len(places)
    at_drive, at_share, at_pick, at_single, at_live, at_mean, height = plan_rows(vectors, walkers, walk_size)

    def kernel(counts_ref, onebody_ref, *refs):
        pack_refs, plan_ref = refs[:-1], refs[-1]
        walk = lax.axis_index("walk")
        lane = lax.broadcasted_iota(jnp.int32, (1, LANES), 1)
        all_slots = slots * walk_size
        tables = [read_table(pack_refs[n], at, vectors) for n, _, at in places]
        table = merge_tables(tables, walk, walk_size, slots, lane)
        source = jnp.where(lane < all_slots, table[vectors : vectors + 1, :], -1.0)
        total_weight = tables[0][vectors + 1 : vectors + 2, :]
        for t in tables[1:]:
            total_weight = total_weight + t[vectors + 1 : vectors + 2, :]
        live_count = jnp.zeros((1, LANES), jnp.int32)
        for q in range(walk_size):
            live_count = jnp.where(lane // slots == q, counts_ref[q], live_count)
        live = (lane < all_slots) & (lane % slots < live_count)
        plan_ref[...] = jnp.zeros_like(plan_ref)
        single = jnp.zeros((1, LANES), jnp.float32)
        for b in range(walkers):
            pick = jnp.where(source == (walk * walkers + b).astype(jnp.float32), 1.0, 0.0)
            plan_ref[at_pick + b : at_pick + b + 1, :] = pick
            plan_ref[at_drive + b * vectors : at_drive + (b + 1) * vectors, :] = -root_step * pick * table[:vectors, :]
            single += pick * jnp.sum(onebody_ref[b : b + 1, :], axis=1, keepdims=True)
        plan_ref[at_single : at_single + 1, :] = single
        for d in range(walk_size):
            group = walk_partner(walk, d, walk_size, True)
            for b in range(walkers):
                row = at_share + d * walkers + b
                plan_ref[row : row + 1, :] = jnp.where(
                    source == (group * walkers + b).astype(jnp.float32), 1.0, 0.0
                )
        plan_ref[at_live : at_live + 1, :] = jnp.where(live, 1.0, 0.0)
        plan_ref[at_mean : at_mean + 1, :] = total_weight / (walkers * walk_size)

    return pl.pallas_call(
        kernel,
        name="prepare",
        out_shape=jax.ShapeDtypeStruct((height, LANES), jnp.float32),
        in_specs=[smem()] + [vmem()] * (1 + len(packs)),
        out_specs=vmem(),
        compiler_params=params(),
        cost_estimate=pl.CostEstimate(flops=10**8, bytes_accessed=10**6, transcendentals=0),
    )(counts, onebody, *packs)


def measure(cholesky_rot, total, last, plan, vectors, walk_size):
    _, walkers, orbitals = last[0].shape
    depth = sum(x.shape[0] for x in last)
    targets = walk_size * lax.axis_size("chol")
    whole = total is None
    quads = orbitals // LANES
    at_drive, _, at_pick, at_single, _, _, _ = plan_rows(vectors, walkers, walk_size)

    def fold(x):
        return jnp.sum(x.reshape(-1, 8, LANES), axis=0)

    def kernel(*refs):
        chol_ref, plan_ref = refs[:2]
        last_refs = refs[2 : 2 + len(last)]
        out_ref, tensor_scr = refs[-2:]
        rhs = [jnp.concatenate([x[:, b, :] for x in last_refs], axis=0) for b in range(walkers)]
        eye = lax.broadcasted_iota(jnp.int32, (LANES, LANES), 0) == lax.broadcasted_iota(
            jnp.int32, (LANES, LANES), 1
        )
        start = 0 if whole else column_start(lax.axis_size("chol") // 2, depth)

        def one_vector(g, slot, exchange, squares, drive):
            top = pl.multiple_of(g * orbitals, orbitals)
            lhs = chol_ref[g, :, pl.ds(start, depth)]
            for b in range(walkers):
                value = jnp.dot(lhs, rhs[b], preferred_element_type=jnp.float32)
                if not whole:
                    value = value + refs[2 + len(last)][b, pl.ds(top, orbitals), :]
                tensor_scr[slot, b] = value
            for b in range(walkers):
                diagonal = jnp.zeros((LANES, LANES), jnp.float32)
                for q in range(quads):
                    for p in range(q + 1):
                        one = tensor_scr[slot, b, q * LANES : (q + 1) * LANES, p * LANES : (p + 1) * LANES]
                        if p == q:
                            exchange[b] = exchange[b] + fold(one * one.T)
                            diagonal = diagonal + one
                        else:
                            two = tensor_scr[slot, b, p * LANES : (p + 1) * LANES, q * LANES : (q + 1) * LANES]
                            exchange[b] = exchange[b] + 2.0 * fold(two * one.T)
                trace = jnp.sum(fold(jnp.where(eye, diagonal, 0.0)), axis=0, keepdims=True)
                trace = jnp.sum(trace, axis=1, keepdims=True)
                squares[b] = squares[b] + trace * trace
                drive = drive + plan_ref[pl.ds(at_drive + b * vectors + g, 1), :] * trace
            return exchange, squares, drive

        together = 2 if vectors % 2 == 0 else 1

        def step(n, carry):
            exchange, squares, drive = list(carry[0]), list(carry[1]), carry[2]
            for slot in range(together):
                exchange, squares, drive = one_vector(n * together + slot, slot, exchange, squares, drive)
            return tuple(exchange), tuple(squares), drive

        exchange, squares, drive = lax.fori_loop(
            0,
            vectors // together,
            step,
            (
                tuple(jnp.zeros((8, LANES), jnp.float32) for _ in range(walkers)),
                tuple(jnp.zeros((1, 1), jnp.float32) for _ in range(walkers)),
                jnp.zeros((1, LANES), jnp.float32),
            ),
        )
        raw = plan_ref[at_single : at_single + 1, :]
        square = jnp.zeros((1, LANES), jnp.float32)
        for b in range(walkers):
            swapped = jnp.sum(jnp.sum(exchange[b], axis=0, keepdims=True), axis=1, keepdims=True)
            pick = plan_ref[at_pick + b : at_pick + b + 1, :]
            raw += pick * (0.5 * squares[b] - 0.5 * swapped)
            square += pick * squares[b]
        power = drive - 0.5 * time_step * square - time_step * raw
        out_ref[...] = jnp.broadcast_to(raw + pltpu.roll(power, LANES // 2, 1), (targets, LANES))

    arrays = list(last) + ([] if whole else [total])
    return pl.pallas_call(
        kernel,
        name="measure",
        out_shape=jax.ShapeDtypeStruct((targets, LANES), jnp.float32),
        in_specs=[vmem()] * (2 + len(arrays)),
        out_specs=vmem(),
        scratch_shapes=[
            pltpu.VMEM((2, walkers, orbitals, orbitals), jnp.float32),
        ],
        compiler_params=params(),
        cost_estimate=pl.CostEstimate(
            flops=2 * vectors * orbitals * depth * walkers * orbitals,
            bytes_accessed=2 * vectors * orbitals * depth,
            transcendentals=0,
        ),
    )(cholesky_rot, plan, *arrays)


def finish(stats, plan, packs, places, vectors, slots, walkers):
    walk_size = len(places)
    rows = (packs[0].shape[0] - 3 * table_height(vectors)) // walkers
    _, at_share, at_pick, _, at_live, at_mean, _ = plan_rows(vectors, walkers, walk_size)

    def kernel(stats_ref, plan_ref, *refs):
        pack_refs = refs[: len(packs)]
        energies_ref, weights_ref, density_ref = refs[len(packs) :]
        walk = lax.axis_index("walk")
        total = jnp.sum(stats_ref[...], axis=0, keepdims=True)
        power = pltpu.roll(total, LANES // 2, 1)
        live = plan_ref[at_live : at_live + 1, :] > 0.0
        energies = jnp.where(live, total, 0.0)
        new_weights = jnp.where(
            live, plan_ref[at_mean : at_mean + 1, :] * jnp.exp(jnp.where(live, power, 0.0)), 0.0
        )
        norm = jnp.sum(new_weights, axis=1, keepdims=True)
        shares = jnp.sum(plan_ref[at_share:at_pick, :] * new_weights, axis=1, keepdims=True) / norm
        density = jnp.zeros((rows, LANES), jnp.float32)
        for d, (n, top, _) in enumerate(places):
            for b in range(walkers):
                share = shares[d * walkers + b : d * walkers + b + 1, :]
                density += share * pack_refs[n][top + b * rows : top + (b + 1) * rows, :].astype(jnp.float32)
        density_ref[...] = density
        first = lax.rem(LANES - walk * slots, LANES)
        energies_ref[...] = pltpu.roll(jnp.broadcast_to(energies, (8, LANES)), first, 1)[:1, :slots]
        weights_ref[...] = pltpu.roll(jnp.broadcast_to(new_weights, (8, LANES)), first, 1)[:1, :slots]

    return pl.pallas_call(
        kernel,
        name="finish",
        out_shape=[
            jax.ShapeDtypeStruct((1, slots), jnp.float32),
            jax.ShapeDtypeStruct((1, slots), jnp.float32),
            jax.ShapeDtypeStruct((rows, LANES), jnp.float32),
        ],
        in_specs=[vmem()] * (2 + len(packs)),
        out_specs=[vmem()] * 3,
        compiler_params=params(),
        cost_estimate=pl.CostEstimate(flops=10**6, bytes_accessed=6 * 10**5, transcendentals=128),
    )(stats, plan, *packs)


def per_device(green_rows, cholesky_rot, one_body, fields, weights, sources, counts, owners):
    chol_size = lax.axis_size("chol")
    walk_size = lax.axis_size("walk")
    vectors, slots = fields.shape
    walkers = green_rows.shape[1]
    onebody, *packed = pack(green_rows, one_body, fields, weights, sources, owners, cholesky_rot)
    table = 3 * table_height(vectors)
    places = walk_places(packed[0].shape[0] - table, table, walk_size)

    def do_prepare(packs):
        return prepare(packs, places, onebody, counts, vectors, slots, walkers)

    if chol_size > RING_LIMIT or chol_size % 2 or chol_size < 8:
        far = exchange_far(packed)
        packs = [packed[0], far] + exchange_near(packed, far)
        plan = do_prepare(packs)
        total, last = None, [lax.all_gather(green_rows, "chol", axis=0, tiled=True)]
    else:
        total, last, packs, plan = ring(green_rows, cholesky_rot, onebody, packed, do_prepare)
    stats = measure(cholesky_rot, total, last, plan, vectors, walk_size)
    stats = lax.all_to_all(stats, ("chol", "walk"), split_axis=0, concat_axis=0, tiled=True)
    energies, new_weights, density = finish(stats, plan, packs, places, vectors, slots, walkers)
    return energies.reshape(slots), new_weights.reshape(slots), density.reshape(1, density.size)


def solution(mesh):
    return jax.shard_map(
        per_device,
        mesh=mesh,
        in_specs=(
            P("chol", "walk", None),
            P("chol", None, None),
            P("chol", None),
            P("chol", "walk"),
            P("walk"),
            P("walk"),
            P(),
            P(),
        ),
        out_specs=(P("walk"), P("walk"), P("walk", "chol")),
        check_vma=False,
    )
```

```python
import jax
import jax.numpy as jnp
from jax import lax
from jax.experimental import pallas as pl
from jax.experimental.pallas import tpu as pltpu
from jax.sharding import PartitionSpec as P

time_step = 0.02
root_step = 0.02**0.5
LANES = 128
VMEM_LIMIT = 16 * 1024 * 1024
PACK_LIMIT = 54 * 1024 * 1024
ACCUMULATE_LIMIT = 24 * 1024 * 1024
RING_LIMIT = 16


def params(limit=VMEM_LIMIT):
    return pltpu.CompilerParams(vmem_limit_bytes=limit)


def vmem():
    return pl.BlockSpec(memory_space=pltpu.VMEM)


def smem():
    return pl.BlockSpec(memory_space=pltpu.SMEM)


def ring_order(size):
    return [2 * q if q < size // 2 else 2 * (size - 1 - q) + 1 for q in range(size)]


def ring_place(index, size):
    return jnp.where(index % 2 == 0, index // 2, size - 1 - index // 2)


def ring_owner(place, size):
    return jnp.where(place < size // 2, 2 * place, 2 * (size - 1 - place) + 1)


def column_start(shift, rows):
    size = lax.axis_size("chol")
    place = ring_place(lax.axis_index("chol"), size)
    owner = ring_owner(lax.rem(place + shift + size, size), size)
    return pl.multiple_of(owner * rows, rows)


def accumulate(cholesky_rot, shifts, parts, total, mark):
    vectors, orbitals, _ = cholesky_rot.shape
    rows, walkers, _ = parts[0].shape
    size = vectors * orbitals
    arrays = list(parts) + ([] if mark is None else [mark]) + ([] if total is None else [total])

    def kernel(chol_ref, *refs):
        shards = refs[: len(parts)]
        total_ref, mark_ref = refs[len(arrays) :]
        mark_ref[...] = jnp.zeros_like(mark_ref)
        lhs = jnp.concatenate(
            [chol_ref[:, :, pl.ds(column_start(shift, rows), rows)].reshape(size, rows) for shift in shifts], axis=1
        )
        for b in range(walkers):
            rhs = jnp.concatenate([x[:, b, :] for x in shards], axis=0)
            value = jnp.dot(lhs, rhs, preferred_element_type=jnp.float32)
            total_ref[b] = value if total is None else refs[len(arrays) - 1][b] + value

    return pl.pallas_call(
        kernel,
        name="accumulate",
        out_shape=[
            jax.ShapeDtypeStruct((walkers, size, orbitals), jnp.float32),
            jax.ShapeDtypeStruct((8, LANES), jnp.float32),
        ],
        in_specs=[vmem()] * (1 + len(arrays)),
        out_specs=[vmem()] * 2,
        compiler_params=params(ACCUMULATE_LIMIT),
        cost_estimate=pl.CostEstimate(
            flops=2 * len(parts) * size * rows * walkers * orbitals,
            bytes_accessed=2 * len(parts) * size * rows,
            transcendentals=0,
        ),
    )(cholesky_rot, *arrays)


def tie(*arrays):
    return lax.optimization_barrier(arrays)


def ring(own, cholesky_rot, onebody, packed, do_prepare):
    size = lax.axis_size("chol")
    rows = own.shape[0]
    order = ring_order(size)
    ahead = [(order[q], order[(q + 1) % size]) for q in range(size)]
    back = [(order[q], order[(q - 1) % size]) for q in range(size)]
    steps = size // 2
    right = left = own
    shifts, parts = [0], [own]
    total = mark = None
    for step in range(1, steps):
        next_right, next_left = lax.ppermute(right, "chol", ahead), lax.ppermute(left, "chol", back)
        if step == 1:
            right, onebody = tie(next_right, onebody)
            left, *packed = tie(next_left, *packed)
        else:
            if step == 2:
                far = exchange_far(packed)
            elif step == 3:
                near = exchange_near(packed, far)
            total, mark = accumulate(cholesky_rot, shifts, parts, total, mark)
            shifts, parts = [], []
            right, mark = tie(next_right, mark)
            left, mark = tie(next_left, mark)
        shifts += [-step, step]
        parts = parts + [right, left]
    last = [lax.ppermute(right[: rows // 2], "chol", ahead), lax.ppermute(left[rows // 2 :], "chol", back)]
    mark, *near = tie(mark, *near)
    packs = [packed[0], far] + near
    plan = do_prepare(packs)
    mark, plan = tie(mark, plan)
    total, _ = accumulate(cholesky_rot, shifts, parts, total, mark)
    return total, last, packs, plan


def table_height(vectors):
    return -(-(vectors + 2) // 16) * 16


def pack(own, one_body, fields, weights, sources, owners, cholesky_rot):
    rows, walkers, orbitals = own.shape
    walk_size = lax.axis_size("walk")
    width = orbitals // walk_size
    pair = LANES // width
    vectors, slots = fields.shape
    table_rows = table_height(vectors)
    panel_rows = walkers * (rows // pair)
    both = panel_rows + 3 * table_rows
    if walk_size == 4:
        heights = [both, both + panel_rows, both]
        spots = [(0, 0), (2, 0), (1, 0), (1, both)]
    else:
        heights = [both] * walk_size
        spots = [(d, 0) for d in range(walk_size)]

    def kernel(own_any, body_any, fields_any, weights_any, sources_any, owners_any, chol_any, *refs):
        onebody_ref = refs[0]
        packs = refs[1 : 1 + len(heights)]
        own_ref, body_ref, fields_ref, weights_ref, sources_ref, owners_ref, table_scr, sems = refs[1 + len(heights) :]
        places = [
            (own_any, own_ref),
            (body_any, body_ref),
            (fields_any, fields_ref),
            (weights_any, weights_ref),
            (sources_any, sources_ref),
            (owners_any, owners_ref),
        ]
        small = [pltpu.make_async_copy(a, b, sems.at[n]) for n, (a, b) in enumerate(places)]
        for copy in small:
            copy.start()
        for copy in small:
            copy.wait()
        green = [own_ref[:, b, :] for b in range(walkers)]
        walk = lax.axis_index("walk")
        lane = lax.broadcasted_iota(jnp.int32, (1, LANES), 1)
        body = body_ref[...].astype(jnp.float32)
        onebody_ref[...] = jnp.zeros_like(onebody_ref)
        for b in range(walkers):
            total = jnp.sum(green[b].astype(jnp.float32) * body, axis=0, keepdims=True)
            folded = total[:, :LANES]
            for start in range(LANES, orbitals, LANES):
                folded = folded + total[:, start : start + LANES]
            onebody_ref[b : b + 1, :] = folded
        r = lax.broadcasted_iota(jnp.int32, (rows // pair, rows), 0)
        m = lax.broadcasted_iota(jnp.int32, (rows // pair, rows), 1)
        k = lax.broadcasted_iota(jnp.int32, (orbitals, LANES), 0)
        c = lax.broadcasted_iota(jnp.int32, (orbitals, LANES), 1)
        thinned = []
        for b in range(walkers):
            values = green[b]
            thinned.append(
                [
                    jnp.dot(
                        (m == r * pair + h).astype(jnp.bfloat16), values, preferred_element_type=jnp.float32
                    ).astype(jnp.bfloat16)
                    for h in range(pair)
                ]
            )
        for d in range(walk_size):
            target = walk_partner(walk, d, walk_size, False)
            out, top = spots[d]
            panel = jnp.int32(0)
            for p in range(walk_size):
                panel = jnp.where(owners_ref[p] == target, p, panel)
            for b in range(walkers):
                total = jnp.zeros((rows // pair, LANES), jnp.float32)
                for h in range(pair):
                    take = (k == panel * width + c - h * width) & (c >= h * width) & (c < (h + 1) * width)
                    total += jnp.dot(
                        thinned[b][h], take.astype(jnp.bfloat16), preferred_element_type=jnp.float32
                    )
                packs[out][top + b * (rows // pair) : top + (b + 1) * (rows // pair), :] = total.astype(jnp.bfloat16)
        spread = jnp.zeros((vectors, LANES), jnp.float32)
        source = jnp.zeros((1, LANES), jnp.float32)
        corner = lax.broadcasted_iota(jnp.int32, (vectors, vectors), 0) == lax.broadcasted_iota(
            jnp.int32, (vectors, vectors), 1
        )
        for j in range(slots):
            mine = lane % slots == j
            upright = jnp.sum(jnp.where(corner, fields_ref[j : j + 1, :], 0.0), axis=1, keepdims=True)
            spread += jnp.where(mine, upright, 0.0)
            source += jnp.where(mine, sources_ref[j].astype(jnp.float32), 0.0)
        weight = weights_ref[0]
        for j in range(1, weights.shape[0]):
            weight = weight + weights_ref[j]
        table_scr[...] = jnp.zeros_like(table_scr)
        table_scr[:vectors, :] = spread
        table_scr[vectors : vectors + 1, :] = source
        table_scr[vectors + 1 : vectors + 2, :] = jnp.zeros((1, LANES), jnp.float32) + weight
        rest = table_scr[...]
        for n in range(3):
            piece = rest.astype(jnp.bfloat16)
            rest = rest - piece.astype(jnp.float32)
            at = panel_rows + n * table_rows
            for d in range(len(heights)):
                packs[d][at : at + table_rows, :] = piece

    return pl.pallas_call(
        kernel,
        name="pack",
        out_shape=[
            jax.ShapeDtypeStruct((8, LANES), jnp.float32),
        ]
        + [jax.ShapeDtypeStruct((height, LANES), jnp.bfloat16) for height in heights],
        in_specs=[pl.BlockSpec(memory_space=pl.ANY)] * 7,
        out_specs=[vmem()] * (len(heights) + 1),
        scratch_shapes=[
            pltpu.VMEM(own.shape, own.dtype),
            pltpu.VMEM(one_body.shape, one_body.dtype),
            pltpu.VMEM((slots, vectors), jnp.float32),
            pltpu.SMEM(weights.shape, weights.dtype),
            pltpu.SMEM(sources.shape, sources.dtype),
            pltpu.SMEM(owners.shape, owners.dtype),
            pltpu.VMEM((table_rows, LANES), jnp.float32),
            pltpu.SemaphoreType.DMA((6,)),
        ],
        compiler_params=params(PACK_LIMIT),
        cost_estimate=pl.CostEstimate(flops=10**8, bytes_accessed=10**6, transcendentals=0),
    )(own, one_body, fields.T, weights, sources, owners, cholesky_rot)


def walk_partner(walk, d, size, back):
    if size == 4:
        return lax.bitwise_xor(walk, d)
    return lax.rem(walk + (size - d if back else d), size)


def exchange_far(packed):
    size = lax.axis_size("walk")
    if size != 4:
        return lax.ppermute(packed[1], "walk", [(q, (q + 1) % size) for q in range(size)])
    return lax.ppermute(packed[1], "walk", [(q, q ^ 2) for q in range(size)])


def exchange_near(packed, far):
    size = lax.axis_size("walk")
    if size != 4:
        return [
            lax.ppermute(packed[d], "walk", [(q, (q + d) % size) for q in range(size)]) for d in range(2, size)
        ]
    keep, _, near = packed
    panel = far.shape[0] - keep.shape[0]
    return [lax.ppermute(jnp.concatenate([near, far[panel:]], axis=0), "walk", [(q, q ^ 1) for q in range(size)])]


def walk_places(panel, table, size):
    if size != 4:
        return [(d, 0, panel) for d in range(size)]
    return [(0, 0, panel), (2, 0, panel), (1, 0, panel), (2, panel + 2 * table, panel + table)]


def read_table(ref, at, vectors):
    height = table_height(vectors)
    parts = [ref[at + n * height : at + (n + 1) * height, :].astype(jnp.float32) for n in range(3)]
    return parts[0] + (parts[1] + parts[2])


def merge_tables(tables, walk, walk_size, slots, lane):
    total = jnp.zeros_like(tables[0])
    for d, table in enumerate(tables):
        group = walk_partner(walk, d, walk_size, True)
        total += jnp.where(lane // slots == group, table, 0.0)
    return total


def plan_rows(vectors, walkers, walk_size):
    shares = walkers * vectors
    picks = shares + walkers * walk_size
    single = picks + walkers
    return 0, shares, picks, single, single + 1, single + 2, -(-(single + 3) // 8) * 8


def prepare(packs, places, onebody, counts, vectors, slots, walkers):
    walk_size = len(places)
    at_drive, at_share, at_pick, at_single, at_live, at_mean, height = plan_rows(vectors, walkers, walk_size)

    def kernel(counts_ref, onebody_ref, *refs):
        pack_refs, plan_ref = refs[:-1], refs[-1]
        walk = lax.axis_index("walk")
        lane = lax.broadcasted_iota(jnp.int32, (1, LANES), 1)
        all_slots = slots * walk_size
        tables = [read_table(pack_refs[n], at, vectors) for n, _, at in places]
        table = merge_tables(tables, walk, walk_size, slots, lane)
        source = jnp.where(lane < all_slots, table[vectors : vectors + 1, :], -1.0)
        total_weight = tables[0][vectors + 1 : vectors + 2, :]
        for t in tables[1:]:
            total_weight = total_weight + t[vectors + 1 : vectors + 2, :]
        live_count = jnp.zeros((1, LANES), jnp.int32)
        for q in range(walk_size):
            live_count = jnp.where(lane // slots == q, counts_ref[q], live_count)
        live = (lane < all_slots) & (lane % slots < live_count)
        plan_ref[...] = jnp.zeros_like(plan_ref)
        single = jnp.zeros((1, LANES), jnp.float32)
        for b in range(walkers):
            pick = jnp.where(source == (walk * walkers + b).astype(jnp.float32), 1.0, 0.0)
            plan_ref[at_pick + b : at_pick + b + 1, :] = pick
            plan_ref[at_drive + b * vectors : at_drive + (b + 1) * vectors, :] = -root_step * pick * table[:vectors, :]
            single += pick * jnp.sum(onebody_ref[b : b + 1, :], axis=1, keepdims=True)
        plan_ref[at_single : at_single + 1, :] = single
        for d in range(walk_size):
            group = walk_partner(walk, d, walk_size, True)
            for b in range(walkers):
                row = at_share + d * walkers + b
                plan_ref[row : row + 1, :] = jnp.where(
                    source == (group * walkers + b).astype(jnp.float32), 1.0, 0.0
                )
        plan_ref[at_live : at_live + 1, :] = jnp.where(live, 1.0, 0.0)
        plan_ref[at_mean : at_mean + 1, :] = total_weight / (walkers * walk_size)

    return pl.pallas_call(
        kernel,
        name="prepare",
        out_shape=jax.ShapeDtypeStruct((height, LANES), jnp.float32),
        in_specs=[smem()] + [vmem()] * (1 + len(packs)),
        out_specs=vmem(),
        compiler_params=params(),
        cost_estimate=pl.CostEstimate(flops=10**8, bytes_accessed=10**6, transcendentals=0),
    )(counts, onebody, *packs)


def measure(cholesky_rot, total, last, plan, vectors, walk_size):
    _, walkers, orbitals = last[0].shape
    depth = sum(x.shape[0] for x in last)
    targets = walk_size * lax.axis_size("chol")
    whole = total is None
    quads = orbitals // LANES
    at_drive, _, at_pick, at_single, _, _, _ = plan_rows(vectors, walkers, walk_size)

    def fold(x):
        return jnp.sum(x.reshape(-1, 8, LANES), axis=0)

    def kernel(*refs):
        chol_ref, plan_ref = refs[:2]
        last_refs = refs[2 : 2 + len(last)]
        out_ref, rhs_scr, tensor_scr = refs[-3:]
        at = 0
        for x in last_refs:
            for b in range(walkers):
                rhs_scr[at : at + x.shape[0], b * orbitals : (b + 1) * orbitals] = x[:, b, :]
            at += x.shape[0]
        eye = lax.broadcasted_iota(jnp.int32, (LANES, LANES), 0) == lax.broadcasted_iota(
            jnp.int32, (LANES, LANES), 1
        )
        exchange = [jnp.zeros((8, LANES), jnp.float32) for _ in range(walkers)]
        squares = [jnp.zeros((1, 1), jnp.float32) for _ in range(walkers)]
        drive = jnp.zeros((1, LANES), jnp.float32)
        start = 0 if whole else column_start(lax.axis_size("chol") // 2, depth)
        for g in range(vectors):
            value = jnp.dot(
                chol_ref[g, :, pl.ds(start, depth)], rhs_scr[...], preferred_element_type=jnp.float32
            )
            for b in range(walkers):
                part = value[:, b * orbitals : (b + 1) * orbitals]
                if not whole:
                    part = part + refs[2 + len(last)][b, g * orbitals : (g + 1) * orbitals, :]
                tensor_scr[g % 2, b] = part
            for b in range(walkers):
                diagonal = jnp.zeros((LANES, LANES), jnp.float32)
                for q in range(quads):
                    for p in range(q + 1):
                        one = tensor_scr[
                            g % 2, b, q * LANES : (q + 1) * LANES, p * LANES : (p + 1) * LANES
                        ]
                        if p == q:
                            exchange[b] = exchange[b] + fold(one * one.T)
                            diagonal = diagonal + one
                        else:
                            two = tensor_scr[
                                g % 2, b, p * LANES : (p + 1) * LANES, q * LANES : (q + 1) * LANES
                            ]
                            exchange[b] = exchange[b] + 2.0 * fold(two * one.T)
                trace = jnp.sum(fold(jnp.where(eye, diagonal, 0.0)), axis=0, keepdims=True)
                trace = jnp.sum(trace, axis=1, keepdims=True)
                squares[b] = squares[b] + trace * trace
                row = at_drive + b * vectors + g
                drive = drive + plan_ref[row : row + 1, :] * trace
        raw = plan_ref[at_single : at_single + 1, :]
        square = jnp.zeros((1, LANES), jnp.float32)
        for b in range(walkers):
            swapped = jnp.sum(jnp.sum(exchange[b], axis=0, keepdims=True), axis=1, keepdims=True)
            pick = plan_ref[at_pick + b : at_pick + b + 1, :]
            raw += pick * (0.5 * squares[b] - 0.5 * swapped)
            square += pick * squares[b]
        power = drive - 0.5 * time_step * square - time_step * raw
        out_ref[...] = jnp.broadcast_to(raw + pltpu.roll(power, LANES // 2, 1), (targets, LANES))

    arrays = list(last) + ([] if whole else [total])
    return pl.pallas_call(
        kernel,
        name="measure",
        out_shape=jax.ShapeDtypeStruct((targets, LANES), jnp.float32),
        in_specs=[vmem()] * (2 + len(arrays)),
        out_specs=vmem(),
        scratch_shapes=[
            pltpu.VMEM((depth, walkers * orbitals), jnp.bfloat16),
            pltpu.VMEM((2, walkers, orbitals, orbitals), jnp.float32),
        ],
        compiler_params=params(),
        cost_estimate=pl.CostEstimate(
            flops=2 * vectors * orbitals * depth * walkers * orbitals,
            bytes_accessed=2 * vectors * orbitals * depth,
            transcendentals=0,
        ),
    )(cholesky_rot, plan, *arrays)


def finish(stats, plan, packs, places, vectors, slots, walkers):
    walk_size = len(places)
    rows = (packs[0].shape[0] - 3 * table_height(vectors)) // walkers
    _, at_share, at_pick, _, at_live, at_mean, _ = plan_rows(vectors, walkers, walk_size)

    def kernel(stats_ref, plan_ref, *refs):
        pack_refs = refs[: len(packs)]
        energies_ref, weights_ref, density_ref = refs[len(packs) :]
        walk = lax.axis_index("walk")
        total = jnp.sum(stats_ref[...], axis=0, keepdims=True)
        power = pltpu.roll(total, LANES // 2, 1)
        live = plan_ref[at_live : at_live + 1, :] > 0.0
        energies = jnp.where(live, total, 0.0)
        new_weights = jnp.where(
            live, plan_ref[at_mean : at_mean + 1, :] * jnp.exp(jnp.where(live, power, 0.0)), 0.0
        )
        norm = jnp.sum(new_weights, axis=1, keepdims=True)
        shares = jnp.sum(plan_ref[at_share:at_pick, :] * new_weights, axis=1, keepdims=True) / norm
        density = jnp.zeros((rows, LANES), jnp.float32)
        for d, (n, top, _) in enumerate(places):
            for b in range(walkers):
                share = shares[d * walkers + b : d * walkers + b + 1, :]
                density += share * pack_refs[n][top + b * rows : top + (b + 1) * rows, :].astype(jnp.float32)
        density_ref[...] = density
        first = lax.rem(LANES - walk * slots, LANES)
        energies_ref[...] = pltpu.roll(jnp.broadcast_to(energies, (8, LANES)), first, 1)[:1, :slots]
        weights_ref[...] = pltpu.roll(jnp.broadcast_to(new_weights, (8, LANES)), first, 1)[:1, :slots]

    return pl.pallas_call(
        kernel,
        name="finish",
        out_shape=[
            jax.ShapeDtypeStruct((1, slots), jnp.float32),
            jax.ShapeDtypeStruct((1, slots), jnp.float32),
            jax.ShapeDtypeStruct((rows, LANES), jnp.float32),
        ],
        in_specs=[vmem()] * (2 + len(packs)),
        out_specs=[vmem()] * 3,
        compiler_params=params(),
        cost_estimate=pl.CostEstimate(flops=10**6, bytes_accessed=6 * 10**5, transcendentals=128),
    )(stats, plan, *packs)


def per_device(green_rows, cholesky_rot, one_body, fields, weights, sources, counts, owners):
    chol_size = lax.axis_size("chol")
    walk_size = lax.axis_size("walk")
    vectors, slots = fields.shape
    walkers = green_rows.shape[1]
    onebody, *packed = pack(green_rows, one_body, fields, weights, sources, owners, cholesky_rot)
    table = 3 * table_height(vectors)
    places = walk_places(packed[0].shape[0] - table, table, walk_size)

    def do_prepare(packs):
        return prepare(packs, places, onebody, counts, vectors, slots, walkers)

    if chol_size > RING_LIMIT or chol_size % 2 or chol_size < 8:
        far = exchange_far(packed)
        packs = [packed[0], far] + exchange_near(packed, far)
        plan = do_prepare(packs)
        total, last = None, [lax.all_gather(green_rows, "chol", axis=0, tiled=True)]
    else:
        total, last, packs, plan = ring(green_rows, cholesky_rot, onebody, packed, do_prepare)
    stats = measure(cholesky_rot, total, last, plan, vectors, walk_size)
    stats = lax.all_to_all(stats, ("chol", "walk"), split_axis=0, concat_axis=0, tiled=True)
    energies, new_weights, density = finish(stats, plan, packs, places, vectors, slots, walkers)
    return energies.reshape(slots), new_weights.reshape(slots), density.reshape(1, density.size)


def solution(mesh):
    return jax.shard_map(
        per_device,
        mesh=mesh,
        in_specs=(
            P("chol", "walk", None),
            P("chol", None, None),
            P("chol", None),
            P("chol", "walk"),
            P("walk"),
            P("walk"),
            P(),
            P(),
        ),
        out_specs=(P("walk"), P("walk"), P("walk", "chol")),
        check_vma=False,
    )
```

```python
import jax
import jax.numpy as jnp
from jax import lax
from jax.experimental import pallas as pl
from jax.experimental.pallas import tpu as pltpu
from jax.sharding import PartitionSpec as P

time_step = 0.02
root_step = 0.02**0.5
LANES = 128
VMEM_LIMIT = 16 * 1024 * 1024
PACK_LIMIT = 54 * 1024 * 1024
ACCUMULATE_LIMIT = 24 * 1024 * 1024
RING_LIMIT = 16


def params(limit=VMEM_LIMIT):
    return pltpu.CompilerParams(vmem_limit_bytes=limit)


def vmem():
    return pl.BlockSpec(memory_space=pltpu.VMEM)


def smem():
    return pl.BlockSpec(memory_space=pltpu.SMEM)


def ring_order(size):
    return [2 * q if q < size // 2 else 2 * (size - 1 - q) + 1 for q in range(size)]


def ring_place(index, size):
    return jnp.where(index % 2 == 0, index // 2, size - 1 - index // 2)


def ring_owner(place, size):
    return jnp.where(place < size // 2, 2 * place, 2 * (size - 1 - place) + 1)


def split_walkers(green_rows):
    rows, walkers, orbitals = green_rows.shape
    steps = 4 if rows % 64 == 0 else 1

    def kernel(green_ref, out_ref):
        for b in range(walkers):
            out_ref[:, b * orbitals : (b + 1) * orbitals] = green_ref[:, b, :]

    return pl.pallas_call(
        kernel,
        name="split_walkers",
        grid=(steps,),
        out_shape=jax.ShapeDtypeStruct((rows, walkers * orbitals), green_rows.dtype),
        in_specs=[pl.BlockSpec((rows // steps, walkers, orbitals), lambda n: (n, 0, 0))],
        out_specs=pl.BlockSpec((rows // steps, walkers * orbitals), lambda n: (n, 0)),
        compiler_params=params(),
        cost_estimate=pl.CostEstimate(flops=0, bytes_accessed=4 * rows * walkers * orbitals, transcendentals=0),
    )(green_rows)


def column_start(shift, rows):
    size = lax.axis_size("chol")
    place = ring_place(lax.axis_index("chol"), size)
    owner = ring_owner(lax.rem(place + shift + size, size), size)
    return pl.multiple_of(owner * rows, rows)


def accumulate(cholesky_rot, shifts, parts, total, mark):
    vectors, orbitals, _ = cholesky_rot.shape
    rows, columns = parts[0].shape
    walkers = columns // orbitals
    size = vectors * orbitals
    arrays = list(parts) + ([] if mark is None else [mark]) + ([] if total is None else [total])

    def kernel(chol_ref, *refs):
        shards = refs[: len(parts)]
        total_ref, mark_ref = refs[len(arrays) :]
        mark_ref[...] = jnp.zeros_like(mark_ref)
        lhs = jnp.concatenate(
            [chol_ref[:, :, pl.ds(column_start(shift, rows), rows)].reshape(size, rows) for shift in shifts], axis=1
        )
        for b in range(walkers):
            rhs = jnp.concatenate([x[:, b * orbitals : (b + 1) * orbitals] for x in shards], axis=0)
            value = jnp.dot(lhs, rhs, preferred_element_type=jnp.float32)
            total_ref[b] = value if total is None else refs[len(arrays) - 1][b] + value

    return pl.pallas_call(
        kernel,
        name="accumulate",
        out_shape=[
            jax.ShapeDtypeStruct((walkers, size, orbitals), jnp.float32),
            jax.ShapeDtypeStruct((8, LANES), jnp.float32),
        ],
        in_specs=[vmem()] * (1 + len(arrays)),
        out_specs=[vmem()] * 2,
        compiler_params=params(ACCUMULATE_LIMIT),
        cost_estimate=pl.CostEstimate(
            flops=2 * len(parts) * size * rows * walkers * orbitals,
            bytes_accessed=2 * len(parts) * size * rows,
            transcendentals=0,
        ),
    )(cholesky_rot, *arrays)


def tie(*arrays):
    return lax.optimization_barrier(arrays)


def ring(own, cholesky_rot, onebody, packed, do_prepare):
    size = lax.axis_size("chol")
    rows = own.shape[0]
    order = ring_order(size)
    ahead = [(order[q], order[(q + 1) % size]) for q in range(size)]
    back = [(order[q], order[(q - 1) % size]) for q in range(size)]
    steps = size // 2
    right = left = own
    shifts, parts = [0], [own]
    total = mark = None
    for step in range(1, steps):
        next_right, next_left = lax.ppermute(right, "chol", ahead), lax.ppermute(left, "chol", back)
        if step == 1:
            right, onebody = tie(next_right, onebody)
            left, *packed = tie(next_left, *packed)
        else:
            if step == 2:
                far = exchange_far(packed)
            elif step == 3:
                near = exchange_near(packed, far)
            total, mark = accumulate(cholesky_rot, shifts, parts, total, mark)
            shifts, parts = [], []
            right, mark = tie(next_right, mark)
            left, mark = tie(next_left, mark)
        shifts += [-step, step]
        parts = parts + [right, left]
    last = [lax.ppermute(right[: rows // 2], "chol", ahead), lax.ppermute(left[rows // 2 :], "chol", back)]
    mark, *near = tie(mark, *near)
    packs = [packed[0], far] + near
    plan = do_prepare(packs)
    mark, plan = tie(mark, plan)
    total, _ = accumulate(cholesky_rot, shifts, parts, total, mark)
    return total, last, packs, plan


def table_height(vectors):
    return -(-(vectors + 2) // 16) * 16


def pack(own, one_body, fields, weights, sources, owners, cholesky_rot):
    rows, orbitals = one_body.shape
    walkers = own.shape[1] // orbitals
    walk_size = lax.axis_size("walk")
    width = orbitals // walk_size
    pair = LANES // width
    vectors, slots = fields.shape
    table_rows = table_height(vectors)
    panel_rows = walkers * (rows // pair)
    both = panel_rows + 3 * table_rows
    if walk_size == 4:
        heights = [both, both + panel_rows, both]
        spots = [(0, 0), (2, 0), (1, 0), (1, both)]
    else:
        heights = [both] * walk_size
        spots = [(d, 0) for d in range(walk_size)]

    def kernel(own_any, body_any, fields_any, weights_any, sources_any, owners_any, chol_any, *refs):
        onebody_ref = refs[0]
        packs = refs[1 : 1 + len(heights)]
        own_ref, body_ref, fields_ref, weights_ref, sources_ref, owners_ref, table_scr, sems = refs[1 + len(heights) :]
        places = [
            (own_any, own_ref),
            (body_any, body_ref),
            (fields_any, fields_ref),
            (weights_any, weights_ref),
            (sources_any, sources_ref),
            (owners_any, owners_ref),
        ]
        small = [pltpu.make_async_copy(a, b, sems.at[n]) for n, (a, b) in enumerate(places)]
        for copy in small:
            copy.start()
        for copy in small:
            copy.wait()
        green = [own_ref[:, b * orbitals : (b + 1) * orbitals] for b in range(walkers)]
        walk = lax.axis_index("walk")
        lane = lax.broadcasted_iota(jnp.int32, (1, LANES), 1)
        body = body_ref[...].astype(jnp.float32)
        onebody_ref[...] = jnp.zeros_like(onebody_ref)
        for b in range(walkers):
            total = jnp.sum(green[b].astype(jnp.float32) * body, axis=0, keepdims=True)
            folded = total[:, :LANES]
            for start in range(LANES, orbitals, LANES):
                folded = folded + total[:, start : start + LANES]
            onebody_ref[b : b + 1, :] = folded
        r = lax.broadcasted_iota(jnp.int32, (rows // pair, rows), 0)
        m = lax.broadcasted_iota(jnp.int32, (rows // pair, rows), 1)
        k = lax.broadcasted_iota(jnp.int32, (orbitals, LANES), 0)
        c = lax.broadcasted_iota(jnp.int32, (orbitals, LANES), 1)
        thinned = []
        for b in range(walkers):
            values = green[b]
            thinned.append(
                [
                    jnp.dot(
                        (m == r * pair + h).astype(jnp.bfloat16), values, preferred_element_type=jnp.float32
                    ).astype(jnp.bfloat16)
                    for h in range(pair)
                ]
            )
        for d in range(walk_size):
            target = walk_partner(walk, d, walk_size, False)
            out, top = spots[d]
            panel = jnp.int32(0)
            for p in range(walk_size):
                panel = jnp.where(owners_ref[p] == target, p, panel)
            for b in range(walkers):
                total = jnp.zeros((rows // pair, LANES), jnp.float32)
                for h in range(pair):
                    take = (k == panel * width + c - h * width) & (c >= h * width) & (c < (h + 1) * width)
                    total += jnp.dot(
                        thinned[b][h], take.astype(jnp.bfloat16), preferred_element_type=jnp.float32
                    )
                packs[out][top + b * (rows // pair) : top + (b + 1) * (rows // pair), :] = total.astype(jnp.bfloat16)
        spread = jnp.zeros((vectors, LANES), jnp.float32)
        source = jnp.zeros((1, LANES), jnp.float32)
        corner = lax.broadcasted_iota(jnp.int32, (vectors, vectors), 0) == lax.broadcasted_iota(
            jnp.int32, (vectors, vectors), 1
        )
        for j in range(slots):
            mine = lane % slots == j
            upright = jnp.sum(jnp.where(corner, fields_ref[j : j + 1, :], 0.0), axis=1, keepdims=True)
            spread += jnp.where(mine, upright, 0.0)
            source += jnp.where(mine, sources_ref[j].astype(jnp.float32), 0.0)
        weight = weights_ref[0]
        for j in range(1, weights.shape[0]):
            weight = weight + weights_ref[j]
        table_scr[...] = jnp.zeros_like(table_scr)
        table_scr[:vectors, :] = spread
        table_scr[vectors : vectors + 1, :] = source
        table_scr[vectors + 1 : vectors + 2, :] = jnp.zeros((1, LANES), jnp.float32) + weight
        rest = table_scr[...]
        for n in range(3):
            piece = rest.astype(jnp.bfloat16)
            rest = rest - piece.astype(jnp.float32)
            at = panel_rows + n * table_rows
            for d in range(len(heights)):
                packs[d][at : at + table_rows, :] = piece

    return pl.pallas_call(
        kernel,
        name="pack",
        out_shape=[
            jax.ShapeDtypeStruct((8, LANES), jnp.float32),
        ]
        + [jax.ShapeDtypeStruct((height, LANES), jnp.bfloat16) for height in heights],
        in_specs=[pl.BlockSpec(memory_space=pl.ANY)] * 7,
        out_specs=[vmem()] * (len(heights) + 1),
        scratch_shapes=[
            pltpu.VMEM(own.shape, own.dtype),
            pltpu.VMEM(one_body.shape, one_body.dtype),
            pltpu.VMEM((slots, vectors), jnp.float32),
            pltpu.SMEM(weights.shape, weights.dtype),
            pltpu.SMEM(sources.shape, sources.dtype),
            pltpu.SMEM(owners.shape, owners.dtype),
            pltpu.VMEM((table_rows, LANES), jnp.float32),
            pltpu.SemaphoreType.DMA((6,)),
        ],
        compiler_params=params(PACK_LIMIT),
        cost_estimate=pl.CostEstimate(flops=10**8, bytes_accessed=10**6, transcendentals=0),
    )(own, one_body, fields.T, weights, sources, owners, cholesky_rot)


def walk_partner(walk, d, size, back):
    if size == 4:
        return lax.bitwise_xor(walk, d)
    return lax.rem(walk + (size - d if back else d), size)


def exchange_far(packed):
    size = lax.axis_size("walk")
    if size != 4:
        return lax.ppermute(packed[1], "walk", [(q, (q + 1) % size) for q in range(size)])
    return lax.ppermute(packed[1], "walk", [(q, q ^ 2) for q in range(size)])


def exchange_near(packed, far):
    size = lax.axis_size("walk")
    if size != 4:
        return [
            lax.ppermute(packed[d], "walk", [(q, (q + d) % size) for q in range(size)]) for d in range(2, size)
        ]
    keep, _, near = packed
    panel = far.shape[0] - keep.shape[0]
    return [lax.ppermute(jnp.concatenate([near, far[panel:]], axis=0), "walk", [(q, q ^ 1) for q in range(size)])]


def walk_places(panel, table, size):
    if size != 4:
        return [(d, 0, panel) for d in range(size)]
    return [(0, 0, panel), (2, 0, panel), (1, 0, panel), (2, panel + 2 * table, panel + table)]


def read_table(ref, at, vectors):
    height = table_height(vectors)
    parts = [ref[at + n * height : at + (n + 1) * height, :].astype(jnp.float32) for n in range(3)]
    return parts[0] + (parts[1] + parts[2])


def merge_tables(tables, walk, walk_size, slots, lane):
    total = jnp.zeros_like(tables[0])
    for d, table in enumerate(tables):
        group = walk_partner(walk, d, walk_size, True)
        total += jnp.where(lane // slots == group, table, 0.0)
    return total


def plan_rows(vectors, walkers, walk_size):
    shares = walkers * vectors
    picks = shares + walkers * walk_size
    single = picks + walkers
    return 0, shares, picks, single, single + 1, single + 2, -(-(single + 3) // 8) * 8


def prepare(packs, places, onebody, counts, vectors, slots, walkers):
    walk_size = len(places)
    at_drive, at_share, at_pick, at_single, at_live, at_mean, height = plan_rows(vectors, walkers, walk_size)

    def kernel(counts_ref, onebody_ref, *refs):
        pack_refs, plan_ref = refs[:-1], refs[-1]
        walk = lax.axis_index("walk")
        lane = lax.broadcasted_iota(jnp.int32, (1, LANES), 1)
        all_slots = slots * walk_size
        tables = [read_table(pack_refs[n], at, vectors) for n, _, at in places]
        table = merge_tables(tables, walk, walk_size, slots, lane)
        source = jnp.where(lane < all_slots, table[vectors : vectors + 1, :], -1.0)
        total_weight = tables[0][vectors + 1 : vectors + 2, :]
        for t in tables[1:]:
            total_weight = total_weight + t[vectors + 1 : vectors + 2, :]
        live_count = jnp.zeros((1, LANES), jnp.int32)
        for q in range(walk_size):
            live_count = jnp.where(lane // slots == q, counts_ref[q], live_count)
        live = (lane < all_slots) & (lane % slots < live_count)
        plan_ref[...] = jnp.zeros_like(plan_ref)
        single = jnp.zeros((1, LANES), jnp.float32)
        for b in range(walkers):
            pick = jnp.where(source == (walk * walkers + b).astype(jnp.float32), 1.0, 0.0)
            plan_ref[at_pick + b : at_pick + b + 1, :] = pick
            plan_ref[at_drive + b * vectors : at_drive + (b + 1) * vectors, :] = -root_step * pick * table[:vectors, :]
            single += pick * jnp.sum(onebody_ref[b : b + 1, :], axis=1, keepdims=True)
        plan_ref[at_single : at_single + 1, :] = single
        for d in range(walk_size):
            group = walk_partner(walk, d, walk_size, True)
            for b in range(walkers):
                row = at_share + d * walkers + b
                plan_ref[row : row + 1, :] = jnp.where(
                    source == (group * walkers + b).astype(jnp.float32), 1.0, 0.0
                )
        plan_ref[at_live : at_live + 1, :] = jnp.where(live, 1.0, 0.0)
        plan_ref[at_mean : at_mean + 1, :] = total_weight / (walkers * walk_size)

    return pl.pallas_call(
        kernel,
        name="prepare",
        out_shape=jax.ShapeDtypeStruct((height, LANES), jnp.float32),
        in_specs=[smem()] + [vmem()] * (1 + len(packs)),
        out_specs=vmem(),
        compiler_params=params(),
        cost_estimate=pl.CostEstimate(flops=10**8, bytes_accessed=10**6, transcendentals=0),
    )(counts, onebody, *packs)


def measure(cholesky_rot, total, last, plan, walk_size):
    vectors, orbitals, _ = cholesky_rot.shape
    walkers = last[0].shape[1] // orbitals
    depth = sum(x.shape[0] for x in last)
    targets = walk_size * lax.axis_size("chol")
    whole = total is None
    quads = orbitals // LANES
    at_drive, _, at_pick, at_single, _, _, _ = plan_rows(vectors, walkers, walk_size)

    def fold(x):
        return jnp.sum(x.reshape(-1, 8, LANES), axis=0)

    def kernel(*refs):
        chol_ref, plan_ref = refs[:2]
        last_refs = refs[2 : 2 + len(last)]
        out_ref, tensor_scr = refs[-2:]
        rhs = [
            jnp.concatenate([x[:, b * orbitals : (b + 1) * orbitals] for x in last_refs], axis=0)
            for b in range(walkers)
        ]
        eye = lax.broadcasted_iota(jnp.int32, (LANES, LANES), 0) == lax.broadcasted_iota(
            jnp.int32, (LANES, LANES), 1
        )
        exchange = [jnp.zeros((8, LANES), jnp.float32) for _ in range(walkers)]
        squares = [jnp.zeros((1, 1), jnp.float32) for _ in range(walkers)]
        drive = jnp.zeros((1, LANES), jnp.float32)
        start = 0 if whole else column_start(lax.axis_size("chol") // 2, depth)
        lhs = chol_ref[:, :, pl.ds(start, depth)].reshape(vectors * orbitals, depth)
        for b in range(walkers):
            value = jnp.dot(lhs, rhs[b], preferred_element_type=jnp.float32)
            tensor_scr[b] = value if whole else refs[2 + len(last)][b] + value
        for g in range(vectors):
            top = g * orbitals
            for b in range(walkers):
                diagonal = jnp.zeros((LANES, LANES), jnp.float32)
                for q in range(quads):
                    for p in range(q + 1):
                        one = tensor_scr[
                            b, top + q * LANES : top + (q + 1) * LANES, p * LANES : (p + 1) * LANES
                        ]
                        if p == q:
                            exchange[b] = exchange[b] + fold(one * one.T)
                            diagonal = diagonal + one
                        else:
                            two = tensor_scr[
                                b, top + p * LANES : top + (p + 1) * LANES, q * LANES : (q + 1) * LANES
                            ]
                            exchange[b] = exchange[b] + 2.0 * fold(two * one.T)
                trace = jnp.sum(fold(jnp.where(eye, diagonal, 0.0)), axis=0, keepdims=True)
                trace = jnp.sum(trace, axis=1, keepdims=True)
                squares[b] = squares[b] + trace * trace
                row = at_drive + b * vectors + g
                drive = drive + plan_ref[row : row + 1, :] * trace
        raw = plan_ref[at_single : at_single + 1, :]
        square = jnp.zeros((1, LANES), jnp.float32)
        for b in range(walkers):
            swapped = jnp.sum(jnp.sum(exchange[b], axis=0, keepdims=True), axis=1, keepdims=True)
            pick = plan_ref[at_pick + b : at_pick + b + 1, :]
            raw += pick * (0.5 * squares[b] - 0.5 * swapped)
            square += pick * squares[b]
        power = drive - 0.5 * time_step * square - time_step * raw
        out_ref[...] = jnp.broadcast_to(raw + pltpu.roll(power, LANES // 2, 1), (targets, LANES))

    arrays = list(last) + ([] if whole else [total])
    return pl.pallas_call(
        kernel,
        name="measure",
        out_shape=jax.ShapeDtypeStruct((targets, LANES), jnp.float32),
        in_specs=[vmem()] * (2 + len(arrays)),
        out_specs=vmem(),
        scratch_shapes=[
            pltpu.VMEM((walkers, vectors * orbitals, orbitals), jnp.float32),
        ],
        compiler_params=params(),
        cost_estimate=pl.CostEstimate(
            flops=2 * vectors * orbitals * depth * walkers * orbitals,
            bytes_accessed=2 * vectors * orbitals * depth,
            transcendentals=0,
        ),
    )(cholesky_rot, plan, *arrays)


def finish(stats, plan, packs, places, vectors, slots, walkers):
    walk_size = len(places)
    rows = (packs[0].shape[0] - 3 * table_height(vectors)) // walkers
    _, at_share, at_pick, _, at_live, at_mean, _ = plan_rows(vectors, walkers, walk_size)

    def kernel(stats_ref, plan_ref, *refs):
        pack_refs = refs[: len(packs)]
        energies_ref, weights_ref, density_ref = refs[len(packs) :]
        walk = lax.axis_index("walk")
        total = jnp.sum(stats_ref[...], axis=0, keepdims=True)
        power = pltpu.roll(total, LANES // 2, 1)
        live = plan_ref[at_live : at_live + 1, :] > 0.0
        energies = jnp.where(live, total, 0.0)
        new_weights = jnp.where(
            live, plan_ref[at_mean : at_mean + 1, :] * jnp.exp(jnp.where(live, power, 0.0)), 0.0
        )
        norm = jnp.sum(new_weights, axis=1, keepdims=True)
        shares = jnp.sum(plan_ref[at_share:at_pick, :] * new_weights, axis=1, keepdims=True) / norm
        density = jnp.zeros((rows, LANES), jnp.float32)
        for d, (n, top, _) in enumerate(places):
            for b in range(walkers):
                share = shares[d * walkers + b : d * walkers + b + 1, :]
                density += share * pack_refs[n][top + b * rows : top + (b + 1) * rows, :].astype(jnp.float32)
        density_ref[...] = density
        first = lax.rem(LANES - walk * slots, LANES)
        energies_ref[...] = pltpu.roll(jnp.broadcast_to(energies, (8, LANES)), first, 1)[:1, :slots]
        weights_ref[...] = pltpu.roll(jnp.broadcast_to(new_weights, (8, LANES)), first, 1)[:1, :slots]

    return pl.pallas_call(
        kernel,
        name="finish",
        out_shape=[
            jax.ShapeDtypeStruct((1, slots), jnp.float32),
            jax.ShapeDtypeStruct((1, slots), jnp.float32),
            jax.ShapeDtypeStruct((rows, LANES), jnp.float32),
        ],
        in_specs=[vmem()] * (2 + len(packs)),
        out_specs=[vmem()] * 3,
        compiler_params=params(),
        cost_estimate=pl.CostEstimate(flops=10**6, bytes_accessed=6 * 10**5, transcendentals=128),
    )(stats, plan, *packs)


def per_device(green_rows, cholesky_rot, one_body, fields, weights, sources, counts, owners):
    chol_size = lax.axis_size("chol")
    walk_size = lax.axis_size("walk")
    vectors, slots = fields.shape
    walkers = green_rows.shape[1]
    own = split_walkers(green_rows)
    onebody, *packed = pack(own, one_body, fields, weights, sources, owners, cholesky_rot)
    table = 3 * table_height(vectors)
    places = walk_places(packed[0].shape[0] - table, table, walk_size)

    def do_prepare(packs):
        return prepare(packs, places, onebody, counts, vectors, slots, walkers)

    if chol_size > RING_LIMIT or chol_size % 2 or chol_size < 8:
        far = exchange_far(packed)
        packs = [packed[0], far] + exchange_near(packed, far)
        plan = do_prepare(packs)
        total, last = None, [lax.all_gather(own, "chol", axis=0, tiled=True)]
    else:
        total, last, packs, plan = ring(own, cholesky_rot, onebody, packed, do_prepare)
    stats = measure(cholesky_rot, total, last, plan, walk_size)
    stats = lax.all_to_all(stats, ("chol", "walk"), split_axis=0, concat_axis=0, tiled=True)
    energies, new_weights, density = finish(stats, plan, packs, places, vectors, slots, walkers)
    return energies.reshape(slots), new_weights.reshape(slots), density.reshape(1, density.size)


def solution(mesh):
    return jax.shard_map(
        per_device,
        mesh=mesh,
        in_specs=(
            P("chol", "walk", None),
            P("chol", None, None),
            P("chol", None),
            P("chol", "walk"),
            P("walk"),
            P("walk"),
            P(),
            P(),
        ),
        out_specs=(P("walk"), P("walk"), P("walk", "chol")),
        check_vma=False,
    )
```

```python
import jax
import jax.numpy as jnp
from jax import lax
from jax.experimental import pallas as pl
from jax.experimental.pallas import tpu as pltpu
from jax.sharding import PartitionSpec as P

time_step = 0.02
root_step = 0.02**0.5
LANES = 128
VMEM_LIMIT = 16 * 1024 * 1024
PACK_LIMIT = 54 * 1024 * 1024
ACCUMULATE_LIMIT = 24 * 1024 * 1024
RING_LIMIT = 16


def params(limit=VMEM_LIMIT):
    return pltpu.CompilerParams(vmem_limit_bytes=limit)


def vmem():
    return pl.BlockSpec(memory_space=pltpu.VMEM)


def smem():
    return pl.BlockSpec(memory_space=pltpu.SMEM)


def ring_order(size):
    return [2 * q if q < size // 2 else 2 * (size - 1 - q) + 1 for q in range(size)]


def ring_place(index, size):
    return jnp.where(index % 2 == 0, index // 2, size - 1 - index // 2)


def ring_owner(place, size):
    return jnp.where(place < size // 2, 2 * place, 2 * (size - 1 - place) + 1)


def column_start(shift, rows):
    size = lax.axis_size("chol")
    place = ring_place(lax.axis_index("chol"), size)
    owner = ring_owner(lax.rem(place + shift + size, size), size)
    return pl.multiple_of(owner * rows, rows)


def accumulate(cholesky_rot, shifts, parts, total, mark):
    vectors, orbitals, _ = cholesky_rot.shape
    rows, walkers, _ = parts[0].shape
    size = vectors * orbitals
    arrays = list(parts) + ([] if mark is None else [mark]) + ([] if total is None else [total])

    def kernel(chol_ref, *refs):
        shards = refs[: len(parts)]
        total_ref, mark_ref = refs[len(arrays) :]
        mark_ref[...] = jnp.zeros_like(mark_ref)
        lhs = jnp.concatenate(
            [chol_ref[:, :, pl.ds(column_start(shift, rows), rows)].reshape(size, rows) for shift in shifts], axis=1
        )
        for b in range(walkers):
            rhs = jnp.concatenate([x[:, b, :] for x in shards], axis=0)
            value = jnp.dot(lhs, rhs, preferred_element_type=jnp.float32)
            total_ref[b] = value if total is None else refs[len(arrays) - 1][b] + value

    return pl.pallas_call(
        kernel,
        name="accumulate",
        out_shape=[
            jax.ShapeDtypeStruct((walkers, size, orbitals), jnp.float32),
            jax.ShapeDtypeStruct((8, LANES), jnp.float32),
        ],
        in_specs=[vmem()] * (1 + len(arrays)),
        out_specs=[vmem()] * 2,
        compiler_params=params(ACCUMULATE_LIMIT),
        cost_estimate=pl.CostEstimate(
            flops=2 * len(parts) * size * rows * walkers * orbitals,
            bytes_accessed=2 * len(parts) * size * rows,
            transcendentals=0,
        ),
    )(cholesky_rot, *arrays)


def cut(right, left):
    rows, walkers, orbitals = right.shape
    half = rows // 2

    def kernel(right_ref, left_ref, upper_ref, lower_ref):
        for b in range(walkers):
            at = slice(b * orbitals, (b + 1) * orbitals)
            upper_ref[:, at] = right_ref[:half, b, :]
            lower_ref[:, at] = left_ref[half:, b, :]

    return pl.pallas_call(
        kernel,
        name="cut",
        out_shape=[jax.ShapeDtypeStruct((n, walkers * orbitals), right.dtype) for n in (half, rows - half)],
        in_specs=[vmem()] * 2,
        out_specs=[vmem()] * 2,
        compiler_params=params(),
        cost_estimate=pl.CostEstimate(flops=0, bytes_accessed=4 * right.size, transcendentals=0),
    )(right, left)


def tie(*arrays):
    return lax.optimization_barrier(arrays)


def ring(own, cholesky_rot, onebody, packed, do_prepare):
    size = lax.axis_size("chol")
    rows = own.shape[0]
    order = ring_order(size)
    ahead = [(order[q], order[(q + 1) % size]) for q in range(size)]
    back = [(order[q], order[(q - 1) % size]) for q in range(size)]
    steps = size // 2
    right = left = own
    shifts, parts = [0], [own]
    total = mark = None
    for step in range(1, steps):
        next_right, next_left = lax.ppermute(right, "chol", ahead), lax.ppermute(left, "chol", back)
        if step == 1:
            right, onebody = tie(next_right, onebody)
            left, *packed = tie(next_left, *packed)
        else:
            if step == 2:
                far = exchange_far(packed)
            elif step == 3:
                near = exchange_near(packed, far)
            total, mark = accumulate(cholesky_rot, shifts, parts, total, mark)
            shifts, parts = [], []
            right, mark = tie(next_right, mark)
            left, mark = tie(next_left, mark)
        shifts += [-step, step]
        parts = parts + [right, left]
    upper, lower = cut(right, left)
    last = [lax.ppermute(upper, "chol", ahead), lax.ppermute(lower, "chol", back)]
    mark, *near = tie(mark, *near)
    packs = [packed[0], far] + near
    plan = do_prepare(packs)
    mark, plan = tie(mark, plan)
    total, _ = accumulate(cholesky_rot, shifts, parts, total, mark)
    return total, last, packs, plan


def table_height(vectors):
    return -(-(vectors + 2) // 16) * 16


def pack(own, one_body, fields, weights, sources, owners, cholesky_rot):
    rows, walkers, orbitals = own.shape
    walk_size = lax.axis_size("walk")
    width = orbitals // walk_size
    pair = LANES // width
    vectors, slots = fields.shape
    table_rows = table_height(vectors)
    panel_rows = walkers * (rows // pair)
    both = panel_rows + 3 * table_rows
    if walk_size == 4:
        heights = [both, both + panel_rows, both]
        spots = [(0, 0), (2, 0), (1, 0), (1, both)]
    else:
        heights = [both] * walk_size
        spots = [(d, 0) for d in range(walk_size)]

    def kernel(own_any, body_any, fields_any, weights_any, sources_any, owners_any, chol_any, *refs):
        onebody_ref = refs[0]
        packs = refs[1 : 1 + len(heights)]
        own_ref, body_ref, fields_ref, weights_ref, sources_ref, owners_ref, table_scr, sems = refs[1 + len(heights) :]
        places = [
            (own_any, own_ref),
            (body_any, body_ref),
            (fields_any, fields_ref),
            (weights_any, weights_ref),
            (sources_any, sources_ref),
            (owners_any, owners_ref),
        ]
        small = [pltpu.make_async_copy(a, b, sems.at[n]) for n, (a, b) in enumerate(places)]
        for copy in small:
            copy.start()
        for copy in small:
            copy.wait()
        green = [own_ref[:, b, :] for b in range(walkers)]
        walk = lax.axis_index("walk")
        lane = lax.broadcasted_iota(jnp.int32, (1, LANES), 1)
        body = body_ref[...].astype(jnp.float32)
        onebody_ref[...] = jnp.zeros_like(onebody_ref)
        for b in range(walkers):
            total = jnp.sum(green[b].astype(jnp.float32) * body, axis=0, keepdims=True)
            folded = total[:, :LANES]
            for start in range(LANES, orbitals, LANES):
                folded = folded + total[:, start : start + LANES]
            onebody_ref[b : b + 1, :] = folded
        r = lax.broadcasted_iota(jnp.int32, (rows // pair, rows), 0)
        m = lax.broadcasted_iota(jnp.int32, (rows // pair, rows), 1)
        k = lax.broadcasted_iota(jnp.int32, (orbitals, LANES), 0)
        c = lax.broadcasted_iota(jnp.int32, (orbitals, LANES), 1)
        thinned = []
        for b in range(walkers):
            values = green[b]
            thinned.append(
                [
                    jnp.dot(
                        (m == r * pair + h).astype(jnp.bfloat16), values, preferred_element_type=jnp.float32
                    ).astype(jnp.bfloat16)
                    for h in range(pair)
                ]
            )
        for d in range(walk_size):
            target = walk_partner(walk, d, walk_size, False)
            out, top = spots[d]
            panel = jnp.int32(0)
            for p in range(walk_size):
                panel = jnp.where(owners_ref[p] == target, p, panel)
            for b in range(walkers):
                total = jnp.zeros((rows // pair, LANES), jnp.float32)
                for h in range(pair):
                    take = (k == panel * width + c - h * width) & (c >= h * width) & (c < (h + 1) * width)
                    total += jnp.dot(
                        thinned[b][h], take.astype(jnp.bfloat16), preferred_element_type=jnp.float32
                    )
                packs[out][top + b * (rows // pair) : top + (b + 1) * (rows // pair), :] = total.astype(jnp.bfloat16)
        spread = jnp.zeros((vectors, LANES), jnp.float32)
        source = jnp.zeros((1, LANES), jnp.float32)
        corner = lax.broadcasted_iota(jnp.int32, (vectors, vectors), 0) == lax.broadcasted_iota(
            jnp.int32, (vectors, vectors), 1
        )
        for j in range(slots):
            mine = lane % slots == j
            upright = jnp.sum(jnp.where(corner, fields_ref[j : j + 1, :], 0.0), axis=1, keepdims=True)
            spread += jnp.where(mine, upright, 0.0)
            source += jnp.where(mine, sources_ref[j].astype(jnp.float32), 0.0)
        weight = weights_ref[0]
        for j in range(1, weights.shape[0]):
            weight = weight + weights_ref[j]
        table_scr[...] = jnp.zeros_like(table_scr)
        table_scr[:vectors, :] = spread
        table_scr[vectors : vectors + 1, :] = source
        table_scr[vectors + 1 : vectors + 2, :] = jnp.zeros((1, LANES), jnp.float32) + weight
        rest = table_scr[...]
        for n in range(3):
            piece = rest.astype(jnp.bfloat16)
            rest = rest - piece.astype(jnp.float32)
            at = panel_rows + n * table_rows
            for d in range(len(heights)):
                packs[d][at : at + table_rows, :] = piece

    return pl.pallas_call(
        kernel,
        name="pack",
        out_shape=[
            jax.ShapeDtypeStruct((8, LANES), jnp.float32),
        ]
        + [jax.ShapeDtypeStruct((height, LANES), jnp.bfloat16) for height in heights],
        in_specs=[pl.BlockSpec(memory_space=pl.ANY)] * 7,
        out_specs=[vmem()] * (len(heights) + 1),
        scratch_shapes=[
            pltpu.VMEM(own.shape, own.dtype),
            pltpu.VMEM(one_body.shape, one_body.dtype),
            pltpu.VMEM((slots, vectors), jnp.float32),
            pltpu.SMEM(weights.shape, weights.dtype),
            pltpu.SMEM(sources.shape, sources.dtype),
            pltpu.SMEM(owners.shape, owners.dtype),
            pltpu.VMEM((table_rows, LANES), jnp.float32),
            pltpu.SemaphoreType.DMA((6,)),
        ],
        compiler_params=params(PACK_LIMIT),
        cost_estimate=pl.CostEstimate(flops=10**8, bytes_accessed=10**6, transcendentals=0),
    )(own, one_body, fields.T, weights, sources, owners, cholesky_rot)


def walk_partner(walk, d, size, back):
    if size == 4:
        return lax.bitwise_xor(walk, d)
    return lax.rem(walk + (size - d if back else d), size)


def exchange_far(packed):
    size = lax.axis_size("walk")
    if size != 4:
        return lax.ppermute(packed[1], "walk", [(q, (q + 1) % size) for q in range(size)])
    return lax.ppermute(packed[1], "walk", [(q, q ^ 2) for q in range(size)])


def exchange_near(packed, far):
    size = lax.axis_size("walk")
    if size != 4:
        return [
            lax.ppermute(packed[d], "walk", [(q, (q + d) % size) for q in range(size)]) for d in range(2, size)
        ]
    keep, _, near = packed
    panel = far.shape[0] - keep.shape[0]
    return [lax.ppermute(jnp.concatenate([near, far[panel:]], axis=0), "walk", [(q, q ^ 1) for q in range(size)])]


def walk_places(panel, table, size):
    if size != 4:
        return [(d, 0, panel) for d in range(size)]
    return [(0, 0, panel), (2, 0, panel), (1, 0, panel), (2, panel + 2 * table, panel + table)]


def read_table(ref, at, vectors):
    height = table_height(vectors)
    parts = [ref[at + n * height : at + (n + 1) * height, :].astype(jnp.float32) for n in range(3)]
    return parts[0] + (parts[1] + parts[2])


def merge_tables(tables, walk, walk_size, slots, lane):
    total = jnp.zeros_like(tables[0])
    for d, table in enumerate(tables):
        group = walk_partner(walk, d, walk_size, True)
        total += jnp.where(lane // slots == group, table, 0.0)
    return total


def plan_rows(vectors, walkers, walk_size):
    shares = walkers * vectors
    picks = shares + walkers * walk_size
    single = picks + walkers
    return 0, shares, picks, single, single + 1, single + 2, -(-(single + 3) // 8) * 8


def prepare(packs, places, onebody, counts, vectors, slots, walkers):
    walk_size = len(places)
    at_drive, at_share, at_pick, at_single, at_live, at_mean, height = plan_rows(vectors, walkers, walk_size)

    def kernel(counts_ref, onebody_ref, *refs):
        pack_refs, plan_ref = refs[:-1], refs[-1]
        walk = lax.axis_index("walk")
        lane = lax.broadcasted_iota(jnp.int32, (1, LANES), 1)
        all_slots = slots * walk_size
        tables = [read_table(pack_refs[n], at, vectors) for n, _, at in places]
        table = merge_tables(tables, walk, walk_size, slots, lane)
        source = jnp.where(lane < all_slots, table[vectors : vectors + 1, :], -1.0)
        total_weight = tables[0][vectors + 1 : vectors + 2, :]
        for t in tables[1:]:
            total_weight = total_weight + t[vectors + 1 : vectors + 2, :]
        live_count = jnp.zeros((1, LANES), jnp.int32)
        for q in range(walk_size):
            live_count = jnp.where(lane // slots == q, counts_ref[q], live_count)
        live = (lane < all_slots) & (lane % slots < live_count)
        plan_ref[...] = jnp.zeros_like(plan_ref)
        single = jnp.zeros((1, LANES), jnp.float32)
        for b in range(walkers):
            pick = jnp.where(source == (walk * walkers + b).astype(jnp.float32), 1.0, 0.0)
            plan_ref[at_pick + b : at_pick + b + 1, :] = pick
            plan_ref[at_drive + b * vectors : at_drive + (b + 1) * vectors, :] = -root_step * pick * table[:vectors, :]
            single += pick * jnp.sum(onebody_ref[b : b + 1, :], axis=1, keepdims=True)
        plan_ref[at_single : at_single + 1, :] = single
        for d in range(walk_size):
            group = walk_partner(walk, d, walk_size, True)
            for b in range(walkers):
                row = at_share + d * walkers + b
                plan_ref[row : row + 1, :] = jnp.where(
                    source == (group * walkers + b).astype(jnp.float32), 1.0, 0.0
                )
        plan_ref[at_live : at_live + 1, :] = jnp.where(live, 1.0, 0.0)
        plan_ref[at_mean : at_mean + 1, :] = total_weight / (walkers * walk_size)

    return pl.pallas_call(
        kernel,
        name="prepare",
        out_shape=jax.ShapeDtypeStruct((height, LANES), jnp.float32),
        in_specs=[smem()] + [vmem()] * (1 + len(packs)),
        out_specs=vmem(),
        compiler_params=params(),
        cost_estimate=pl.CostEstimate(flops=10**8, bytes_accessed=10**6, transcendentals=0),
    )(counts, onebody, *packs)


def measure(cholesky_rot, total, last, plan, vectors, walk_size):
    _, orbitals, _ = cholesky_rot.shape
    walkers = last[0].size // (last[0].shape[0] * orbitals)
    depth = sum(x.shape[0] for x in last)
    targets = walk_size * lax.axis_size("chol")
    whole = total is None
    quads = orbitals // LANES
    at_drive, _, at_pick, at_single, _, _, _ = plan_rows(vectors, walkers, walk_size)

    def fold(x):
        return jnp.sum(x.reshape(-1, 8, LANES), axis=0)

    def kernel(*refs):
        chol_ref, plan_ref = refs[:2]
        last_refs = refs[2 : 2 + len(last)]
        out_ref, tensor_scr = refs[-2:]

        def walker_rows(x, b):
            return x[:, b, :] if len(x.shape) == 3 else x[:, b * orbitals : (b + 1) * orbitals]

        rhs = [jnp.concatenate([walker_rows(x, b) for x in last_refs], axis=0) for b in range(walkers)]
        eye = lax.broadcasted_iota(jnp.int32, (LANES, LANES), 0) == lax.broadcasted_iota(
            jnp.int32, (LANES, LANES), 1
        )
        exchange = [jnp.zeros((8, LANES), jnp.float32) for _ in range(walkers)]
        squares = [jnp.zeros((1, 1), jnp.float32) for _ in range(walkers)]
        drive = jnp.zeros((1, LANES), jnp.float32)
        start = 0 if whole else column_start(lax.axis_size("chol") // 2, depth)
        lhs = chol_ref[:, :, pl.ds(start, depth)].reshape(vectors * orbitals, depth)
        for b in range(walkers):
            value = jnp.dot(lhs, rhs[b], preferred_element_type=jnp.float32)
            tensor_scr[b] = value if whole else refs[2 + len(last)][b] + value
        for g in range(vectors):
            top = g * orbitals
            for b in range(walkers):
                diagonal = jnp.zeros((LANES, LANES), jnp.float32)
                for q in range(quads):
                    for p in range(q + 1):
                        one = tensor_scr[
                            b, top + q * LANES : top + (q + 1) * LANES, p * LANES : (p + 1) * LANES
                        ]
                        if p == q:
                            exchange[b] = exchange[b] + fold(one * one.T)
                            diagonal = diagonal + one
                        else:
                            two = tensor_scr[
                                b, top + p * LANES : top + (p + 1) * LANES, q * LANES : (q + 1) * LANES
                            ]
                            exchange[b] = exchange[b] + 2.0 * fold(two * one.T)
                trace = jnp.sum(fold(jnp.where(eye, diagonal, 0.0)), axis=0, keepdims=True)
                trace = jnp.sum(trace, axis=1, keepdims=True)
                squares[b] = squares[b] + trace * trace
                row = at_drive + b * vectors + g
                drive = drive + plan_ref[row : row + 1, :] * trace
        raw = plan_ref[at_single : at_single + 1, :]
        square = jnp.zeros((1, LANES), jnp.float32)
        for b in range(walkers):
            swapped = jnp.sum(jnp.sum(exchange[b], axis=0, keepdims=True), axis=1, keepdims=True)
            pick = plan_ref[at_pick + b : at_pick + b + 1, :]
            raw += pick * (0.5 * squares[b] - 0.5 * swapped)
            square += pick * squares[b]
        power = drive - 0.5 * time_step * square - time_step * raw
        out_ref[...] = jnp.broadcast_to(raw + pltpu.roll(power, LANES // 2, 1), (targets, LANES))

    arrays = list(last) + ([] if whole else [total])
    return pl.pallas_call(
        kernel,
        name="measure",
        out_shape=jax.ShapeDtypeStruct((targets, LANES), jnp.float32),
        in_specs=[vmem()] * (2 + len(arrays)),
        out_specs=vmem(),
        scratch_shapes=[
            pltpu.VMEM((walkers, vectors * orbitals, orbitals), jnp.float32),
        ],
        compiler_params=params(),
        cost_estimate=pl.CostEstimate(
            flops=2 * vectors * orbitals * depth * walkers * orbitals,
            bytes_accessed=2 * vectors * orbitals * depth,
            transcendentals=0,
        ),
    )(cholesky_rot, plan, *arrays)


def finish(stats, plan, packs, places, vectors, slots, walkers):
    walk_size = len(places)
    rows = (packs[0].shape[0] - 3 * table_height(vectors)) // walkers
    _, at_share, at_pick, _, at_live, at_mean, _ = plan_rows(vectors, walkers, walk_size)

    def kernel(stats_ref, plan_ref, *refs):
        pack_refs = refs[: len(packs)]
        energies_ref, weights_ref, density_ref = refs[len(packs) :]
        walk = lax.axis_index("walk")
        total = jnp.sum(stats_ref[...], axis=0, keepdims=True)
        power = pltpu.roll(total, LANES // 2, 1)
        live = plan_ref[at_live : at_live + 1, :] > 0.0
        energies = jnp.where(live, total, 0.0)
        new_weights = jnp.where(
            live, plan_ref[at_mean : at_mean + 1, :] * jnp.exp(jnp.where(live, power, 0.0)), 0.0
        )
        norm = jnp.sum(new_weights, axis=1, keepdims=True)
        shares = jnp.sum(plan_ref[at_share:at_pick, :] * new_weights, axis=1, keepdims=True) / norm
        density = jnp.zeros((rows, LANES), jnp.float32)
        for d, (n, top, _) in enumerate(places):
            for b in range(walkers):
                share = shares[d * walkers + b : d * walkers + b + 1, :]
                density += share * pack_refs[n][top + b * rows : top + (b + 1) * rows, :].astype(jnp.float32)
        density_ref[...] = density
        first = lax.rem(LANES - walk * slots, LANES)
        energies_ref[...] = pltpu.roll(jnp.broadcast_to(energies, (8, LANES)), first, 1)[:1, :slots]
        weights_ref[...] = pltpu.roll(jnp.broadcast_to(new_weights, (8, LANES)), first, 1)[:1, :slots]

    return pl.pallas_call(
        kernel,
        name="finish",
        out_shape=[
            jax.ShapeDtypeStruct((1, slots), jnp.float32),
            jax.ShapeDtypeStruct((1, slots), jnp.float32),
            jax.ShapeDtypeStruct((rows, LANES), jnp.float32),
        ],
        in_specs=[vmem()] * (2 + len(packs)),
        out_specs=[vmem()] * 3,
        compiler_params=params(),
        cost_estimate=pl.CostEstimate(flops=10**6, bytes_accessed=6 * 10**5, transcendentals=128),
    )(stats, plan, *packs)


def per_device(green_rows, cholesky_rot, one_body, fields, weights, sources, counts, owners):
    chol_size = lax.axis_size("chol")
    walk_size = lax.axis_size("walk")
    vectors, slots = fields.shape
    walkers = green_rows.shape[1]
    onebody, *packed = pack(green_rows, one_body, fields, weights, sources, owners, cholesky_rot)
    table = 3 * table_height(vectors)
    places = walk_places(packed[0].shape[0] - table, table, walk_size)

    def do_prepare(packs):
        return prepare(packs, places, onebody, counts, vectors, slots, walkers)

    if chol_size > RING_LIMIT or chol_size % 2 or chol_size < 8:
        far = exchange_far(packed)
        packs = [packed[0], far] + exchange_near(packed, far)
        plan = do_prepare(packs)
        total, last = None, [lax.all_gather(green_rows, "chol", axis=0, tiled=True)]
    else:
        total, last, packs, plan = ring(green_rows, cholesky_rot, onebody, packed, do_prepare)
    stats = measure(cholesky_rot, total, last, plan, vectors, walk_size)
    stats = lax.all_to_all(stats, ("chol", "walk"), split_axis=0, concat_axis=0, tiled=True)
    energies, new_weights, density = finish(stats, plan, packs, places, vectors, slots, walkers)
    return energies.reshape(slots), new_weights.reshape(slots), density.reshape(1, density.size)


def solution(mesh):
    return jax.shard_map(
        per_device,
        mesh=mesh,
        in_specs=(
            P("chol", "walk", None),
            P("chol", None, None),
            P("chol", None),
            P("chol", "walk"),
            P("walk"),
            P("walk"),
            P(),
            P(),
        ),
        out_specs=(P("walk"), P("walk"), P("walk", "chol")),
        check_vma=False,
    )
```

```python
import jax
import jax.numpy as jnp
from jax import lax
from jax.experimental import pallas as pl
from jax.experimental.pallas import tpu as pltpu
from jax.sharding import PartitionSpec as P

time_step = 0.02
root_step = 0.02**0.5
LANES = 128
VMEM_LIMIT = 16 * 1024 * 1024
PACK_LIMIT = 54 * 1024 * 1024
ACCUMULATE_LIMIT = 24 * 1024 * 1024
RING_LIMIT = 16


def params(limit=VMEM_LIMIT):
    return pltpu.CompilerParams(vmem_limit_bytes=limit)


def vmem():
    return pl.BlockSpec(memory_space=pltpu.VMEM)


def smem():
    return pl.BlockSpec(memory_space=pltpu.SMEM)


def ring_order(size):
    return [2 * q if q < size // 2 else 2 * (size - 1 - q) + 1 for q in range(size)]


def ring_place(index, size):
    return jnp.where(index % 2 == 0, index // 2, size - 1 - index // 2)


def ring_owner(place, size):
    return jnp.where(place < size // 2, 2 * place, 2 * (size - 1 - place) + 1)


def column_start(shift, rows):
    size = lax.axis_size("chol")
    place = ring_place(lax.axis_index("chol"), size)
    owner = ring_owner(lax.rem(place + shift + size, size), size)
    return pl.multiple_of(owner * rows, rows)


def accumulate(cholesky_rot, shifts, parts, total, mark):
    vectors, orbitals, _ = cholesky_rot.shape
    rows, walkers, _ = parts[0].shape
    size = vectors * orbitals
    arrays = list(parts) + ([] if mark is None else [mark]) + ([] if total is None else [total])

    def kernel(chol_ref, *refs):
        shards = refs[: len(parts)]
        total_ref, mark_ref = refs[len(arrays) :]
        mark_ref[...] = jnp.zeros_like(mark_ref)
        lhs = jnp.concatenate(
            [chol_ref[:, :, pl.ds(column_start(shift, rows), rows)].reshape(size, rows) for shift in shifts], axis=1
        )
        for b in range(walkers):
            rhs = jnp.concatenate([x[:, b, :] for x in shards], axis=0)
            value = jnp.dot(lhs, rhs, preferred_element_type=jnp.float32)
            total_ref[b] = value if total is None else refs[len(arrays) - 1][b] + value

    return pl.pallas_call(
        kernel,
        name="accumulate",
        out_shape=[
            jax.ShapeDtypeStruct((walkers, size, orbitals), jnp.float32),
            jax.ShapeDtypeStruct((8, LANES), jnp.float32),
        ],
        in_specs=[vmem()] * (1 + len(arrays)),
        out_specs=[vmem()] * 2,
        compiler_params=params(ACCUMULATE_LIMIT),
        cost_estimate=pl.CostEstimate(
            flops=2 * len(parts) * size * rows * walkers * orbitals,
            bytes_accessed=2 * len(parts) * size * rows,
            transcendentals=0,
        ),
    )(cholesky_rot, *arrays)


def cut(right, left):
    rows, walkers, orbitals = right.shape
    half = rows // 2

    def kernel(right_ref, left_ref, upper_ref, lower_ref):
        for b in range(walkers):
            at = slice(b * orbitals, (b + 1) * orbitals)
            upper_ref[:, at] = right_ref[:half, b, :]
            lower_ref[:, at] = left_ref[half:, b, :]

    return pl.pallas_call(
        kernel,
        name="cut",
        out_shape=[jax.ShapeDtypeStruct((n, walkers * orbitals), right.dtype) for n in (half, rows - half)],
        in_specs=[vmem()] * 2,
        out_specs=[vmem()] * 2,
        compiler_params=params(),
        cost_estimate=pl.CostEstimate(flops=0, bytes_accessed=4 * right.size, transcendentals=0),
    )(right, left)


def tie(*arrays):
    return lax.optimization_barrier(arrays)


def ring(own, cholesky_rot, onebody, packed, do_prepare):
    size = lax.axis_size("chol")
    rows = own.shape[0]
    order = ring_order(size)
    ahead = [(order[q], order[(q + 1) % size]) for q in range(size)]
    back = [(order[q], order[(q - 1) % size]) for q in range(size)]
    steps = size // 2
    right = left = own
    shifts, parts = [0], [own]
    total = mark = None
    for step in range(1, steps):
        next_right, next_left = lax.ppermute(right, "chol", ahead), lax.ppermute(left, "chol", back)
        if step == 1:
            right, onebody = tie(next_right, onebody)
            left, *packed = tie(next_left, *packed)
        else:
            if step == 2:
                far = exchange_far(packed)
            elif step == 3:
                near = exchange_near(packed, far)
            total, mark = accumulate(cholesky_rot, shifts, parts, total, mark)
            shifts, parts = [], []
            if step == 2:
                left, mark = tie(next_left, mark)
                right, mark = tie(next_right, mark)
            else:
                right, mark = tie(next_right, mark)
                left, mark = tie(next_left, mark)
        shifts += [-step, step]
        parts = parts + [right, left]
    upper, lower = cut(right, left)
    last = [lax.ppermute(upper, "chol", ahead), lax.ppermute(lower, "chol", back)]
    mark, *near = tie(mark, *near)
    packs = [packed[0], far] + near
    plan = do_prepare(packs)
    mark, plan = tie(mark, plan)
    total, _ = accumulate(cholesky_rot, shifts, parts, total, mark)
    return total, last, packs, plan


def table_height(vectors):
    return -(-(vectors + 2) // 16) * 16


def pack(own, one_body, fields, weights, sources, owners, cholesky_rot):
    rows, walkers, orbitals = own.shape
    walk_size = lax.axis_size("walk")
    width = orbitals // walk_size
    pair = LANES // width
    vectors, slots = fields.shape
    table_rows = table_height(vectors)
    panel_rows = walkers * (rows // pair)
    both = panel_rows + 3 * table_rows
    if walk_size == 4:
        heights = [both, both + panel_rows, both]
        spots = [(0, 0), (2, 0), (1, 0), (1, both)]
    else:
        heights = [both] * walk_size
        spots = [(d, 0) for d in range(walk_size)]

    def kernel(own_any, body_any, fields_any, weights_any, sources_any, owners_any, chol_any, *refs):
        onebody_ref = refs[0]
        packs = refs[1 : 1 + len(heights)]
        own_ref, body_ref, fields_ref, weights_ref, sources_ref, owners_ref, table_scr, sems = refs[1 + len(heights) :]
        places = [
            (own_any, own_ref),
            (body_any, body_ref),
            (fields_any, fields_ref),
            (weights_any, weights_ref),
            (sources_any, sources_ref),
            (owners_any, owners_ref),
        ]
        small = [pltpu.make_async_copy(a, b, sems.at[n]) for n, (a, b) in enumerate(places)]
        for copy in small:
            copy.start()
        for copy in small:
            copy.wait()
        green = [own_ref[:, b, :] for b in range(walkers)]
        walk = lax.axis_index("walk")
        lane = lax.broadcasted_iota(jnp.int32, (1, LANES), 1)
        body = body_ref[...].astype(jnp.float32)
        onebody_ref[...] = jnp.zeros_like(onebody_ref)
        for b in range(walkers):
            total = jnp.sum(green[b].astype(jnp.float32) * body, axis=0, keepdims=True)
            folded = total[:, :LANES]
            for start in range(LANES, orbitals, LANES):
                folded = folded + total[:, start : start + LANES]
            onebody_ref[b : b + 1, :] = folded
        r = lax.broadcasted_iota(jnp.int32, (rows // pair, rows), 0)
        m = lax.broadcasted_iota(jnp.int32, (rows // pair, rows), 1)
        k = lax.broadcasted_iota(jnp.int32, (orbitals, LANES), 0)
        c = lax.broadcasted_iota(jnp.int32, (orbitals, LANES), 1)
        thinned = []
        for b in range(walkers):
            values = green[b]
            thinned.append(
                [
                    jnp.dot(
                        (m == r * pair + h).astype(jnp.bfloat16), values, preferred_element_type=jnp.float32
                    ).astype(jnp.bfloat16)
                    for h in range(pair)
                ]
            )
        for d in range(walk_size):
            target = walk_partner(walk, d, walk_size, False)
            out, top = spots[d]
            panel = jnp.int32(0)
            for p in range(walk_size):
                panel = jnp.where(owners_ref[p] == target, p, panel)
            for b in range(walkers):
                total = jnp.zeros((rows // pair, LANES), jnp.float32)
                for h in range(pair):
                    take = (k == panel * width + c - h * width) & (c >= h * width) & (c < (h + 1) * width)
                    total += jnp.dot(
                        thinned[b][h], take.astype(jnp.bfloat16), preferred_element_type=jnp.float32
                    )
                packs[out][top + b * (rows // pair) : top + (b + 1) * (rows // pair), :] = total.astype(jnp.bfloat16)
        spread = jnp.zeros((vectors, LANES), jnp.float32)
        source = jnp.zeros((1, LANES), jnp.float32)
        corner = lax.broadcasted_iota(jnp.int32, (vectors, vectors), 0) == lax.broadcasted_iota(
            jnp.int32, (vectors, vectors), 1
        )
        for j in range(slots):
            mine = lane % slots == j
            upright = jnp.sum(jnp.where(corner, fields_ref[j : j + 1, :], 0.0), axis=1, keepdims=True)
            spread += jnp.where(mine, upright, 0.0)
            source += jnp.where(mine, sources_ref[j].astype(jnp.float32), 0.0)
        weight = weights_ref[0]
        for j in range(1, weights.shape[0]):
            weight = weight + weights_ref[j]
        table_scr[...] = jnp.zeros_like(table_scr)
        table_scr[:vectors, :] = spread
        table_scr[vectors : vectors + 1, :] = source
        table_scr[vectors + 1 : vectors + 2, :] = jnp.zeros((1, LANES), jnp.float32) + weight
        rest = table_scr[...]
        for n in range(3):
            piece = rest.astype(jnp.bfloat16)
            rest = rest - piece.astype(jnp.float32)
            at = panel_rows + n * table_rows
            for d in range(len(heights)):
                packs[d][at : at + table_rows, :] = piece

    return pl.pallas_call(
        kernel,
        name="pack",
        out_shape=[
            jax.ShapeDtypeStruct((8, LANES), jnp.float32),
        ]
        + [jax.ShapeDtypeStruct((height, LANES), jnp.bfloat16) for height in heights],
        in_specs=[pl.BlockSpec(memory_space=pl.ANY)] * 7,
        out_specs=[vmem()] * (len(heights) + 1),
        scratch_shapes=[
            pltpu.VMEM(own.shape, own.dtype),
            pltpu.VMEM(one_body.shape, one_body.dtype),
            pltpu.VMEM((slots, vectors), jnp.float32),
            pltpu.SMEM(weights.shape, weights.dtype),
            pltpu.SMEM(sources.shape, sources.dtype),
            pltpu.SMEM(owners.shape, owners.dtype),
            pltpu.VMEM((table_rows, LANES), jnp.float32),
            pltpu.SemaphoreType.DMA((6,)),
        ],
        compiler_params=params(PACK_LIMIT),
        cost_estimate=pl.CostEstimate(flops=10**8, bytes_accessed=10**6, transcendentals=0),
    )(own, one_body, fields.T, weights, sources, owners, cholesky_rot)


def walk_partner(walk, d, size, back):
    if size == 4:
        return lax.bitwise_xor(walk, d)
    return lax.rem(walk + (size - d if back else d), size)


def exchange_far(packed):
    size = lax.axis_size("walk")
    if size != 4:
        return lax.ppermute(packed[1], "walk", [(q, (q + 1) % size) for q in range(size)])
    return lax.ppermute(packed[1], "walk", [(q, q ^ 2) for q in range(size)])


def exchange_near(packed, far):
    size = lax.axis_size("walk")
    if size != 4:
        return [
            lax.ppermute(packed[d], "walk", [(q, (q + d) % size) for q in range(size)]) for d in range(2, size)
        ]
    keep, _, near = packed
    panel = far.shape[0] - keep.shape[0]
    return [lax.ppermute(jnp.concatenate([near, far[panel:]], axis=0), "walk", [(q, q ^ 1) for q in range(size)])]


def walk_places(panel, table, size):
    if size != 4:
        return [(d, 0, panel) for d in range(size)]
    return [(0, 0, panel), (2, 0, panel), (1, 0, panel), (2, panel + 2 * table, panel + table)]


def read_table(ref, at, vectors):
    height = table_height(vectors)
    parts = [ref[at + n * height : at + (n + 1) * height, :].astype(jnp.float32) for n in range(3)]
    return parts[0] + (parts[1] + parts[2])


def merge_tables(tables, walk, walk_size, slots, lane):
    total = jnp.zeros_like(tables[0])
    for d, table in enumerate(tables):
        group = walk_partner(walk, d, walk_size, True)
        total += jnp.where(lane // slots == group, table, 0.0)
    return total


def plan_rows(vectors, walkers, walk_size):
    shares = walkers * vectors
    picks = shares + walkers * walk_size
    single = picks + walkers
    return 0, shares, picks, single, single + 1, single + 2, -(-(single + 3) // 8) * 8


def prepare(packs, places, onebody, counts, vectors, slots, walkers):
    walk_size = len(places)
    at_drive, at_share, at_pick, at_single, at_live, at_mean, height = plan_rows(vectors, walkers, walk_size)

    def kernel(counts_ref, onebody_ref, *refs):
        pack_refs, plan_ref = refs[:-1], refs[-1]
        walk = lax.axis_index("walk")
        lane = lax.broadcasted_iota(jnp.int32, (1, LANES), 1)
        all_slots = slots * walk_size
        tables = [read_table(pack_refs[n], at, vectors) for n, _, at in places]
        table = merge_tables(tables, walk, walk_size, slots, lane)
        source = jnp.where(lane < all_slots, table[vectors : vectors + 1, :], -1.0)
        total_weight = tables[0][vectors + 1 : vectors + 2, :]
        for t in tables[1:]:
            total_weight = total_weight + t[vectors + 1 : vectors + 2, :]
        live_count = jnp.zeros((1, LANES), jnp.int32)
        for q in range(walk_size):
            live_count = jnp.where(lane // slots == q, counts_ref[q], live_count)
        live = (lane < all_slots) & (lane % slots < live_count)
        plan_ref[...] = jnp.zeros_like(plan_ref)
        single = jnp.zeros((1, LANES), jnp.float32)
        for b in range(walkers):
            pick = jnp.where(source == (walk * walkers + b).astype(jnp.float32), 1.0, 0.0)
            plan_ref[at_pick + b : at_pick + b + 1, :] = pick
            plan_ref[at_drive + b * vectors : at_drive + (b + 1) * vectors, :] = -root_step * pick * table[:vectors, :]
            single += pick * jnp.sum(onebody_ref[b : b + 1, :], axis=1, keepdims=True)
        plan_ref[at_single : at_single + 1, :] = single
        for d in range(walk_size):
            group = walk_partner(walk, d, walk_size, True)
            for b in range(walkers):
                row = at_share + d * walkers + b
                plan_ref[row : row + 1, :] = jnp.where(
                    source == (group * walkers + b).astype(jnp.float32), 1.0, 0.0
                )
        plan_ref[at_live : at_live + 1, :] = jnp.where(live, 1.0, 0.0)
        plan_ref[at_mean : at_mean + 1, :] = total_weight / (walkers * walk_size)

    return pl.pallas_call(
        kernel,
        name="prepare",
        out_shape=jax.ShapeDtypeStruct((height, LANES), jnp.float32),
        in_specs=[smem()] + [vmem()] * (1 + len(packs)),
        out_specs=vmem(),
        compiler_params=params(),
        cost_estimate=pl.CostEstimate(flops=10**8, bytes_accessed=10**6, transcendentals=0),
    )(counts, onebody, *packs)


def measure(cholesky_rot, total, last, plan, vectors, walk_size):
    _, orbitals, _ = cholesky_rot.shape
    walkers = last[0].size // (last[0].shape[0] * orbitals)
    depth = sum(x.shape[0] for x in last)
    targets = walk_size * lax.axis_size("chol")
    whole = total is None
    quads = orbitals // LANES
    at_drive, _, at_pick, at_single, _, _, _ = plan_rows(vectors, walkers, walk_size)

    def fold(x):
        return jnp.sum(x.reshape(-1, 8, LANES), axis=0)

    def kernel(*refs):
        chol_ref, plan_ref = refs[:2]
        last_refs = refs[2 : 2 + len(last)]
        out_ref, tensor_scr = refs[-2:]

        def walker_rows(x, b):
            return x[:, b, :] if len(x.shape) == 3 else x[:, b * orbitals : (b + 1) * orbitals]

        rhs = [jnp.concatenate([walker_rows(x, b) for x in last_refs], axis=0) for b in range(walkers)]
        eye = lax.broadcasted_iota(jnp.int32, (LANES, LANES), 0) == lax.broadcasted_iota(
            jnp.int32, (LANES, LANES), 1
        )
        exchange = [jnp.zeros((8, LANES), jnp.float32) for _ in range(walkers)]
        squares = [jnp.zeros((1, 1), jnp.float32) for _ in range(walkers)]
        drive = jnp.zeros((1, LANES), jnp.float32)
        start = 0 if whole else column_start(lax.axis_size("chol") // 2, depth)
        lhs = chol_ref[:, :, pl.ds(start, depth)].reshape(vectors * orbitals, depth)
        for b in range(walkers):
            value = jnp.dot(lhs, rhs[b], preferred_element_type=jnp.float32)
            tensor_scr[b] = value if whole else refs[2 + len(last)][b] + value
        for g in range(vectors):
            top = g * orbitals
            for b in range(walkers):
                diagonal = jnp.zeros((LANES, LANES), jnp.float32)
                for q in range(quads):
                    for p in range(q + 1):
                        one = tensor_scr[
                            b, top + q * LANES : top + (q + 1) * LANES, p * LANES : (p + 1) * LANES
                        ]
                        if p == q:
                            exchange[b] = exchange[b] + fold(one * one.T)
                            diagonal = diagonal + one
                        else:
                            two = tensor_scr[
                                b, top + p * LANES : top + (p + 1) * LANES, q * LANES : (q + 1) * LANES
                            ]
                            exchange[b] = exchange[b] + 2.0 * fold(two * one.T)
                trace = jnp.sum(fold(jnp.where(eye, diagonal, 0.0)), axis=0, keepdims=True)
                trace = jnp.sum(trace, axis=1, keepdims=True)
                squares[b] = squares[b] + trace * trace
                row = at_drive + b * vectors + g
                drive = drive + plan_ref[row : row + 1, :] * trace
        raw = plan_ref[at_single : at_single + 1, :]
        square = jnp.zeros((1, LANES), jnp.float32)
        for b in range(walkers):
            swapped = jnp.sum(jnp.sum(exchange[b], axis=0, keepdims=True), axis=1, keepdims=True)
            pick = plan_ref[at_pick + b : at_pick + b + 1, :]
            raw += pick * (0.5 * squares[b] - 0.5 * swapped)
            square += pick * squares[b]
        power = drive - 0.5 * time_step * square - time_step * raw
        out_ref[...] = jnp.broadcast_to(raw + pltpu.roll(power, LANES // 2, 1), (targets, LANES))

    arrays = list(last) + ([] if whole else [total])
    return pl.pallas_call(
        kernel,
        name="measure",
        out_shape=jax.ShapeDtypeStruct((targets, LANES), jnp.float32),
        in_specs=[vmem()] * (2 + len(arrays)),
        out_specs=vmem(),
        scratch_shapes=[
            pltpu.VMEM((walkers, vectors * orbitals, orbitals), jnp.float32),
        ],
        compiler_params=params(),
        cost_estimate=pl.CostEstimate(
            flops=2 * vectors * orbitals * depth * walkers * orbitals,
            bytes_accessed=2 * vectors * orbitals * depth,
            transcendentals=0,
        ),
    )(cholesky_rot, plan, *arrays)


def finish(stats, plan, packs, places, vectors, slots, walkers):
    walk_size = len(places)
    rows = (packs[0].shape[0] - 3 * table_height(vectors)) // walkers
    _, at_share, at_pick, _, at_live, at_mean, _ = plan_rows(vectors, walkers, walk_size)

    def kernel(stats_ref, plan_ref, *refs):
        pack_refs = refs[: len(packs)]
        energies_ref, weights_ref, density_ref = refs[len(packs) :]
        walk = lax.axis_index("walk")
        total = jnp.sum(stats_ref[...], axis=0, keepdims=True)
        power = pltpu.roll(total, LANES // 2, 1)
        live = plan_ref[at_live : at_live + 1, :] > 0.0
        energies = jnp.where(live, total, 0.0)
        new_weights = jnp.where(
            live, plan_ref[at_mean : at_mean + 1, :] * jnp.exp(jnp.where(live, power, 0.0)), 0.0
        )
        norm = jnp.sum(new_weights, axis=1, keepdims=True)
        shares = jnp.sum(plan_ref[at_share:at_pick, :] * new_weights, axis=1, keepdims=True) / norm
        density = jnp.zeros((rows, LANES), jnp.float32)
        for d, (n, top, _) in enumerate(places):
            for b in range(walkers):
                share = shares[d * walkers + b : d * walkers + b + 1, :]
                density += share * pack_refs[n][top + b * rows : top + (b + 1) * rows, :].astype(jnp.float32)
        density_ref[...] = density
        first = lax.rem(LANES - walk * slots, LANES)
        energies_ref[...] = pltpu.roll(jnp.broadcast_to(energies, (8, LANES)), first, 1)[:1, :slots]
        weights_ref[...] = pltpu.roll(jnp.broadcast_to(new_weights, (8, LANES)), first, 1)[:1, :slots]

    return pl.pallas_call(
        kernel,
        name="finish",
        out_shape=[
            jax.ShapeDtypeStruct((1, slots), jnp.float32),
            jax.ShapeDtypeStruct((1, slots), jnp.float32),
            jax.ShapeDtypeStruct((rows, LANES), jnp.float32),
        ],
        in_specs=[vmem()] * (2 + len(packs)),
        out_specs=[vmem()] * 3,
        compiler_params=params(),
        cost_estimate=pl.CostEstimate(flops=10**6, bytes_accessed=6 * 10**5, transcendentals=128),
    )(stats, plan, *packs)


def per_device(green_rows, cholesky_rot, one_body, fields, weights, sources, counts, owners):
    chol_size = lax.axis_size("chol")
    walk_size = lax.axis_size("walk")
    vectors, slots = fields.shape
    walkers = green_rows.shape[1]
    onebody, *packed = pack(green_rows, one_body, fields, weights, sources, owners, cholesky_rot)
    table = 3 * table_height(vectors)
    places = walk_places(packed[0].shape[0] - table, table, walk_size)

    def do_prepare(packs):
        return prepare(packs, places, onebody, counts, vectors, slots, walkers)

    if chol_size > RING_LIMIT or chol_size % 2 or chol_size < 8:
        far = exchange_far(packed)
        packs = [packed[0], far] + exchange_near(packed, far)
        plan = do_prepare(packs)
        total, last = None, [lax.all_gather(green_rows, "chol", axis=0, tiled=True)]
    else:
        total, last, packs, plan = ring(green_rows, cholesky_rot, onebody, packed, do_prepare)
    stats = measure(cholesky_rot, total, last, plan, vectors, walk_size)
    stats = lax.all_to_all(stats, ("chol", "walk"), split_axis=0, concat_axis=0, tiled=True)
    energies, new_weights, density = finish(stats, plan, packs, places, vectors, slots, walkers)
    return energies.reshape(slots), new_weights.reshape(slots), density.reshape(1, density.size)


def solution(mesh):
    return jax.shard_map(
        per_device,
        mesh=mesh,
        in_specs=(
            P("chol", "walk", None),
            P("chol", None, None),
            P("chol", None),
            P("chol", "walk"),
            P("walk"),
            P("walk"),
            P(),
            P(),
        ),
        out_specs=(P("walk"), P("walk"), P("walk", "chol")),
        check_vma=False,
    )
```

```python
import jax
import jax.numpy as jnp
from jax import lax
from jax.experimental import pallas as pl
from jax.experimental.pallas import tpu as pltpu
from jax.sharding import PartitionSpec as P

time_step = 0.02
root_step = 0.02**0.5
LANES = 128
VMEM_LIMIT = 16 * 1024 * 1024
PACK_LIMIT = 54 * 1024 * 1024
ACCUMULATE_LIMIT = 24 * 1024 * 1024
RING_LIMIT = 16


def params(limit=VMEM_LIMIT):
    return pltpu.CompilerParams(vmem_limit_bytes=limit)


def vmem():
    return pl.BlockSpec(memory_space=pltpu.VMEM)


def smem():
    return pl.BlockSpec(memory_space=pltpu.SMEM)


def ring_order(size):
    return [2 * q if q < size // 2 else 2 * (size - 1 - q) + 1 for q in range(size)]


def ring_place(index, size):
    return jnp.where(index % 2 == 0, index // 2, size - 1 - index // 2)


def ring_owner(place, size):
    return jnp.where(place < size // 2, 2 * place, 2 * (size - 1 - place) + 1)


def column_start(shift, rows):
    size = lax.axis_size("chol")
    place = ring_place(lax.axis_index("chol"), size)
    owner = ring_owner(lax.rem(place + shift + size, size), size)
    return pl.multiple_of(owner * rows, rows)


def accumulate(cholesky_rot, shifts, parts, total, mark):
    vectors, orbitals, _ = cholesky_rot.shape
    rows, walkers, _ = parts[0].shape
    size = vectors * orbitals
    arrays = list(parts) + ([] if mark is None else [mark]) + ([] if total is None else [total])

    def kernel(chol_ref, *refs):
        shards = refs[: len(parts)]
        total_ref, mark_ref = refs[len(arrays) :]
        mark_ref[...] = jnp.zeros_like(mark_ref)
        lhs = jnp.concatenate(
            [chol_ref[:, :, pl.ds(column_start(shift, rows), rows)].reshape(size, rows) for shift in shifts], axis=1
        )
        for b in range(walkers):
            rhs = jnp.concatenate([x[:, b, :] for x in shards], axis=0)
            value = jnp.dot(lhs, rhs, preferred_element_type=jnp.float32)
            total_ref[b] = value if total is None else refs[len(arrays) - 1][b] + value

    return pl.pallas_call(
        kernel,
        name="accumulate",
        out_shape=[
            jax.ShapeDtypeStruct((walkers, size, orbitals), jnp.float32),
            jax.ShapeDtypeStruct((8, LANES), jnp.float32),
        ],
        in_specs=[vmem()] * (1 + len(arrays)),
        out_specs=[vmem()] * 2,
        compiler_params=params(ACCUMULATE_LIMIT),
        cost_estimate=pl.CostEstimate(
            flops=2 * len(parts) * size * rows * walkers * orbitals,
            bytes_accessed=2 * len(parts) * size * rows,
            transcendentals=0,
        ),
    )(cholesky_rot, *arrays)


def cut(right, left):
    rows, walkers, orbitals = right.shape
    half = rows // 2

    def kernel(right_ref, left_ref, upper_ref, lower_ref):
        for b in range(walkers):
            at = slice(b * orbitals, (b + 1) * orbitals)
            upper_ref[:, at] = right_ref[:half, b, :]
            lower_ref[:, at] = left_ref[half:, b, :]

    return pl.pallas_call(
        kernel,
        name="cut",
        out_shape=[jax.ShapeDtypeStruct((n, walkers * orbitals), right.dtype) for n in (half, rows - half)],
        in_specs=[vmem()] * 2,
        out_specs=[vmem()] * 2,
        compiler_params=params(),
        cost_estimate=pl.CostEstimate(flops=0, bytes_accessed=4 * right.size, transcendentals=0),
    )(right, left)


def tie(*arrays):
    return lax.optimization_barrier(arrays)


def ring(own, cholesky_rot, onebody, packed, do_prepare):
    size = lax.axis_size("chol")
    rows = own.shape[0]
    order = ring_order(size)
    ahead = [(order[q], order[(q + 1) % size]) for q in range(size)]
    back = [(order[q], order[(q - 1) % size]) for q in range(size)]
    steps = size // 2
    right = left = own
    shifts, parts = [0], [own]
    total = mark = None
    for step in range(1, steps):
        next_right, next_left = lax.ppermute(right, "chol", ahead), lax.ppermute(left, "chol", back)
        if step == 1:
            right, onebody = tie(next_right, onebody)
            left, *packed = tie(next_left, *packed)
        else:
            if step == 2:
                far = exchange_far(packed)
            elif step == 3:
                near = exchange_near(packed, far)
            total, mark = accumulate(cholesky_rot, shifts, parts, total, mark)
            shifts, parts = [], []
            right, mark = tie(next_right, mark)
            left, mark = tie(next_left, mark)
        shifts += [-step, step]
        parts = parts + [right, left]
    upper, lower = cut(right, left)
    last = [lax.ppermute(upper, "chol", ahead), lax.ppermute(lower, "chol", back)]
    mark, *near = tie(mark, *near)
    packs = [packed[0], far] + near
    plan = do_prepare(packs)
    mark, plan = tie(mark, plan)
    total, _ = accumulate(cholesky_rot, shifts, parts, total, mark)
    return total, last, packs, plan


def table_height(vectors):
    return -(-(vectors + 2) // 16) * 16


def pack(own, one_body, fields, weights, sources, owners, cholesky_rot):
    rows, walkers, orbitals = own.shape
    walk_size = lax.axis_size("walk")
    width = orbitals // walk_size
    pair = LANES // width
    vectors, slots = fields.shape
    table_rows = table_height(vectors)
    panel_rows = walkers * (rows // pair)
    both = panel_rows + 3 * table_rows
    if walk_size == 4:
        heights = [both, both + panel_rows, both]
        spots = [(0, 0), (2, 0), (1, 0), (1, both)]
    else:
        heights = [both] * walk_size
        spots = [(d, 0) for d in range(walk_size)]

    def kernel(own_any, body_any, fields_any, weights_any, sources_any, owners_any, chol_any, *refs):
        onebody_ref = refs[0]
        packs = refs[1 : 1 + len(heights)]
        own_ref, body_ref, fields_ref, weights_ref, sources_ref, owners_ref, table_scr, sems = refs[1 + len(heights) :]
        places = [
            (own_any, own_ref),
            (body_any, body_ref),
            (fields_any, fields_ref),
            (weights_any, weights_ref),
            (sources_any, sources_ref),
            (owners_any, owners_ref),
        ]
        small = [pltpu.make_async_copy(a, b, sems.at[n]) for n, (a, b) in enumerate(places)]
        for copy in small:
            copy.start()
        for copy in small:
            copy.wait()
        green = [own_ref[:, b, :] for b in range(walkers)]
        walk = lax.axis_index("walk")
        lane = lax.broadcasted_iota(jnp.int32, (1, LANES), 1)
        body = body_ref[...].astype(jnp.float32)
        onebody_ref[...] = jnp.zeros_like(onebody_ref)
        for b in range(walkers):
            total = jnp.sum(green[b].astype(jnp.float32) * body, axis=0, keepdims=True)
            folded = total[:, :LANES]
            for start in range(LANES, orbitals, LANES):
                folded = folded + total[:, start : start + LANES]
            onebody_ref[b : b + 1, :] = folded
        r = lax.broadcasted_iota(jnp.int32, (rows // pair, rows), 0)
        m = lax.broadcasted_iota(jnp.int32, (rows // pair, rows), 1)
        k = lax.broadcasted_iota(jnp.int32, (orbitals, LANES), 0)
        c = lax.broadcasted_iota(jnp.int32, (orbitals, LANES), 1)
        thinned = []
        for b in range(walkers):
            values = green[b]
            thinned.append(
                [
                    jnp.dot(
                        (m == r * pair + h).astype(jnp.bfloat16), values, preferred_element_type=jnp.float32
                    ).astype(jnp.bfloat16)
                    for h in range(pair)
                ]
            )
        for d in range(walk_size):
            target = walk_partner(walk, d, walk_size, False)
            out, top = spots[d]
            panel = jnp.int32(0)
            for p in range(walk_size):
                panel = jnp.where(owners_ref[p] == target, p, panel)
            for b in range(walkers):
                total = jnp.zeros((rows // pair, LANES), jnp.float32)
                for h in range(pair):
                    take = (k == panel * width + c - h * width) & (c >= h * width) & (c < (h + 1) * width)
                    total += jnp.dot(
                        thinned[b][h], take.astype(jnp.bfloat16), preferred_element_type=jnp.float32
                    )
                packs[out][top + b * (rows // pair) : top + (b + 1) * (rows // pair), :] = total.astype(jnp.bfloat16)
        spread = jnp.zeros((vectors, LANES), jnp.float32)
        source = jnp.zeros((1, LANES), jnp.float32)
        corner = lax.broadcasted_iota(jnp.int32, (vectors, vectors), 0) == lax.broadcasted_iota(
            jnp.int32, (vectors, vectors), 1
        )
        for j in range(slots):
            mine = lane % slots == j
            upright = jnp.sum(jnp.where(corner, fields_ref[j : j + 1, :], 0.0), axis=1, keepdims=True)
            spread += jnp.where(mine, upright, 0.0)
            source += jnp.where(mine, sources_ref[j].astype(jnp.float32), 0.0)
        weight = weights_ref[0]
        for j in range(1, weights.shape[0]):
            weight = weight + weights_ref[j]
        table_scr[...] = jnp.zeros_like(table_scr)
        table_scr[:vectors, :] = spread
        table_scr[vectors : vectors + 1, :] = source
        table_scr[vectors + 1 : vectors + 2, :] = jnp.zeros((1, LANES), jnp.float32) + weight
        rest = table_scr[...]
        for n in range(3):
            piece = rest.astype(jnp.bfloat16)
            rest = rest - piece.astype(jnp.float32)
            at = panel_rows + n * table_rows
            for d in range(len(heights)):
                packs[d][at : at + table_rows, :] = piece

    return pl.pallas_call(
        kernel,
        name="pack",
        out_shape=[
            jax.ShapeDtypeStruct((8, LANES), jnp.float32),
        ]
        + [jax.ShapeDtypeStruct((height, LANES), jnp.bfloat16) for height in heights],
        in_specs=[pl.BlockSpec(memory_space=pl.ANY)] * 7,
        out_specs=[vmem()] * (len(heights) + 1),
        scratch_shapes=[
            pltpu.VMEM(own.shape, own.dtype),
            pltpu.VMEM(one_body.shape, one_body.dtype),
            pltpu.VMEM((slots, vectors), jnp.float32),
            pltpu.SMEM(weights.shape, weights.dtype),
            pltpu.SMEM(sources.shape, sources.dtype),
            pltpu.SMEM(owners.shape, owners.dtype),
            pltpu.VMEM((table_rows, LANES), jnp.float32),
            pltpu.SemaphoreType.DMA((6,)),
        ],
        compiler_params=params(PACK_LIMIT),
        cost_estimate=pl.CostEstimate(flops=10**8, bytes_accessed=10**6, transcendentals=0),
    )(own, one_body, fields.T, weights, sources, owners, cholesky_rot)


def walk_partner(walk, d, size, back):
    if size == 4:
        return lax.bitwise_xor(walk, d)
    return lax.rem(walk + (size - d if back else d), size)


def exchange_far(packed):
    size = lax.axis_size("walk")
    if size != 4:
        return lax.ppermute(packed[1], "walk", [(q, (q + 1) % size) for q in range(size)])
    return lax.ppermute(packed[1], "walk", [(q, q ^ 2) for q in range(size)])


def exchange_near(packed, far):
    size = lax.axis_size("walk")
    if size != 4:
        return [
            lax.ppermute(packed[d], "walk", [(q, (q + d) % size) for q in range(size)]) for d in range(2, size)
        ]
    keep, _, near = packed
    panel = far.shape[0] - keep.shape[0]
    return [lax.ppermute(jnp.concatenate([near, far[panel:]], axis=0), "walk", [(q, q ^ 1) for q in range(size)])]


def walk_places(panel, table, size):
    if size != 4:
        return [(d, 0, panel) for d in range(size)]
    return [(0, 0, panel), (2, 0, panel), (1, 0, panel), (2, panel + 2 * table, panel + table)]


def read_table(ref, at, vectors):
    height = table_height(vectors)
    parts = [ref[at + n * height : at + (n + 1) * height, :].astype(jnp.float32) for n in range(3)]
    return parts[0] + (parts[1] + parts[2])


def merge_tables(tables, walk, walk_size, slots, lane):
    total = jnp.zeros_like(tables[0])
    for d, table in enumerate(tables):
        group = walk_partner(walk, d, walk_size, True)
        total += jnp.where(lane // slots == group, table, 0.0)
    return total


def plan_rows(vectors, walkers, walk_size):
    shares = walkers * vectors
    picks = shares + walkers * walk_size
    single = picks + walkers
    return 0, shares, picks, single, single + 1, single + 2, -(-(single + 3) // 8) * 8


def prepare(packs, places, onebody, counts, vectors, slots, walkers):
    walk_size = len(places)
    at_drive, at_share, at_pick, at_single, at_live, at_mean, height = plan_rows(vectors, walkers, walk_size)

    def kernel(counts_ref, onebody_ref, *refs):
        pack_refs, plan_ref = refs[:-1], refs[-1]
        walk = lax.axis_index("walk")
        lane = lax.broadcasted_iota(jnp.int32, (1, LANES), 1)
        all_slots = slots * walk_size
        tables = [read_table(pack_refs[n], at, vectors) for n, _, at in places]
        table = merge_tables(tables, walk, walk_size, slots, lane)
        source = jnp.where(lane < all_slots, table[vectors : vectors + 1, :], -1.0)
        total_weight = tables[0][vectors + 1 : vectors + 2, :]
        for t in tables[1:]:
            total_weight = total_weight + t[vectors + 1 : vectors + 2, :]
        live_count = jnp.zeros((1, LANES), jnp.int32)
        for q in range(walk_size):
            live_count = jnp.where(lane // slots == q, counts_ref[q], live_count)
        live = (lane < all_slots) & (lane % slots < live_count)
        plan_ref[...] = jnp.zeros_like(plan_ref)
        single = jnp.zeros((1, LANES), jnp.float32)
        for b in range(walkers):
            pick = jnp.where(source == (walk * walkers + b).astype(jnp.float32), 1.0, 0.0)
            plan_ref[at_pick + b : at_pick + b + 1, :] = pick
            plan_ref[at_drive + b * vectors : at_drive + (b + 1) * vectors, :] = -root_step * pick * table[:vectors, :]
            single += pick * jnp.sum(onebody_ref[b : b + 1, :], axis=1, keepdims=True)
        plan_ref[at_single : at_single + 1, :] = single
        for d in range(walk_size):
            group = walk_partner(walk, d, walk_size, True)
            for b in range(walkers):
                row = at_share + d * walkers + b
                plan_ref[row : row + 1, :] = jnp.where(
                    source == (group * walkers + b).astype(jnp.float32), 1.0, 0.0
                )
        plan_ref[at_live : at_live + 1, :] = jnp.where(live, 1.0, 0.0)
        plan_ref[at_mean : at_mean + 1, :] = total_weight / (walkers * walk_size)

    return pl.pallas_call(
        kernel,
        name="prepare",
        out_shape=jax.ShapeDtypeStruct((height, LANES), jnp.float32),
        in_specs=[smem()] + [vmem()] * (1 + len(packs)),
        out_specs=vmem(),
        compiler_params=params(),
        cost_estimate=pl.CostEstimate(flops=10**8, bytes_accessed=10**6, transcendentals=0),
    )(counts, onebody, *packs)


def measure(cholesky_rot, total, last, plan, vectors, walk_size):
    _, orbitals, _ = cholesky_rot.shape
    walkers = last[0].size // (last[0].shape[0] * orbitals)
    depth = sum(x.shape[0] for x in last)
    targets = walk_size * lax.axis_size("chol")
    whole = total is None
    quads = orbitals // LANES
    at_drive, _, at_pick, at_single, _, _, _ = plan_rows(vectors, walkers, walk_size)

    def fold(x):
        return jnp.sum(x.reshape(-1, 8, LANES), axis=0)

    def kernel(*refs):
        chol_ref, plan_ref = refs[:2]
        last_refs = refs[2 : 2 + len(last)]
        out_ref, tensor_scr = refs[-2:]

        def walker_rows(x, b):
            return x[:, b, :] if len(x.shape) == 3 else x[:, b * orbitals : (b + 1) * orbitals]

        rhs = [jnp.concatenate([walker_rows(x, b) for x in last_refs], axis=0) for b in range(walkers)]
        eye = lax.broadcasted_iota(jnp.int32, (LANES, LANES), 0) == lax.broadcasted_iota(
            jnp.int32, (LANES, LANES), 1
        )
        exchange = [jnp.zeros((8, LANES), jnp.float32) for _ in range(walkers)]
        crossed = [jnp.zeros((8, LANES), jnp.float32) for _ in range(walkers)]
        squares = [jnp.zeros((1, 1), jnp.float32) for _ in range(walkers)]
        drive = jnp.zeros((1, LANES), jnp.float32)
        start = 0 if whole else column_start(lax.axis_size("chol") // 2, depth)
        lhs = chol_ref[:, :, pl.ds(start, depth)].reshape(vectors * orbitals, depth)
        for b in range(walkers):
            value = jnp.dot(lhs, rhs[b], preferred_element_type=jnp.float32)
            tensor_scr[b] = value if whole else refs[2 + len(last)][b] + value
        for g in range(vectors):
            top = g * orbitals
            for b in range(walkers):
                diagonal = jnp.zeros((LANES, LANES), jnp.float32)
                for q in range(quads):
                    for p in range(q + 1):
                        one = tensor_scr[
                            b, top + q * LANES : top + (q + 1) * LANES, p * LANES : (p + 1) * LANES
                        ]
                        if p == q:
                            exchange[b] = exchange[b] + fold(one * one.T)
                            diagonal = diagonal + one
                        else:
                            two = tensor_scr[
                                b, top + p * LANES : top + (p + 1) * LANES, q * LANES : (q + 1) * LANES
                            ]
                            crossed[b] = crossed[b] + fold(two * one.T)
                trace = jnp.sum(fold(jnp.where(eye, diagonal, 0.0)), axis=0, keepdims=True)
                trace = jnp.sum(trace, axis=1, keepdims=True)
                squares[b] = squares[b] + trace * trace
                row = at_drive + b * vectors + g
                drive = drive + plan_ref[row : row + 1, :] * trace
        raw = plan_ref[at_single : at_single + 1, :]
        square = jnp.zeros((1, LANES), jnp.float32)
        for b in range(walkers):
            both = exchange[b] + 2.0 * crossed[b]
            swapped = jnp.sum(jnp.sum(both, axis=0, keepdims=True), axis=1, keepdims=True)
            pick = plan_ref[at_pick + b : at_pick + b + 1, :]
            raw += pick * (0.5 * squares[b] - 0.5 * swapped)
            square += pick * squares[b]
        power = drive - 0.5 * time_step * square - time_step * raw
        out_ref[...] = jnp.broadcast_to(raw + pltpu.roll(power, LANES // 2, 1), (targets, LANES))

    arrays = list(last) + ([] if whole else [total])
    return pl.pallas_call(
        kernel,
        name="measure",
        out_shape=jax.ShapeDtypeStruct((targets, LANES), jnp.float32),
        in_specs=[vmem()] * (2 + len(arrays)),
        out_specs=vmem(),
        scratch_shapes=[
            pltpu.VMEM((walkers, vectors * orbitals, orbitals), jnp.float32),
        ],
        compiler_params=params(),
        cost_estimate=pl.CostEstimate(
            flops=2 * vectors * orbitals * depth * walkers * orbitals,
            bytes_accessed=2 * vectors * orbitals * depth,
            transcendentals=0,
        ),
    )(cholesky_rot, plan, *arrays)


def finish(stats, plan, packs, places, vectors, slots, walkers):
    walk_size = len(places)
    rows = (packs[0].shape[0] - 3 * table_height(vectors)) // walkers
    _, at_share, at_pick, _, at_live, at_mean, _ = plan_rows(vectors, walkers, walk_size)

    def kernel(stats_ref, plan_ref, *refs):
        pack_refs = refs[: len(packs)]
        energies_ref, weights_ref, density_ref = refs[len(packs) :]
        walk = lax.axis_index("walk")
        total = jnp.sum(stats_ref[...], axis=0, keepdims=True)
        power = pltpu.roll(total, LANES // 2, 1)
        live = plan_ref[at_live : at_live + 1, :] > 0.0
        energies = jnp.where(live, total, 0.0)
        new_weights = jnp.where(
            live, plan_ref[at_mean : at_mean + 1, :] * jnp.exp(jnp.where(live, power, 0.0)), 0.0
        )
        norm = jnp.sum(new_weights, axis=1, keepdims=True)
        shares = jnp.sum(plan_ref[at_share:at_pick, :] * new_weights, axis=1, keepdims=True) / norm
        density = jnp.zeros((rows, LANES), jnp.float32)
        for d, (n, top, _) in enumerate(places):
            for b in range(walkers):
                share = shares[d * walkers + b : d * walkers + b + 1, :]
                density += share * pack_refs[n][top + b * rows : top + (b + 1) * rows, :].astype(jnp.float32)
        density_ref[...] = density
        first = lax.rem(LANES - walk * slots, LANES)
        energies_ref[...] = pltpu.roll(jnp.broadcast_to(energies, (8, LANES)), first, 1)[:1, :slots]
        weights_ref[...] = pltpu.roll(jnp.broadcast_to(new_weights, (8, LANES)), first, 1)[:1, :slots]

    return pl.pallas_call(
        kernel,
        name="finish",
        out_shape=[
            jax.ShapeDtypeStruct((1, slots), jnp.float32),
            jax.ShapeDtypeStruct((1, slots), jnp.float32),
            jax.ShapeDtypeStruct((rows, LANES), jnp.float32),
        ],
        in_specs=[vmem()] * (2 + len(packs)),
        out_specs=[vmem()] * 3,
        compiler_params=params(),
        cost_estimate=pl.CostEstimate(flops=10**6, bytes_accessed=6 * 10**5, transcendentals=128),
    )(stats, plan, *packs)


def per_device(green_rows, cholesky_rot, one_body, fields, weights, sources, counts, owners):
    chol_size = lax.axis_size("chol")
    walk_size = lax.axis_size("walk")
    vectors, slots = fields.shape
    walkers = green_rows.shape[1]
    onebody, *packed = pack(green_rows, one_body, fields, weights, sources, owners, cholesky_rot)
    table = 3 * table_height(vectors)
    places = walk_places(packed[0].shape[0] - table, table, walk_size)

    def do_prepare(packs):
        return prepare(packs, places, onebody, counts, vectors, slots, walkers)

    if chol_size > RING_LIMIT or chol_size % 2 or chol_size < 8:
        far = exchange_far(packed)
        packs = [packed[0], far] + exchange_near(packed, far)
        plan = do_prepare(packs)
        total, last = None, [lax.all_gather(green_rows, "chol", axis=0, tiled=True)]
    else:
        total, last, packs, plan = ring(green_rows, cholesky_rot, onebody, packed, do_prepare)
    stats = measure(cholesky_rot, total, last, plan, vectors, walk_size)
    stats = lax.all_to_all(stats, ("chol", "walk"), split_axis=0, concat_axis=0, tiled=True)
    energies, new_weights, density = finish(stats, plan, packs, places, vectors, slots, walkers)
    return energies.reshape(slots), new_weights.reshape(slots), density.reshape(1, density.size)


def solution(mesh):
    return jax.shard_map(
        per_device,
        mesh=mesh,
        in_specs=(
            P("chol", "walk", None),
            P("chol", None, None),
            P("chol", None),
            P("chol", "walk"),
            P("walk"),
            P("walk"),
            P(),
            P(),
        ),
        out_specs=(P("walk"), P("walk"), P("walk", "chol")),
        check_vma=False,
    )
```
